32 devices in a mesh: dp: 16 (over z, y, core), mp: 2 (over x).
Axes of the slice: x: 2, y: 2, z: 4, core: 2. Of those that a mesh axis runs over, the one named last changes fastest.
Arguments:
- cell_input: bfloat16 [8192, 512], P(('dp', 'mp')), may hold values from -6 to 6
- lengths: int32 [32], P(('dp', 'mp')), may hold values from 64 to 256, as said below
- out_grad: bfloat16 [8192, 512], P(('dp', 'mp')), may hold values from -6 to 6
- norm_params: bfloat16 [4, 2, 512], replicated, may hold values from -0.9 to 1.5, as said below
- gated_weight: bfloat16 [512, 1024], replicated, may hold values from -0.25 to 0.25
- gated_bias: bfloat16 [1024], replicated, may hold values from -3 to 3
- left_weight: bfloat16 [512, 2048], P(None, 'mp'), may hold values from -0.25 to 0.25
- left_bias: bfloat16 [2048], P('mp'), may hold values from -3.6 to 3.6
- conv_weight: bfloat16 [3, 512, 256], replicated, may hold values from -0.15625 to 0.15625
- conv_bias: bfloat16 [256], replicated, may hold values from -3 to 3
- inner_norm: bfloat16 [2, 2048], P(None, 'mp'), may hold values from -0.9 to 1.5, as said below
- depth_weight: bfloat16 [9, 2048], P(None, 'mp'), may hold values from -2 to 2
- point_weight: bfloat16 [2048, 256], P('mp'), may hold values from -0.125 to 0.125
- point_bias: bfloat16 [256], replicated, may hold values from -3 to 3
- project_weight: bfloat16 [512, 1536], replicated, may hold values from -0.25 to 0.25
- project_bias: bfloat16 [2, 512], replicated, may hold values from -3 to 3
- output_weight: bfloat16 [512, 512], replicated, may hold values from -2 to 2
- output_bias: bfloat16 [512], replicated, may hold values from -3 to 3
- expand_weight: bfloat16 [512, 2048], P(None, 'mp'), may hold values from -0.25 to 0.25
- expand_bias: bfloat16 [2048], P('mp'), may hold values from -3 to 3
- shrink_weight: bfloat16 [2048, 512], P('mp'), may hold values from -0.125 to 0.125
- shrink_bias: bfloat16 [512], replicated, may hold values from -3 to 3
Outputs:
- cell_output: bfloat16 [8192, 512], P(('dp', 'mp'))
- input_grad: float32 [8192, 512], P(('dp', 'mp'))
- grad_norm_params: float32 [4, 2, 512], replicated
- grad_gated_weight: float32 [512, 1024], replicated
- grad_gated_bias: float32 [1024], replicated
- grad_left_weight: float32 [512, 2048], P(None, 'mp')
- grad_left_bias: float32 [2048], P('mp')
- grad_conv_weight: float32 [3, 512, 256], replicated
- grad_conv_bias: float32 [256], replicated
- grad_inner_norm: float32 [2, 2048], P(None, 'mp')
- grad_depth_weight: float32 [9, 2048], P(None, 'mp')
- grad_point_weight: float32 [2048, 256], P('mp')
- grad_point_bias: float32 [256], replicated
- grad_project_weight: float32 [512, 1536], replicated
- grad_project_bias: float32 [2, 512], replicated
- grad_output_weight: float32 [512, 512], replicated
- grad_output_bias: float32 [512], replicated
- grad_expand_weight: float32 [512, 2048], P(None, 'mp')
- grad_expand_bias: float32 [2048], P('mp')
- grad_shrink_weight: float32 [2048, 512], P('mp')
- grad_shrink_bias: float32 [512], replicated
The draws below stay inside these ranges and needn't reach their ends.
Inputs may be any that keep to these rules, and one draw needn't show every extreme that they name: Positions below lengths[r] of row r are real tokens, the others padding; some row is full in every draw. `norm_params`: index 0 of the second dimension holds gains, index 1 biases. `inner_norm`: index 0 holds gains, index 1 biases.
All inputs are finite; a program needn't handle non-finite values.
Results may differ from the reference program's by a relative error of at most 0.02.
Values may be sent and summed in bfloat16 or wider, within the bound.
No kernel may reach another device: no remote copies, remote signals or barrier semaphores. Data moves between devices by JAX's collectives and lax.ppermute only.
A program may use at most 192 MiB of HBM per device.

```python
import math
import jax
import jax.numpy as jnp
from jax import lax

D = 512
HEADS = 8
FF = 2048
SEQ = 256
HALF = 256
ROWS = 32
TOKENS = 8192


def draw_lengths(key, part):
    key = jax.random.fold_in(key, 11)
    first, second = jax.random.split(key)
    drawn = jax.random.randint(first, (ROWS,), SEQ // 4, SEQ + 1)
    chosen = jax.random.randint(second, (), 0, ROWS)
    return jnp.where(jnp.arange(ROWS) == chosen, SEQ, drawn).astype(jnp.int32)


def draw_norm_params(key, part):
    key = jax.random.fold_in(key, 12)
    first, second = jax.random.split(key)
    gains = 1.0 + 0.2 * jax.random.truncated_normal(first, -2.5, 2.5, (4, 1, D), jnp.float32)
    biases = 0.3 * jax.random.truncated_normal(second, -3.0, 3.0, (4, 1, D), jnp.float32)
    return jnp.concatenate([gains, biases], 1).astype(jnp.bfloat16)


def draw_inner_norm(key, part):
    key = jax.random.fold_in(key, 13)
    first, second = jax.random.split(key)
    gains = 1.0 + 0.2 * jax.random.truncated_normal(first, -2.5, 2.5, (1, FF), jnp.float32)
    biases = 0.3 * jax.random.truncated_normal(second, -3.0, 3.0, (1, FF), jnp.float32)
    return jnp.concatenate([gains, biases], 0).astype(jnp.bfloat16)


def draw_left_bias(key, part):
    key = jax.random.fold_in(key, 14)
    channel = jnp.arange(FF, dtype=jnp.float32) / FF
    noise = jax.random.truncated_normal(key, -3.0, 3.0, (FF,), jnp.float32)
    ramp = 0.4 * jnp.exp(math.log(3.0) * channel)
    return (noise * ramp).astype(jnp.bfloat16)


def level_of(key, extent, cuts, least, high):
    factor_of = 1.0
    for axis_at, parts in cuts:
        heights = jax.random.uniform(jax.random.fold_in(jax.random.fold_in(key, 6), axis_at), (parts,), jnp.float32, least / len(cuts), high / len(cuts))
        factor_of = factor_of * jnp.repeat(jnp.exp(heights), extent[axis_at] // parts).reshape((-1,) + (1,) * (len(extent) - 1 - axis_at))
    return factor_of


def bell_draw(own_key, dims, width, limit, pieces=(), kind=jnp.bfloat16):
    factor_of = level_of(own_key, dims, pieces, -0.22, 0.18) if pieces else 1.0
    entries = jax.random.normal(own_key, dims, jnp.float32) * width * factor_of
    return jnp.minimum(jnp.maximum(entries, -limit), limit).astype(kind)


def setup_inputs(seed: int = 0) -> dict:
    seeds = jax.random.split(jax.random.key(seed), 23)
    cell_input = bell_draw(seeds[0], (TOKENS, D), 1.0, 6.0, ((0, 32),))
    lengths = draw_lengths(jax.random.fold_in(seeds[22], 71), 0)
    out_grad = bell_draw(seeds[2], (TOKENS, D), 1.0, 6.0, ((0, 32),))
    norm_params = draw_norm_params(jax.random.fold_in(seeds[22], 71), 0)
    gated_weight = bell_draw(seeds[4], (D, 2 * D), D ** -0.5, 0.25)
    gated_bias = bell_draw(seeds[5], (2 * D,), 0.3, 3.0)
    left_weight = bell_draw(seeds[6], (D, FF), D ** -0.5, 0.25, ((1, 2),))
    left_bias = draw_left_bias(jax.random.fold_in(seeds[22], 71), 0)
    conv_weight = bell_draw(seeds[8], (3, D, HALF), (3 * D) ** -0.5, 0.15625)
    conv_bias = bell_draw(seeds[9], (HALF,), 0.3, 3.0)
    inner_norm = draw_inner_norm(jax.random.fold_in(seeds[22], 71), 0)
    depth_weight = bell_draw(seeds[11], (9, FF), 9 ** -0.5, 2.0, ((1, 2),))
    point_weight = bell_draw(seeds[12], (FF, HALF), FF ** -0.5, 0.125, ((0, 2),))
    point_bias = bell_draw(seeds[13], (HALF,), 0.3, 3.0)
    project_weight = bell_draw(seeds[14], (D, 3 * D), D ** -0.5, 0.25)
    project_bias = bell_draw(seeds[15], (2, D), 0.3, 3.0)
    output_weight = bell_draw(seeds[16], (D, D), (max(1, 4 * D // SEQ)) ** -0.5, 2.0)
    output_bias = bell_draw(seeds[17], (D,), 0.3, 3.0)
    expand_weight = bell_draw(seeds[18], (D, FF), D ** -0.5, 0.25, ((1, 2),))
    expand_bias = bell_draw(seeds[19], (FF,), 0.3, 3.0, ((0, 2),))
    shrink_weight = bell_draw(seeds[20], (FF, D), FF ** -0.5, 0.125, ((0, 2),))
    shrink_bias = bell_draw(seeds[21], (D,), 0.3, 3.0)
    return {"cell_input": cell_input, "lengths": lengths, "out_grad": out_grad, "norm_params": norm_params, "gated_weight": gated_weight, "gated_bias": gated_bias, "left_weight": left_weight, "left_bias": left_bias, "conv_weight": conv_weight, "conv_bias": conv_bias, "inner_norm": inner_norm, "depth_weight": depth_weight, "point_weight": point_weight, "point_bias": point_bias, "project_weight": project_weight, "project_bias": project_bias, "output_weight": output_weight, "output_bias": output_bias, "expand_weight": expand_weight, "expand_bias": expand_bias, "shrink_weight": shrink_weight, "shrink_bias": shrink_bias}


EPS = 1e-06

@jax.custom_vjp
def low(v):
    return lax.optimization_barrier(v.astype(jnp.bfloat16)).astype(jnp.float32)

@jax.custom_vjp
def low_back(v):
    return v

def low_keep(v):
    return (low(v), None)

def low_pass(kept, grad):
    return (grad,)

def back_keep(v):
    return (v, None)

def back_low(kept, grad):
    return (low(grad),)
low.defvjp(low_keep, low_pass)
low_back.defvjp(back_keep, back_low)

def product(left, right):
    return jnp.dot(left, right, precision=lax.Precision.HIGHEST)

def shift_rows(values, offset):
    channels = values.shape[1]
    framed = values.reshape(-1, SEQ, channels)
    if offset > 0:
        framed = jnp.pad(framed[:, offset:], ((0, 0), (0, offset), (0, 0)))
    elif offset < 0:
        framed = jnp.pad(framed[:, :offset], ((0, 0), (-offset, 0), (0, 0)))
    return framed.reshape(-1, channels)

def layer_norm(values, gain, bias):
    centre = lax.optimization_barrier(jnp.mean(values, -1, keepdims=True))
    centered = values - centre
    variance = lax.optimization_barrier(jnp.mean(centered * centered, -1, keepdims=True))
    return centered * lax.rsqrt(variance + EPS) * gain + bias

def inner_layer_norm(values, gain, bias):
    centre = lax.optimization_barrier(jnp.mean(values, -1, keepdims=True))
    square = lax.optimization_barrier(jnp.mean(values * values, -1, keepdims=True))
    return (values - centre) * lax.rsqrt(square - centre * centre + EPS) * gain + bias

def attention(queries, keys, values, keep_rows):
    row_count = queries.shape[0] // SEQ
    head_size = D // HEADS
    shape = (row_count, SEQ, HEADS, head_size)
    scores = jnp.einsum('rqhd,rkhd->rhqk', queries.reshape(shape), keys.reshape(shape), precision=lax.Precision.HIGHEST) * head_size ** (-0.5)
    scores = low_back(jnp.where(keep_rows.reshape(row_count, 1, 1, SEQ) > 0, scores, -1000000000.0))
    probs = low(jax.nn.softmax(scores, axis=-1))
    mixed = jnp.einsum('rhqk,rkhd->rqhd', probs, values.reshape(shape), precision=lax.Precision.HIGHEST)
    return mixed.reshape(-1, D)

def cell(weights, start, keep_rows):
    norms, gated_w, gated_b, left_w, left_b, conv_w, conv_b, inner_n, depth_w, point_w, point_b, project_w, project_b, output_w, output_b, expand_w, expand_b, shrink_w, shrink_b = weights
    first = low(layer_norm(start, norms[0, 0], norms[0, 1]))
    gated = low_back(product(first, gated_w) + gated_b)
    resid_one = start + gated[:, :D] * jax.nn.sigmoid(gated[:, D:])
    second = low(layer_norm(resid_one, norms[1, 0], norms[1, 1]) * keep_rows[:, None])
    left_pre = low_back(product(second, left_w) + left_b)
    stacked = jnp.concatenate([shift_rows(second, -1), second, shift_rows(second, 1)], 1)
    right_pre = low_back(product(stacked, conv_w.reshape(3 * D, HALF)) + conv_b)
    right = low(jax.nn.silu(right_pre))
    mixed = jax.nn.silu(left_pre) + jnp.pad(right, ((0, 0), (0, FF - HALF)))
    third = inner_layer_norm(mixed, inner_n[0], inner_n[1]) * keep_rows[:, None]
    depth = jnp.zeros_like(third)
    for tap in range(9):
        depth = depth + shift_rows(third, tap - 4) * depth_w[tap]
    depth = low(depth)
    sep = low_back(product(depth, point_w) + point_b)
    resid_two = resid_one + jnp.pad(sep, ((0, 0), (0, D - HALF)))
    fourth = low(layer_norm(resid_two, norms[2, 0], norms[2, 1]))
    projected = product(fourth, project_w)
    queries = low(low_back(projected[:, :D] + project_b[0]))
    keys = low(low_back(projected[:, D:2 * D]))
    values = low(low_back(projected[:, 2 * D:] + project_b[1]))
    attended = low(low_back(attention(queries, keys, values, keep_rows)))
    resid_three = resid_two + low_back(product(attended, output_w) + output_b)
    fifth = low(layer_norm(resid_three, norms[3, 0], norms[3, 1]))
    hidden = low(jax.nn.silu(low_back(product(fifth, expand_w) + expand_b)))
    return resid_three + low_back(product(hidden, shrink_w) + shrink_b)

def reference(cell_input, lengths, out_grad, norm_params, gated_weight, gated_bias, left_weight, left_bias, conv_weight, conv_bias, inner_norm, depth_weight, point_weight, point_bias, project_weight, project_bias, output_weight, output_bias, expand_weight, expand_bias, shrink_weight, shrink_bias):
    weights = tuple((item.astype(jnp.float32) for item in (norm_params, gated_weight, gated_bias, left_weight, left_bias, conv_weight, conv_bias, inner_norm, depth_weight, point_weight, point_bias, project_weight, project_bias, output_weight, output_bias, expand_weight, expand_bias, shrink_weight, shrink_bias)))
    positions = jnp.arange(SEQ, dtype=jnp.int32)
    keep = (positions[None, :] < lengths[:, None]).astype(jnp.float32)
    group = math.gcd(ROWS, 16)
    blocks = ROWS // group
    inputs = cell_input.astype(jnp.float32).reshape(blocks, group * SEQ, D)
    cotangents = out_grad.astype(jnp.float32).reshape(blocks, group * SEQ, D)
    keeps = keep.reshape(blocks, group * SEQ)

    def step(totals, item):
        block_input, block_grad, block_keep = item
        out_value, pull = jax.vjp(lambda params, start: cell(params, start, block_keep), weights, block_input)
        weight_grads, start_grads = pull(block_grad)
        totals = jax.tree.map(lambda total, extra: total + extra, totals, weight_grads)
        return (totals, (out_value.astype(jnp.bfloat16), start_grads))
    zeros = jax.tree.map(jnp.zeros_like, weights)
    totals, (outputs, start_grads) = lax.scan(step, zeros, (inputs, cotangents, keeps))
    return (outputs.reshape(TOKENS, D), start_grads.reshape(TOKENS, D), totals[0], totals[1], totals[2], totals[3], totals[4], totals[5], totals[6], totals[7], totals[8], totals[9], totals[10], totals[11], totals[12], totals[13], totals[14], totals[15], totals[16], totals[17], totals[18])
```

```python
import jax
import jax.numpy as jnp
from jax import lax
from jax.sharding import PartitionSpec as P

HEADS = 8
SEQ = 256
EPS = 1e-06
LOW = jnp.bfloat16
F32 = jnp.float32


def as_low(values):
    return values.astype(LOW)


def matmul(left, right):
    return jnp.dot(left, right, preferred_element_type=F32)


def left_turned(left, right):
    return lax.dot_general(left, right, (((0,), (0,)), ((), ())), preferred_element_type=F32)


def right_turned(left, right):
    return lax.dot_general(left, right, (((1,), (1,)), ((), ())), preferred_element_type=F32)


def shift_rows(values, offset):
    channels = values.shape[1]
    framed = values.reshape(-1, SEQ, channels)
    if offset > 0:
        framed = jnp.pad(framed[:, offset:], ((0, 0), (0, offset), (0, 0)))
    elif offset < 0:
        framed = jnp.pad(framed[:, :offset], ((0, 0), (-offset, 0), (0, 0)))
    return framed.reshape(-1, channels)


def silu_slope(values):
    sigma = jax.nn.sigmoid(values)
    return sigma * (1.0 + values * (1.0 - sigma))


def layer_norm(values, gain, bias):
    centre = jnp.mean(values, -1, keepdims=True)
    centered = values - centre
    variance = jnp.mean(centered * centered, -1, keepdims=True)
    rstd = lax.rsqrt(variance + EPS)
    normed = centered * rstd
    return (normed * gain + bias, normed, rstd)


def norm_back(grad_out, normed, rstd, gain):
    scaled = grad_out * gain
    first_mean = jnp.mean(scaled, -1, keepdims=True)
    second_mean = jnp.mean(scaled * normed, -1, keepdims=True)
    grad_in = rstd * (scaled - first_mean - normed * second_mean)
    return (grad_in, jnp.stack([jnp.sum(grad_out * normed, 0), jnp.sum(grad_out, 0)]))


def scores_of(query_heads, key_heads, keep_rows, head_size):
    row_count = query_heads.shape[0]
    scores = jnp.einsum("rqhd,rkhd->rhqk", query_heads, key_heads, preferred_element_type=F32)
    scores = scores * head_size ** (-0.5)
    return jnp.where(keep_rows.reshape(row_count, 1, 1, SEQ) > 0, scores, -1000000000.0)


def attend_forward(queries, keys, values, keep_rows):
    row_count = queries.shape[0] // SEQ
    head_size = queries.shape[1] // HEADS
    shape = (row_count, SEQ, HEADS, head_size)
    scores = scores_of(queries.reshape(shape), keys.reshape(shape), keep_rows, head_size)
    highest = jnp.max(scores, -1, keepdims=True)
    weights = jnp.exp(scores - highest)
    total = jnp.sum(weights, -1, keepdims=True)
    probs = weights / total
    mixed = jnp.einsum(
        "rhqk,rkhd->rqhd", as_low(probs), values.reshape(shape), preferred_element_type=F32
    )
    return (mixed.reshape(queries.shape), probs)


def attend_backward(queries, keys, values, probs, grad_attended):
    row_count = queries.shape[0] // SEQ
    head_size = queries.shape[1] // HEADS
    shape = (row_count, SEQ, HEADS, head_size)
    query_heads = queries.reshape(shape)
    key_heads = keys.reshape(shape)
    grad_heads = grad_attended.reshape(shape)
    probs_low = as_low(probs)
    grad_values = jnp.einsum("rhqk,rqhd->rkhd", probs_low, grad_heads, preferred_element_type=F32)
    grad_probs = jnp.einsum(
        "rqhd,rkhd->rhqk", grad_heads, values.reshape(shape), preferred_element_type=F32
    )
    weighted = jnp.sum(grad_probs * probs, -1, keepdims=True)
    grad_scores = as_low(probs * (grad_probs - weighted))
    grad_queries = jnp.einsum(
        "rhqk,rkhd->rqhd", grad_scores, key_heads, preferred_element_type=F32
    ) * head_size ** (-0.5)
    grad_keys = jnp.einsum(
        "rhqk,rqhd->rkhd", grad_scores, query_heads, preferred_element_type=F32
    ) * head_size ** (-0.5)
    flat = queries.shape
    return (grad_queries.reshape(flat), grad_keys.reshape(flat), grad_values.reshape(flat))


def swap(values, axis, bit):
    count = lax.axis_size(axis)
    return lax.ppermute(values, axis, [(at, at ^ bit) for at in range(count)])


def bit_of(axis, bit):
    return (lax.axis_index(axis) // bit) % 2


def bits_of(axis):
    bits, bit = [], 1
    while bit < lax.axis_size(axis):
        bits.append(bit)
        bit *= 2
    return bits


def add_low(first, second):
    return as_low(first.astype(F32) + second.astype(F32))


def split(values, own):
    half = values.shape[0] // 2
    mine = lax.dynamic_slice_in_dim(values, own * half, half, 0)
    other = lax.dynamic_slice_in_dim(values, (1 - own) * half, half, 0)
    return mine, other


def join(mine, other, own):
    swapped = own == 1
    return jnp.concatenate(
        [jnp.where(swapped, other, mine), jnp.where(swapped, mine, other)], 0
    )


def gather_inner(own_piece):
    core = bit_of("dp", 1)
    mine, _ = split(own_piece, core)
    halves = [mine]
    for bit in bits_of("mp"):
        halves = halves + [swap(item, "mp", bit) for item in halves]
    rest = [join(item, swap(item, "dp", 1), core) for item in halves[1:]]
    return [own_piece] + rest


def gather_small(own_piece):
    items = [own_piece]
    for bit in bits_of("mp"):
        items = items + [swap(item, "mp", bit) for item in items]
    return items


def sum_shared(values, order):
    held = []
    steps = [("dp", 1)] + order
    for axis, bit in steps[:-1]:
        own = bit_of(axis, bit)
        mine, other = split(values, own)
        values = add_low(mine, swap(other, axis, bit))
        held.append((axis, bit, own))
    axis, bit = steps[-1]
    values = add_low(values, swap(values, axis, bit))
    for axis, bit, own in reversed(held):
        values = join(values, swap(values, axis, bit), own)
    return values.astype(F32)


def sum_inner(pieces, order):
    held = []
    steps = [("dp", 1)] + order
    for axis, bit in steps[:-1]:
        if axis == "mp":
            keep_count = len(pieces) // 2
            moved = [swap(item, axis, bit) for item in pieces[keep_count:]]
            pieces = [add_low(one, two) for one, two in zip(pieces[:keep_count], moved)]
            continue
        own = bit_of(axis, bit)
        parts = [split(item, own) for item in pieces]
        pieces = [add_low(mine, swap(other, axis, bit)) for mine, other in parts]
        held.append((axis, bit, own))
    axis, bit = steps[-1]
    values = add_low(pieces[0], swap(pieces[0], axis, bit))
    for axis, bit, own in reversed(held):
        values = join(values, swap(values, axis, bit), own)
    return values.astype(F32)


def sum_small(values):
    for axis in ("dp", "mp"):
        for bit in bits_of(axis):
            values = values + swap(values, axis, bit)
    return values


def body(
    cell_input,
    lengths,
    out_grad,
    norm_params,
    gated_weight,
    gated_bias,
    left_weight,
    left_bias,
    conv_weight,
    conv_bias,
    inner_norm,
    depth_weight,
    point_weight,
    point_bias,
    project_weight,
    project_bias,
    output_weight,
    output_bias,
    expand_weight,
    expand_bias,
    shrink_weight,
    shrink_bias,
):
    width = cell_input.shape[1]
    half_width = conv_weight.shape[2]
    local = left_weight.shape[1]
    inner = local * lax.axis_size("mp")
    offset = lax.axis_index("mp") * local
    mp_bits = bits_of("mp")[::-1]
    dp_bits = bits_of("dp")[1:]
    mp_first = [("mp", bit) for bit in mp_bits] + [("dp", bit) for bit in dp_bits]
    dp_first = (
        [("dp", dp_bits[0])] + [("mp", bit) for bit in mp_bits] + [("dp", bit) for bit in dp_bits[1:]]
    )

    vectors = jnp.concatenate(
        [left_bias[None], expand_bias[None], inner_norm, depth_weight], 0
    )
    vectors = jnp.concatenate(gather_small(vectors), 1).astype(F32)
    left_bias_all, expand_bias_all = vectors[0], vectors[1]
    inner_all, depth_all = vectors[2:4], vectors[4:13]
    left_all = jnp.concatenate(gather_inner(left_weight), 1)
    point_all = jnp.concatenate(gather_inner(point_weight), 0)
    expand_all = jnp.concatenate(gather_inner(expand_weight), 1)
    shrink_all = jnp.concatenate(gather_inner(shrink_weight), 0)

    positions = jnp.arange(SEQ, dtype=jnp.int32)
    keep = (positions[None, :] < lengths[:, None]).astype(F32).reshape(-1)
    start_x = cell_input.astype(F32)
    norms = norm_params.astype(F32)
    norm_one, normed_one, rstd_one = layer_norm(start_x, norms[0, 0], norms[0, 1])
    low_one = as_low(norm_one)
    gated_pre = matmul(low_one, gated_weight) + gated_bias.astype(F32)
    values_one = gated_pre[:, :width]
    gates_one = jax.nn.sigmoid(gated_pre[:, width:])
    resid_one = start_x + values_one * gates_one
    norm_two, normed_two, rstd_two = layer_norm(resid_one, norms[1, 0], norms[1, 1])
    low_two = as_low(norm_two * keep[:, None])
    stacked = jnp.concatenate([shift_rows(low_two, -1), low_two, shift_rows(low_two, 1)], 1)
    conv_flat = conv_weight.reshape(3 * width, half_width)
    right_pre = matmul(stacked, conv_flat) + conv_bias.astype(F32)
    right_low = as_low(jax.nn.silu(right_pre))

    left_pre = matmul(low_two, left_all) + left_bias_all
    right_part = lax.dynamic_update_slice_in_dim(
        jnp.zeros((low_two.shape[0], inner), LOW), right_low, offset, 1
    )
    mixed = jax.nn.silu(left_pre) + right_part.astype(F32)
    centre = jnp.sum(mixed, 1, keepdims=True) / inner
    variance = jnp.sum(mixed * mixed, 1, keepdims=True) / inner - centre * centre
    inner_rstd = lax.rsqrt(variance + EPS)
    inner_normed = (mixed - centre) * inner_rstd
    normal_out = (inner_normed * inner_all[0] + inner_all[1]) * keep[:, None]
    depth = jnp.zeros_like(normal_out)
    for tap in range(9):
        depth = depth + shift_rows(normal_out, tap - 4) * depth_all[tap]
    depth_low = as_low(depth)
    sep = matmul(depth_low, point_all) + point_bias.astype(F32)
    resid_two = resid_one + jnp.pad(sep, ((0, 0), (0, width - half_width)))
    norm_four, normed_four, rstd_four = layer_norm(resid_two, norms[2, 0], norms[2, 1])
    low_four = as_low(norm_four)
    projected = matmul(low_four, project_weight)
    biases = project_bias.astype(F32)
    queries = as_low(projected[:, :width] + biases[0])
    keys = as_low(projected[:, width : 2 * width])
    values = as_low(projected[:, 2 * width :] + biases[1])
    attended, probs = attend_forward(queries, keys, values, keep)
    attended_low = as_low(attended)
    resid_three = resid_two + matmul(attended_low, output_weight) + output_bias.astype(F32)
    norm_five, normed_five, rstd_five = layer_norm(resid_three, norms[3, 0], norms[3, 1])
    low_five = as_low(norm_five)
    expand_pre = matmul(low_five, expand_all) + expand_bias_all
    hidden_low = as_low(jax.nn.silu(expand_pre))
    shrunk = matmul(hidden_low, shrink_all)
    cell_output = as_low(resid_three + shrunk + shrink_bias.astype(F32))

    grad_top = out_grad.astype(F32)
    grad_shrink_bias = jnp.sum(grad_top, 0)
    cols = [slice(at, at + local) for at in range(0, inner, local)]
    grad_shrink = sum_inner(
        [as_low(left_turned(hidden_low[:, col], out_grad)) for col in cols], mp_first
    )
    grad_expand_pre = as_low(right_turned(out_grad, shrink_all) * silu_slope(expand_pre))
    grad_expand_bias = jnp.sum(grad_expand_pre.astype(F32), 0)
    grad_expand = sum_inner(
        [as_low(left_turned(low_five, grad_expand_pre[:, col])) for col in cols], dp_first
    )
    grad_five = right_turned(grad_expand_pre, expand_all)
    grad_in_five, grad_norm_five = norm_back(grad_five, normed_five, rstd_five, norms[3, 0])
    grad_three = grad_top + grad_in_five
    grad_attn_low = as_low(grad_three)
    grad_output_bias = jnp.sum(grad_attn_low.astype(F32), 0)
    grad_output_weight = as_low(left_turned(attended_low, grad_attn_low))
    grad_attended = as_low(right_turned(grad_attn_low, output_weight))
    grad_queries, grad_keys, grad_values = attend_backward(
        queries, keys, values, probs, grad_attended
    )
    grad_projected = as_low(jnp.concatenate([grad_queries, grad_keys, grad_values], 1))
    grad_project_weight = as_low(left_turned(low_four, grad_projected))
    both = sum_shared(jnp.concatenate([grad_project_weight, grad_output_weight], 1), mp_first)
    grad_project_weight = both[:, : 3 * width]
    grad_output_weight = both[:, 3 * width :]
    grad_proj_float = grad_projected.astype(F32)
    grad_query_bias = jnp.sum(grad_proj_float[:, :width], 0)
    grad_value_bias = jnp.sum(grad_proj_float[:, 2 * width :], 0)
    grad_four = right_turned(grad_projected, project_weight)
    grad_in_four, grad_norm_four = norm_back(grad_four, normed_four, rstd_four, norms[2, 0])
    grad_two = grad_three + grad_in_four
    grad_sep = as_low(grad_two[:, :half_width])
    grad_point_bias = jnp.sum(grad_sep.astype(F32), 0)

    grad_point = sum_inner(
        [as_low(left_turned(depth_low[:, col], grad_sep)) for col in cols], mp_first
    )
    grad_depth = right_turned(grad_sep, point_all)
    grad_taps = jnp.stack(
        [jnp.sum(shift_rows(normal_out, tap - 4) * grad_depth, 0) for tap in range(9)]
    )
    grad_normal = jnp.zeros_like(grad_depth)
    for tap in range(9):
        grad_normal = grad_normal + shift_rows(grad_depth * depth_all[tap], 4 - tap)
    grad_normal = grad_normal * keep[:, None]
    scaled = grad_normal * inner_all[0]
    first = jnp.sum(scaled, 1, keepdims=True) / inner
    second = jnp.sum(scaled * inner_normed, 1, keepdims=True) / inner
    grad_mixed = inner_rstd * (scaled - first - inner_normed * second)
    grad_inner_gain = jnp.sum(grad_normal * inner_normed, 0)
    grad_inner_bias = jnp.sum(grad_normal, 0)
    grad_left_pre = as_low(grad_mixed * silu_slope(left_pre))
    grad_left_b = jnp.sum(grad_left_pre.astype(F32), 0)
    grad_left = sum_inner(
        [as_low(left_turned(low_two, grad_left_pre[:, col])) for col in cols], dp_first
    )
    grad_low_left = right_turned(grad_left_pre, left_all)
    grad_right = lax.dynamic_slice_in_dim(grad_mixed, offset, half_width, 1)
    grad_right_pre = as_low(grad_right * silu_slope(right_pre))
    grad_conv_bias = jnp.sum(grad_right_pre.astype(F32), 0)
    grad_conv = as_low(left_turned(stacked, grad_right_pre))
    grad_stacked = right_turned(grad_right_pre, conv_flat)
    grad_low_two = (
        grad_low_left
        + shift_rows(grad_stacked[:, :width], 1)
        + grad_stacked[:, width : 2 * width]
        + shift_rows(grad_stacked[:, 2 * width :], -1)
    )
    grad_in_two, grad_norm_two = norm_back(
        grad_low_two * keep[:, None], normed_two, rstd_two, norms[1, 0]
    )
    grad_one = grad_two + grad_in_two
    grad_gated = as_low(
        jnp.concatenate(
            [grad_one * gates_one, grad_one * values_one * gates_one * (1.0 - gates_one)], 1
        )
    )
    grad_gated_bias = jnp.sum(grad_gated.astype(F32), 0)
    grad_gated_weight = as_low(left_turned(low_one, grad_gated))
    last = sum_shared(
        jnp.concatenate(
            [grad_gated_weight] + [grad_conv[at * width : (at + 1) * width] for at in range(3)], 1
        ),
        dp_first,
    )
    grad_gated_weight = last[:, : 2 * width]
    grad_conv = jnp.stack(
        [
            last[:, 2 * width + at * half_width : 2 * width + (at + 1) * half_width]
            for at in range(3)
        ]
    )
    grad_in_one, grad_norm_one = norm_back(
        right_turned(grad_gated, gated_weight), normed_one, rstd_one, norms[0, 0]
    )
    input_grad = grad_one + grad_in_one

    wide = jnp.concatenate(
        [grad_left_b[None], grad_expand_bias[None], grad_inner_gain[None], grad_inner_bias[None], grad_taps], 0
    )
    fixed = [
        grad_norm_one.reshape(-1),
        grad_norm_two.reshape(-1),
        grad_norm_four.reshape(-1),
        grad_norm_five.reshape(-1),
        grad_gated_bias,
        grad_query_bias,
        grad_value_bias,
        grad_output_bias,
        grad_shrink_bias,
        grad_conv_bias,
        grad_point_bias,
    ]
    fixed = jnp.concatenate(fixed)
    fixed = jnp.pad(fixed, (0, -fixed.shape[0] % local)).reshape(-1, local)
    fixed_rows = fixed.shape[0]
    wide_chunks = [wide[:, col] for col in cols]
    for bit in mp_bits:
        half_count = len(wide_chunks) // 2
        moved = [swap(item, "mp", bit) for item in wide_chunks[half_count:]]
        wide_chunks = [one + two for one, two in zip(wide_chunks[:half_count], moved)]
    for bit in mp_bits:
        fixed = fixed + swap(fixed, "mp", bit)
    small = jnp.concatenate([fixed, wide_chunks[0]], 0)
    for bit in bits_of("dp"):
        small = small + swap(small, "dp", bit)
    fixed, wide = small[:fixed_rows].reshape(-1), small[fixed_rows:]
    sizes = [2 * width] * 4 + [2 * width, width, width, width, width, half_width, half_width]
    starts = [sum(sizes[:at]) for at in range(len(sizes))]
    picked = [fixed[start : start + size] for start, size in zip(starts, sizes)]
    return (
        cell_output,
        input_grad,
        fixed[: 8 * width].reshape(4, 2, width),
        grad_gated_weight,
        picked[4],
        grad_left,
        wide[0],
        grad_conv,
        picked[9],
        wide[2:4],
        wide[4:13],
        grad_point,
        picked[10],
        grad_project_weight,
        jnp.stack([picked[5], picked[6]]),
        both[:, 3 * width :],
        picked[7],
        grad_expand,
        wide[1],
        grad_shrink,
        picked[8],
    )


def solution(mesh):
    return jax.shard_map(
        body,
        mesh=mesh,
        in_specs=(
            P(("dp", "mp"), None),
            P(("dp", "mp")),
            P(("dp", "mp"), None),
            P(),
            P(),
            P(),
            P(None, "mp"),
            P("mp"),
            P(),
            P(),
            P(None, "mp"),
            P(None, "mp"),
            P("mp", None),
            P(),
            P(),
            P(),
            P(),
            P(),
            P(None, "mp"),
            P("mp"),
            P("mp", None),
            P(),
        ),
        out_specs=(
            P(("dp", "mp"), None),
            P(("dp", "mp"), None),
            P(),
            P(),
            P(),
            P(None, "mp"),
            P("mp"),
            P(),
            P(),
            P(None, "mp"),
            P(None, "mp"),
            P("mp", None),
            P(),
            P(),
            P(),
            P(),
            P(),
            P(None, "mp"),
            P("mp"),
            P("mp", None),
            P(),
        ),
        check_vma=False,
    )
```

```python
import jax
import jax.numpy as jnp
from jax import lax
from jax.experimental import pallas as pl
from jax.experimental.pallas import tpu as pltpu
from jax.sharding import PartitionSpec as P

HEADS = 8
SEQ = 256
EPS = 1e-06
NEGATIVE = -1000000000.0
LOW = jnp.bfloat16
F32 = jnp.float32
STEP = 64
LIMIT = 40 * 2**20


def as_low(values):
    return values.astype(LOW)


def dot(left, right):
    return jnp.dot(left, right, preferred_element_type=F32)


def dot_left(left, right):
    return lax.dot_general(left, right, (((0,), (0,)), ((), ())), preferred_element_type=F32)


def dot_right(left, right):
    return lax.dot_general(left, right, (((1,), (1,)), ((), ())), preferred_element_type=F32)


def swap(values, axis, bit):
    count = lax.axis_size(axis)
    return lax.ppermute(values, axis, [(at, at ^ bit) for at in range(count)])


def bit_of(axis, bit):
    return (lax.axis_index(axis) // bit) % 2


def bits_of(axis):
    bits, bit = [], 1
    while bit < lax.axis_size(axis):
        bits.append(bit)
        bit *= 2
    return bits


def add_low(first, second):
    return as_low(first.astype(F32) + second.astype(F32))


def split(values, own):
    half = values.shape[0] // 2
    mine = lax.dynamic_slice_in_dim(values, own * half, half, 0)
    other = lax.dynamic_slice_in_dim(values, (1 - own) * half, half, 0)
    return mine, other


def join(mine, other, own):
    swapped = own == 1
    return jnp.concatenate(
        [jnp.where(swapped, other, mine), jnp.where(swapped, mine, other)], 0
    )


def sum_shared(values, order):
    held = []
    steps = [("dp", 1)] + order
    for axis, bit in steps[:-1]:
        own = bit_of(axis, bit)
        mine, other = split(values, own)
        values = add_low(mine, swap(other, axis, bit))
        held.append((axis, bit, own))
    axis, bit = steps[-1]
    values = add_low(values, swap(values, axis, bit))
    for axis, bit, own in reversed(held):
        values = join(values, swap(values, axis, bit), own)
    return values.astype(F32)


def sum_inner(pieces, order):
    held = []
    steps = [("dp", 1)] + order
    for axis, bit in steps[:-1]:
        if axis == "mp":
            keep_count = len(pieces) // 2
            moved = [swap(item, axis, bit) for item in pieces[keep_count:]]
            pieces = [add_low(one, two) for one, two in zip(pieces[:keep_count], moved)]
            continue
        own = bit_of(axis, bit)
        parts = [split(item, own) for item in pieces]
        pieces = [add_low(mine, swap(other, axis, bit)) for mine, other in parts]
        held.append((axis, bit, own))
    axis, bit = steps[-1]
    values = add_low(pieces[0], swap(pieces[0], axis, bit))
    for axis, bit, own in reversed(held):
        values = join(values, swap(values, axis, bit), own)
    return values.astype(F32)


def sigmoid(values):
    return 0.5 * jnp.tanh(0.5 * values) + 0.5


def spans(total, step):
    return [slice(at, at + step) for at in range(0, total, step)]


def at_lane(start, size):
    return pl.ds(pl.multiple_of(start, 128), size)


def normalize(values):
    width = values.shape[1]
    centre = jnp.sum(values, -1, keepdims=True) * (1.0 / width)
    centered = values - centre
    variance = jnp.sum(centered * centered, -1, keepdims=True) * (1.0 / width)
    rstd = lax.rsqrt(variance + EPS)
    return centered * rstd, rstd


def normalize_back(grad, normed, rstd, gain):
    width = grad.shape[1]
    scaled = grad * gain
    first = jnp.sum(scaled, -1, keepdims=True) * (1.0 / width)
    second = jnp.sum(scaled * normed, -1, keepdims=True) * (1.0 / width)
    return rstd * (scaled - first - normed * second)


def columns_sum(values):
    return jnp.sum(values, 0, keepdims=True)


def low_columns_sum(values):
    ones = jnp.ones((16, values.shape[0]), LOW)
    return dot(ones, values)[0:1]


def keep_rows(info, start, rows):
    return jnp.where(
        lax.broadcasted_iota(jnp.int32, (rows, 1), 0) + start < info[2], 1.0, 0.0
    ).astype(F32)


def run(kernel, outs, ins, scratch, flops):
    specs = [pl.BlockSpec(memory_space=pltpu.SMEM)] + [
        pl.BlockSpec(memory_space=pltpu.VMEM) for _ in ins[1:]
    ]
    moved = sum(item.size * item.dtype.itemsize for item in list(ins) + list(outs))
    return pl.pallas_call(
        kernel,
        out_shape=outs,
        in_specs=specs,
        out_specs=[pl.BlockSpec(memory_space=pltpu.VMEM) for _ in outs],
        scratch_shapes=scratch,
        compiler_params=pltpu.CompilerParams(vmem_limit_bytes=LIMIT),
        cost_estimate=pl.CostEstimate(flops=flops, bytes_accessed=moved, transcendentals=0),
    )(*ins)


def shaped(shape, kind):
    return jax.ShapeDtypeStruct(shape, kind)


def pre_kernel(info, x_ref, vec, gated_w, conv_w, a1, values, gates, x1, a2, right_pre, right):
    width = x_ref.shape[1]
    for row in spans(SEQ, STEP):
        normed, _ = normalize(x_ref[row].astype(F32))
        a1[row] = as_low(normed * vec[0:1] + vec[1:2])
    for col in spans(width, 256):
        gate_col = slice(col.start + width, col.stop + width)
        value = dot(a1[...], gated_w[:, col]) + vec[8:9, col]
        gate = sigmoid(dot(a1[...], gated_w[:, gate_col]) + vec[9:10, col])
        values[:, col] = value
        gates[:, col] = gate
        x1[:, col] = x_ref[:, col].astype(F32) + value * gate
    for row in spans(SEQ, STEP):
        normed, _ = normalize(x1[row])
        kept = keep_rows(info, row.start, STEP)
        a2[row] = as_low((normed * vec[2:3] + vec[3:4]) * kept)
    rows = lax.broadcasted_iota(jnp.int32, right_pre.shape, 0)
    first = jnp.where(rows == 0, 0.0, pltpu.roll(dot(a2[...], conv_w[0]), 1, 0))
    last = jnp.where(rows == SEQ - 1, 0.0, pltpu.roll(dot(a2[...], conv_w[2]), SEQ - 1, 0))
    total = first + dot(a2[...], conv_w[1]) + last + vec[10:11, 0 : right_pre.shape[1]]
    right_pre[...] = total
    right[...] = as_low(total * sigmoid(total))


def unpack(refs, counts):
    groups, at = [], 0
    for count in counts:
        groups.append(refs[at : at + count])
        at += count
    return groups


def inner_forward_kernel(pieces, refs):
    info, refs = refs[0], refs[1:]
    (x1, a2, right, vec), left, point, wide, outs, scratch = unpack(
        refs, [4, 2 * pieces - 1, 2 * pieces - 1, pieces, 5, 6]
    )
    x2, normed_ref, slope_ref, depth, rstd_ref = outs
    mixed, total, square, centre_ref, padded, padded_two = scratch
    local = left[0].shape[1]
    inner = local * pieces
    core, offset = info[0], info[1]
    half = a2.shape[1] // 2
    near = a2[:, at_lane(core * half, half)]
    far = a2[:, at_lane((1 - core) * half, half)]
    right_rows = right[...].astype(F32)
    total[...] = jnp.zeros_like(total)
    square[...] = jnp.zeros_like(square)
    for piece in range(pieces):
        for col in spans(local, 256):
            if piece == 0:
                pre = dot(a2[...], left[0][:, col])
            else:
                pre = dot(near, left[2 * piece - 1][:, col]) + dot(far, left[2 * piece][:, col])
            pre = pre + wide[piece][0:16, col].astype(F32)[0:1]
            sigma = sigmoid(pre)
            at = piece * local + col.start
            here = slice(at, at + 256)
            slope_ref[:, here] = as_low(sigma * (1.0 + pre * (1.0 - sigma)))
            value = pre * sigma + right_rows * jnp.where(offset == at, 1.0, 0.0)
            mixed[:, here] = value
            total[...] += value[:, 0:128] + value[:, 128:256]
            squared = value * value
            square[...] += squared[:, 0:128] + squared[:, 128:256]
    centre = jnp.sum(total[...], 1, keepdims=True) * (1.0 / inner)
    variance = jnp.sum(square[...], 1, keepdims=True) * (1.0 / inner) - centre * centre
    rstd = lax.rsqrt(variance + EPS)
    centre_ref[...] = jnp.broadcast_to(centre, centre_ref.shape)
    rstd_ref[...] = jnp.broadcast_to(rstd, rstd_ref.shape)
    for pad in (padded, padded_two):
        pad[0:8] = jnp.zeros((8, 128), F32)
        pad[SEQ + 8 : SEQ + 16] = jnp.zeros((8, 128), F32)
    kept = keep_rows(info, 0, SEQ)
    for piece in range(pieces):

        def one(at, pad):
            col = at_lane(at, 128)
            here = at_lane(piece * local + at, 128)
            vectors = wide[piece][:, col].astype(F32)
            normed = (mixed[:, here] - centre_ref[...]) * rstd_ref[...]
            normed_ref[:, here] = as_low(normed)
            pad[8 : SEQ + 8] = (normed * vectors[2:3] + vectors[3:4]) * kept
            result = pad[4 : SEQ + 4] * vectors[4:5]
            for tap in range(1, 9):
                result = result + pad[4 + tap : SEQ + 4 + tap] * vectors[4 + tap : 5 + tap]
            depth[:, here] = as_low(result)

        def step(index, carry):
            one(index * 256, padded)
            one(index * 256 + 128, padded_two)
            return carry

        lax.fori_loop(0, local // 256, step, 0)
    width = x1.shape[1]
    channels = point[0].shape[1]
    sep = dot(depth[:, 0:local], point[0][...])
    rows = local // 2
    for piece in range(1, pieces):
        base = piece * local
        sep = sep + dot(depth[:, at_lane(base + core * rows, rows)], point[2 * piece - 1][...])
        sep = sep + dot(depth[:, at_lane(base + (1 - core) * rows, rows)], point[2 * piece][...])
    x2[:, 0:channels] = x1[:, 0:channels] + sep + vec[10:11, channels : 2 * channels]
    x2[:, channels:width] = x1[:, channels:width]


def masked_scores(queries, keys, valid, scale):
    return jnp.where(valid, dot_right(queries, keys) * scale, NEGATIVE)


def attention_forward_kernel(
    info, x2, vec, project_w, output_w, a4, qkv, lse, attended, x3, a5
):
    width = x2.shape[1]
    for row in spans(SEQ, STEP):
        normed, _ = normalize(x2[row])
        a4[row] = as_low(normed * vec[4:5] + vec[5:6])
    for col in spans(3 * width, 256):
        part = dot(a4[...], project_w[:, col])
        if col.start < width:
            part = part + vec[11:12, col]
        elif col.start >= 2 * width:
            part = part + vec[12:13, col.start - 2 * width : col.stop - 2 * width]
        qkv[:, col] = as_low(part)
    scale = (width // HEADS) ** (-0.5)
    lanes = lax.broadcasted_iota(jnp.int32, (SEQ, 128), 1)
    valid = lax.broadcasted_iota(jnp.int32, (SEQ, SEQ), 1) < info[2]
    logs = jnp.zeros((SEQ, 128), F32)
    for pair in range(width // 128):
        at = pair * 128
        queries = qkv[:, at : at + 128]
        keys = qkv[:, width + at : width + at + 128]
        vals = qkv[:, 2 * width + at : 2 * width + at + 128]
        mixed = []
        for side in range(2):
            mine = (lanes < 64) if side == 0 else (lanes >= 64)
            scores = masked_scores(jnp.where(mine, queries, 0), keys, valid, scale)
            highest = jnp.max(scores, -1, keepdims=True)
            weights = jnp.exp(scores - highest)
            total = jnp.sum(weights, -1, keepdims=True)
            mixed.append(dot(as_low(weights * (1.0 / total)), vals))
            logs = jnp.where(lanes == 2 * pair + side, highest + jnp.log(total), logs)
        attended[:, at : at + 128] = as_low(jnp.where(lanes < 64, mixed[0], mixed[1]))
    lse[...] = logs
    x3[...] = x2[...] + dot(attended[...], output_w[...]) + vec[13:14]
    for row in spans(SEQ, STEP):
        normed, _ = normalize(x3[row])
        a5[row] = as_low(normed * vec[6:7] + vec[7:8])


def feed_kernel(pieces, refs):
    info, refs = refs[0], refs[1:]
    (a5, x3, top, vec), expand, shrink, wide, outs, scratch = unpack(
        refs, [4, 2 * pieces - 1, 2 * pieces - 1, pieces, 8, 5]
    )
    output, shrink_keep, shrink_send, expand_keep, expand_send, dx3, fixed, grad_bias = outs
    hidden, slope, d_expand, shrunk, d_a5 = scratch
    local = expand[0].shape[1]
    width = x3.shape[1]
    half, rows = width // 2, local // 2
    core = info[0]
    near = a5[:, at_lane(core * half, half)]
    far = a5[:, at_lane((1 - core) * half, half)]
    for piece in range(pieces):
        for col in spans(local, 256):
            if piece == 0:
                pre = dot(a5[...], expand[0][:, col])
            else:
                pre = dot(near, expand[2 * piece - 1][:, col]) + dot(
                    far, expand[2 * piece][:, col]
                )
            pre = pre + wide[piece][0:16, col].astype(F32)[1:2]
            sigma = sigmoid(pre)
            here = slice(piece * local + col.start, piece * local + col.stop)
            hidden[:, here] = as_low(pre * sigma)
            slope[:, here] = sigma * (1.0 + pre * (1.0 - sigma))
    blocks = [(0, shrink[0])]
    for piece in range(1, pieces):
        blocks.append((piece * local + core * rows, shrink[2 * piece - 1]))
        blocks.append((piece * local + (1 - core) * rows, shrink[2 * piece]))
    for base, weights in blocks:
        count = weights.shape[0]
        part = dot(hidden[:, at_lane(base, count)], weights[...])
        if weights is shrink[0]:
            shrunk[...] = part
        else:
            shrunk[...] += part
        for row in spans(count, min(256, count)):
            size = row.stop - row.start
            here = at_lane(base + row.start, size)
            back = dot_right(top[...], weights[row])
            d_expand[:, here] = as_low(back * slope[:, here])
    for row in spans(SEQ, STEP):
        output[row] = as_low(x3[row] + shrunk[row] + vec[14:15])
    for piece in range(pieces):
        base = piece * local
        cols = slice(base, base + local)
        for side, shrink_out, expand_out in (
            (1 - core, shrink_send, expand_send),
            (core, shrink_keep, expand_keep),
        ):
            shrink_out[piece] = as_low(
                dot_left(hidden[:, at_lane(base + side * rows, rows)], top[...])
            )
            expand_out[piece] = as_low(
                dot_left(a5[:, at_lane(side * half, half)], d_expand[:, cols])
            )
        grad_bias[:, cols] = jnp.broadcast_to(low_columns_sum(d_expand[:, cols]), (8, local))
        if piece == 0:
            d_a5[...] = dot_right(d_expand[:, cols], expand[0][...])
        else:
            d_a5[:, at_lane(core * half, half)] += dot_right(
                d_expand[:, cols], expand[2 * piece - 1][...]
            )
            d_a5[:, at_lane((1 - core) * half, half)] += dot_right(
                d_expand[:, cols], expand[2 * piece][...]
            )
    fixed[...] = jnp.zeros_like(fixed)
    for row in spans(SEQ, STEP):
        normed, rstd = normalize(x3[row])
        grad = d_a5[row]
        dx3[row] = top[row].astype(F32) + normalize_back(grad, normed, rstd, vec[6:7])
        fixed[6:7] += columns_sum(grad * normed)
        fixed[7:8] += columns_sum(grad)
    fixed[13:14] = low_columns_sum(top[...])


def attention_backward_kernel(
    info, dx3, attended, output_w, qkv, lse, a4, project_w, x2, vec, before,
    send, keep, dx2, d_sep, fixed, d_out, d_att, d_proj
):
    width = x2.shape[1]
    half = width // 2
    core = info[0]
    fixed[...] = before[...]
    d_out[...] = as_low(dx3[...])
    d_att[...] = as_low(dot_right(d_out[...], output_w[...]))
    scale = (width // HEADS) ** (-0.5)
    lanes = lax.broadcasted_iota(jnp.int32, (SEQ, 128), 1)
    valid = lax.broadcasted_iota(jnp.int32, (SEQ, SEQ), 1) < info[2]
    for pair in range(width // 128):
        at = pair * 128
        queries = qkv[:, at : at + 128]
        keys = qkv[:, width + at : width + at + 128]
        vals = qkv[:, 2 * width + at : 2 * width + at + 128]
        grads = d_att[:, at : at + 128]
        parts = []
        for side in range(2):
            head = 2 * pair + side
            mine = (lanes < 64) if side == 0 else (lanes >= 64)
            scores = masked_scores(jnp.where(mine, queries, 0), keys, valid, scale)
            probs = jnp.exp(scores - lse[:, head : head + 1])
            d_vals = dot_left(as_low(probs), grads)
            d_probs = dot_right(jnp.where(mine, grads, 0), vals)
            weighted = jnp.sum(d_probs * probs, -1, keepdims=True)
            d_scores = as_low(probs * (d_probs - weighted))
            parts.append((dot(d_scores, keys) * scale, dot_left(d_scores, queries) * scale, d_vals))
        for kind in range(3):
            here = slice(kind * width + at, kind * width + at + 128)
            d_proj[:, here] = as_low(jnp.where(lanes < 64, parts[0][kind], parts[1][kind]))
    for side, out in ((1 - core, send), (core, keep)):
        here = at_lane(side * half, half)
        out[:, 3 * width :] = as_low(dot_left(attended[:, here], d_out[...]))
        out[:, : 3 * width] = as_low(dot_left(a4[:, here], d_proj[...]))
    fixed[12:13] = low_columns_sum(d_out[...])
    fixed[10:11] = low_columns_sum(d_proj[:, :width])
    fixed[11:12] = low_columns_sum(d_proj[:, 2 * width :])
    dx2[...] = dot_right(d_proj[...], project_w[...])
    for row in spans(SEQ, STEP):
        normed, rstd = normalize(x2[row])
        grad = dx2[row]
        dx2[row] = dx3[row] + normalize_back(grad, normed, rstd, vec[4:5])
        fixed[4:5] += columns_sum(grad * normed)
        fixed[5:6] += columns_sum(grad)
    channels = d_sep.shape[1]
    d_sep[...] = as_low(dx2[:, :channels])
    fixed[14:15, channels : 2 * channels] = low_columns_sum(d_sep[...])


def inner_backward_kernel(pieces, refs):
    info, refs = refs[0], refs[1:]
    (d_sep, depth, normed_ref, slope_ref, rstd_ref, a2, bias_before), point, left, wide, outs, scratch = unpack(
        refs, [7, 2 * pieces - 1, 2 * pieces - 1, pieces, 7, 6]
    )
    left_keep, left_send, point_keep, point_send, d_a2, d_right, grads = outs
    d_depth, padded, padded_two, d_left, first_ref, second_ref = scratch
    local = left[0].shape[1]
    inner = local * pieces
    core, offset = info[0], info[1]
    rows = local // 2
    half = a2.shape[1] // 2
    blocks = [(0, point[0])]
    for piece in range(1, pieces):
        blocks.append((piece * (local // 128) + core * (rows // 128), point[2 * piece - 1]))
        blocks.append((piece * (local // 128) + (1 - core) * (rows // 128), point[2 * piece]))
    for base, weights in blocks:
        count = weights.shape[0]
        for row in spans(count, min(256, count)):
            back = dot_right(d_sep[...], weights[row])
            for part in range((row.stop - row.start) // 128):
                d_depth[base + row.start // 128 + part, 8 : SEQ + 8] = back[
                    :, part * 128 : (part + 1) * 128
                ]
    first_ref[...] = jnp.zeros_like(first_ref)
    second_ref[...] = jnp.zeros_like(second_ref)
    for pad in (padded, padded_two):
        pad[0:8] = jnp.zeros((8, 128), F32)
        pad[SEQ + 8 : SEQ + 16] = jnp.zeros((8, 128), F32)
    grads[...] = jnp.zeros_like(grads)
    grads[1:2] = bias_before[0:1]
    kept = keep_rows(info, 0, SEQ)
    for piece in range(pieces):

        def one(at, pad):
            col = at_lane(at, 128)
            here = at_lane(piece * local + at, 128)
            index = (piece * local + at) // 128
            vectors = wide[piece][:, col].astype(F32)
            d_depth[index, 0:8] = jnp.zeros((8, 128), F32)
            d_depth[index, SEQ + 8 : SEQ + 16] = jnp.zeros((8, 128), F32)
            normed = normed_ref[:, here].astype(F32)
            pad[8 : SEQ + 8] = (normed * vectors[2:3] + vectors[3:4]) * kept
            own = d_depth[index, 8 : SEQ + 8]
            result = d_depth[index, 12 : SEQ + 12] * vectors[4:5]
            grads[4:5, here] = columns_sum(pad[4 : SEQ + 4] * own)
            for tap in range(1, 9):
                result = result + d_depth[index, 12 - tap : SEQ + 12 - tap] * vectors[4 + tap : 5 + tap]
                grads[4 + tap : 5 + tap, here] = columns_sum(pad[4 + tap : SEQ + 4 + tap] * own)
            result = result * kept
            grads[2:3, here] = columns_sum(result * normed)
            grads[3:4, here] = columns_sum(result)
            scaled = result * vectors[2:3]
            first_ref[...] += scaled
            second_ref[...] += scaled * normed
            d_depth[index, 8 : SEQ + 8] = scaled

        def step(index, carry):
            one(index * 256, padded)
            one(index * 256 + 128, padded_two)
            return carry

        lax.fori_loop(0, local // 256, step, 0)
    first_ref[...] = jnp.broadcast_to(
        jnp.sum(first_ref[...], 1, keepdims=True) * (1.0 / inner), first_ref.shape
    )
    second_ref[...] = jnp.broadcast_to(
        jnp.sum(second_ref[...], 1, keepdims=True) * (1.0 / inner), second_ref.shape
    )

    def back(index, carry):
        here = at_lane(index * 128, 128)
        normed = normed_ref[:, here].astype(F32)
        d_mixed = rstd_ref[...] * (
            d_depth[index, 8 : SEQ + 8] - first_ref[...] - normed * second_ref[...]
        )
        d_depth[index, 8 : SEQ + 8] = d_mixed
        d_left[:, here] = as_low(d_mixed * slope_ref[:, here].astype(F32))
        return carry

    lax.fori_loop(0, inner // 128, back, 0)
    for part in range(d_right.shape[1] // 128):
        d_right[:, part * 128 : (part + 1) * 128] = d_depth[offset // 128 + part, 8 : SEQ + 8]
    for piece in range(pieces):
        base = piece * local
        cols = slice(base, base + local)
        for side, left_out, point_out in (
            (1 - core, left_send, point_send),
            (core, left_keep, point_keep),
        ):
            left_out[piece] = as_low(
                dot_left(a2[:, at_lane(side * half, half)], d_left[:, cols])
            )
            point_out[piece] = as_low(
                dot_left(depth[:, at_lane(base + side * rows, rows)], d_sep[...])
            )
        grads[0:1, cols] = low_columns_sum(d_left[:, cols])
        if piece == 0:
            d_a2[...] = dot_right(d_left[:, cols], left[0][...])
        else:
            d_a2[:, at_lane(core * half, half)] += dot_right(d_left[:, cols], left[2 * piece - 1][...])
            d_a2[:, at_lane((1 - core) * half, half)] += dot_right(d_left[:, cols], left[2 * piece][...])


def last_kernel(
    info, d_a2_left, d_right, right_pre, conv_w, a2, x1, dx2, values, gates, a1, gated_w, x_ref, vec, before,
    send, keep, input_grad, fixed, shifted, d_a2, d_gated
):
    width = x1.shape[1]
    half = width // 2
    channels = right_pre.shape[1]
    core = info[0]
    fixed[...] = before[...]
    pre = right_pre[...]
    sigma = sigmoid(pre)
    low = as_low(d_right[...] * (sigma * (1.0 + pre * (1.0 - sigma))))
    fixed[14:15, 0:channels] = low_columns_sum(low)
    wide = low.astype(F32)
    rows = lax.broadcasted_iota(jnp.int32, wide.shape, 0)
    shifted[:, 0:channels] = as_low(
        jnp.where(rows == SEQ - 1, 0.0, pltpu.roll(wide, SEQ - 1, 0))
    )
    shifted[:, channels : 2 * channels] = low
    shifted[:, 2 * channels :] = as_low(jnp.where(rows == 0, 0.0, pltpu.roll(wide, 1, 0)))
    total = d_a2_left[...]
    for tap in range(3):
        total = total + dot_right(shifted[:, tap * channels : (tap + 1) * channels], conv_w[tap])
    d_a2[...] = total
    for row in spans(SEQ, STEP):
        normed, rstd = normalize(x1[row])
        grad = d_a2[row] * keep_rows(info, row.start, STEP)
        fixed[2:3] += columns_sum(grad * normed)
        fixed[3:4] += columns_sum(grad)
        dx1 = dx2[row] + normalize_back(grad, normed, rstd, vec[2:3])
        input_grad[row] = dx1
        gate = gates[row]
        scaled = dx1 * gate
        d_gated[row, 0:width] = as_low(scaled)
        d_gated[row, width:] = as_low(scaled * values[row] * (1.0 - gate))
    for side, out in ((1 - core, send), (core, keep)):
        here = at_lane(side * half, half)
        out[:, 0 : 2 * width] = as_low(dot_left(a1[:, here], d_gated[...]))
        out[:, 2 * width :] = as_low(dot_left(a2[:, here], shifted[...]))
    sums = low_columns_sum(d_gated[...])
    fixed[8:9] = sums[:, 0:width]
    fixed[9:10] = sums[:, width:]
    d_a2[...] = dot_right(d_gated[...], gated_w[...])
    for row in spans(SEQ, STEP):
        normed, rstd = normalize(x_ref[row].astype(F32))
        grad = d_a2[row]
        fixed[0:1] += columns_sum(grad * normed)
        fixed[1:2] += columns_sum(grad)
        input_grad[row] += normalize_back(grad, normed, rstd, vec[0:1])


def gather_inner(own_piece):
    core = bit_of("dp", 1)
    mine, _ = split(own_piece, core)
    halves = [mine]
    for bit in bits_of("mp"):
        halves = halves + [swap(item, "mp", bit) for item in halves]
    found = [own_piece]
    for item in halves[1:]:
        found += [item, swap(item, "dp", 1)]
    return found


def gather_small(own_piece):
    items = [own_piece]
    for bit in bits_of("mp"):
        items = items + [swap(item, "mp", bit) for item in items]
    return items


def finish_shared(mine, other, order):
    own = bit_of("dp", 1)
    values = add_low(mine, swap(other, "dp", 1))
    held = [("dp", 1, own)]
    for axis, bit in order[:-1]:
        own = bit_of(axis, bit)
        mine, other = split(values, own)
        values = add_low(mine, swap(other, axis, bit))
        held.append((axis, bit, own))
    axis, bit = order[-1]
    values = add_low(values, swap(values, axis, bit))
    for axis, bit, own in reversed(held):
        values = join(values, swap(values, axis, bit), own)
    return values.astype(F32)


def finish_inner(mine, other, order):
    values = add_low(mine, swap(other, "dp", 1))
    pieces = [values[at] for at in range(values.shape[0])]
    held = [("dp", 1, bit_of("dp", 1))]
    for axis, bit in order[:-1]:
        if axis == "mp":
            keep_count = len(pieces) // 2
            moved = [swap(item, axis, bit) for item in pieces[keep_count:]]
            pieces = [add_low(one, two) for one, two in zip(pieces[:keep_count], moved)]
            continue
        own = bit_of(axis, bit)
        parts = [split(item, own) for item in pieces]
        pieces = [add_low(mine, swap(other, axis, bit)) for mine, other in parts]
        held.append((axis, bit, own))
    axis, bit = order[-1]
    values = add_low(pieces[0], swap(pieces[0], axis, bit))
    for axis, bit, own in reversed(held):
        values = join(values, swap(values, axis, bit), own)
    return values.astype(F32)


def body(
    cell_input,
    lengths,
    out_grad,
    norm_params,
    gated_weight,
    gated_bias,
    left_weight,
    left_bias,
    conv_weight,
    conv_bias,
    inner_norm,
    depth_weight,
    point_weight,
    point_bias,
    project_weight,
    project_bias,
    output_weight,
    output_bias,
    expand_weight,
    expand_bias,
    shrink_weight,
    shrink_bias,
):
    width = cell_input.shape[1]
    channels = conv_weight.shape[2]
    local = left_weight.shape[1]
    pieces = lax.axis_size("mp")
    inner = local * pieces
    tokens = cell_input.shape[0]
    assert tokens == SEQ
    mp_bits = bits_of("mp")[::-1]
    dp_bits = bits_of("dp")[1:]
    mp_first = [("mp", bit) for bit in mp_bits] + [("dp", bit) for bit in dp_bits]
    dp_first = (
        [("dp", dp_bits[0])] + [("mp", bit) for bit in mp_bits] + [("dp", bit) for bit in dp_bits[1:]]
    )
    core = bit_of("dp", 1)
    info = jnp.stack([core, lax.axis_index("mp") * local, lengths[0]]).astype(jnp.int32)

    left = gather_inner(left_weight)
    point = gather_inner(point_weight)
    wide = gather_small(
        jnp.concatenate(
            [
                left_bias[None],
                expand_bias[None],
                inner_norm,
                depth_weight,
                jnp.zeros((3, local), LOW),
            ],
            0,
        )
    )
    expand = gather_inner(expand_weight)
    shrink = gather_inner(shrink_weight)
    vec = jnp.concatenate(
        [
            norm_params.reshape(8, width),
            gated_bias.reshape(2, width),
            jnp.concatenate([conv_bias, point_bias]).reshape(1, width),
            project_bias,
            output_bias[None],
            shrink_bias[None],
            jnp.zeros((1, width), LOW),
        ],
        0,
    ).astype(F32)

    a1, values, gates, x1, a2, right_pre, right = run(
        pre_kernel,
        [
            shaped((tokens, width), LOW),
            shaped((tokens, width), F32),
            shaped((tokens, width), F32),
            shaped((tokens, width), F32),
            shaped((tokens, width), LOW),
            shaped((tokens, channels), F32),
            shaped((tokens, channels), LOW),
        ],
        [info, cell_input, vec, gated_weight, conv_weight],
        [],
        10**9,
    )
    x2, normed, slope, depth, rstd = run(
        lambda *refs: inner_forward_kernel(pieces, refs),
        [
            shaped((tokens, width), F32),
            shaped((tokens, inner), LOW),
            shaped((tokens, inner), LOW),
            shaped((tokens, inner), LOW),
            shaped((tokens, 128), F32),
        ],
        [info, x1, a2, right, vec] + left + point + wide,
        [
            pltpu.VMEM((tokens, inner), F32),
            pltpu.VMEM((tokens, 128), F32),
            pltpu.VMEM((tokens, 128), F32),
            pltpu.VMEM((tokens, 128), F32),
            pltpu.VMEM((tokens + 16, 128), F32),
            pltpu.VMEM((tokens + 16, 128), F32),
        ],
        2 * 10**9,
    )
    a4, qkv, lse, attended, x3, a5 = run(
        attention_forward_kernel,
        [
            shaped((tokens, width), LOW),
            shaped((tokens, 3 * width), LOW),
            shaped((tokens, 128), F32),
            shaped((tokens, width), LOW),
            shaped((tokens, width), F32),
            shaped((tokens, width), LOW),
        ],
        [info, x2, vec, project_weight, output_weight],
        [],
        10**9,
    )
    cell_output, shrink_keep, shrink_send, expand_keep, expand_send, dx3, fixed, expand_sum = run(
        lambda *refs: feed_kernel(pieces, refs),
        [
            shaped((tokens, width), LOW),
            shaped((pieces, local // 2, width), LOW),
            shaped((pieces, local // 2, width), LOW),
            shaped((pieces, width // 2, local), LOW),
            shaped((pieces, width // 2, local), LOW),
            shaped((tokens, width), F32),
            shaped((16, width), F32),
            shaped((8, inner), F32),
        ],
        [info, a5, x3, out_grad, vec] + expand + shrink + wide,
        [
            pltpu.VMEM((tokens, inner), LOW),
            pltpu.VMEM((tokens, inner), F32),
            pltpu.VMEM((tokens, inner), LOW),
            pltpu.VMEM((tokens, width), F32),
            pltpu.VMEM((tokens, width), F32),
        ],
        3 * 10**9,
    )
    grad_shrink = finish_inner(shrink_keep, shrink_send, mp_first)
    grad_expand = finish_inner(expand_keep, expand_send, dp_first)
    proj_send, proj_keep, dx2, d_sep, fixed = run(
        attention_backward_kernel,
        [
            shaped((width // 2, 4 * width), LOW),
            shaped((width // 2, 4 * width), LOW),
            shaped((tokens, width), F32),
            shaped((tokens, channels), LOW),
            shaped((16, width), F32),
        ],
        [info, dx3, attended, output_weight, qkv, lse, a4, project_weight, x2, vec, fixed],
        [
            pltpu.VMEM((tokens, width), LOW),
            pltpu.VMEM((tokens, width), LOW),
            pltpu.VMEM((tokens, 3 * width), LOW),
        ],
        2 * 10**9,
    )
    both = finish_shared(proj_keep, proj_send, mp_first)
    left_keep, left_send, point_keep, point_send, d_a2, d_right, wide_sums = run(
        lambda *refs: inner_backward_kernel(pieces, refs),
        [
            shaped((pieces, width // 2, local), LOW),
            shaped((pieces, width // 2, local), LOW),
            shaped((pieces, local // 2, channels), LOW),
            shaped((pieces, local // 2, channels), LOW),
            shaped((tokens, width), F32),
            shaped((tokens, channels), F32),
            shaped((16, inner), F32),
        ],
        [info, d_sep, depth, normed, slope, rstd, a2, expand_sum] + point + left + wide,
        [
            pltpu.VMEM((inner // 128, tokens + 16, 128), F32),
            pltpu.VMEM((tokens + 16, 128), F32),
            pltpu.VMEM((tokens + 16, 128), F32),
            pltpu.VMEM((tokens, inner), LOW),
            pltpu.VMEM((tokens, 128), F32),
            pltpu.VMEM((tokens, 128), F32),
        ],
        3 * 10**9,
    )
    grad_left = finish_inner(left_keep, left_send, dp_first)
    grad_point = finish_inner(point_keep, point_send, mp_first)
    last_send, last_keep, input_grad, fixed = run(
        last_kernel,
        [
            shaped((width // 2, 2 * width + 3 * channels), LOW),
            shaped((width // 2, 2 * width + 3 * channels), LOW),
            shaped((tokens, width), F32),
            shaped((16, width), F32),
        ],
        [
            info,
            d_a2,
            d_right,
            right_pre,
            conv_weight,
            a2,
            x1,
            dx2,
            values,
            gates,
            a1,
            gated_weight,
            cell_input,
            vec,
            fixed,
        ],
        [
            pltpu.VMEM((tokens, 3 * channels), LOW),
            pltpu.VMEM((tokens, width), F32),
            pltpu.VMEM((tokens, 2 * width), LOW),
        ],
        2 * 10**9,
    )
    last = finish_shared(last_keep, last_send, dp_first)
    grad_conv = jnp.stack(
        [
            last[:, 2 * width + at * channels : 2 * width + (at + 1) * channels]
            for at in range(3)
        ]
    )

    chunks = [wide_sums[:, at : at + local] for at in range(0, inner, local)]
    for bit in mp_bits:
        count = len(chunks) // 2
        moved = [swap(item, "mp", bit) for item in chunks[count:]]
        chunks = [one + two for one, two in zip(chunks[:count], moved)]
        fixed = fixed + swap(fixed, "mp", bit)
    wide_total = chunks[0]
    for bit in bits_of("dp"):
        fixed = fixed + swap(fixed, "dp", bit)
        wide_total = wide_total + swap(wide_total, "dp", bit)
    return (
        cell_output,
        input_grad,
        fixed[0:8].reshape(4, 2, width),
        last[:, : 2 * width],
        fixed[8:10].reshape(2 * width),
        grad_left,
        wide_total[0],
        grad_conv,
        fixed[14, :channels],
        wide_total[2:4],
        wide_total[4:13],
        grad_point,
        fixed[14, channels:],
        both[:, : 3 * width],
        fixed[10:12],
        both[:, 3 * width :],
        fixed[12],
        grad_expand,
        wide_total[1],
        grad_shrink,
        fixed[13],
    )


def solution(mesh):
    return jax.shard_map(
        body,
        mesh=mesh,
        in_specs=(
            P(("dp", "mp"), None),
            P(("dp", "mp")),
            P(("dp", "mp"), None),
            P(),
            P(),
            P(),
            P(None, "mp"),
            P("mp"),
            P(),
            P(),
            P(None, "mp"),
            P(None, "mp"),
            P("mp", None),
            P(),
            P(),
            P(),
            P(),
            P(),
            P(None, "mp"),
            P("mp"),
            P("mp", None),
            P(),
        ),
        out_specs=(
            P(("dp", "mp"), None),
            P(("dp", "mp"), None),
            P(),
            P(),
            P(),
            P(None, "mp"),
            P("mp"),
            P(),
            P(),
            P(None, "mp"),
            P(None, "mp"),
            P("mp", None),
            P(),
            P(),
            P(),
            P(),
            P(),
            P(None, "mp"),
            P("mp"),
            P("mp", None),
            P(),
        ),
        check_vma=False,
    )
```

```python
import jax
import jax.numpy as jnp
from jax import lax
from jax.experimental import pallas as pl
from jax.experimental.pallas import tpu as pltpu
from jax.sharding import PartitionSpec as P

HEADS = 8
SEQ = 256
EPS = 1e-06
NEGATIVE = -1000000000.0
LOW = jnp.bfloat16
F32 = jnp.float32
STEP = 64
LIMIT = 40 * 2**20
SCALE = 4
ADV = 20 * 10**9


def as_low(values):
    return values.astype(LOW)


def dot(left, right):
    return jnp.dot(left, right, preferred_element_type=F32)


def dot_left(left, right):
    return lax.dot_general(left, right, (((0,), (0,)), ((), ())), preferred_element_type=F32)


def dot_right(left, right):
    return lax.dot_general(left, right, (((1,), (1,)), ((), ())), preferred_element_type=F32)


def swap(values, axis, bit):
    count = lax.axis_size(axis)
    return lax.ppermute(values, axis, [(at, at ^ bit) for at in range(count)])


def bit_of(axis, bit):
    return (lax.axis_index(axis) // bit) % 2


def bits_of(axis):
    bits, bit = [], 1
    while bit < lax.axis_size(axis):
        bits.append(bit)
        bit *= 2
    return bits


def add_low(first, second):
    return as_low(first.astype(F32) + second.astype(F32))


def split(values, own):
    half = values.shape[0] // 2
    mine = lax.dynamic_slice_in_dim(values, own * half, half, 0)
    other = lax.dynamic_slice_in_dim(values, (1 - own) * half, half, 0)
    return mine, other


def join(mine, other, own):
    swapped = own == 1
    return jnp.concatenate(
        [jnp.where(swapped, other, mine), jnp.where(swapped, mine, other)], 0
    )


def sum_shared(values, order):
    held = []
    steps = [("dp", 1)] + order
    for axis, bit in steps[:-1]:
        own = bit_of(axis, bit)
        mine, other = split(values, own)
        values = add_low(mine, swap(other, axis, bit))
        held.append((axis, bit, own))
    axis, bit = steps[-1]
    values = add_low(values, swap(values, axis, bit))
    for axis, bit, own in reversed(held):
        values = join(values, swap(values, axis, bit), own)
    return values.astype(F32)


def sum_inner(pieces, order):
    held = []
    steps = [("dp", 1)] + order
    for axis, bit in steps[:-1]:
        if axis == "mp":
            keep_count = len(pieces) // 2
            moved = [swap(item, axis, bit) for item in pieces[keep_count:]]
            pieces = [add_low(one, two) for one, two in zip(pieces[:keep_count], moved)]
            continue
        own = bit_of(axis, bit)
        parts = [split(item, own) for item in pieces]
        pieces = [add_low(mine, swap(other, axis, bit)) for mine, other in parts]
        held.append((axis, bit, own))
    axis, bit = steps[-1]
    values = add_low(pieces[0], swap(pieces[0], axis, bit))
    for axis, bit, own in reversed(held):
        values = join(values, swap(values, axis, bit), own)
    return values.astype(F32)


def sigmoid(values):
    return 0.5 * jnp.tanh(0.5 * values) + 0.5


def spans(total, step):
    return [slice(at, at + step) for at in range(0, total, step)]


def at_lane(start, size):
    return pl.ds(pl.multiple_of(start, 128), size)


def normalize(values):
    width = values.shape[1]
    centre = jnp.sum(values, -1, keepdims=True) * (1.0 / width)
    centered = values - centre
    variance = jnp.sum(centered * centered, -1, keepdims=True) * (1.0 / width)
    rstd = lax.rsqrt(variance + EPS)
    return centered * rstd, rstd


def normalize_back(grad, normed, rstd, gain):
    width = grad.shape[1]
    scaled = grad * gain
    first = jnp.sum(scaled, -1, keepdims=True) * (1.0 / width)
    second = jnp.sum(scaled * normed, -1, keepdims=True) * (1.0 / width)
    return rstd * (scaled - first - normed * second)


def columns_sum(values):
    return jnp.sum(values, 0, keepdims=True)


def low_columns_sum(values):
    ones = jnp.ones((16, values.shape[0]), LOW)
    return dot(ones, values)[0:1]


def keep_rows(info, start, rows):
    return jnp.where(
        lax.broadcasted_iota(jnp.int32, (rows, 1), 0) + start < info[2], 1.0, 0.0
    ).astype(F32)


class Chain:
    def __init__(self):
        self.link = None

    def run(self, kernel, outs, ins, scratch, flops):
        specs = [pl.BlockSpec(memory_space=pltpu.SMEM)] + [
            pl.BlockSpec(memory_space=pltpu.VMEM) for _ in ins[1:]
        ]
        count = len(ins)
        moved = sum(item.size * item.dtype.itemsize for item in list(ins) + list(outs))
        ins = list(ins)
        linked = self.link is not None
        if linked:
            ins.append(self.link)
            specs.append(pl.BlockSpec(memory_space=pl.ANY))

        def call(*refs):
            kernel(*(refs[:count] + refs[count + 1 :] if linked else refs))

        results = pl.pallas_call(
            call,
            out_shape=outs,
            in_specs=specs,
            out_specs=[pl.BlockSpec(memory_space=pltpu.VMEM) for _ in outs],
            scratch_shapes=scratch,
            compiler_params=pltpu.CompilerParams(vmem_limit_bytes=LIMIT),
            cost_estimate=pl.CostEstimate(flops=flops, bytes_accessed=moved + flops // 50, transcendentals=0),
        )(*ins)
        self.link = results[-1]
        return results


def put(out, first, count, offset, values):
    rows = values.shape[0] // count
    low = as_low(values)
    for quarter in range(count):
        for part in range(values.shape[1] // 256):
            at = offset + part * rows
            out[first + quarter, at : at + rows] = low[
                quarter * rows : (quarter + 1) * rows, part * 256 : (part + 1) * 256
            ]


def shaped(shape, kind):
    return jax.ShapeDtypeStruct(shape, kind)


def pre_kernel(info, x_ref, vec, gated_w, conv_w, a1, values, gates, x1, a2, right_pre, right):
    width = x_ref.shape[1]
    for row in spans(SEQ, STEP):
        normed, _ = normalize(x_ref[row].astype(F32))
        a1[row] = as_low(normed * vec[0:1] + vec[1:2])
    for col in spans(width, 256):
        gate_col = slice(col.start + width, col.stop + width)
        value = dot(a1[...], gated_w[:, col]) + vec[8:9, col]
        gate = sigmoid(dot(a1[...], gated_w[:, gate_col]) + vec[9:10, col])
        values[:, col] = value
        gates[:, col] = gate
        x1[:, col] = x_ref[:, col].astype(F32) + value * gate
    for row in spans(SEQ, STEP):
        normed, _ = normalize(x1[row])
        kept = keep_rows(info, row.start, STEP)
        a2[row] = as_low((normed * vec[2:3] + vec[3:4]) * kept)
    rows = lax.broadcasted_iota(jnp.int32, right_pre.shape, 0)
    first = jnp.where(rows == 0, 0.0, pltpu.roll(dot(a2[...], conv_w[0]), 1, 0))
    last = jnp.where(rows == SEQ - 1, 0.0, pltpu.roll(dot(a2[...], conv_w[2]), SEQ - 1, 0))
    total = first + dot(a2[...], conv_w[1]) + last + vec[10:11, 0 : right_pre.shape[1]]
    right_pre[...] = total
    right[...] = as_low(total * sigmoid(total))


def unpack(refs, counts):
    groups, at = [], 0
    for count in counts:
        groups.append(refs[at : at + count])
        at += count
    return groups


def assemble(target, blocks, code):
    rows = blocks[0].shape[0]
    for at, block in enumerate(blocks):
        spot = jnp.bitwise_xor(code, at) if at else code
        target[pl.ds(pl.multiple_of(spot * rows, 16), rows)] = block[...]


def code_of(info, count):
    return info[0] if count == 2 else info[0] * 2 + info[4]


def code_z(info, count):
    return info[0] if count == 2 else info[0] * 2 + info[5]


def group_blocks(refs, pieces):
    count = len(refs) // (pieces - 1)
    return [refs[at : at + count] for at in range(0, len(refs), count)]


def inner_forward_kernel(pieces, sizes, refs):
    info, refs = refs[0], refs[1:]
    (a2, right, left), left_in, wide, outs, scratch = unpack(refs, [3, sizes[0], pieces, 5, 6])
    normed_ref, slope_ref, depth, rstd_ref, left_rest = outs
    mixed, total, square, centre_ref, padded, padded_two = scratch
    local = left.shape[1]
    inner = local * pieces
    offset = info[1]
    right_rows = right[...].astype(F32)
    total[...] = jnp.zeros_like(total)
    square[...] = jnp.zeros_like(square)
    for piece in range(pieces):
        if piece:
            blocks = group_blocks(left_in, pieces)[piece - 1]
            assemble(left_rest.at[piece - 1], blocks, code_of(info, len(blocks)))
        for col in spans(local, 256):
            weights = left[:, col] if piece == 0 else left_rest[piece - 1, :, col]
            pre = dot(a2[...], weights) + wide[piece][0:16, col].astype(F32)[0:1]
            sigma = sigmoid(pre)
            at = piece * local + col.start
            here = slice(at, at + 256)
            slope_ref[:, here] = as_low(sigma * (1.0 + pre * (1.0 - sigma)))
            value = pre * sigma + right_rows * jnp.where(offset == at, 1.0, 0.0)
            mixed[:, here] = value
            total[...] += value[:, 0:128] + value[:, 128:256]
            squared = value * value
            square[...] += squared[:, 0:128] + squared[:, 128:256]
    centre = jnp.sum(total[...], 1, keepdims=True) * (1.0 / inner)
    variance = jnp.sum(square[...], 1, keepdims=True) * (1.0 / inner) - centre * centre
    rstd = lax.rsqrt(variance + EPS)
    centre_ref[...] = jnp.broadcast_to(centre, centre_ref.shape)
    rstd_ref[...] = jnp.broadcast_to(rstd, rstd_ref.shape)
    for pad in (padded, padded_two):
        pad[0:8] = jnp.zeros((8, 128), F32)
        pad[SEQ + 8 : SEQ + 16] = jnp.zeros((8, 128), F32)
    kept = keep_rows(info, 0, SEQ)
    for piece in range(pieces):

        def one(at, pad):
            col = at_lane(at, 128)
            here = at_lane(piece * local + at, 128)
            vectors = wide[piece][:, col].astype(F32)
            normed = (mixed[:, here] - centre_ref[...]) * rstd_ref[...]
            normed_ref[:, here] = as_low(normed)
            pad[8 : SEQ + 8] = (normed * vectors[2:3] + vectors[3:4]) * kept
            result = pad[4 : SEQ + 4] * vectors[4:5]
            for tap in range(1, 9):
                result = result + pad[4 + tap : SEQ + 4 + tap] * vectors[4 + tap : 5 + tap]
            depth[:, here] = as_low(result)

        def step(index, carry):
            one(index * 256, padded)
            one(index * 256 + 128, padded_two)
            return carry

        lax.fori_loop(0, local // 256, step, 0)


def masked_scores(queries, keys, valid, scale):
    return jnp.where(valid, dot_right(queries, keys) * scale, NEGATIVE)


def attention_forward_kernel(pieces, sizes, refs):
    (info, x1, depth, point, vec, project_w, output_w), point_in, outs = unpack(
        refs, [7, sizes[1], 8]
    )
    x2, a4, qkv, lse, attended, x3, a5, point_rest = outs
    width = x2.shape[1]
    local, channels = point.shape
    sep = dot(depth[:, 0:local], point[...])
    for piece in range(1, pieces):
        blocks = group_blocks(point_in, pieces)[piece - 1]
        assemble(point_rest.at[piece - 1], blocks, code_of(info, len(blocks)))
        sep = sep + dot(depth[:, piece * local : (piece + 1) * local], point_rest[piece - 1])
    x2[:, 0:channels] = x1[:, 0:channels] + sep + vec[10:11, channels : 2 * channels]
    x2[:, channels:width] = x1[:, channels:width]
    for row in spans(SEQ, STEP):
        normed, _ = normalize(x2[row])
        a4[row] = as_low(normed * vec[4:5] + vec[5:6])
    for col in spans(3 * width, 256):
        part = dot(a4[...], project_w[:, col])
        if col.start < width:
            part = part + vec[11:12, col]
        elif col.start >= 2 * width:
            part = part + vec[12:13, col.start - 2 * width : col.stop - 2 * width]
        qkv[:, col] = as_low(part)
    scale = (width // HEADS) ** (-0.5)
    lanes = lax.broadcasted_iota(jnp.int32, (SEQ, 128), 1)
    valid = lax.broadcasted_iota(jnp.int32, (SEQ, SEQ), 1) < info[2]
    logs = jnp.zeros((SEQ, 128), F32)
    for pair in range(width // 128):
        at = pair * 128
        queries = qkv[:, at : at + 128]
        keys = qkv[:, width + at : width + at + 128]
        vals = qkv[:, 2 * width + at : 2 * width + at + 128]
        mixed = []
        for side in range(2):
            mine = (lanes < 64) if side == 0 else (lanes >= 64)
            scores = masked_scores(jnp.where(mine, queries, 0), keys, valid, scale)
            highest = jnp.max(scores, -1, keepdims=True)
            weights = jnp.exp(scores - highest)
            total = jnp.sum(weights, -1, keepdims=True)
            mixed.append(dot(as_low(weights * (1.0 / total)), vals))
            logs = jnp.where(lanes == 2 * pair + side, highest + jnp.log(total), logs)
        attended[:, at : at + 128] = as_low(jnp.where(lanes < 64, mixed[0], mixed[1]))
    lse[...] = logs
    x3[...] = x2[...] + dot(attended[...], output_w[...]) + vec[13:14]
    for row in spans(SEQ, STEP):
        normed, _ = normalize(x3[row])
        a5[row] = as_low(normed * vec[6:7] + vec[7:8])


def feed_kernel(pieces, sizes, refs):
    info, refs = refs[0], refs[1:]
    (a5, top, expand), expand_in, wide, outs = unpack(refs, [3, sizes[2], pieces, 5])
    hidden, slope, keep, send, expand_rest = outs
    local = expand.shape[1]
    core, rows = info[0], local // 2
    for piece in range(pieces):
        if piece:
            blocks = group_blocks(expand_in, pieces)[piece - 1]
            assemble(expand_rest.at[piece - 1], blocks, code_of(info, len(blocks)))
        for col in spans(local, 256):
            weights = expand[:, col] if piece == 0 else expand_rest[piece - 1, :, col]
            pre = dot(a5[...], weights) + wide[piece][0:16, col].astype(F32)[1:2]
            sigma = sigmoid(pre)
            here = slice(piece * local + col.start, piece * local + col.stop)
            hidden[:, here] = as_low(pre * sigma)
            slope[:, here] = as_low(sigma * (1.0 + pre * (1.0 - sigma)))
    for piece in range(pieces):
        for side, out in ((1 - core, send), (core, keep)):
            put(
                out,
                2 * piece,
                2,
                0,
                dot_left(hidden[:, at_lane(piece * local + side * rows, rows)], top[...]),
            )


def feed_back_kernel(pieces, sizes, refs):
    info, refs = refs[0], refs[1:]
    (a5, x3, top, vec, hidden, slope, expand, expand_rest, shrink), shrink_in, outs, scratch = unpack(
        refs, [9, sizes[3], 6, 4]
    )
    output, keep, send, dx3, fixed, grad_bias = outs
    d_expand, shrunk, d_a5, shrink_rest = scratch
    local = expand.shape[1]
    half = x3.shape[1] // 2
    core = info[0]
    for piece in range(pieces):
        base = piece * local
        if piece:
            blocks = group_blocks(shrink_in, pieces)[piece - 1]
            assemble(shrink_rest.at[piece - 1], blocks, code_z(info, len(blocks)))
        weights = shrink if piece == 0 else shrink_rest.at[piece - 1]
        part = dot(hidden[:, base : base + local], weights[...])
        if piece == 0:
            shrunk[...] = part
        else:
            shrunk[...] += part
        for row in spans(local, 256):
            here = slice(base + row.start, base + row.stop)
            d_expand[:, here] = as_low(
                dot_right(top[...], weights[row]) * slope[:, here].astype(F32)
            )
    for row in spans(SEQ, STEP):
        output[row] = as_low(x3[row] + shrunk[row] + vec[14:15])
    for piece in range(pieces):
        cols = slice(piece * local, (piece + 1) * local)
        for side, out in ((1 - core, send), (core, keep)):
            grad = dot_left(a5[:, at_lane(side * half, half)], d_expand[:, cols])
            put(out, 2 * piece, 2, 0, grad)
        grad_bias[:, cols] = jnp.broadcast_to(low_columns_sum(d_expand[:, cols]), (8, local))
        weights = expand[...] if piece == 0 else expand_rest[piece - 1]
        if piece == 0:
            d_a5[...] = dot_right(d_expand[:, cols], weights)
        else:
            d_a5[...] += dot_right(d_expand[:, cols], weights)
    fixed[...] = jnp.zeros_like(fixed)
    for row in spans(SEQ, STEP):
        normed, rstd = normalize(x3[row])
        grad = d_a5[row]
        dx3[row] = top[row].astype(F32) + normalize_back(grad, normed, rstd, vec[6:7])
        fixed[6:7] += columns_sum(grad * normed)
        fixed[7:8] += columns_sum(grad)
    fixed[13:14] = low_columns_sum(top[...])


def attention_backward_kernel(
    info, dx3, attended, output_w, qkv, lse, a4, project_w, x2, vec, before,
    send, keep, dx2, d_sep, fixed, d_out, d_att, d_proj
):
    width = x2.shape[1]
    half = width // 2
    core = info[0]
    fixed[...] = before[...]
    d_out[...] = as_low(dx3[...])
    d_att[...] = as_low(dot_right(d_out[...], output_w[...]))
    scale = (width // HEADS) ** (-0.5)
    lanes = lax.broadcasted_iota(jnp.int32, (SEQ, 128), 1)
    valid = lax.broadcasted_iota(jnp.int32, (SEQ, SEQ), 1) < info[2]
    for pair in range(width // 128):
        at = pair * 128
        queries = qkv[:, at : at + 128]
        keys = qkv[:, width + at : width + at + 128]
        vals = qkv[:, 2 * width + at : 2 * width + at + 128]
        grads = d_att[:, at : at + 128]
        parts = []
        for side in range(2):
            head = 2 * pair + side
            mine = (lanes < 64) if side == 0 else (lanes >= 64)
            scores = masked_scores(jnp.where(mine, queries, 0), keys, valid, scale)
            probs = jnp.exp(scores - lse[:, head : head + 1])
            d_vals = dot_left(as_low(probs), grads)
            d_probs = dot_right(jnp.where(mine, grads, 0), vals)
            weighted = jnp.sum(d_probs * probs, -1, keepdims=True)
            d_scores = as_low(probs * (d_probs - weighted))
            parts.append((dot(d_scores, keys) * scale, dot_left(d_scores, queries) * scale, d_vals))
        for kind in range(3):
            here = slice(kind * width + at, kind * width + at + 128)
            d_proj[:, here] = as_low(jnp.where(lanes < 64, parts[0][kind], parts[1][kind]))
    for side, out in ((1 - core, send), (core, keep)):
        here = at_lane(side * half, half)
        put(out, 0, 4, 0, dot_left(a4[:, here], d_proj[...]))
        put(out, 0, 4, 3 * width * half // 1024, dot_left(attended[:, here], d_out[...]))
    fixed[12:13] = low_columns_sum(d_out[...])
    fixed[10:11] = low_columns_sum(d_proj[:, :width])
    fixed[11:12] = low_columns_sum(d_proj[:, 2 * width :])
    dx2[...] = dot_right(d_proj[...], project_w[...])
    for row in spans(SEQ, STEP):
        normed, rstd = normalize(x2[row])
        grad = dx2[row]
        dx2[row] = dx3[row] + normalize_back(grad, normed, rstd, vec[4:5])
        fixed[4:5] += columns_sum(grad * normed)
        fixed[5:6] += columns_sum(grad)
    channels = d_sep.shape[1]
    d_sep[...] = as_low(dx2[:, :channels])
    fixed[14:15, channels : 2 * channels] = low_columns_sum(d_sep[...])


def inner_backward_kernel(pieces, refs):
    info, refs = refs[0], refs[1:]
    (
        (d_sep, depth, normed_ref, slope_ref, rstd_ref, a2, bias_before, point, point_rest, left, left_rest),
        wide,
        outs,
        scratch,
    ) = unpack(refs, [11, pieces, 5, 6])
    keep, send, d_a2, d_right, grads = outs
    d_depth, padded, padded_two, d_left, first_ref, second_ref = scratch
    local = left.shape[1]
    inner = local * pieces
    core, offset = info[0], info[1]
    rows = local // 2
    half = a2.shape[1] // 2
    for piece in range(pieces):
        weights = point if piece == 0 else point_rest.at[piece - 1]
        for row in spans(local, 256):
            back = dot_right(d_sep[...], weights[row])
            index = (piece * local + row.start) // 128
            d_depth[index, 8 : SEQ + 8] = back[:, 0:128]
            d_depth[index + 1, 8 : SEQ + 8] = back[:, 128:256]
    first_ref[...] = jnp.zeros_like(first_ref)
    second_ref[...] = jnp.zeros_like(second_ref)
    for pad in (padded, padded_two):
        pad[0:8] = jnp.zeros((8, 128), F32)
        pad[SEQ + 8 : SEQ + 16] = jnp.zeros((8, 128), F32)
    grads[...] = jnp.zeros_like(grads)
    grads[1:2] = bias_before[0:1]
    kept = keep_rows(info, 0, SEQ)
    for piece in range(pieces):

        def one(at, pad):
            col = at_lane(at, 128)
            here = at_lane(piece * local + at, 128)
            index = (piece * local + at) // 128
            vectors = wide[piece][:, col].astype(F32)
            d_depth[index, 0:8] = jnp.zeros((8, 128), F32)
            d_depth[index, SEQ + 8 : SEQ + 16] = jnp.zeros((8, 128), F32)
            normed = normed_ref[:, here].astype(F32)
            pad[8 : SEQ + 8] = (normed * vectors[2:3] + vectors[3:4]) * kept
            own = d_depth[index, 8 : SEQ + 8]
            result = d_depth[index, 12 : SEQ + 12] * vectors[4:5]
            grads[4:5, here] = columns_sum(pad[4 : SEQ + 4] * own)
            for tap in range(1, 9):
                result = result + d_depth[index, 12 - tap : SEQ + 12 - tap] * vectors[4 + tap : 5 + tap]
                grads[4 + tap : 5 + tap, here] = columns_sum(pad[4 + tap : SEQ + 4 + tap] * own)
            result = result * kept
            grads[2:3, here] = columns_sum(result * normed)
            grads[3:4, here] = columns_sum(result)
            scaled = result * vectors[2:3]
            first_ref[...] += scaled
            second_ref[...] += scaled * normed
            d_depth[index, 8 : SEQ + 8] = scaled

        def step(index, carry):
            one(index * 256, padded)
            one(index * 256 + 128, padded_two)
            return carry

        lax.fori_loop(0, local // 256, step, 0)
    first_ref[...] = jnp.broadcast_to(
        jnp.sum(first_ref[...], 1, keepdims=True) * (1.0 / inner), first_ref.shape
    )
    second_ref[...] = jnp.broadcast_to(
        jnp.sum(second_ref[...], 1, keepdims=True) * (1.0 / inner), second_ref.shape
    )

    def back(index, carry):
        here = at_lane(index * 128, 128)
        normed = normed_ref[:, here].astype(F32)
        d_mixed = rstd_ref[...] * (
            d_depth[index, 8 : SEQ + 8] - first_ref[...] - normed * second_ref[...]
        )
        d_depth[index, 8 : SEQ + 8] = d_mixed
        d_left[:, here] = as_low(d_mixed * slope_ref[:, here].astype(F32))
        return carry

    lax.fori_loop(0, inner // 128, back, 0)
    for part in range(d_right.shape[1] // 128):
        d_right[:, part * 128 : (part + 1) * 128] = d_depth[offset // 128 + part, 8 : SEQ + 8]
    for piece in range(pieces):
        base = piece * local
        cols = slice(base, base + local)
        for side, out in ((1 - core, send), (core, keep)):
            grad = dot_left(a2[:, at_lane(side * half, half)], d_left[:, cols])
            put(out, 2 * piece, 2, 0, grad)
            grad = dot_left(depth[:, at_lane(base + side * rows, rows)], d_sep[...])
            put(out, 2 * piece, 2, half * local // 512, grad)
        grads[0:1, cols] = low_columns_sum(d_left[:, cols])
        if piece == 0:
            d_a2[...] = dot_right(d_left[:, cols], left[...])
        else:
            d_a2[...] += dot_right(d_left[:, cols], left_rest[piece - 1])


def last_kernel(
    info, d_a2_left, d_right, right_pre, conv_w, a2, x1, dx2, values, gates, a1, gated_w, x_ref, vec, before, wide_sums,
    send, keep, input_grad, fixed, shifted, d_a2, d_gated, rows_ref
):
    width = x1.shape[1]
    half = width // 2
    channels = right_pre.shape[1]
    core = info[0]
    fixed[...] = before[...]
    pre = right_pre[...]
    sigma = sigmoid(pre)
    low = as_low(d_right[...] * (sigma * (1.0 + pre * (1.0 - sigma))))
    fixed[14:15, 0:channels] = low_columns_sum(low)
    wide = low.astype(F32)
    rows = lax.broadcasted_iota(jnp.int32, wide.shape, 0)
    shifted[:, 0:channels] = as_low(
        jnp.where(rows == SEQ - 1, 0.0, pltpu.roll(wide, SEQ - 1, 0))
    )
    shifted[:, channels : 2 * channels] = low
    shifted[:, 2 * channels :] = as_low(jnp.where(rows == 0, 0.0, pltpu.roll(wide, 1, 0)))
    total = d_a2_left[...]
    for tap in range(3):
        total = total + dot_right(shifted[:, tap * channels : (tap + 1) * channels], conv_w[tap])
    d_a2[...] = total
    for row in spans(SEQ, STEP):
        normed, rstd = normalize(x1[row])
        grad = d_a2[row] * keep_rows(info, row.start, STEP)
        fixed[2:3] += columns_sum(grad * normed)
        fixed[3:4] += columns_sum(grad)
        dx1 = dx2[row] + normalize_back(grad, normed, rstd, vec[2:3])
        input_grad[row] = dx1
        gate = gates[row]
        scaled = dx1 * gate
        d_gated[row, 0:width] = as_low(scaled)
        d_gated[row, width:] = as_low(scaled * values[row] * (1.0 - gate))
    for side, out in ((1 - core, send), (core, keep)):
        here = at_lane(side * half, half)
        put(out, 0, 4, 0, dot_left(a1[:, here], d_gated[...]))
        put(out, 0, 4, half * width // 512, dot_left(a2[:, here], shifted[...]))
    sums = low_columns_sum(d_gated[...])
    fixed[8:9] = sums[:, 0:width]
    fixed[9:10] = sums[:, width:]
    d_a2[...] = dot_right(d_gated[...], gated_w[...])
    for row in spans(SEQ, STEP):
        normed, rstd = normalize(x_ref[row].astype(F32))
        grad = d_a2[row]
        fixed[0:1] += columns_sum(grad * normed)
        fixed[1:2] += columns_sum(grad)
        input_grad[row] += normalize_back(grad, normed, rstd, vec[0:1])
    pack_small(info, wide_sums, fixed, send, keep, rows_ref)


def pack_small(info, wide, fixed, send, keep, rows_ref):
    if rows_ref is None:
        return
    pieces = lax.axis_size("mp")
    local = wide.shape[1] // pieces
    parts = local // 256
    rows_ref[...] = jnp.zeros_like(rows_ref)
    for piece in range(pieces):
        owner = jnp.bitwise_xor(info[1] // local, piece)
        for part in range(parts):
            spot = pl.multiple_of((owner * parts + part) * 16, 16)
            at = piece * local + part * 256
            rows_ref[pl.ds(spot, 16)] = wide[:, at : at + 256]
    base = wide.shape[1] // 16
    for part in range(fixed.shape[1] // 256):
        rows_ref[base + part * 16 : base + (part + 1) * 16] = fixed[:, part * 256 : (part + 1) * 256]
    count = rows_ref.shape[0] // 2
    offset = send.shape[1] - count // 4
    for side, out in ((1 - info[0], send), (info[0], keep)):
        put(out, 0, 4, offset, rows_ref[pl.ds(pl.multiple_of(side * count, 16), count)])


def cut_kernel(parts, counts, refs):
    info, ins, outs, sems = refs[0], refs[1 : parts + 1], refs[parts + 1 : -1], refs[-1]
    copies = []
    for at, (source, target) in enumerate(zip(ins, outs)):
        rows = target.shape[0]
        code = (info[0], code_of(info, 4), code_z(info, 4))[counts[at]]
        here = pl.ds(pl.multiple_of(code * rows, 16), rows)
        copies.append(pltpu.make_async_copy(source.at[here], target, sems.at[at]))
    for copy in copies:
        copy.start()
    for copy in copies:
        copy.wait()


def cut(info, arrays, counts):
    outs = [
        shaped((item.shape[0] // (2 if kind == 0 else 4), item.shape[1]), item.dtype)
        for item, kind in zip(arrays, counts)
    ]
    return pl.pallas_call(
        lambda *refs: cut_kernel(len(arrays), counts, refs),
        out_shape=outs,
        in_specs=[pl.BlockSpec(memory_space=pltpu.SMEM)]
        + [pl.BlockSpec(memory_space=pl.ANY) for _ in arrays],
        out_specs=[pl.BlockSpec(memory_space=pltpu.VMEM) for _ in arrays],
        scratch_shapes=[pltpu.SemaphoreType.DMA((len(arrays),))],
    )(info, *arrays)


def flat_swap(values, partner):
    count = lax.axis_size("dp") * lax.axis_size("mp")
    return lax.ppermute(values, ("dp", "mp"), [(at, partner(at)) for at in range(count)])


PARTNERS = {
    "core": lambda at: at ^ 2,
    "first": lambda at: at ^ (4 if at & 2 else 1),
    "second": lambda at: at ^ (1 if at & 2 else 4),
    "x": lambda at: at ^ 1,
    "y": lambda at: at ^ 4,
    "near": lambda at: at ^ 8,
    "far": lambda at: at ^ 16,
}
INNER_STEPS = [
    ("quarter", "first"),
    ("half_mix", "second"),
    ("half_near", "near"),
    ("sum", "far"),
    ("sum", "near"),
    ("join_near", "y"),
    ("join_y", "core"),
    ("final", None),
]
SHARED_STEPS = [
    ("quarter", "first"),
    ("half_mix", "second"),
    ("half_near", "near"),
    ("sum", "far"),
    ("sum", "near"),
    ("join_near", "second"),
    ("join_mix", "first"),
    ("spread", "core"),
    ("final", None),
]


PLAN = "ab d c ab d c ab cd b a cd ep a c d p e c d p c d d d".split()


class Stream:
    def __init__(self, inner, mine, other, parts):
        self.inner = inner
        self.mine = mine
        self.flight = flat_swap(other, PARTNERS["core"])
        self.steps = list(INNER_STEPS if inner else SHARED_STEPS)
        self.parts = parts


def advance_kernel(jobs, refs):
    info, refs = refs[0], refs[1:]
    core, y, near = info[0], info[4], info[5]
    ins, outs = list(refs[: 2 * len(jobs)]), list(refs[2 * len(jobs) :])
    for inner, step, parts in jobs:
        mine, flight = ins.pop(0), ins.pop(0)
        x = 0 if inner else info[3]
        mix = core * x + (1 - core) * y

        def added(spot):
            return as_low(mine[spot].astype(F32) + flight[spot].astype(F32))

        if step == "quarter":
            keep, send = outs.pop(0), outs.pop(0)
            for at in range(2):
                send[at] = added(core * (2 * at + 1 - y) + (1 - core) * (2 * (1 - x) + at))
                keep[at] = added(core * (2 * at + y) + (1 - core) * (2 * x + at))
        elif step == "half_mix":
            keep, send = outs.pop(0), outs.pop(0)
            send[0] = added(1 - mix)
            keep[0] = added(mix)
        elif step == "half_near":
            keep, send = outs.pop(0), outs.pop(0)
            rows = keep.shape[1]
            for out, side in ((send, 1 - near), (keep, near)):
                here = pl.ds(pl.multiple_of(side * rows, 16), rows)
                out[0] = as_low(mine[0, here].astype(F32) + flight[0, here].astype(F32))
        elif step == "sum":
            outs.pop(0)[0] = added(0)
        elif step == "join_near":
            out = outs.pop(0)
            rows = mine.shape[1]
            out[0, pl.ds(pl.multiple_of(near * rows, 16), rows)] = mine[0]
            out[0, pl.ds(pl.multiple_of((1 - near) * rows, 16), rows)] = flight[0]
        elif step in ("join_y", "join_mix"):
            out = outs.pop(0)
            side = y if step == "join_y" else mix
            out[side] = mine[0]
            out[1 - side] = flight[0]
        elif step == "spread":
            out = outs.pop(0)
            for at in range(2):
                out[core * (2 * at + y) + (1 - core) * (2 * x + at)] = mine[at]
                out[core * (2 * at + 1 - y) + (1 - core) * (2 * (1 - x) + at)] = flight[at]
        else:
            for offset, rows, shape in parts:
                out = outs.pop(0)
                columns = shape[-1] // 256
                for source, side in ((mine, core), (flight, 1 - core)):
                    for quarter in range(mine.shape[0]):
                        spot = (side * mine.shape[0] + quarter) * rows
                        here = pl.ds(pl.multiple_of(spot, 16), rows)
                        for part in range(columns * (shape[0] if len(shape) == 3 else 1)):
                            at = offset + part * rows
                            block = source[quarter, at : at + rows].astype(F32)
                            if len(shape) == 3:
                                out[part, here] = block
                            else:
                                out[here, part * 256 : (part + 1) * 256] = block


def advance(chain, info, streams):
    jobs, ins, outs = [], [info], []
    for stream in streams:
        step = stream.steps[0][0]
        jobs.append((stream.inner, step, stream.parts))
        ins += [stream.mine, stream.flight]
        lead, rows, columns = stream.mine.shape
        if step in ("quarter", "half_mix"):
            outs += [shaped((lead // 2, rows, columns), LOW)] * 2
        elif step == "half_near":
            outs += [shaped((lead, rows // 2, columns), LOW)] * 2
        elif step == "sum":
            outs.append(shaped((lead, rows, columns), LOW))
        elif step == "join_near":
            outs.append(shaped((lead, rows * 2, columns), LOW))
        elif step == "final":
            outs += [shaped(shape, F32) for _, _, shape in stream.parts]
        else:
            outs.append(shaped((lead * 2, rows, columns), LOW))
    results = list(chain.run(lambda *refs: advance_kernel(jobs, refs), outs, ins, [], ADV))
    for stream in streams:
        step, partner = stream.steps.pop(0)
        if step == "final":
            stream.mine = [results.pop(0) for _ in stream.parts]
            continue
        stream.mine = results.pop(0)
        if step in ("quarter", "half_mix", "half_near"):
            stream.flight = flat_swap(results.pop(0), PARTNERS[partner])
        else:
            stream.flight = flat_swap(stream.mine, PARTNERS[partner])


def opened(packed, first, count, offset, rows, columns):
    parts = [
        packed[first : first + count, offset + at * rows : offset + (at + 1) * rows]
        for at in range(columns // 256)
    ]
    return jnp.concatenate(parts, 2).reshape(count * rows, columns)


def small_kernel(info, total, wide, fixed):
    local = wide.shape[1]
    parts = local // 256
    for part in range(parts):
        spot = pl.multiple_of((info[1] // local * parts + part) * 16, 16)
        wide[:, part * 256 : (part + 1) * 256] = total[pl.ds(spot, 16)]
    base = local * 2 // 16
    for part in range(fixed.shape[1] // 256):
        fixed[:, part * 256 : (part + 1) * 256] = total[base + part * 16 : base + (part + 1) * 16]


class Weights:
    def __init__(self, piece, kind):
        pieces = [piece]
        for bit in bits_of("mp"):
            pieces = pieces + [swap(item, "mp", bit) for item in pieces]
        self.blocks = [[item] for item in pieces[1:]]
        self.kind = kind

    def hop(self, after):
        for blocks in self.blocks:
            item, _ = lax.optimization_barrier((blocks[0], after))
            blocks[0] = item
            blocks.append(swap(item, "dp", (2, 4)[self.kind - 1]))

    def share(self, after):
        found = []
        for blocks in self.blocks:
            held = [lax.optimization_barrier((item, after))[0] for item in blocks]
            found += held + [swap(item, "dp", 1) for item in held]
        return found


def gather_small(own_piece):
    items = [own_piece]
    for bit in bits_of("mp"):
        items = items + [swap(item, "mp", bit) for item in items]
    return items


def finish_shared(mine, other, order):
    own = bit_of("dp", 1)
    values = add_low(mine, swap(other, "dp", 1))
    held = [("dp", 1, own)]
    for axis, bit in order[:-1]:
        own = bit_of(axis, bit)
        mine, other = split(values, own)
        values = add_low(mine, swap(other, axis, bit))
        held.append((axis, bit, own))
    axis, bit = order[-1]
    values = add_low(values, swap(values, axis, bit))
    for axis, bit, own in reversed(held):
        values = join(values, swap(values, axis, bit), own)
    return values.astype(F32)


def finish_inner(mine, other, order):
    values = add_low(mine, swap(other, "dp", 1))
    pieces = [values[at] for at in range(values.shape[0])]
    held = [("dp", 1, bit_of("dp", 1))]
    for axis, bit in order[:-1]:
        if axis == "mp":
            keep_count = len(pieces) // 2
            moved = [swap(item, axis, bit) for item in pieces[keep_count:]]
            pieces = [add_low(one, two) for one, two in zip(pieces[:keep_count], moved)]
            continue
        own = bit_of(axis, bit)
        parts = [split(item, own) for item in pieces]
        pieces = [add_low(mine, swap(other, axis, bit)) for mine, other in parts]
        held.append((axis, bit, own))
    axis, bit = order[-1]
    values = add_low(pieces[0], swap(pieces[0], axis, bit))
    for axis, bit, own in reversed(held):
        values = join(values, swap(values, axis, bit), own)
    return values.astype(F32)


def body(
    cell_input,
    lengths,
    out_grad,
    norm_params,
    gated_weight,
    gated_bias,
    left_weight,
    left_bias,
    conv_weight,
    conv_bias,
    inner_norm,
    depth_weight,
    point_weight,
    point_bias,
    project_weight,
    project_bias,
    output_weight,
    output_bias,
    expand_weight,
    expand_bias,
    shrink_weight,
    shrink_bias,
):
    width = cell_input.shape[1]
    channels = conv_weight.shape[2]
    local = left_weight.shape[1]
    pieces = lax.axis_size("mp")
    inner = local * pieces
    tokens = cell_input.shape[0]
    assert tokens == SEQ
    tuned = lax.axis_size("dp") == 16 and pieces == 2
    mp_bits = bits_of("mp")[::-1]
    dp_bits = bits_of("dp")[1:]
    mp_first = [("mp", bit) for bit in mp_bits] + [("dp", bit) for bit in dp_bits]
    core = bit_of("dp", 1)
    info = jnp.stack(
        [
            core,
            lax.axis_index("mp") * local,
            lengths[0],
            lax.axis_index("mp") % 2,
            bit_of("dp", 2),
            bit_of("dp", 4),
        ]
    ).astype(jnp.int32)
    chain = Chain()

    def inner_rows(size):
        return (2 * pieces, size // 1024, 256)


    kinds = (0, 1, 1, 2)
    owned = (left_weight, point_weight, expand_weight, shrink_weight)
    cuts = cut(info, owned, kinds)
    chain.link = cuts[-1]
    left, point, expand, shrink = [Weights(part, kind) for part, kind in zip(cuts, kinds)]
    wide = gather_small(
        jnp.concatenate(
            [
                left_bias[None],
                expand_bias[None],
                inner_norm,
                depth_weight,
                jnp.zeros((3, local), LOW),
            ],
            0,
        )
    )
    sizes = [(pieces - 1) * (2 if kind == 0 else 4) for kind in kinds]
    vec = jnp.concatenate(
        [
            norm_params.reshape(8, width),
            gated_bias.reshape(2, width),
            jnp.concatenate([conv_bias, point_bias]).reshape(1, width),
            project_bias,
            output_bias[None],
            shrink_bias[None],
            jnp.zeros((1, width), LOW),
        ],
        0,
    ).astype(F32)

    a1, values, gates, x1, a2, right_pre, right = chain.run(
        pre_kernel,
        [
            shaped((tokens, width), LOW),
            shaped((tokens, width), F32),
            shaped((tokens, width), F32),
            shaped((tokens, width), F32),
            shaped((tokens, width), LOW),
            shaped((tokens, channels), F32),
            shaped((tokens, channels), LOW),
        ],
        [info, cell_input, vec, gated_weight, conv_weight],
        [],
        int(2.2e9 * SCALE),
    )
    left_blocks = left.share(right)
    point.hop(right)
    normed, slope, depth, rstd, left_rest = chain.run(
        lambda *refs: inner_forward_kernel(pieces, sizes, refs),
        [
            shaped((tokens, inner), LOW),
            shaped((tokens, inner), LOW),
            shaped((tokens, inner), LOW),
            shaped((tokens, 128), F32),
            shaped((pieces - 1, width, local), LOW),
        ],
        [info, a2, right, left_weight] + left_blocks + wide,
        [
            pltpu.VMEM((tokens, inner), F32),
            pltpu.VMEM((tokens, 128), F32),
            pltpu.VMEM((tokens, 128), F32),
            pltpu.VMEM((tokens, 128), F32),
            pltpu.VMEM((tokens + 16, 128), F32),
            pltpu.VMEM((tokens + 16, 128), F32),
        ],
        int(6.5e9 * SCALE),
    )
    point_blocks = point.share(rstd)
    expand.hop(rstd)
    x2, a4, qkv, lse, attended, x3, a5, point_rest = chain.run(
        lambda *refs: attention_forward_kernel(pieces, sizes, refs),
        [
            shaped((tokens, width), F32),
            shaped((tokens, width), LOW),
            shaped((tokens, 3 * width), LOW),
            shaped((tokens, 128), F32),
            shaped((tokens, width), LOW),
            shaped((tokens, width), F32),
            shaped((tokens, width), LOW),
            shaped((pieces - 1, local, channels), LOW),
        ],
        [info, x1, depth, point_weight, vec, project_weight, output_weight] + point_blocks,
        [],
        int(4.4e9 * SCALE),
    )
    expand_blocks = expand.share(a5)
    shrink.hop(a5)
    hidden, feed_slope, shrink_keep, shrink_send, expand_rest = chain.run(
        lambda *refs: feed_kernel(pieces, sizes, refs),
        [
            shaped((tokens, inner), LOW),
            shaped((tokens, inner), LOW),
            shaped(inner_rows(local * width), LOW),
            shaped(inner_rows(local * width), LOW),
            shaped((pieces - 1, width, local), LOW),
        ],
        [info, a5, out_grad, expand_weight] + expand_blocks + wide,
        [],
        int(3.4e9 * SCALE),
    )
    if tuned:
        shr = Stream(True, shrink_keep, shrink_send, [(0, local // 4, (local, width))])
    shrink_blocks = shrink.share(hidden)
    cell_output, expand_keep, expand_send, dx3, fixed, expand_sum = chain.run(
        lambda *refs: feed_back_kernel(pieces, sizes, refs),
        [
            shaped((tokens, width), LOW),
            shaped(inner_rows(local * width), LOW),
            shaped(inner_rows(local * width), LOW),
            shaped((tokens, width), F32),
            shaped((16, width), F32),
            shaped((8, inner), F32),
        ],
        [info, a5, x3, out_grad, vec, hidden, feed_slope, expand_weight, expand_rest, shrink_weight]
        + shrink_blocks,
        [
            pltpu.VMEM((tokens, inner), LOW),
            pltpu.VMEM((tokens, width), F32),
            pltpu.VMEM((tokens, width), F32),
            pltpu.VMEM((pieces - 1, local, width), LOW),
        ],
        int(4.6e9 * SCALE),
    )
    if tuned:
        exp = Stream(True, expand_keep, expand_send, [(0, width // 4, (width, local))])
        advance(chain, info, [shr])
    proj_send, proj_keep, dx2, d_sep, fixed = chain.run(
        attention_backward_kernel,
        [
            shaped((4, width * width // 512, 256), LOW),
            shaped((4, width * width // 512, 256), LOW),
            shaped((tokens, width), F32),
            shaped((tokens, channels), LOW),
            shaped((16, width), F32),
        ],
        [info, dx3, attended, output_weight, qkv, lse, a4, project_weight, x2, vec, fixed],
        [
            pltpu.VMEM((tokens, width), LOW),
            pltpu.VMEM((tokens, width), LOW),
            pltpu.VMEM((tokens, 3 * width), LOW),
        ],
        int(6.7e9 * SCALE),
    )
    if tuned:
        pro = Stream(
            False,
            proj_keep,
            proj_send,
            [
                (0, width // 8, (width, 3 * width)),
                (3 * width * width // 2048, width // 8, (width, width)),
            ],
        )
        advance(chain, info, [exp, shr])
        advance(chain, info, [pro])
    left_keep, left_send, d_a2, d_right, wide_sums = chain.run(
        lambda *refs: inner_backward_kernel(pieces, refs),
        [
            shaped(inner_rows(local * (width + channels)), LOW),
            shaped(inner_rows(local * (width + channels)), LOW),
            shaped((tokens, width), F32),
            shaped((tokens, channels), F32),
            shaped((16, inner), F32),
        ],
        [
            info,
            d_sep,
            depth,
            normed,
            slope,
            rstd,
            a2,
            expand_sum,
            point_weight,
            point_rest,
            left_weight,
            left_rest,
        ]
        + wide,
        [
            pltpu.VMEM((inner // 128, tokens + 16, 128), F32),
            pltpu.VMEM((tokens + 16, 128), F32),
            pltpu.VMEM((tokens + 16, 128), F32),
            pltpu.VMEM((tokens, inner), LOW),
            pltpu.VMEM((tokens, 128), F32),
            pltpu.VMEM((tokens, 128), F32),
        ],
        int(11.5e9 * SCALE),
    )
    if tuned:
        lef = Stream(
            True,
            left_keep,
            left_send,
            [
                (0, width // 4, (width, local)),
                (width * local // 1024, local // 4, (local, channels)),
            ],
        )
        advance(chain, info, [shr, exp, pro])
    small = 32 if tuned else 0
    last_rows = width * (2 * width + 3 * channels) // 2048 + small
    last_send, last_keep, input_grad, fixed = chain.run(
        last_kernel if tuned else lambda *refs: last_kernel(*refs, None),
        [
            shaped((4, last_rows, 256), LOW),
            shaped((4, last_rows, 256), LOW),
            shaped((tokens, width), F32),
            shaped((16, width), F32),
        ],
        [
            info,
            d_a2,
            d_right,
            right_pre,
            conv_weight,
            a2,
            x1,
            dx2,
            values,
            gates,
            a1,
            gated_weight,
            cell_input,
            vec,
            fixed,
            wide_sums,
        ],
        [
            pltpu.VMEM((tokens, 3 * channels), LOW),
            pltpu.VMEM((tokens, width), F32),
            pltpu.VMEM((tokens, 2 * width), LOW),
        ]
        + ([pltpu.VMEM((8 * small, 256), F32)] if tuned else []),
        int(4.0e9 * SCALE),
    )
    if tuned:
        lat = Stream(
            False,
            last_keep,
            last_send,
            [
                (0, width // 8, (width, 2 * width)),
                (width * width // 1024, width // 8, (3, width, channels)),
                (last_rows - small, small, (8 * small, 256)),
            ],
        )
        advance(chain, info, [lef])
        groups = {"a": [shr], "b": [exp, pro], "e": [exp], "p": [pro], "c": [lef], "d": [lat]}
        for names in PLAN:
            advance(chain, info, [item for name in names for item in groups[name]])
        wide_total, fixed = chain.run(
            small_kernel,
            [shaped((16, local), F32), shaped((16, width), F32)],
            [info, lat.mine[2]],
            [],
            10**6,
        )
        (grad_shrink,), (grad_expand,), (grad_left, grad_point) = shr.mine, exp.mine, lef.mine
        (grad_proj, grad_out), (grad_gated, grad_conv, _) = pro.mine, lat.mine
    else:

        def whole(keep, send, offset, rows, columns):
            both = [
                jnp.stack([opened(item, 2 * at, 2, offset, rows, columns) for at in range(pieces)])
                for item in (keep, send)
            ]
            return finish_inner(both[0], both[1], mp_first)

        def shared(keep, send, offset, rows, columns):
            both = [opened(item, 0, 4, offset, rows, columns) for item in (keep, send)]
            return finish_shared(both[0], both[1], mp_first)

        eighth = width // 8
        grad_shrink = whole(shrink_keep, shrink_send, 0, local // 4, width)
        grad_expand = whole(expand_keep, expand_send, 0, width // 4, local)
        grad_left = whole(left_keep, left_send, 0, width // 4, local)
        grad_point = whole(left_keep, left_send, width * local // 1024, local // 4, channels)
        grad_proj = shared(proj_keep, proj_send, 0, eighth, 3 * width)
        grad_out = shared(proj_keep, proj_send, 6 * eighth, eighth, width)
        grad_gated = shared(last_keep, last_send, 0, eighth, 2 * width)
        grad_conv = jnp.stack(
            [shared(last_keep, last_send, (4 + at) * eighth, eighth, channels) for at in range(3)]
        )
        chunks = [wide_sums[:, at : at + local] for at in range(0, inner, local)]
        for bit in mp_bits:
            count = len(chunks) // 2
            moved = [swap(item, "mp", bit) for item in chunks[count:]]
            chunks = [one + two for one, two in zip(chunks[:count], moved)]
            fixed = fixed + swap(fixed, "mp", bit)
        wide_total = chunks[0]
        for bit in bits_of("dp"):
            fixed = fixed + swap(fixed, "dp", bit)
            wide_total = wide_total + swap(wide_total, "dp", bit)
    return (
        cell_output,
        input_grad,
        fixed[0:8].reshape(4, 2, width),
        grad_gated,
        fixed[8:10].reshape(2 * width),
        grad_left,
        wide_total[0],
        grad_conv,
        fixed[14, :channels],
        wide_total[2:4],
        wide_total[4:13],
        grad_point,
        fixed[14, channels:],
        grad_proj,
        fixed[10:12],
        grad_out,
        fixed[12],
        grad_expand,
        wide_total[1],
        grad_shrink,
        fixed[13],
    )


def solution(mesh):
    return jax.shard_map(
        body,
        mesh=mesh,
        in_specs=(
            P(("dp", "mp"), None),
            P(("dp", "mp")),
            P(("dp", "mp"), None),
            P(),
            P(),
            P(),
            P(None, "mp"),
            P("mp"),
            P(),
            P(),
            P(None, "mp"),
            P(None, "mp"),
            P("mp", None),
            P(),
            P(),
            P(),
            P(),
            P(),
            P(None, "mp"),
            P("mp"),
            P("mp", None),
            P(),
        ),
        out_specs=(
            P(("dp", "mp"), None),
            P(("dp", "mp"), None),
            P(),
            P(),
            P(),
            P(None, "mp"),
            P("mp"),
            P(),
            P(),
            P(None, "mp"),
            P(None, "mp"),
            P("mp", None),
            P(),
            P(),
            P(),
            P(),
            P(),
            P(None, "mp"),
            P("mp"),
            P("mp", None),
            P(),
        ),
        check_vma=False,
    )
```

```python
import jax
import jax.numpy as jnp
from jax import lax
from jax.experimental import pallas as pl
from jax.experimental.pallas import tpu as pltpu
from jax.sharding import PartitionSpec as P

HEADS = 8
SEQ = 256
EPS = 1e-06
NEGATIVE = -1000000000.0
LOW = jnp.bfloat16
F32 = jnp.float32
STEP = 64
LIMIT = 24 * 2**20
SCALE = 4
EARLY = 0.001
ADV = 20 * 10**9


def as_low(values):
    return values.astype(LOW)


def dot(left, right):
    return jnp.dot(left, right, preferred_element_type=F32)


def dot_left(left, right):
    return lax.dot_general(left, right, (((0,), (0,)), ((), ())), preferred_element_type=F32)


def dot_right(left, right):
    return lax.dot_general(left, right, (((1,), (1,)), ((), ())), preferred_element_type=F32)


def swap(values, axis, bit):
    count = lax.axis_size(axis)
    return lax.ppermute(values, axis, [(at, at ^ bit) for at in range(count)])


def bit_of(axis, bit):
    return (lax.axis_index(axis) // bit) % 2


def bits_of(axis):
    bits, bit = [], 1
    while bit < lax.axis_size(axis):
        bits.append(bit)
        bit *= 2
    return bits


def add_low(first, second):
    return as_low(first.astype(F32) + second.astype(F32))


def split(values, own):
    half = values.shape[0] // 2
    mine = lax.dynamic_slice_in_dim(values, own * half, half, 0)
    other = lax.dynamic_slice_in_dim(values, (1 - own) * half, half, 0)
    return mine, other


def join(mine, other, own):
    swapped = own == 1
    return jnp.concatenate(
        [jnp.where(swapped, other, mine), jnp.where(swapped, mine, other)], 0
    )


def sum_shared(values, order):
    held = []
    steps = [("dp", 1)] + order
    for axis, bit in steps[:-1]:
        own = bit_of(axis, bit)
        mine, other = split(values, own)
        values = add_low(mine, swap(other, axis, bit))
        held.append((axis, bit, own))
    axis, bit = steps[-1]
    values = add_low(values, swap(values, axis, bit))
    for axis, bit, own in reversed(held):
        values = join(values, swap(values, axis, bit), own)
    return values.astype(F32)


def sum_inner(pieces, order):
    held = []
    steps = [("dp", 1)] + order
    for axis, bit in steps[:-1]:
        if axis == "mp":
            keep_count = len(pieces) // 2
            moved = [swap(item, axis, bit) for item in pieces[keep_count:]]
            pieces = [add_low(one, two) for one, two in zip(pieces[:keep_count], moved)]
            continue
        own = bit_of(axis, bit)
        parts = [split(item, own) for item in pieces]
        pieces = [add_low(mine, swap(other, axis, bit)) for mine, other in parts]
        held.append((axis, bit, own))
    axis, bit = steps[-1]
    values = add_low(pieces[0], swap(pieces[0], axis, bit))
    for axis, bit, own in reversed(held):
        values = join(values, swap(values, axis, bit), own)
    return values.astype(F32)


def sigmoid(values):
    return 0.5 * jnp.tanh(0.5 * values) + 0.5


def spans(total, step):
    return [slice(at, at + step) for at in range(0, total, step)]


def at_lane(start, size):
    return pl.ds(pl.multiple_of(start, 128), size)


def normalize(values):
    width = values.shape[1]
    centre = jnp.sum(values, -1, keepdims=True) * (1.0 / width)
    centered = values - centre
    variance = jnp.sum(centered * centered, -1, keepdims=True) * (1.0 / width)
    rstd = lax.rsqrt(variance + EPS)
    return centered * rstd, rstd


def normalize_back(grad, normed, rstd, gain):
    width = grad.shape[1]
    scaled = grad * gain
    first = jnp.sum(scaled, -1, keepdims=True) * (1.0 / width)
    second = jnp.sum(scaled * normed, -1, keepdims=True) * (1.0 / width)
    return rstd * (scaled - first - normed * second)


def columns_sum(values):
    return jnp.sum(values, 0, keepdims=True)


def low_columns_sum(values):
    ones = jnp.ones((16, values.shape[0]), LOW)
    return dot(ones, values)[0:1]


def keep_rows(info, start, rows):
    return jnp.where(
        lax.broadcasted_iota(jnp.int32, (rows, 1), 0) + start < info[2], 1.0, 0.0
    ).astype(F32)


class Chain:
    def __init__(self):
        self.link = None

    def run(self, kernel, outs, ins, scratch, flops, placed=0):
        specs = [pl.BlockSpec(memory_space=pltpu.SMEM)] + [
            pl.BlockSpec(memory_space=pltpu.VMEM) for _ in ins[1:]
        ]
        count = len(ins)
        moved = sum(item.size * item.dtype.itemsize for item in list(ins) + list(outs))
        ins = list(ins)
        linked = self.link is not None
        if linked:
            ins.append(self.link)
            specs.append(pl.BlockSpec(memory_space=pl.ANY))

        def call(*refs):
            kernel(*(refs[:count] + refs[count + 1 :] if linked else refs))

        results = pl.pallas_call(
            call,
            out_shape=outs,
            in_specs=specs,
            out_specs=[
                pl.BlockSpec(memory_space=pltpu.HBM if at < placed else pltpu.VMEM)
                for at in range(len(outs))
            ],
            scratch_shapes=scratch,
            compiler_params=pltpu.CompilerParams(vmem_limit_bytes=LIMIT),
            cost_estimate=pl.CostEstimate(flops=flops, bytes_accessed=moved + flops // 50, transcendentals=0),
        )(*ins)
        self.link = min(results, key=lambda item: item.size)
        return results


def put(out, first, count, offset, values):
    rows = values.shape[0] // count
    low = as_low(values)
    for quarter in range(count):
        for part in range(values.shape[1] // 256):
            at = offset + part * rows
            out[first + quarter, at : at + rows] = low[
                quarter * rows : (quarter + 1) * rows, part * 256 : (part + 1) * 256
            ]


def shaped(shape, kind):
    return jax.ShapeDtypeStruct(shape, kind)


def pre_kernel(
    info, x_ref, gated_w, conv_w, norms, gated_b, conv_b, point_b, project_b, output_b, shrink_b,
    a1, values, gates, x1, a2, right_pre, vec, right
):
    width = x_ref.shape[1]
    channels = right.shape[1]
    vec[...] = jnp.zeros_like(vec)
    for at in range(4):
        vec[2 * at : 2 * at + 2] = norms[at].astype(F32)
    for row, item in ((8, gated_b.at[0:width]), (9, gated_b.at[width:]), (13, output_b), (14, shrink_b)):
        vec[row : row + 1] = item[...].astype(F32).reshape(1, width)
    vec[10:11, 0:channels] = conv_b[...].astype(F32).reshape(1, channels)
    vec[10:11, channels:] = point_b[...].astype(F32).reshape(1, channels)
    vec[11:13] = project_b[...].astype(F32)
    for row in spans(SEQ, STEP):
        normed, _ = normalize(x_ref[row].astype(F32))
        a1[row] = as_low(normed * vec[0:1] + vec[1:2])
    for col in spans(width, 256):
        gate_col = slice(col.start + width, col.stop + width)
        value = dot(a1[...], gated_w[:, col]) + vec[8:9, col]
        gate = sigmoid(dot(a1[...], gated_w[:, gate_col]) + vec[9:10, col])
        values[:, col] = value
        gates[:, col] = gate
        x1[:, col] = x_ref[:, col].astype(F32) + value * gate
    for row in spans(SEQ, STEP):
        normed, _ = normalize(x1[row])
        kept = keep_rows(info, row.start, STEP)
        a2[row] = as_low((normed * vec[2:3] + vec[3:4]) * kept)
    rows = lax.broadcasted_iota(jnp.int32, right_pre.shape, 0)
    first = jnp.where(rows == 0, 0.0, pltpu.roll(dot(a2[...], conv_w[0]), 1, 0))
    last = jnp.where(rows == SEQ - 1, 0.0, pltpu.roll(dot(a2[...], conv_w[2]), SEQ - 1, 0))
    total = first + dot(a2[...], conv_w[1]) + last + vec[10:11, 0 : right_pre.shape[1]]
    right_pre[...] = total
    right[...] = as_low(total * sigmoid(total))


def unpack(refs, counts):
    groups, at = [], 0
    for count in counts:
        groups.append(refs[at : at + count])
        at += count
    return groups


def places(info, count):
    core, y, near = info[0], info[4], info[5]
    if count == 2:
        return [core, 1 - core]
    mine = (1 - core) * y + core * near
    theirs = (1 - core) * near + core * y
    return [2 * core + mine, 2 * core + 1 - mine, 2 - 2 * core + theirs, 3 - 2 * core - theirs]


def assemble(info, target, blocks, offset):
    rows = target.shape[0] // len(blocks)
    for spot, block in zip(places(info, len(blocks)), blocks):
        here = pl.ds(pl.multiple_of(spot * rows, 16), rows)
        for part in range(target.shape[1] // 256):
            at = offset + part * rows
            target[here, part * 256 : (part + 1) * 256] = block[at : at + rows]


def vectors_of(own, blocks, per_piece, offset):
    found = [(own, 0)]
    for at in range(0, len(blocks), per_piece):
        found.append((blocks[at], offset))
    return found


def rows_of(vectors, index, lanes):
    ref, offset = vectors
    return ref[pl.ds(pl.multiple_of(offset + index * 16, 16), 16), lanes].astype(F32)


def inner_forward_kernel(pieces, per, refs):
    info, refs = refs[0], refs[1:]
    (a2, right, left, own), packed, outs, scratch = unpack(refs, [4, per * (pieces - 1), 5, 6])
    normed_ref, slope_ref, depth, rstd_ref, left_rest = outs
    mixed, total, square, centre_ref, padded, padded_two = scratch
    local = left.shape[1]
    inner = local * pieces
    offset = info[1]
    skipped = a2.shape[1] * local // (256 * per) + local // per
    wide = vectors_of(own, packed, per, skipped)
    right_rows = right[...].astype(F32)
    total[...] = jnp.zeros_like(total)
    square[...] = jnp.zeros_like(square)
    for piece in range(pieces):
        if piece:
            assemble(info, left_rest.at[piece - 1], packed[(piece - 1) * per : piece * per], 0)
        for col in spans(local, 256):
            weights = left[:, col] if piece == 0 else left_rest[piece - 1, :, col]
            pre = dot(a2[...], weights)
            pre = pre + rows_of(wide[piece], col.start // 256, slice(0, 256))[0:1]
            sigma = sigmoid(pre)
            at = piece * local + col.start
            here = slice(at, at + 256)
            slope_ref[:, here] = as_low(sigma * (1.0 + pre * (1.0 - sigma)))
            value = pre * sigma + right_rows * jnp.where(offset == at, 1.0, 0.0)
            mixed[:, here] = value
            total[...] += value[:, 0:128] + value[:, 128:256]
            squared = value * value
            square[...] += squared[:, 0:128] + squared[:, 128:256]
    centre = jnp.sum(total[...], 1, keepdims=True) * (1.0 / inner)
    variance = jnp.sum(square[...], 1, keepdims=True) * (1.0 / inner) - centre * centre
    rstd = lax.rsqrt(variance + EPS)
    centre_ref[...] = jnp.broadcast_to(centre, centre_ref.shape)
    rstd_ref[...] = jnp.broadcast_to(rstd, rstd_ref.shape)
    for pad in (padded, padded_two):
        pad[0:8] = jnp.zeros((8, 128), F32)
        pad[SEQ + 8 : SEQ + 16] = jnp.zeros((8, 128), F32)
    kept = keep_rows(info, 0, SEQ)
    for piece in range(pieces):

        def one(index, part, pad):
            here = at_lane(piece * local + index * 256 + part, 128)
            vectors = rows_of(wide[piece], index, slice(part, part + 128))
            normed = (mixed[:, here] - centre_ref[...]) * rstd_ref[...]
            normed_ref[:, here] = as_low(normed)
            pad[8 : SEQ + 8] = (normed * vectors[2:3] + vectors[3:4]) * kept
            result = pad[4 : SEQ + 4] * vectors[4:5]
            for tap in range(1, 9):
                result = result + pad[4 + tap : SEQ + 4 + tap] * vectors[4 + tap : 5 + tap]
            depth[:, here] = as_low(result)

        def step(index, carry):
            one(index, 0, padded)
            one(index, 128, padded_two)
            return carry

        lax.fori_loop(0, local // 256, step, 0)


def masked_scores(queries, keys, valid, scale):
    return jnp.where(valid, dot_right(queries, keys) * scale, NEGATIVE)


def attention_forward_kernel(pieces, per, refs):
    (info, x1, depth, point, vec, project_w, output_w), packed, outs = unpack(
        refs, [7, per * (pieces - 1), 8]
    )
    x2, a4, qkv, lse, attended, x3, a5, point_rest = outs
    width = x2.shape[1]
    local, channels = point.shape
    sep = dot(depth[:, 0:local], point[...])
    for piece in range(1, pieces):
        blocks = packed[(piece - 1) * per : piece * per]
        assemble(info, point_rest.at[piece - 1], blocks, width * local // (256 * per))
        sep = sep + dot(depth[:, piece * local : (piece + 1) * local], point_rest[piece - 1])
    x2[:, 0:channels] = x1[:, 0:channels] + sep + vec[10:11, channels : 2 * channels]
    x2[:, channels:width] = x1[:, channels:width]
    for row in spans(SEQ, STEP):
        normed, _ = normalize(x2[row])
        a4[row] = as_low(normed * vec[4:5] + vec[5:6])
    for col in spans(3 * width, 256):
        part = dot(a4[...], project_w[:, col])
        if col.start < width:
            part = part + vec[11:12, col]
        elif col.start >= 2 * width:
            part = part + vec[12:13, col.start - 2 * width : col.stop - 2 * width]
        qkv[:, col] = as_low(part)
    scale = (width // HEADS) ** (-0.5)
    lanes = lax.broadcasted_iota(jnp.int32, (SEQ, 128), 1)
    valid = lax.broadcasted_iota(jnp.int32, (SEQ, SEQ), 1) < info[2]
    logs = jnp.zeros((SEQ, 128), F32)
    for pair in range(width // 128):
        at = pair * 128
        queries = qkv[:, at : at + 128]
        keys = qkv[:, width + at : width + at + 128]
        vals = qkv[:, 2 * width + at : 2 * width + at + 128]
        mixed = []
        for side in range(2):
            mine = (lanes < 64) if side == 0 else (lanes >= 64)
            scores = masked_scores(jnp.where(mine, queries, 0), keys, valid, scale)
            highest = jnp.max(scores, -1, keepdims=True)
            weights = jnp.exp(scores - highest)
            total = jnp.sum(weights, -1, keepdims=True)
            mixed.append(dot(as_low(weights * (1.0 / total)), vals))
            logs = jnp.where(lanes == 2 * pair + side, highest + jnp.log(total), logs)
        attended[:, at : at + 128] = as_low(jnp.where(lanes < 64, mixed[0], mixed[1]))
    lse[...] = logs
    x3[...] = x2[...] + dot(attended[...], output_w[...]) + vec[13:14]
    for row in spans(SEQ, STEP):
        normed, _ = normalize(x3[row])
        a5[row] = as_low(normed * vec[6:7] + vec[7:8])


def feed_kernel(pieces, per, refs):
    info, refs = refs[0], refs[1:]
    (a5, x3, top, vec, expand, shrink, own), first, packed, outs, scratch = unpack(
        refs, [7, per * (pieces - 1), per * (pieces - 1), 6, 7]
    )
    output, keep, send, dx3, fixed, grad_bias = outs
    hidden, slope, d_expand, shrunk, d_a5, expand_rest, shrink_rest = scratch
    local = expand.shape[1]
    width = x3.shape[1]
    half, rows = width // 2, local // 2
    core = info[0]
    wide = vectors_of(own, first, per, width * local // (256 * per) + local // per)
    for piece in range(pieces):
        if piece:
            blocks = packed[(piece - 1) * per : piece * per]
            assemble(info, expand_rest.at[piece - 1], blocks, 0)
            assemble(info, shrink_rest.at[piece - 1], blocks, width * local // (256 * per))
        for col in spans(local, 256):
            weights = expand[:, col] if piece == 0 else expand_rest[piece - 1, :, col]
            pre = dot(a5[...], weights)
            pre = pre + rows_of(wide[piece], col.start // 256, slice(0, 256))[1:2]
            sigma = sigmoid(pre)
            here = slice(piece * local + col.start, piece * local + col.stop)
            hidden[:, here] = as_low(pre * sigma)
            slope[:, here] = sigma * (1.0 + pre * (1.0 - sigma))
    for piece in range(pieces):
        base = piece * local
        weights = shrink if piece == 0 else shrink_rest.at[piece - 1]
        part = dot(hidden[:, base : base + local], weights[...])
        if piece == 0:
            shrunk[...] = part
        else:
            shrunk[...] += part
        for row in spans(local, 256):
            here = slice(base + row.start, base + row.stop)
            d_expand[:, here] = as_low(dot_right(top[...], weights[row]) * slope[:, here])
    for row in spans(SEQ, STEP):
        output[row] = as_low(x3[row] + shrunk[row] + vec[14:15])
    for piece in range(pieces):
        base = piece * local
        cols = slice(base, base + local)
        for side, out in ((1 - core, send), (core, keep)):
            grad = dot_left(hidden[:, at_lane(base + side * rows, rows)], top[...])
            put(out, 2 * piece, 2, 0, grad)
            grad = dot_left(a5[:, at_lane(side * half, half)], d_expand[:, cols])
            put(out, 2 * piece, 2, width * local // 1024, grad)
        grad_bias[:, cols] = jnp.broadcast_to(low_columns_sum(d_expand[:, cols]), (8, local))
        if piece == 0:
            d_a5[...] = dot_right(d_expand[:, cols], expand[...])
        else:
            d_a5[...] += dot_right(d_expand[:, cols], expand_rest[piece - 1])
    fixed[...] = jnp.zeros_like(fixed)
    for row in spans(SEQ, STEP):
        normed, rstd = normalize(x3[row])
        grad = d_a5[row]
        dx3[row] = top[row].astype(F32) + normalize_back(grad, normed, rstd, vec[6:7])
        fixed[6:7] += columns_sum(grad * normed)
        fixed[7:8] += columns_sum(grad)
    fixed[13:14] = low_columns_sum(top[...])


def attention_backward_kernel(
    info, dx3, attended, output_w, qkv, lse, a4, project_w, x2, vec, before,
    send, keep, dx2, d_sep, fixed, d_out, d_att, d_proj
):
    width = x2.shape[1]
    half = width // 2
    core = info[0]
    fixed[...] = before[...]
    d_out[...] = as_low(dx3[...])
    d_att[...] = as_low(dot_right(d_out[...], output_w[...]))
    scale = (width // HEADS) ** (-0.5)
    lanes = lax.broadcasted_iota(jnp.int32, (SEQ, 128), 1)
    valid = lax.broadcasted_iota(jnp.int32, (SEQ, SEQ), 1) < info[2]
    for pair in range(width // 128):
        at = pair * 128
        queries = qkv[:, at : at + 128]
        keys = qkv[:, width + at : width + at + 128]
        vals = qkv[:, 2 * width + at : 2 * width + at + 128]
        grads = d_att[:, at : at + 128]
        parts = []
        for side in range(2):
            head = 2 * pair + side
            mine = (lanes < 64) if side == 0 else (lanes >= 64)
            scores = masked_scores(jnp.where(mine, queries, 0), keys, valid, scale)
            probs = jnp.exp(scores - lse[:, head : head + 1])
            d_vals = dot_left(as_low(probs), grads)
            d_probs = dot_right(jnp.where(mine, grads, 0), vals)
            weighted = jnp.sum(d_probs * probs, -1, keepdims=True)
            d_scores = as_low(probs * (d_probs - weighted))
            parts.append((dot(d_scores, keys) * scale, dot_left(d_scores, queries) * scale, d_vals))
        for kind in range(3):
            here = slice(kind * width + at, kind * width + at + 128)
            d_proj[:, here] = as_low(jnp.where(lanes < 64, parts[0][kind], parts[1][kind]))
    for side, out in ((1 - core, send), (core, keep)):
        here = at_lane(side * half, half)
        put(out, 0, 4, 0, dot_left(a4[:, here], d_proj[...]))
        put(out, 0, 4, 3 * width * half // 1024, dot_left(attended[:, here], d_out[...]))
    fixed[12:13] = low_columns_sum(d_out[...])
    fixed[10:11] = low_columns_sum(d_proj[:, :width])
    fixed[11:12] = low_columns_sum(d_proj[:, 2 * width :])
    dx2[...] = dot_right(d_proj[...], project_w[...])
    for row in spans(SEQ, STEP):
        normed, rstd = normalize(x2[row])
        grad = dx2[row]
        dx2[row] = dx3[row] + normalize_back(grad, normed, rstd, vec[4:5])
        fixed[4:5] += columns_sum(grad * normed)
        fixed[5:6] += columns_sum(grad)
    channels = d_sep.shape[1]
    d_sep[...] = as_low(dx2[:, :channels])
    fixed[14:15, channels : 2 * channels] = low_columns_sum(d_sep[...])


def inner_backward_kernel(pieces, per, refs):
    info, refs = refs[0], refs[1:]
    (
        (d_sep, depth, normed_ref, slope_ref, rstd_ref, a2, bias_before, point, point_rest),
        (left, left_rest, own),
        packed,
        outs,
        scratch,
    ) = unpack(refs, [9, 3, per * (pieces - 1), 5, 6])
    keep, send, d_a2, d_right, grads = outs
    d_depth, padded, padded_two, d_left, first_ref, second_ref = scratch
    local = left.shape[1]
    inner = local * pieces
    core, offset = info[0], info[1]
    rows = local // 2
    half = a2.shape[1] // 2
    wide = vectors_of(own, packed, per, a2.shape[1] * local // (256 * per) + local // per)
    for piece in range(pieces):
        weights = point if piece == 0 else point_rest.at[piece - 1]
        for row in spans(local, 256):
            back = dot_right(d_sep[...], weights[row])
            index = (piece * local + row.start) // 128
            d_depth[index, 8 : SEQ + 8] = back[:, 0:128]
            d_depth[index + 1, 8 : SEQ + 8] = back[:, 128:256]
    first_ref[...] = jnp.zeros_like(first_ref)
    second_ref[...] = jnp.zeros_like(second_ref)
    for pad in (padded, padded_two):
        pad[0:8] = jnp.zeros((8, 128), F32)
        pad[SEQ + 8 : SEQ + 16] = jnp.zeros((8, 128), F32)
    grads[...] = jnp.zeros_like(grads)
    grads[1:2] = bias_before[0:1]
    kept = keep_rows(info, 0, SEQ)
    for piece in range(pieces):

        def one(pair, part, pad):
            here = at_lane(piece * local + pair * 256 + part, 128)
            index = piece * (local // 128) + 2 * pair + part // 128
            vectors = rows_of(wide[piece], pair, slice(part, part + 128))
            d_depth[index, 0:8] = jnp.zeros((8, 128), F32)
            d_depth[index, SEQ + 8 : SEQ + 16] = jnp.zeros((8, 128), F32)
            normed = normed_ref[:, here].astype(F32)
            pad[8 : SEQ + 8] = (normed * vectors[2:3] + vectors[3:4]) * kept
            own = d_depth[index, 8 : SEQ + 8]
            result = d_depth[index, 12 : SEQ + 12] * vectors[4:5]
            grads[4:5, here] = columns_sum(pad[4 : SEQ + 4] * own)
            for tap in range(1, 9):
                result = result + d_depth[index, 12 - tap : SEQ + 12 - tap] * vectors[4 + tap : 5 + tap]
                grads[4 + tap : 5 + tap, here] = columns_sum(pad[4 + tap : SEQ + 4 + tap] * own)
            result = result * kept
            grads[2:3, here] = columns_sum(result * normed)
            grads[3:4, here] = columns_sum(result)
            scaled = result * vectors[2:3]
            first_ref[...] += scaled
            second_ref[...] += scaled * normed
            d_depth[index, 8 : SEQ + 8] = scaled

        def step(index, carry):
            one(index, 0, padded)
            one(index, 128, padded_two)
            return carry

        lax.fori_loop(0, local // 256, step, 0)
    first_ref[...] = jnp.broadcast_to(
        jnp.sum(first_ref[...], 1, keepdims=True) * (1.0 / inner), first_ref.shape
    )
    second_ref[...] = jnp.broadcast_to(
        jnp.sum(second_ref[...], 1, keepdims=True) * (1.0 / inner), second_ref.shape
    )

    def back(index, carry):
        here = at_lane(index * 128, 128)
        normed = normed_ref[:, here].astype(F32)
        d_mixed = rstd_ref[...] * (
            d_depth[index, 8 : SEQ + 8] - first_ref[...] - normed * second_ref[...]
        )
        d_depth[index, 8 : SEQ + 8] = d_mixed
        d_left[:, here] = as_low(d_mixed * slope_ref[:, here].astype(F32))
        return carry

    lax.fori_loop(0, inner // 128, back, 0)
    for part in range(d_right.shape[1] // 128):
        d_right[:, part * 128 : (part + 1) * 128] = d_depth[offset // 128 + part, 8 : SEQ + 8]
    for piece in range(pieces):
        base = piece * local
        cols = slice(base, base + local)
        for side, out in ((1 - core, send), (core, keep)):
            grad = dot_left(a2[:, at_lane(side * half, half)], d_left[:, cols])
            put(out, 2 * piece, 2, 0, grad)
            grad = dot_left(depth[:, at_lane(base + side * rows, rows)], d_sep[...])
            put(out, 2 * piece, 2, half * local // 512, grad)
        grads[0:1, cols] = low_columns_sum(d_left[:, cols])
        if piece == 0:
            d_a2[...] = dot_right(d_left[:, cols], left[...])
        else:
            d_a2[...] += dot_right(d_left[:, cols], left_rest[piece - 1])


def last_kernel(
    info, d_a2_left, d_right, right_pre, conv_w, a2, x1, dx2, values, gates, a1, gated_w, x_ref, vec, before, wide_sums,
    send, keep, input_grad, fixed, shifted, d_a2, d_gated, rows_ref
):
    width = x1.shape[1]
    half = width // 2
    channels = right_pre.shape[1]
    core = info[0]
    fixed[...] = before[...]
    pre = right_pre[...]
    sigma = sigmoid(pre)
    low = as_low(d_right[...] * (sigma * (1.0 + pre * (1.0 - sigma))))
    fixed[14:15, 0:channels] = low_columns_sum(low)
    wide = low.astype(F32)
    rows = lax.broadcasted_iota(jnp.int32, wide.shape, 0)
    shifted[:, 0:channels] = as_low(
        jnp.where(rows == SEQ - 1, 0.0, pltpu.roll(wide, SEQ - 1, 0))
    )
    shifted[:, channels : 2 * channels] = low
    shifted[:, 2 * channels :] = as_low(jnp.where(rows == 0, 0.0, pltpu.roll(wide, 1, 0)))
    total = d_a2_left[...]
    for tap in range(3):
        total = total + dot_right(shifted[:, tap * channels : (tap + 1) * channels], conv_w[tap])
    d_a2[...] = total
    for row in spans(SEQ, STEP):
        normed, rstd = normalize(x1[row])
        grad = d_a2[row] * keep_rows(info, row.start, STEP)
        fixed[2:3] += columns_sum(grad * normed)
        fixed[3:4] += columns_sum(grad)
        dx1 = dx2[row] + normalize_back(grad, normed, rstd, vec[2:3])
        input_grad[row] = dx1
        gate = gates[row]
        scaled = dx1 * gate
        d_gated[row, 0:width] = as_low(scaled)
        d_gated[row, width:] = as_low(scaled * values[row] * (1.0 - gate))
    for side, out in ((1 - core, send), (core, keep)):
        here = at_lane(side * half, half)
        put(out, 0, 4, 0, dot_left(a1[:, here], d_gated[...]))
        put(out, 0, 4, half * width // 512, dot_left(a2[:, here], shifted[...]))
    sums = low_columns_sum(d_gated[...])
    fixed[8:9] = sums[:, 0:width]
    fixed[9:10] = sums[:, width:]
    d_a2[...] = dot_right(d_gated[...], gated_w[...])
    for row in spans(SEQ, STEP):
        normed, rstd = normalize(x_ref[row].astype(F32))
        grad = d_a2[row]
        fixed[0:1] += columns_sum(grad * normed)
        fixed[1:2] += columns_sum(grad)
        input_grad[row] += normalize_back(grad, normed, rstd, vec[0:1])
    pack_small(info, wide_sums, fixed, send, keep, rows_ref)


def pack_small(info, wide, fixed, send, keep, rows_ref):
    if rows_ref is None:
        return
    pieces = lax.axis_size("mp")
    local = wide.shape[1] // pieces
    parts = local // 256
    rows_ref[...] = jnp.zeros_like(rows_ref)
    for piece in range(pieces):
        owner = jnp.bitwise_xor(info[1] // local, piece)
        for part in range(parts):
            spot = pl.multiple_of((owner * parts + part) * 16, 16)
            at = piece * local + part * 256
            rows_ref[pl.ds(spot, 16)] = wide[:, at : at + 256]
    base = wide.shape[1] // 16
    for part in range(fixed.shape[1] // 256):
        rows_ref[base + part * 16 : base + (part + 1) * 16] = fixed[:, part * 256 : (part + 1) * 256]
    count = rows_ref.shape[0] // 2
    offset = send.shape[1] - count // 4
    for side, out in ((1 - info[0], send), (info[0], keep)):
        put(out, 0, 4, offset, rows_ref[pl.ds(pl.multiple_of(side * count, 16), count)])


def own_place(count):
    core = lax.axis_index("dp") % 2
    if count == 2:
        return core
    y = lax.axis_index("dp") // 2 % 2
    near = lax.axis_index("dp") // 4 % 2
    return 2 * core + (1 - core) * y + core * near


def cut(weights, vectors, per, link):
    shapes = [(item.shape[0] // per, item.shape[1]) for item in weights]
    total = sum(rows * columns // 256 for rows, columns in shapes)
    local = weights[0].shape[1]
    small = local // 16 if vectors else 0
    chained = [] if link is None else [link]

    def kernel(*refs):
        refs = list(refs)
        sources = [refs.pop(0) for _ in weights]
        small_in = [refs.pop(0) for _ in vectors]
        for _ in chained:
            refs.pop(0)
        packed = refs.pop(0)
        own = refs.pop(0) if vectors else None
        blocks = [refs.pop(0) for _ in weights]
        sems = refs.pop(0)
        held = refs.pop(0)
        held[...] = jnp.zeros_like(held)
        place = own_place(per)
        copies = []
        for at, (source, block) in enumerate(zip(sources, blocks)):
            rows = block.shape[0]
            here = pl.ds(pl.multiple_of(place * rows, 16), rows)
            copies.append(pltpu.make_async_copy(source.at[here], block, sems.at[at]))
        for copy in copies:
            copy.start()
        if vectors:
            for part in range(local // 256):
                lanes = slice(part * 256, (part + 1) * 256)
                row = 0
                for item in small_in:
                    count = item.shape[0] if len(item.shape) == 2 else 1
                    held[row : row + count] = item[..., lanes].astype(F32).reshape(count, 256)
                    row += count
                chunk = as_low(held[...])
                own[part * 16 : (part + 1) * 16] = chunk
                packed[total + part * 16 : total + (part + 1) * 16] = chunk
        for copy in copies:
            copy.wait()
        offset = 0
        for block in blocks:
            rows, columns = block.shape
            for part in range(columns // 256):
                packed[offset : offset + rows] = block[:, part * 256 : (part + 1) * 256]
                offset += rows

    outs = [shaped((total + small, 256), LOW)]
    if vectors:
        outs.append(shaped((small, 256), LOW))
    return pl.pallas_call(
        kernel,
        out_shape=outs,
        in_specs=[pl.BlockSpec(memory_space=pl.ANY) for _ in weights]
        + [pl.BlockSpec(memory_space=pltpu.VMEM) for _ in vectors]
        + [pl.BlockSpec(memory_space=pl.ANY) for _ in chained],
        out_specs=[pl.BlockSpec(memory_space=pltpu.VMEM) for _ in outs],
        scratch_shapes=[pltpu.VMEM(shape, LOW) for shape in shapes]
        + [pltpu.SemaphoreType.DMA((len(weights),)), pltpu.VMEM((16, 256), F32)],
    )(*weights, *vectors, *chained)


def flat_swap(values, partner):
    count = lax.axis_size("dp") * lax.axis_size("mp")
    return lax.ppermute(values, ("dp", "mp"), [(at, partner(at)) for at in range(count)])


PARTNERS = {
    "core": lambda at: at ^ 2,
    "first": lambda at: at ^ (4 if at & 2 else 1),
    "second": lambda at: at ^ (1 if at & 2 else 4),
    "x": lambda at: at ^ 1,
    "y": lambda at: at ^ 4,
    "near": lambda at: at ^ 8,
    "far": lambda at: at ^ 16,
    "hop": lambda at: at ^ (8 if at & 2 else 4),
}
INNER_STEPS = [
    ("quarter", "first"),
    ("half_mix", "second"),
    ("half_near", "near"),
    ("sum", "far"),
    ("sum", "near"),
    ("join_near", "y"),
    ("join_y", "core"),
    ("final", None),
]
SHARED_STEPS = [
    ("quarter", "first"),
    ("half_mix", "second"),
    ("half_near", "near"),
    ("sum", "far"),
    ("sum", "near"),
    ("join_near", "second"),
    ("join_mix", "first"),
    ("spread", "core"),
    ("final", None),
]


PLAN = (
    "p",
    "a",
    "d",
    "p",
    "a",
    "d",
    "p",
    "c",
    "d",
    "p",
    "a",
    "c",
    "d",
    "a",
    "c",
    "d",
    "p",
    "c",
    "d",
    "p",
    "d",
    "c",
    "p",
    "a",
    "d",
    "c",
    "!d",
    "p",
    "!a",
    "!p",
    "c",
    "!c",
)


class Stream:
    def __init__(self, inner, mine, other, parts):
        self.inner = inner
        self.mine = mine
        self.flight = flat_swap(other, PARTNERS["core"])
        self.steps = list(INNER_STEPS if inner else SHARED_STEPS)
        self.parts = parts


def advance_kernel(jobs, refs):
    info, refs = refs[0], refs[1:]
    core, y, near = info[0], info[4], info[5]
    ins, outs = list(refs[: 2 * len(jobs)]), list(refs[2 * len(jobs) :])
    for inner, step, parts in jobs:
        mine, flight = ins.pop(0), ins.pop(0)
        x = 0 if inner else info[3]
        mix = core * x + (1 - core) * y

        def added(spot):
            return as_low(mine[spot].astype(F32) + flight[spot].astype(F32))

        if step == "quarter":
            keep, send = outs.pop(0), outs.pop(0)
            for at in range(2):
                send[at] = added(core * (2 * at + 1 - y) + (1 - core) * (2 * (1 - x) + at))
                keep[at] = added(core * (2 * at + y) + (1 - core) * (2 * x + at))
        elif step == "half_mix":
            keep, send = outs.pop(0), outs.pop(0)
            send[0] = added(1 - mix)
            keep[0] = added(mix)
        elif step == "half_near":
            keep, send = outs.pop(0), outs.pop(0)
            rows = keep.shape[1]
            for out, side in ((send, 1 - near), (keep, near)):
                here = pl.ds(pl.multiple_of(side * rows, 16), rows)
                out[0] = as_low(mine[0, here].astype(F32) + flight[0, here].astype(F32))
        elif step == "sum":
            outs.pop(0)[0] = added(0)
        elif step == "join_near":
            out = outs.pop(0)
            rows = mine.shape[1]
            out[0, pl.ds(pl.multiple_of(near * rows, 16), rows)] = mine[0]
            out[0, pl.ds(pl.multiple_of((1 - near) * rows, 16), rows)] = flight[0]
        elif step in ("join_y", "join_mix"):
            out = outs.pop(0)
            side = y if step == "join_y" else mix
            out[side] = mine[0]
            out[1 - side] = flight[0]
        elif step == "spread":
            out = outs.pop(0)
            for at in range(2):
                out[core * (2 * at + y) + (1 - core) * (2 * x + at)] = mine[at]
                out[core * (2 * at + 1 - y) + (1 - core) * (2 * (1 - x) + at)] = flight[at]


def finish_kernel(parts, small, refs):
    info, mine, flight, refs = refs[0], refs[1], refs[2], list(refs[3:])
    core = info[0]
    outs = [refs.pop(0) for _ in parts]
    smalls = [refs.pop(0) for _ in range(11)] if small else []
    link = refs.pop(0)
    link[...] = jnp.zeros_like(link)
    held = [refs.pop(0) for _ in parts]
    sems = refs.pop(0)
    copies = []
    for at, (offset, rows, shape) in enumerate(parts):
        target = held[at]
        for source, side in ((mine, core), (flight, 1 - core)):
            for quarter in range(mine.shape[0]):
                spot = (side * mine.shape[0] + quarter) * rows
                here = pl.ds(pl.multiple_of(spot, 16), rows)
                for part in range(shape[-1] // 256 * (shape[0] if len(shape) == 3 else 1)):
                    row = offset + part * rows
                    block = source[quarter, row : row + rows].astype(F32)
                    if len(shape) == 3:
                        target[part, here] = block
                    else:
                        target[here, part * 256 : (part + 1) * 256] = block
        copies.append(pltpu.make_async_copy(target, outs[at], sems.at[at]))
        copies[-1].start()
    if small:
        total = refs.pop(0)
        offset, rows = small
        for source, side in ((mine, core), (flight, 1 - core)):
            for quarter in range(mine.shape[0]):
                spot = (side * mine.shape[0] + quarter) * rows
                total[pl.ds(pl.multiple_of(spot, 16), rows)] = source[
                    quarter, offset : offset + rows
                ].astype(F32)
        norm, gated, left, conv, inner, depth, point, project, output, expand, shrink = smalls
        local, width = left.shape[-1], output.shape[-1]
        for part in range(local // 256):
            lanes = slice(part * 256, (part + 1) * 256)
            spot = (info[1] // local * (local // 256) + part) * 16
            block = total[pl.ds(pl.multiple_of(spot, 16), 16)]
            left[:, lanes] = block[0:1]
            expand[:, lanes] = block[1:2]
            inner[:, lanes] = block[2:4]
            depth[:, lanes] = block[4:13]
        for part in range(width // 256):
            lanes = slice(part * 256, (part + 1) * 256)
            base = local * 2 // 16 + part * 16
            block = total[base : base + 16]
            for at in range(4):
                norm[at, :, lanes] = block[2 * at : 2 * at + 2]
            gated[:, lanes] = block[8:9]
            gated[:, width + part * 256 : width + (part + 1) * 256] = block[9:10]
            project[:, lanes] = block[10:12]
            output[:, lanes] = block[12:13]
            shrink[:, lanes] = block[13:14]
            (conv if part == 0 else point)[...] = block[14:15]
    for copy in copies:
        copy.wait()


def finish(chain, info, stream, small):
    parts = stream.parts
    shapes = [shaped(shape, F32) for _, _, shape in parts]
    scratch = [pltpu.VMEM(shape, F32) for _, _, shape in parts]
    scratch.append(pltpu.SemaphoreType.DMA((len(parts),)))
    names = []
    if small:
        scratch.append(pltpu.VMEM((256, 256), F32))
        names = [shaped(shape, F32) for shape in small[1]]
    stream.mine = chain.run(
        lambda *refs: finish_kernel(parts, small[0] if small else None, refs),
        shapes + names + [shaped((8, 128), F32)],
        [info, stream.mine, stream.flight],
        scratch,
        ADV,
        len(parts),
    )


def advance(chain, info, streams):
    jobs, ins, outs = [], [info], []
    for stream in streams:
        step = stream.steps[0][0]
        jobs.append((stream.inner, step, stream.parts))
        ins += [stream.mine, stream.flight]
        lead, rows, columns = stream.mine.shape
        if step in ("quarter", "half_mix"):
            outs += [shaped((lead // 2, rows, columns), LOW)] * 2
        elif step == "half_near":
            outs += [shaped((lead, rows // 2, columns), LOW)] * 2
        elif step == "sum":
            outs.append(shaped((lead, rows, columns), LOW))
        elif step == "join_near":
            outs.append(shaped((lead, rows * 2, columns), LOW))
        else:
            outs.append(shaped((lead * 2, rows, columns), LOW))
    results = list(chain.run(lambda *refs: advance_kernel(jobs, refs), outs, ins, [], ADV))
    for stream in streams:
        step, partner = stream.steps.pop(0)
        stream.mine = results.pop(0)
        if step in ("quarter", "half_mix", "half_near"):
            stream.flight = flat_swap(results.pop(0), PARTNERS[partner])
        else:
            stream.flight = flat_swap(stream.mine, PARTNERS[partner])


def opened(packed, first, count, offset, rows, columns):
    parts = [
        packed[first : first + count, offset + at * rows : offset + (at + 1) * rows]
        for at in range(columns // 256)
    ]
    return jnp.concatenate(parts, 2).reshape(count * rows, columns)


class Weights:
    def __init__(self, packed, per):
        pieces = [packed]
        for bit in bits_of("mp"):
            pieces = pieces + [swap(item, "mp", bit) for item in pieces]
        self.blocks = [[item] for item in pieces[1:]]
        self.per = per

    def hop(self, after):
        if self.per == 4:
            for blocks in self.blocks:
                blocks[0], _ = lax.optimization_barrier((blocks[0], after))
                blocks.append(flat_swap(blocks[0], PARTNERS["hop"]))

    def share(self, after):
        found = []
        for blocks in self.blocks:
            held = [lax.optimization_barrier((item, after))[0] for item in blocks]
            found += held + [swap(item, "dp", 1) for item in held]
        return found


def finish_shared(mine, other, order):
    own = bit_of("dp", 1)
    values = add_low(mine, swap(other, "dp", 1))
    held = [("dp", 1, own)]
    for axis, bit in order[:-1]:
        own = bit_of(axis, bit)
        mine, other = split(values, own)
        values = add_low(mine, swap(other, axis, bit))
        held.append((axis, bit, own))
    axis, bit = order[-1]
    values = add_low(values, swap(values, axis, bit))
    for axis, bit, own in reversed(held):
        values = join(values, swap(values, axis, bit), own)
    return values.astype(F32)


def finish_inner(mine, other, order):
    values = add_low(mine, swap(other, "dp", 1))
    pieces = [values[at] for at in range(values.shape[0])]
    held = [("dp", 1, bit_of("dp", 1))]
    for axis, bit in order[:-1]:
        if axis == "mp":
            keep_count = len(pieces) // 2
            moved = [swap(item, axis, bit) for item in pieces[keep_count:]]
            pieces = [add_low(one, two) for one, two in zip(pieces[:keep_count], moved)]
            continue
        own = bit_of(axis, bit)
        parts = [split(item, own) for item in pieces]
        pieces = [add_low(mine, swap(other, axis, bit)) for mine, other in parts]
        held.append((axis, bit, own))
    axis, bit = order[-1]
    values = add_low(pieces[0], swap(pieces[0], axis, bit))
    for axis, bit, own in reversed(held):
        values = join(values, swap(values, axis, bit), own)
    return values.astype(F32)


def body(
    cell_input,
    lengths,
    out_grad,
    norm_params,
    gated_weight,
    gated_bias,
    left_weight,
    left_bias,
    conv_weight,
    conv_bias,
    inner_norm,
    depth_weight,
    point_weight,
    point_bias,
    project_weight,
    project_bias,
    output_weight,
    output_bias,
    expand_weight,
    expand_bias,
    shrink_weight,
    shrink_bias,
):
    width = cell_input.shape[1]
    channels = conv_weight.shape[2]
    local = left_weight.shape[1]
    pieces = lax.axis_size("mp")
    inner = local * pieces
    tokens = cell_input.shape[0]
    assert tokens == SEQ
    tuned = lax.axis_size("dp") == 16 and pieces == 2
    mp_bits = bits_of("mp")[::-1]
    dp_bits = bits_of("dp")[1:]
    mp_first = [("mp", bit) for bit in mp_bits] + [("dp", bit) for bit in dp_bits]
    core = bit_of("dp", 1)
    info = jnp.stack(
        [
            core,
            lax.axis_index("mp") * local,
            lengths[0],
            lax.axis_index("mp") % 2,
            bit_of("dp", 2),
            bit_of("dp", 4),
        ]
    ).astype(jnp.int32)
    chain = Chain()

    def inner_rows(size):
        return (2 * pieces, size // 1024, 256)


    per = 4 if tuned else 2
    vectors = [left_bias, expand_bias, inner_norm, depth_weight]
    packed, own = cut([left_weight, point_weight], vectors, per, None)
    early = Weights(packed, per)
    (packed,) = cut([expand_weight, shrink_weight], [], per, own)
    late = Weights(packed, per)
    chain.link = packed
    a1, values, gates, x1, a2, right_pre, vec, right = chain.run(
        pre_kernel,
        [
            shaped((tokens, width), LOW),
            shaped((tokens, width), F32),
            shaped((tokens, width), F32),
            shaped((tokens, width), F32),
            shaped((tokens, width), LOW),
            shaped((tokens, channels), F32),
            shaped((16, width), F32),
            shaped((tokens, channels), LOW),
        ],
        [
            info,
            cell_input,
            gated_weight,
            conv_weight,
            norm_params,
            gated_bias,
            conv_bias,
            point_bias,
            project_bias,
            output_bias,
            shrink_bias,
        ],
        [],
        int(2.2e9 * EARLY),
    )
    early.hop(right)
    early_blocks = early.share(right)
    normed, slope, depth, rstd, left_rest = chain.run(
        lambda *refs: inner_forward_kernel(pieces, per, refs),
        [
            shaped((tokens, inner), LOW),
            shaped((tokens, inner), LOW),
            shaped((tokens, inner), LOW),
            shaped((tokens, 128), F32),
            shaped((pieces - 1, width, local), LOW),
        ],
        [info, a2, right, left_weight, own] + early_blocks,
        [
            pltpu.VMEM((tokens, inner), F32),
            pltpu.VMEM((tokens, 128), F32),
            pltpu.VMEM((tokens, 128), F32),
            pltpu.VMEM((tokens, 128), F32),
            pltpu.VMEM((tokens + 16, 128), F32),
            pltpu.VMEM((tokens + 16, 128), F32),
        ],
        int(6.5e9 * EARLY),
    )
    late.hop(rstd)
    x2, a4, qkv, lse, attended, x3, a5, point_rest = chain.run(
        lambda *refs: attention_forward_kernel(pieces, per, refs),
        [
            shaped((tokens, width), F32),
            shaped((tokens, width), LOW),
            shaped((tokens, 3 * width), LOW),
            shaped((tokens, 128), F32),
            shaped((tokens, width), LOW),
            shaped((tokens, width), F32),
            shaped((tokens, width), LOW),
            shaped((pieces - 1, local, channels), LOW),
        ],
        [info, x1, depth, point_weight, vec, project_weight, output_weight]
        + early_blocks,
        [],
        int(4.4e9 * EARLY),
    )
    late_blocks = late.share(a5)
    cell_output, feed_keep, feed_send, dx3, fixed, expand_sum = chain.run(
        lambda *refs: feed_kernel(pieces, per, refs),
        [
            shaped((tokens, width), LOW),
            shaped(inner_rows(2 * local * width), LOW),
            shaped(inner_rows(2 * local * width), LOW),
            shaped((tokens, width), F32),
            shaped((16, width), F32),
            shaped((8, inner), F32),
        ],
        [info, a5, x3, out_grad, vec, expand_weight, shrink_weight, own]
        + early_blocks
        + late_blocks,
        [
            pltpu.VMEM((tokens, inner), LOW),
            pltpu.VMEM((tokens, inner), F32),
            pltpu.VMEM((tokens, inner), LOW),
            pltpu.VMEM((tokens, width), F32),
            pltpu.VMEM((tokens, width), F32),
            pltpu.VMEM((pieces - 1, width, local), LOW),
            pltpu.VMEM((pieces - 1, local, width), LOW),
        ],
        int(8e9 * SCALE),
    )
    if tuned:
        fee = Stream(
            True,
            feed_keep,
            feed_send,
            [
                (0, local // 4, (local, width)),
                (width * local // 1024, width // 4, (width, local)),
            ],
        )
    proj_send, proj_keep, dx2, d_sep, fixed = chain.run(
        attention_backward_kernel,
        [
            shaped((4, width * width // 512, 256), LOW),
            shaped((4, width * width // 512, 256), LOW),
            shaped((tokens, width), F32),
            shaped((tokens, channels), LOW),
            shaped((16, width), F32),
        ],
        [info, dx3, attended, output_weight, qkv, lse, a4, project_weight, x2, vec, fixed],
        [
            pltpu.VMEM((tokens, width), LOW),
            pltpu.VMEM((tokens, width), LOW),
            pltpu.VMEM((tokens, 3 * width), LOW),
        ],
        int(6.7e9 * SCALE),
    )
    if tuned:
        pro = Stream(
            False,
            proj_keep,
            proj_send,
            [
                (0, width // 8, (width, 3 * width)),
                (3 * width * width // 2048, width // 8, (width, width)),
            ],
        )
        advance(chain, info, [fee])
    left_keep, left_send, d_a2, d_right, wide_sums = chain.run(
        lambda *refs: inner_backward_kernel(pieces, per, refs),
        [
            shaped(inner_rows(local * (width + channels)), LOW),
            shaped(inner_rows(local * (width + channels)), LOW),
            shaped((tokens, width), F32),
            shaped((tokens, channels), F32),
            shaped((16, inner), F32),
        ],
        [
            info,
            d_sep,
            depth,
            normed,
            slope,
            rstd,
            a2,
            expand_sum,
            point_weight,
            point_rest,
            left_weight,
            left_rest,
            own,
        ]
        + early_blocks,
        [
            pltpu.VMEM((inner // 128, tokens + 16, 128), F32),
            pltpu.VMEM((tokens + 16, 128), F32),
            pltpu.VMEM((tokens + 16, 128), F32),
            pltpu.VMEM((tokens, inner), LOW),
            pltpu.VMEM((tokens, 128), F32),
            pltpu.VMEM((tokens, 128), F32),
        ],
        int(11.5e9 * SCALE),
    )
    if tuned:
        lef = Stream(
            True,
            left_keep,
            left_send,
            [
                (0, width // 4, (width, local)),
                (width * local // 1024, local // 4, (local, channels)),
            ],
        )
        advance(chain, info, [fee])
    small = 32 if tuned else 0
    last_rows = width * (2 * width + 3 * channels) // 2048 + small
    last_send, last_keep, input_grad, fixed = chain.run(
        last_kernel if tuned else lambda *refs: last_kernel(*refs, None),
        [
            shaped((4, last_rows, 256), LOW),
            shaped((4, last_rows, 256), LOW),
            shaped((tokens, width), F32),
            shaped((16, width), F32),
        ],
        [
            info,
            d_a2,
            d_right,
            right_pre,
            conv_weight,
            a2,
            x1,
            dx2,
            values,
            gates,
            a1,
            gated_weight,
            cell_input,
            vec,
            fixed,
            wide_sums,
        ],
        [
            pltpu.VMEM((tokens, 3 * channels), LOW),
            pltpu.VMEM((tokens, width), F32),
            pltpu.VMEM((tokens, 2 * width), LOW),
        ]
        + ([pltpu.VMEM((8 * small, 256), F32)] if tuned else []),
        int(4.0e9 * SCALE),
    )
    if tuned:
        lat = Stream(
            False,
            last_keep,
            last_send,
            [
                (0, width // 8, (width, 2 * width)),
                (width * width // 1024, width // 8, (3, width, channels)),
            ],
        )
        groups = {"a": [fee], "p": [pro], "c": [lef], "d": [lat]}
        small_shapes = [
            (4, 2, width),
            (1, 2 * width),
            (1, local),
            (1, channels),
            (2, local),
            (9, local),
            (1, channels),
            (2, width),
            (1, width),
            (1, local),
            (1, width),
        ]
        small_part = ((last_rows - small, small), small_shapes)
        for names in PLAN:
            if names[0] == "!":
                stream = groups[names[1]][0]
                finish(chain, info, stream, small_part if names == "!d" else None)
            else:
                advance(chain, info, [groups[name][0] for name in names])
        (grad_shrink, grad_expand, _), (grad_left, grad_point, _) = fee.mine, lef.mine
        (grad_proj, grad_out, _), (grad_gated, grad_conv) = pro.mine, lat.mine[:2]
        smalls = [
            item.reshape(-1) if item.shape[0] == 1 else item for item in lat.mine[2:-1]
        ]
    else:

        def whole(keep, send, offset, rows, columns):
            both = [
                jnp.stack([opened(item, 2 * at, 2, offset, rows, columns) for at in range(pieces)])
                for item in (keep, send)
            ]
            return finish_inner(both[0], both[1], mp_first)

        def shared(keep, send, offset, rows, columns):
            both = [opened(item, 0, 4, offset, rows, columns) for item in (keep, send)]
            return finish_shared(both[0], both[1], mp_first)

        eighth = width // 8
        grad_shrink = whole(feed_keep, feed_send, 0, local // 4, width)
        grad_expand = whole(
            feed_keep, feed_send, width * local // 1024, width // 4, local
        )
        grad_left = whole(left_keep, left_send, 0, width // 4, local)
        grad_point = whole(left_keep, left_send, width * local // 1024, local // 4, channels)
        grad_proj = shared(proj_keep, proj_send, 0, eighth, 3 * width)
        grad_out = shared(proj_keep, proj_send, 6 * eighth, eighth, width)
        grad_gated = shared(last_keep, last_send, 0, eighth, 2 * width)
        grad_conv = jnp.stack(
            [shared(last_keep, last_send, (4 + at) * eighth, eighth, channels) for at in range(3)]
        )
        chunks = [wide_sums[:, at : at + local] for at in range(0, inner, local)]
        for bit in mp_bits:
            count = len(chunks) // 2
            moved = [swap(item, "mp", bit) for item in chunks[count:]]
            chunks = [one + two for one, two in zip(chunks[:count], moved)]
            fixed = fixed + swap(fixed, "mp", bit)
        wide_total = chunks[0]
        for bit in bits_of("dp"):
            fixed = fixed + swap(fixed, "dp", bit)
            wide_total = wide_total + swap(wide_total, "dp", bit)
        smalls = [
            fixed[0:8].reshape(4, 2, width),
            fixed[8:10].reshape(2 * width),
            wide_total[0],
            fixed[14, :channels],
            wide_total[2:4],
            wide_total[4:13],
            fixed[14, channels:],
            fixed[10:12],
            fixed[12],
            wide_total[1],
            fixed[13],
        ]
    return (
        cell_output,
        input_grad,
        smalls[0],
        grad_gated,
        smalls[1],
        grad_left,
        smalls[2],
        grad_conv,
        smalls[3],
        smalls[4],
        smalls[5],
        grad_point,
        smalls[6],
        grad_proj,
        smalls[7],
        grad_out,
        smalls[8],
        grad_expand,
        smalls[9],
        grad_shrink,
        smalls[10],
    )


def solution(mesh):
    return jax.shard_map(
        body,
        mesh=mesh,
        in_specs=(
            P(("dp", "mp"), None),
            P(("dp", "mp")),
            P(("dp", "mp"), None),
            P(),
            P(),
            P(),
            P(None, "mp"),
            P("mp"),
            P(),
            P(),
            P(None, "mp"),
            P(None, "mp"),
            P("mp", None),
            P(),
            P(),
            P(),
            P(),
            P(),
            P(None, "mp"),
            P("mp"),
            P("mp", None),
            P(),
        ),
        out_specs=(
            P(("dp", "mp"), None),
            P(("dp", "mp"), None),
            P(),
            P(),
            P(),
            P(None, "mp"),
            P("mp"),
            P(),
            P(),
            P(None, "mp"),
            P(None, "mp"),
            P("mp", None),
            P(),
            P(),
            P(),
            P(),
            P(),
            P(None, "mp"),
            P("mp"),
            P("mp", None),
            P(),
        ),
        check_vma=False,
    )
```

```python
import jax
import jax.numpy as jnp
from jax import lax
from jax.experimental import pallas as pl
from jax.experimental.pallas import tpu as pltpu
from jax.sharding import PartitionSpec as P

HEADS = 8
SEQ = 256
EPS = 1e-06
NEGATIVE = -1000000000.0
LOW = jnp.bfloat16
F32 = jnp.float32
STEP = 64
LIMIT = 24 * 2**20
SCALE = 4
EARLY = 0.001
ADV = 20 * 10**9


def as_low(values):
    return values.astype(LOW)


def dot(left, right):
    return jnp.dot(left, right, preferred_element_type=F32)


def dot_left(left, right):
    return lax.dot_general(left, right, (((0,), (0,)), ((), ())), preferred_element_type=F32)


def dot_right(left, right):
    return lax.dot_general(left, right, (((1,), (1,)), ((), ())), preferred_element_type=F32)


def swap(values, axis, bit):
    count = lax.axis_size(axis)
    return lax.ppermute(values, axis, [(at, at ^ bit) for at in range(count)])


def bit_of(axis, bit):
    return (lax.axis_index(axis) // bit) % 2


def bits_of(axis):
    bits, bit = [], 1
    while bit < lax.axis_size(axis):
        bits.append(bit)
        bit *= 2
    return bits


def add_low(first, second):
    return as_low(first.astype(F32) + second.astype(F32))


def split(values, own):
    half = values.shape[0] // 2
    mine = lax.dynamic_slice_in_dim(values, own * half, half, 0)
    other = lax.dynamic_slice_in_dim(values, (1 - own) * half, half, 0)
    return mine, other


def join(mine, other, own):
    swapped = own == 1
    return jnp.concatenate(
        [jnp.where(swapped, other, mine), jnp.where(swapped, mine, other)], 0
    )


def sum_shared(values, order):
    held = []
    steps = [("dp", 1)] + order
    for axis, bit in steps[:-1]:
        own = bit_of(axis, bit)
        mine, other = split(values, own)
        values = add_low(mine, swap(other, axis, bit))
        held.append((axis, bit, own))
    axis, bit = steps[-1]
    values = add_low(values, swap(values, axis, bit))
    for axis, bit, own in reversed(held):
        values = join(values, swap(values, axis, bit), own)
    return values.astype(F32)


def sum_inner(pieces, order):
    held = []
    steps = [("dp", 1)] + order
    for axis, bit in steps[:-1]:
        if axis == "mp":
            keep_count = len(pieces) // 2
            moved = [swap(item, axis, bit) for item in pieces[keep_count:]]
            pieces = [add_low(one, two) for one, two in zip(pieces[:keep_count], moved)]
            continue
        own = bit_of(axis, bit)
        parts = [split(item, own) for item in pieces]
        pieces = [add_low(mine, swap(other, axis, bit)) for mine, other in parts]
        held.append((axis, bit, own))
    axis, bit = steps[-1]
    values = add_low(pieces[0], swap(pieces[0], axis, bit))
    for axis, bit, own in reversed(held):
        values = join(values, swap(values, axis, bit), own)
    return values.astype(F32)


def sigmoid(values):
    return 0.5 * jnp.tanh(0.5 * values) + 0.5


def spans(total, step):
    return [slice(at, at + step) for at in range(0, total, step)]


def at_lane(start, size):
    return pl.ds(pl.multiple_of(start, 128), size)


def normalize(values):
    width = values.shape[1]
    centre = jnp.sum(values, -1, keepdims=True) * (1.0 / width)
    centered = values - centre
    variance = jnp.sum(centered * centered, -1, keepdims=True) * (1.0 / width)
    rstd = lax.rsqrt(variance + EPS)
    return centered * rstd, rstd


def normalize_back(grad, normed, rstd, gain):
    width = grad.shape[1]
    scaled = grad * gain
    first = jnp.sum(scaled, -1, keepdims=True) * (1.0 / width)
    second = jnp.sum(scaled * normed, -1, keepdims=True) * (1.0 / width)
    return rstd * (scaled - first - normed * second)


def columns_sum(values):
    return jnp.sum(values, 0, keepdims=True)


def eighths_sum(values):
    return jnp.sum(values.reshape(-1, 8, values.shape[1]), 0)


def low_columns_sum(values):
    ones = jnp.ones((16, values.shape[0]), LOW)
    return dot(ones, values)[0:1]


def place(local):
    dp, mp = lax.axis_index("dp"), lax.axis_index("mp")
    return dp % 2, mp * local, None, mp % 2, dp // 2 % 2, dp // 4 % 2


class Chain:
    def __init__(self, local):
        self.link = None
        self.local = local

    def run(self, kernel, outs, ins, scratch, flops, placed=0):
        ins = list(ins)
        specs = [
            pl.BlockSpec(memory_space=pltpu.SMEM if item.dtype == jnp.int32 else pltpu.VMEM)
            for item in ins
        ]
        count = len(ins)
        moved = sum(item.size * item.dtype.itemsize for item in ins + list(outs))
        linked = self.link is not None
        if linked:
            ins.append(self.link)
            specs.append(pl.BlockSpec(memory_space=pl.ANY))

        def call(*refs):
            kernel(place(self.local), *(refs[:count] + refs[count + 1 :] if linked else refs))

        results = pl.pallas_call(
            call,
            out_shape=outs,
            in_specs=specs,
            out_specs=[
                pl.BlockSpec(memory_space=pltpu.HBM if at < placed else pltpu.VMEM)
                for at in range(len(outs))
            ],
            scratch_shapes=scratch,
            compiler_params=pltpu.CompilerParams(vmem_limit_bytes=LIMIT),
            cost_estimate=pl.CostEstimate(
                flops=flops, bytes_accessed=moved + flops // 50, transcendentals=0
            ),
        )(*ins)
        self.link = min(results, key=lambda item: item.size)
        return results


def put(out, first, count, offset, values):
    rows = values.shape[0] // count
    low = as_low(values)
    for quarter in range(count):
        for part in range(values.shape[1] // 256):
            at = offset + part * rows
            out[first + quarter, at : at + rows] = low[
                quarter * rows : (quarter + 1) * rows, part * 256 : (part + 1) * 256
            ]


def shaped(shape, kind):
    return jax.ShapeDtypeStruct(shape, kind)


def pre_kernel(
    info, lengths, x_ref, gated_w, conv_w, norms, gated_b, conv_b, point_b, project_b, output_b, shrink_b,
    a1, values, gates, x1, a2, right_pre, vec, kept, valid, right
):
    width = x_ref.shape[1]
    channels = right.shape[1]
    length = lengths[0]
    for ref, axis in ((kept, 0), (valid, 1)):
        spots = lax.broadcasted_iota(jnp.int32, ref.shape, axis)
        ref[...] = jnp.where(spots < length, 1.0, 0.0).astype(F32)
    vec[...] = jnp.zeros_like(vec)
    for at in range(4):
        vec[2 * at : 2 * at + 2] = norms[at].astype(F32)
    for row, item in ((8, gated_b.at[0:width]), (9, gated_b.at[width:]), (13, output_b), (14, shrink_b)):
        vec[row : row + 1] = item[...].astype(F32).reshape(1, width)
    vec[10:11, 0:channels] = conv_b[...].astype(F32).reshape(1, channels)
    vec[10:11, channels:] = point_b[...].astype(F32).reshape(1, channels)
    vec[11:13] = project_b[...].astype(F32)
    for row in spans(SEQ, STEP):
        normed, _ = normalize(x_ref[row].astype(F32))
        a1[row] = as_low(normed * vec[0:1] + vec[1:2])
    for col in spans(width, 256):
        gate_col = slice(col.start + width, col.stop + width)
        value = dot(a1[...], gated_w[:, col]) + vec[8:9, col]
        gate = sigmoid(dot(a1[...], gated_w[:, gate_col]) + vec[9:10, col])
        values[:, col] = value
        gates[:, col] = gate
        x1[:, col] = x_ref[:, col].astype(F32) + value * gate
    for row in spans(SEQ, STEP):
        normed, _ = normalize(x1[row])
        a2[row] = as_low((normed * vec[2:3] + vec[3:4]) * kept[row, 0:1])
    rows = lax.broadcasted_iota(jnp.int32, right_pre.shape, 0)
    first = jnp.where(rows == 0, 0.0, pltpu.roll(dot(a2[...], conv_w[0]), 1, 0))
    last = jnp.where(rows == SEQ - 1, 0.0, pltpu.roll(dot(a2[...], conv_w[2]), SEQ - 1, 0))
    total = first + dot(a2[...], conv_w[1]) + last + vec[10:11, 0 : right_pre.shape[1]]
    right_pre[...] = total
    right[...] = as_low(total * sigmoid(total))


def unpack(refs, counts):
    groups, at = [], 0
    for count in counts:
        groups.append(refs[at : at + count])
        at += count
    return groups


def places(info, count):
    core, y, near = info[0], info[4], info[5]
    if count == 2:
        return [core, 1 - core]
    mine = (1 - core) * y + core * near
    theirs = (1 - core) * near + core * y
    return [2 * core + mine, 2 * core + 1 - mine, 2 - 2 * core + theirs, 3 - 2 * core - theirs]


def assemble(info, target, blocks, offset):
    rows = target.shape[0] // len(blocks)
    for spot, block in zip(places(info, len(blocks)), blocks):
        here = pl.ds(pl.multiple_of(spot * rows, 16), rows)
        for part in range(target.shape[1] // 256):
            at = offset + part * rows
            target[here, part * 256 : (part + 1) * 256] = block[at : at + rows]


def vectors_of(own, blocks, per_piece, offset):
    found = [(own, 0)]
    for at in range(0, len(blocks), per_piece):
        found.append((blocks[at], offset))
    return found


def rows_of(vectors, index, lanes):
    ref, offset = vectors
    return ref[pl.ds(pl.multiple_of(offset + index * 16, 16), 16), lanes].astype(F32)


def inner_forward_kernel(pieces, per, refs):
    info, refs = refs[0], refs[1:]
    (a2, right, left, own, keep), packed, outs, scratch = unpack(
        refs, [5, per * (pieces - 1), 5, 6]
    )
    normed_ref, slope_ref, depth, rstd_ref, left_rest = outs
    mixed, total, square, centre_ref, padded, padded_two = scratch
    local = left.shape[1]
    inner = local * pieces
    offset = info[1]
    skipped = a2.shape[1] * local // (256 * per) + local // per
    wide = vectors_of(own, packed, per, skipped)
    right_rows = right[...].astype(F32)
    total[...] = jnp.zeros_like(total)
    square[...] = jnp.zeros_like(square)
    for piece in range(pieces):
        if piece:
            assemble(info, left_rest.at[piece - 1], packed[(piece - 1) * per : piece * per], 0)
        for col in spans(local, 256):
            weights = left[:, col] if piece == 0 else left_rest[piece - 1, :, col]
            pre = dot(a2[...], weights)
            pre = pre + rows_of(wide[piece], col.start // 256, slice(0, 256))[0:1]
            sigma = sigmoid(pre)
            at = piece * local + col.start
            here = slice(at, at + 256)
            slope_ref[:, here] = as_low(sigma * (1.0 + pre * (1.0 - sigma)))
            value = pre * sigma + right_rows * jnp.where(offset == at, 1.0, 0.0)
            mixed[:, here] = value
            total[...] += value[:, 0:128] + value[:, 128:256]
            squared = value * value
            square[...] += squared[:, 0:128] + squared[:, 128:256]
    centre = jnp.sum(total[...], 1, keepdims=True) * (1.0 / inner)
    variance = jnp.sum(square[...], 1, keepdims=True) * (1.0 / inner) - centre * centre
    rstd = lax.rsqrt(variance + EPS)
    centre_ref[...] = jnp.broadcast_to(centre, centre_ref.shape)
    rstd_ref[...] = jnp.broadcast_to(rstd, rstd_ref.shape)
    for pad in (padded, padded_two):
        pad[0:8] = jnp.zeros((8, 128), F32)
        pad[SEQ + 8 : SEQ + 16] = jnp.zeros((8, 128), F32)
    kept = keep[:, 0:1]
    for piece in range(pieces):

        def one(index, part, pad):
            here = at_lane(piece * local + index * 256 + part, 128)
            vectors = rows_of(wide[piece], index, slice(part, part + 128))
            normed = (mixed[:, here] - centre_ref[...]) * rstd_ref[...]
            normed_ref[:, here] = as_low(normed)
            pad[8 : SEQ + 8] = (normed * vectors[2:3] + vectors[3:4]) * kept
            result = pad[4 : SEQ + 4] * vectors[4:5]
            for tap in range(1, 9):
                result = result + pad[4 + tap : SEQ + 4 + tap] * vectors[4 + tap : 5 + tap]
            depth[:, here] = as_low(result)

        def step(index, carry):
            one(index, 0, padded)
            one(index, 128, padded_two)
            return carry

        lax.fori_loop(0, local // 256, step, 0)


def masked_scores(queries, keys, valid, scale):
    return jnp.where(valid, dot_right(queries, keys) * scale, NEGATIVE)


def attention_forward_kernel(pieces, per, refs):
    (info, x1, depth, point, vec, project_w, output_w, mask), packed, outs = unpack(
        refs, [8, per * (pieces - 1), 8]
    )
    x2, a4, qkv, lse, attended, x3, a5, point_rest = outs
    width = x2.shape[1]
    local, channels = point.shape
    sep = dot(depth[:, 0:local], point[...])
    for piece in range(1, pieces):
        blocks = packed[(piece - 1) * per : piece * per]
        assemble(info, point_rest.at[piece - 1], blocks, width * local // (256 * per))
        sep = sep + dot(depth[:, piece * local : (piece + 1) * local], point_rest[piece - 1])
    x2[:, 0:channels] = x1[:, 0:channels] + sep + vec[10:11, channels : 2 * channels]
    x2[:, channels:width] = x1[:, channels:width]
    for row in spans(SEQ, STEP):
        normed, _ = normalize(x2[row])
        a4[row] = as_low(normed * vec[4:5] + vec[5:6])
    for col in spans(3 * width, 256):
        part = dot(a4[...], project_w[:, col])
        if col.start < width:
            part = part + vec[11:12, col]
        elif col.start >= 2 * width:
            part = part + vec[12:13, col.start - 2 * width : col.stop - 2 * width]
        qkv[:, col] = as_low(part)
    scale = (width // HEADS) ** (-0.5)
    lanes = lax.broadcasted_iota(jnp.int32, (SEQ, 128), 1)
    valid = jnp.broadcast_to(mask[0:1], (SEQ, SEQ)) > 0.5
    logs = jnp.zeros((SEQ, 128), F32)
    for pair in range(width // 128):
        at = pair * 128
        queries = qkv[:, at : at + 128]
        keys = qkv[:, width + at : width + at + 128]
        vals = qkv[:, 2 * width + at : 2 * width + at + 128]
        mixed = []
        for side in range(2):
            mine = (lanes < 64) if side == 0 else (lanes >= 64)
            scores = masked_scores(jnp.where(mine, queries, 0), keys, valid, scale)
            highest = jnp.max(scores, -1, keepdims=True)
            weights = jnp.exp(scores - highest)
            total = jnp.sum(weights, -1, keepdims=True)
            mixed.append(dot(as_low(weights * (1.0 / total)), vals))
            logs = jnp.where(lanes == 2 * pair + side, highest + jnp.log(total), logs)
        attended[:, at : at + 128] = as_low(jnp.where(lanes < 64, mixed[0], mixed[1]))
    lse[...] = logs
    x3[...] = x2[...] + dot(attended[...], output_w[...]) + vec[13:14]
    for row in spans(SEQ, STEP):
        normed, _ = normalize(x3[row])
        a5[row] = as_low(normed * vec[6:7] + vec[7:8])


def feed_piece(a5, top, expand, shrink, vectors, hidden, slope, d_expand):
    local = expand.shape[1]
    for col in spans(local, 256):
        pre = dot(a5[...], expand[:, col])
        pre = pre + rows_of(vectors, col.start // 256, slice(0, 256))[1:2]
        sigma = sigmoid(pre)
        hidden[:, col] = as_low(pre * sigma)
        slope[:, col] = sigma * (1.0 + pre * (1.0 - sigma))
    part = dot(hidden[...], shrink[...])
    for row in spans(local, 256):
        d_expand[:, row] = as_low(dot_right(top[...], shrink[row]) * slope[:, row])
    return part


def feed_grads(core, a5, top, hidden, d_expand, keep, send, first):
    local = hidden.shape[1]
    half, rows = a5.shape[1] // 2, local // 2
    for side, out in ((1 - core, send), (core, keep)):
        put(out, first, 2, 0, dot_left(hidden[:, at_lane(side * rows, rows)], top[...]))
        grad = dot_left(a5[:, at_lane(side * half, half)], d_expand[...])
        put(out, first, 2, a5.shape[1] * local // 1024, grad)


def feed_own_kernel(
    info, a5, top, expand, shrink, own, keep, send, shrunk, d_a5, grad_bias, hidden, slope, d_expand
):
    shrunk[...] = feed_piece(a5, top, expand, shrink, (own, 0), hidden, slope, d_expand)
    feed_grads(info[0], a5, top, hidden, d_expand, keep, send, 0)
    grad_bias[...] = jnp.broadcast_to(low_columns_sum(d_expand[...]), grad_bias.shape)
    d_a5[...] = dot_right(d_expand[...], expand[...])


def feed_kernel(pieces, per, refs):
    info, refs = refs[0], refs[1:]
    (a5, x3, top, vec, keep_own, send_own, shrunk_own, d_a5_own, bias_own), first, packed, outs, scratch = unpack(
        refs, [9, per * (pieces - 1), per * (pieces - 1), 6, 7]
    )
    output, keep, send, dx3, fixed, grad_bias = outs
    hidden, slope, d_expand, shrunk, d_a5, expand, shrink = scratch
    local, width = shrink.shape
    wide = vectors_of(None, first, per, width * local // (256 * per) + local // per)
    keep[0:2] = keep_own[...]
    send[0:2] = send_own[...]
    shrunk[...] = shrunk_own[...]
    d_a5[...] = d_a5_own[...]
    grad_bias[:, 0:local] = bias_own[...]
    for piece in range(1, pieces):
        blocks = packed[(piece - 1) * per : piece * per]
        assemble(info, expand, blocks, 0)
        assemble(info, shrink, blocks, width * local // (256 * per))
        shrunk[...] += feed_piece(
            a5, top, expand, shrink, wide[piece], hidden, slope, d_expand
        )
        feed_grads(info[0], a5, top, hidden, d_expand, keep, send, 2 * piece)
        cols = slice(piece * local, (piece + 1) * local)
        grad_bias[:, cols] = jnp.broadcast_to(low_columns_sum(d_expand[...]), (8, local))
        d_a5[...] += dot_right(d_expand[...], expand[...])
    for row in spans(SEQ, STEP):
        output[row] = as_low(x3[row] + shrunk[row] + vec[14:15])
    fixed[...] = jnp.zeros_like(fixed)
    for row in spans(SEQ, STEP):
        normed, rstd = normalize(x3[row])
        grad = d_a5[row]
        dx3[row] = top[row].astype(F32) + normalize_back(grad, normed, rstd, vec[6:7])
        fixed[6:7] += columns_sum(grad * normed)
        fixed[7:8] += columns_sum(grad)
    fixed[13:14] = low_columns_sum(top[...])


def attention_backward_kernel(
    info, dx3, attended, output_w, qkv, lse, a4, project_w, x2, vec, mask, before,
    send, keep, dx2, d_sep, fixed, d_out, d_att, d_proj
):
    width = x2.shape[1]
    half = width // 2
    core = info[0]
    fixed[...] = before[...]
    d_out[...] = as_low(dx3[...])
    d_att[...] = as_low(dot_right(d_out[...], output_w[...]))
    scale = (width // HEADS) ** (-0.5)
    lanes = lax.broadcasted_iota(jnp.int32, (SEQ, 128), 1)
    valid = jnp.broadcast_to(mask[0:1], (SEQ, SEQ)) > 0.5
    for pair in range(width // 128):
        at = pair * 128
        queries = qkv[:, at : at + 128]
        keys = qkv[:, width + at : width + at + 128]
        vals = qkv[:, 2 * width + at : 2 * width + at + 128]
        grads = d_att[:, at : at + 128]
        parts = []
        for side in range(2):
            head = 2 * pair + side
            mine = (lanes < 64) if side == 0 else (lanes >= 64)
            scores = masked_scores(jnp.where(mine, queries, 0), keys, valid, scale)
            probs = jnp.exp(scores - lse[:, head : head + 1])
            d_vals = dot_left(as_low(probs), grads)
            d_probs = dot_right(jnp.where(mine, grads, 0), vals)
            weighted = jnp.sum(d_probs * probs, -1, keepdims=True)
            d_scores = as_low(probs * (d_probs - weighted))
            parts.append((dot(d_scores, keys) * scale, dot_left(d_scores, queries) * scale, d_vals))
        for kind in range(3):
            here = slice(kind * width + at, kind * width + at + 128)
            d_proj[:, here] = as_low(jnp.where(lanes < 64, parts[0][kind], parts[1][kind]))
    for side, out in ((1 - core, send), (core, keep)):
        here = at_lane(side * half, half)
        put(out, 0, 4, 0, dot_left(a4[:, here], d_proj[...]))
        put(out, 0, 4, 3 * width * half // 1024, dot_left(attended[:, here], d_out[...]))
    fixed[12:13] = low_columns_sum(d_out[...])
    fixed[10:11] = low_columns_sum(d_proj[:, :width])
    fixed[11:12] = low_columns_sum(d_proj[:, 2 * width :])
    dx2[...] = dot_right(d_proj[...], project_w[...])
    for row in spans(SEQ, STEP):
        normed, rstd = normalize(x2[row])
        grad = dx2[row]
        dx2[row] = dx3[row] + normalize_back(grad, normed, rstd, vec[4:5])
        fixed[4:5] += columns_sum(grad * normed)
        fixed[5:6] += columns_sum(grad)
    channels = d_sep.shape[1]
    d_sep[...] = as_low(dx2[:, :channels])
    fixed[14:15, channels : 2 * channels] = low_columns_sum(d_sep[...])


def inner_backward_kernel(pieces, per, refs):
    info, refs = refs[0], refs[1:]
    (
        (d_sep, depth, normed_ref, slope_ref, rstd_ref, a2, bias_before, point, point_rest),
        (left, left_rest, own, keep_mask),
        packed,
        outs,
        scratch,
    ) = unpack(refs, [9, 4, per * (pieces - 1), 5, 7])
    keep, send, d_a2, d_right, grads = outs
    d_depth, padded, padded_two, d_left, first_ref, second_ref, sums = scratch
    local = left.shape[1]
    inner = local * pieces
    core, offset = info[0], info[1]
    rows = local // 2
    half = a2.shape[1] // 2
    wide = vectors_of(own, packed, per, a2.shape[1] * local // (256 * per) + local // per)
    for piece in range(pieces):
        weights = point if piece == 0 else point_rest.at[piece - 1]
        for row in spans(local, 256):
            back = dot_right(d_sep[...], weights[row])
            index = (piece * local + row.start) // 128
            d_depth[index] = back[:, 0:128]
            d_depth[index + 1] = back[:, 128:256]
    first_ref[...] = jnp.zeros_like(first_ref)
    second_ref[...] = jnp.zeros_like(second_ref)
    for pad in (padded, padded_two):
        pad[0:8] = jnp.zeros((8, 128), F32)
        pad[SEQ + 8 : SEQ + 16] = jnp.zeros((8, 128), F32)
    grads[...] = jnp.zeros_like(grads)
    grads[1:2] = bias_before[0:1]
    kept = keep_mask[:, 0:1]
    for piece in range(pieces):

        def one(pair, part, pad):
            here = at_lane(piece * local + pair * 256 + part, 128)
            index = piece * (local // 128) + 2 * pair + part // 128
            vectors = rows_of(wide[piece], pair, slice(part, part + 128))
            normed = normed_ref[:, here].astype(F32)
            normal = (normed * vectors[2:3] + vectors[3:4]) * kept
            pad[8 : SEQ + 8] = d_depth[index]
            result = pad[12 : SEQ + 12] * vectors[4:5]
            sums[2, :, here] = eighths_sum(normal * pad[12 : SEQ + 12])
            for tap in range(1, 9):
                shifted = pad[12 - tap : SEQ + 12 - tap]
                result = result + shifted * vectors[4 + tap : 5 + tap]
                sums[2 + tap, :, here] = eighths_sum(normal * shifted)
            result = result * kept
            sums[0, :, here] = eighths_sum(result * normed)
            sums[1, :, here] = eighths_sum(result)
            scaled = result * vectors[2:3]
            first_ref[...] += scaled
            second_ref[...] += scaled * normed
            d_depth[index] = scaled

        def step(index, carry):
            one(index, 0, padded)
            one(index, 128, padded_two)
            return carry

        lax.fori_loop(0, local // 256, step, 0)
    for col in spans(inner, 512):
        grads[2:13, col] = jnp.sum(sums[:, :, col], 1)
    first_ref[...] = jnp.broadcast_to(
        jnp.sum(first_ref[...], 1, keepdims=True) * (1.0 / inner), first_ref.shape
    )
    second_ref[...] = jnp.broadcast_to(
        jnp.sum(second_ref[...], 1, keepdims=True) * (1.0 / inner), second_ref.shape
    )

    def back(index, carry):
        here = at_lane(index * 128, 128)
        normed = normed_ref[:, here].astype(F32)
        d_mixed = rstd_ref[...] * (
            d_depth[index] - first_ref[...] - normed * second_ref[...]
        )
        d_depth[index] = d_mixed
        d_left[:, here] = as_low(d_mixed * slope_ref[:, here].astype(F32))
        return carry

    lax.fori_loop(0, inner // 128, back, 0)
    for part in range(d_right.shape[1] // 128):
        d_right[:, part * 128 : (part + 1) * 128] = d_depth[offset // 128 + part]
    for piece in range(pieces):
        base = piece * local
        cols = slice(base, base + local)
        for side, out in ((1 - core, send), (core, keep)):
            grad = dot_left(a2[:, at_lane(side * half, half)], d_left[:, cols])
            put(out, 2 * piece, 2, 0, grad)
            grad = dot_left(depth[:, at_lane(base + side * rows, rows)], d_sep[...])
            put(out, 2 * piece, 2, half * local // 512, grad)
        grads[0:1, cols] = low_columns_sum(d_left[:, cols])
        if piece == 0:
            d_a2[...] = dot_right(d_left[:, cols], left[...])
        else:
            d_a2[...] += dot_right(d_left[:, cols], left_rest[piece - 1])


def last_kernel(
    info, d_a2_left, d_right, right_pre, conv_w, a2, x1, dx2, values, gates, a1, gated_w, x_ref, vec, kept, before, wide_sums,
    send, keep, input_grad, fixed, shifted, d_a2, d_gated, rows_ref
):
    width = x1.shape[1]
    half = width // 2
    channels = right_pre.shape[1]
    core = info[0]
    fixed[...] = before[...]
    pre = right_pre[...]
    sigma = sigmoid(pre)
    low = as_low(d_right[...] * (sigma * (1.0 + pre * (1.0 - sigma))))
    fixed[14:15, 0:channels] = low_columns_sum(low)
    wide = low.astype(F32)
    rows = lax.broadcasted_iota(jnp.int32, wide.shape, 0)
    shifted[:, 0:channels] = as_low(
        jnp.where(rows == SEQ - 1, 0.0, pltpu.roll(wide, SEQ - 1, 0))
    )
    shifted[:, channels : 2 * channels] = low
    shifted[:, 2 * channels :] = as_low(jnp.where(rows == 0, 0.0, pltpu.roll(wide, 1, 0)))
    total = d_a2_left[...]
    for tap in range(3):
        total = total + dot_right(shifted[:, tap * channels : (tap + 1) * channels], conv_w[tap])
    d_a2[...] = total
    for row in spans(SEQ, STEP):
        normed, rstd = normalize(x1[row])
        grad = d_a2[row] * kept[row, 0:1]
        fixed[2:3] += columns_sum(grad * normed)
        fixed[3:4] += columns_sum(grad)
        dx1 = dx2[row] + normalize_back(grad, normed, rstd, vec[2:3])
        input_grad[row] = dx1
        gate = gates[row]
        scaled = dx1 * gate
        d_gated[row, 0:width] = as_low(scaled)
        d_gated[row, width:] = as_low(scaled * values[row] * (1.0 - gate))
    for side, out in ((1 - core, send), (core, keep)):
        here = at_lane(side * half, half)
        put(out, 0, 4, 0, dot_left(a1[:, here], d_gated[...]))
        put(out, 0, 4, half * width // 512, dot_left(a2[:, here], shifted[...]))
    sums = low_columns_sum(d_gated[...])
    fixed[8:9] = sums[:, 0:width]
    fixed[9:10] = sums[:, width:]
    d_a2[...] = dot_right(d_gated[...], gated_w[...])
    for row in spans(SEQ, STEP):
        normed, rstd = normalize(x_ref[row].astype(F32))
        grad = d_a2[row]
        fixed[0:1] += columns_sum(grad * normed)
        fixed[1:2] += columns_sum(grad)
        input_grad[row] += normalize_back(grad, normed, rstd, vec[0:1])
    pack_small(info, wide_sums, fixed, send, keep, rows_ref)


def pack_small(info, wide, fixed, send, keep, rows_ref):
    if rows_ref is None:
        return
    pieces = lax.axis_size("mp")
    local = wide.shape[1] // pieces
    parts = local // 256
    rows_ref[...] = jnp.zeros_like(rows_ref)
    for piece in range(pieces):
        owner = jnp.bitwise_xor(info[1] // local, piece)
        for part in range(parts):
            spot = pl.multiple_of((owner * parts + part) * 16, 16)
            at = piece * local + part * 256
            rows_ref[pl.ds(spot, 16)] = wide[:, at : at + 256]
    base = wide.shape[1] // 16
    for part in range(fixed.shape[1] // 256):
        rows_ref[base + part * 16 : base + (part + 1) * 16] = fixed[:, part * 256 : (part + 1) * 256]
    count = rows_ref.shape[0] // 2
    offset = send.shape[1] - count // 4
    for side, out in ((1 - info[0], send), (info[0], keep)):
        put(out, 0, 4, offset, rows_ref[pl.ds(pl.multiple_of(side * count, 16), count)])


def own_place(count):
    core = lax.axis_index("dp") % 2
    if count == 2:
        return core
    y = lax.axis_index("dp") // 2 % 2
    near = lax.axis_index("dp") // 4 % 2
    return 2 * core + (1 - core) * y + core * near


def cut(weights, vectors, per, link):
    shapes = [(item.shape[0] // per, item.shape[1]) for item in weights]
    total = sum(rows * columns // 256 for rows, columns in shapes)
    local = weights[0].shape[1]
    small = local // 16 if vectors else 0
    chained = [] if link is None else [link]

    def kernel(*refs):
        refs = list(refs)
        sources = [refs.pop(0) for _ in weights]
        small_in = [refs.pop(0) for _ in vectors]
        for _ in chained:
            refs.pop(0)
        packed = refs.pop(0)
        own = refs.pop(0) if vectors else None
        blocks = [refs.pop(0) for _ in weights]
        sems = refs.pop(0)
        held = refs.pop(0)
        held[...] = jnp.zeros_like(held)
        place = own_place(per)
        copies = []
        for at, (source, block) in enumerate(zip(sources, blocks)):
            rows = block.shape[0]
            here = pl.ds(pl.multiple_of(place * rows, 16), rows)
            copies.append(pltpu.make_async_copy(source.at[here], block, sems.at[at]))
        for copy in copies:
            copy.start()
        if vectors:
            for part in range(local // 256):
                lanes = slice(part * 256, (part + 1) * 256)
                row = 0
                for item in small_in:
                    count = item.shape[0] if len(item.shape) == 2 else 1
                    held[row : row + count] = item[..., lanes].astype(F32).reshape(count, 256)
                    row += count
                chunk = as_low(held[...])
                own[part * 16 : (part + 1) * 16] = chunk
                packed[total + part * 16 : total + (part + 1) * 16] = chunk
        for copy in copies:
            copy.wait()
        offset = 0
        for block in blocks:
            rows, columns = block.shape
            for part in range(columns // 256):
                packed[offset : offset + rows] = block[:, part * 256 : (part + 1) * 256]
                offset += rows

    outs = [shaped((total + small, 256), LOW)]
    if vectors:
        outs.append(shaped((small, 256), LOW))
    return pl.pallas_call(
        kernel,
        out_shape=outs,
        in_specs=[pl.BlockSpec(memory_space=pl.ANY) for _ in weights]
        + [pl.BlockSpec(memory_space=pltpu.VMEM) for _ in vectors]
        + [pl.BlockSpec(memory_space=pl.ANY) for _ in chained],
        out_specs=[pl.BlockSpec(memory_space=pltpu.VMEM) for _ in outs],
        scratch_shapes=[pltpu.VMEM(shape, LOW) for shape in shapes]
        + [pltpu.SemaphoreType.DMA((len(weights),)), pltpu.VMEM((16, 256), F32)],
    )(*weights, *vectors, *chained)


def flat_swap(values, partner):
    count = lax.axis_size("dp") * lax.axis_size("mp")
    return lax.ppermute(values, ("dp", "mp"), [(at, partner(at)) for at in range(count)])


PARTNERS = {
    "core": lambda at: at ^ 2,
    "first": lambda at: at ^ (4 if at & 2 else 1),
    "second": lambda at: at ^ (1 if at & 2 else 4),
    "x": lambda at: at ^ 1,
    "y": lambda at: at ^ 4,
    "near": lambda at: at ^ 8,
    "far": lambda at: at ^ 16,
    "hop": lambda at: at ^ (8 if at & 2 else 4),
}
INNER_STEPS = [
    ("quarter", "first"),
    ("half_mix", "second"),
    ("half_near", "near"),
    ("sum", "far"),
    ("sum", "near"),
    ("join_near", "y"),
    ("join_y", "core"),
    ("final", None),
]
SHARED_STEPS = [
    ("quarter", "first"),
    ("half_mix", "second"),
    ("half_near", "near"),
    ("sum", "far"),
    ("sum", "near"),
    ("join_near", "second"),
    ("join_mix", "first"),
    ("spread", "core"),
    ("final", None),
]


PLAN = (
    "p",
    "a",
    "d",
    "p",
    "a",
    "d",
    "p",
    "c",
    "d",
    "p",
    "a",
    "c",
    "d",
    "a",
    "c",
    "d",
    "p",
    "c",
    "d",
    "p",
    "d",
    "c",
    "p",
    "a",
    "d",
    "c",
    "!d",
    "p",
    "!a",
    "!p",
    "c",
    "!c",
)


class Stream:
    def __init__(self, inner, mine, other, parts):
        self.inner = inner
        self.mine = mine
        self.flight = flat_swap(other, PARTNERS["core"])
        self.steps = list(INNER_STEPS if inner else SHARED_STEPS)
        self.parts = parts


def advance_kernel(jobs, refs):
    info, refs = refs[0], refs[1:]
    core, y, near = info[0], info[4], info[5]
    ins, outs = list(refs[: 2 * len(jobs)]), list(refs[2 * len(jobs) :])
    for inner, step, parts in jobs:
        mine, flight = ins.pop(0), ins.pop(0)
        x = 0 if inner else info[3]
        mix = core * x + (1 - core) * y

        def added(spot):
            return as_low(mine[spot].astype(F32) + flight[spot].astype(F32))

        if step == "quarter":
            keep, send = outs.pop(0), outs.pop(0)
            for at in range(2):
                send[at] = added(core * (2 * at + 1 - y) + (1 - core) * (2 * (1 - x) + at))
                keep[at] = added(core * (2 * at + y) + (1 - core) * (2 * x + at))
        elif step == "half_mix":
            keep, send = outs.pop(0), outs.pop(0)
            send[0] = added(1 - mix)
            keep[0] = added(mix)
        elif step == "half_near":
            keep, send = outs.pop(0), outs.pop(0)
            rows = keep.shape[1]
            for out, side in ((send, 1 - near), (keep, near)):
                here = pl.ds(pl.multiple_of(side * rows, 16), rows)
                out[0] = as_low(mine[0, here].astype(F32) + flight[0, here].astype(F32))
        elif step == "sum":
            outs.pop(0)[0] = added(0)
        elif step == "join_near":
            out = outs.pop(0)
            rows = mine.shape[1]
            out[0, pl.ds(pl.multiple_of(near * rows, 16), rows)] = mine[0]
            out[0, pl.ds(pl.multiple_of((1 - near) * rows, 16), rows)] = flight[0]
        elif step in ("join_y", "join_mix"):
            out = outs.pop(0)
            side = y if step == "join_y" else mix
            out[side] = mine[0]
            out[1 - side] = flight[0]
        elif step == "spread":
            out = outs.pop(0)
            for at in range(2):
                out[core * (2 * at + y) + (1 - core) * (2 * x + at)] = mine[at]
                out[core * (2 * at + 1 - y) + (1 - core) * (2 * (1 - x) + at)] = flight[at]


def finish_kernel(parts, small, refs):
    info, mine, flight, refs = refs[0], refs[1], refs[2], list(refs[3:])
    core = info[0]
    outs = [refs.pop(0) for _ in parts]
    smalls = [refs.pop(0) for _ in range(11)] if small else []
    link = refs.pop(0)
    link[...] = jnp.zeros_like(link)
    held = [refs.pop(0) for _ in parts]
    sems = refs.pop(0)
    copies = []
    quarters = mine.shape[0]
    for at, (offset, rows, shape) in enumerate(parts):
        target, columns, deep = held[at], shape[-1] // 256, len(shape) == 3
        for half, (source, side) in enumerate(((mine, core), (flight, 1 - core))):
            for quarter in range(quarters):
                here = slice(quarter * rows, (quarter + 1) * rows)
                for part in range(columns * (shape[0] if deep else 1)):
                    row = offset + part * rows
                    block = source[quarter, row : row + rows].astype(F32)
                    if deep:
                        target[half, part, here] = block
                    else:
                        target[half, here, part * 256 : (part + 1) * 256] = block
            spot = pl.ds(pl.multiple_of(side * quarters * rows, 16), quarters * rows)
            spot = (slice(None), spot) if deep else (spot,)
            copies.append(
                pltpu.make_async_copy(target.at[half], outs[at].at[spot], sems.at[len(copies)])
            )
            copies[-1].start()
    if small:
        total = refs.pop(0)
        offset, rows = small
        for source, side in ((mine, core), (flight, 1 - core)):
            for quarter in range(mine.shape[0]):
                spot = (side * mine.shape[0] + quarter) * rows
                total[pl.ds(pl.multiple_of(spot, 16), rows)] = source[
                    quarter, offset : offset + rows
                ].astype(F32)
        norm, gated, left, conv, inner, depth, point, project, output, expand, shrink = smalls
        local, width = left.shape[-1], output.shape[-1]
        for part in range(local // 256):
            lanes = slice(part * 256, (part + 1) * 256)
            spot = (info[1] // local * (local // 256) + part) * 16
            block = total[pl.ds(pl.multiple_of(spot, 16), 16)]
            left[:, lanes] = block[0:1]
            expand[:, lanes] = block[1:2]
            inner[:, lanes] = block[2:4]
            depth[:, lanes] = block[4:13]
        for part in range(width // 256):
            lanes = slice(part * 256, (part + 1) * 256)
            base = local * 2 // 16 + part * 16
            block = total[base : base + 16]
            for at in range(4):
                norm[at, :, lanes] = block[2 * at : 2 * at + 2]
            gated[:, lanes] = block[8:9]
            gated[:, width + part * 256 : width + (part + 1) * 256] = block[9:10]
            project[:, lanes] = block[10:12]
            output[:, lanes] = block[12:13]
            shrink[:, lanes] = block[13:14]
            (conv if part == 0 else point)[...] = block[14:15]
    for copy in copies:
        copy.wait()


def finish(chain, stream, small):
    parts = stream.parts
    shapes = [shaped(shape, F32) for _, _, shape in parts]
    scratch = [
        pltpu.VMEM((2,) + shape[:-2] + (shape[-2] // 2, shape[-1]), F32) for _, _, shape in parts
    ]
    scratch.append(pltpu.SemaphoreType.DMA((2 * len(parts),)))
    names = []
    if small:
        scratch.append(pltpu.VMEM((256, 256), F32))
        names = [shaped(shape, F32) for shape in small[1]]
    stream.mine = chain.run(
        lambda *refs: finish_kernel(parts, small[0] if small else None, refs),
        shapes + names + [shaped((8, 128), F32)],
        [stream.mine, stream.flight],
        scratch,
        ADV,
        len(parts),
    )


def advance(chain, streams):
    jobs, ins, outs = [], [], []
    for stream in streams:
        step = stream.steps[0][0]
        jobs.append((stream.inner, step, stream.parts))
        ins += [stream.mine, stream.flight]
        lead, rows, columns = stream.mine.shape
        if step in ("quarter", "half_mix"):
            outs += [shaped((lead // 2, rows, columns), LOW)] * 2
        elif step == "half_near":
            outs += [shaped((lead, rows // 2, columns), LOW)] * 2
        elif step == "sum":
            outs.append(shaped((lead, rows, columns), LOW))
        elif step == "join_near":
            outs.append(shaped((lead, rows * 2, columns), LOW))
        else:
            outs.append(shaped((lead * 2, rows, columns), LOW))
    results = list(chain.run(lambda *refs: advance_kernel(jobs, refs), outs, ins, [], ADV))
    for stream in streams:
        step, partner = stream.steps.pop(0)
        stream.mine = results.pop(0)
        if step in ("quarter", "half_mix", "half_near"):
            stream.flight = flat_swap(results.pop(0), PARTNERS[partner])
        else:
            stream.flight = flat_swap(stream.mine, PARTNERS[partner])


def opened(packed, first, count, offset, rows, columns):
    parts = [
        packed[first : first + count, offset + at * rows : offset + (at + 1) * rows]
        for at in range(columns // 256)
    ]
    return jnp.concatenate(parts, 2).reshape(count * rows, columns)


class Weights:
    def __init__(self, packed, per):
        pieces = [packed]
        for bit in bits_of("mp"):
            pieces = pieces + [swap(item, "mp", bit) for item in pieces]
        self.blocks = [[item] for item in pieces[1:]]
        self.per = per

    def hop(self, after):
        if self.per == 4:
            for blocks in self.blocks:
                blocks[0], _ = lax.optimization_barrier((blocks[0], after))
                blocks.append(flat_swap(blocks[0], PARTNERS["hop"]))

    def share(self, after):
        found = []
        for blocks in self.blocks:
            held = [lax.optimization_barrier((item, after))[0] for item in blocks]
            found += held + [swap(item, "dp", 1) for item in held]
        return found


def finish_shared(mine, other, order):
    own = bit_of("dp", 1)
    values = add_low(mine, swap(other, "dp", 1))
    held = [("dp", 1, own)]
    for axis, bit in order[:-1]:
        own = bit_of(axis, bit)
        mine, other = split(values, own)
        values = add_low(mine, swap(other, axis, bit))
        held.append((axis, bit, own))
    axis, bit = order[-1]
    values = add_low(values, swap(values, axis, bit))
    for axis, bit, own in reversed(held):
        values = join(values, swap(values, axis, bit), own)
    return values.astype(F32)


def finish_inner(mine, other, order):
    values = add_low(mine, swap(other, "dp", 1))
    pieces = [values[at] for at in range(values.shape[0])]
    held = [("dp", 1, bit_of("dp", 1))]
    for axis, bit in order[:-1]:
        if axis == "mp":
            keep_count = len(pieces) // 2
            moved = [swap(item, axis, bit) for item in pieces[keep_count:]]
            pieces = [add_low(one, two) for one, two in zip(pieces[:keep_count], moved)]
            continue
        own = bit_of(axis, bit)
        parts = [split(item, own) for item in pieces]
        pieces = [add_low(mine, swap(other, axis, bit)) for mine, other in parts]
        held.append((axis, bit, own))
    axis, bit = order[-1]
    values = add_low(pieces[0], swap(pieces[0], axis, bit))
    for axis, bit, own in reversed(held):
        values = join(values, swap(values, axis, bit), own)
    return values.astype(F32)


def body(
    cell_input,
    lengths,
    out_grad,
    norm_params,
    gated_weight,
    gated_bias,
    left_weight,
    left_bias,
    conv_weight,
    conv_bias,
    inner_norm,
    depth_weight,
    point_weight,
    point_bias,
    project_weight,
    project_bias,
    output_weight,
    output_bias,
    expand_weight,
    expand_bias,
    shrink_weight,
    shrink_bias,
):
    width = cell_input.shape[1]
    channels = conv_weight.shape[2]
    local = left_weight.shape[1]
    pieces = lax.axis_size("mp")
    inner = local * pieces
    tokens = cell_input.shape[0]
    assert tokens == SEQ
    tuned = lax.axis_size("dp") == 16 and pieces == 2
    mp_bits = bits_of("mp")[::-1]
    dp_bits = bits_of("dp")[1:]
    mp_first = [("mp", bit) for bit in mp_bits] + [("dp", bit) for bit in dp_bits]
    core = bit_of("dp", 1)
    chain = Chain(local)

    def inner_rows(size):
        return (2 * pieces, size // 1024, 256)


    per = 4 if tuned else 2
    vectors = [left_bias, expand_bias, inner_norm, depth_weight]
    packed, own = cut([left_weight, point_weight], vectors, per, None)
    early = Weights(packed, per)
    (packed,) = cut([expand_weight, shrink_weight], [], per, own)
    late = Weights(packed, per)
    chain.link = packed
    a1, values, gates, x1, a2, right_pre, vec, kept, valid, right = chain.run(
        pre_kernel,
        [
            shaped((tokens, width), LOW),
            shaped((tokens, width), F32),
            shaped((tokens, width), F32),
            shaped((tokens, width), F32),
            shaped((tokens, width), LOW),
            shaped((tokens, channels), F32),
            shaped((16, width), F32),
            shaped((tokens, 128), F32),
            shaped((8, tokens), F32),
            shaped((tokens, channels), LOW),
        ],
        [
            lengths,
            cell_input,
            gated_weight,
            conv_weight,
            norm_params,
            gated_bias,
            conv_bias,
            point_bias,
            project_bias,
            output_bias,
            shrink_bias,
        ],
        [],
        int(2.2e9 * EARLY),
    )
    early.hop(right)
    early_blocks = early.share(right)
    normed, slope, depth, rstd, left_rest = chain.run(
        lambda *refs: inner_forward_kernel(pieces, per, refs),
        [
            shaped((tokens, inner), LOW),
            shaped((tokens, inner), LOW),
            shaped((tokens, inner), LOW),
            shaped((tokens, 128), F32),
            shaped((pieces - 1, width, local), LOW),
        ],
        [a2, right, left_weight, own, kept] + early_blocks,
        [
            pltpu.VMEM((tokens, inner), F32),
            pltpu.VMEM((tokens, 128), F32),
            pltpu.VMEM((tokens, 128), F32),
            pltpu.VMEM((tokens, 128), F32),
            pltpu.VMEM((tokens + 16, 128), F32),
            pltpu.VMEM((tokens + 16, 128), F32),
        ],
        int(6.5e9 * EARLY),
    )
    late.hop(rstd)
    x2, a4, qkv, lse, attended, x3, a5, point_rest = chain.run(
        lambda *refs: attention_forward_kernel(pieces, per, refs),
        [
            shaped((tokens, width), F32),
            shaped((tokens, width), LOW),
            shaped((tokens, 3 * width), LOW),
            shaped((tokens, 128), F32),
            shaped((tokens, width), LOW),
            shaped((tokens, width), F32),
            shaped((tokens, width), LOW),
            shaped((pieces - 1, local, channels), LOW),
        ],
        [x1, depth, point_weight, vec, project_weight, output_weight, valid]
        + early_blocks,
        [],
        int(4.4e9 * EARLY),
    )
    keep_own, send_own, shrunk_own, d_a5_own, bias_own = chain.run(
        feed_own_kernel,
        [
            shaped((2, 2 * local * width // 1024, 256), LOW),
            shaped((2, 2 * local * width // 1024, 256), LOW),
            shaped((tokens, width), F32),
            shaped((tokens, width), F32),
            shaped((8, local), F32),
        ],
        [a5, out_grad, expand_weight, shrink_weight, own],
        [
            pltpu.VMEM((tokens, local), LOW),
            pltpu.VMEM((tokens, local), F32),
            pltpu.VMEM((tokens, local), LOW),
        ],
        int(3e9 * EARLY),
    )
    late_blocks = late.share(bias_own)
    cell_output, feed_keep, feed_send, dx3, fixed, expand_sum = chain.run(
        lambda *refs: feed_kernel(pieces, per, refs),
        [
            shaped((tokens, width), LOW),
            shaped(inner_rows(2 * local * width), LOW),
            shaped(inner_rows(2 * local * width), LOW),
            shaped((tokens, width), F32),
            shaped((16, width), F32),
            shaped((8, inner), F32),
        ],
        [a5, x3, out_grad, vec, keep_own, send_own, shrunk_own, d_a5_own, bias_own]
        + early_blocks
        + late_blocks,
        [
            pltpu.VMEM((tokens, local), LOW),
            pltpu.VMEM((tokens, local), F32),
            pltpu.VMEM((tokens, local), LOW),
            pltpu.VMEM((tokens, width), F32),
            pltpu.VMEM((tokens, width), F32),
            pltpu.VMEM((width, local), LOW),
            pltpu.VMEM((local, width), LOW),
        ],
        int(8e9 * SCALE),
    )
    if tuned:
        fee = Stream(
            True,
            feed_keep,
            feed_send,
            [
                (0, local // 4, (local, width)),
                (width * local // 1024, width // 4, (width, local)),
            ],
        )
    proj_send, proj_keep, dx2, d_sep, fixed = chain.run(
        attention_backward_kernel,
        [
            shaped((4, width * width // 512, 256), LOW),
            shaped((4, width * width // 512, 256), LOW),
            shaped((tokens, width), F32),
            shaped((tokens, channels), LOW),
            shaped((16, width), F32),
        ],
        [dx3, attended, output_weight, qkv, lse, a4, project_weight, x2, vec, valid, fixed],
        [
            pltpu.VMEM((tokens, width), LOW),
            pltpu.VMEM((tokens, width), LOW),
            pltpu.VMEM((tokens, 3 * width), LOW),
        ],
        int(6.7e9 * SCALE),
    )
    if tuned:
        pro = Stream(
            False,
            proj_keep,
            proj_send,
            [
                (0, width // 8, (width, 3 * width)),
                (3 * width * width // 2048, width // 8, (width, width)),
            ],
        )
        advance(chain, [fee])
    left_keep, left_send, d_a2, d_right, wide_sums = chain.run(
        lambda *refs: inner_backward_kernel(pieces, per, refs),
        [
            shaped(inner_rows(local * (width + channels)), LOW),
            shaped(inner_rows(local * (width + channels)), LOW),
            shaped((tokens, width), F32),
            shaped((tokens, channels), F32),
            shaped((16, inner), F32),
        ],
        [
            d_sep,
            depth,
            normed,
            slope,
            rstd,
            a2,
            expand_sum,
            point_weight,
            point_rest,
            left_weight,
            left_rest,
            own,
            kept,
        ]
        + early_blocks,
        [
            pltpu.VMEM((inner // 128, tokens, 128), F32),
            pltpu.VMEM((tokens + 16, 128), F32),
            pltpu.VMEM((tokens + 16, 128), F32),
            pltpu.VMEM((tokens, inner), LOW),
            pltpu.VMEM((tokens, 128), F32),
            pltpu.VMEM((tokens, 128), F32),
            pltpu.VMEM((11, 8, inner), F32),
        ],
        int(11.5e9 * SCALE),
    )
    if tuned:
        lef = Stream(
            True,
            left_keep,
            left_send,
            [
                (0, width // 4, (width, local)),
                (width * local // 1024, local // 4, (local, channels)),
            ],
        )
        advance(chain, [fee])
    small = 32 if tuned else 0
    last_rows = width * (2 * width + 3 * channels) // 2048 + small
    last_send, last_keep, input_grad, fixed = chain.run(
        last_kernel if tuned else lambda *refs: last_kernel(*refs, None),
        [
            shaped((4, last_rows, 256), LOW),
            shaped((4, last_rows, 256), LOW),
            shaped((tokens, width), F32),
            shaped((16, width), F32),
        ],
        [
            d_a2,
            d_right,
            right_pre,
            conv_weight,
            a2,
            x1,
            dx2,
            values,
            gates,
            a1,
            gated_weight,
            cell_input,
            vec,
            kept,
            fixed,
            wide_sums,
        ],
        [
            pltpu.VMEM((tokens, 3 * channels), LOW),
            pltpu.VMEM((tokens, width), F32),
            pltpu.VMEM((tokens, 2 * width), LOW),
        ]
        + ([pltpu.VMEM((8 * small, 256), F32)] if tuned else []),
        int(4.0e9 * SCALE),
    )
    if tuned:
        lat = Stream(
            False,
            last_keep,
            last_send,
            [
                (0, width // 8, (width, 2 * width)),
                (width * width // 1024, width // 8, (3, width, channels)),
            ],
        )
        groups = {"a": [fee], "p": [pro], "c": [lef], "d": [lat]}
        small_shapes = [
            (4, 2, width),
            (1, 2 * width),
            (1, local),
            (1, channels),
            (2, local),
            (9, local),
            (1, channels),
            (2, width),
            (1, width),
            (1, local),
            (1, width),
        ]
        small_part = ((last_rows - small, small), small_shapes)
        for names in PLAN:
            if names[0] == "!":
                stream = groups[names[1]][0]
                finish(chain, stream, small_part if names == "!d" else None)
            else:
                advance(chain, [groups[name][0] for name in names])
        (grad_shrink, grad_expand, _), (grad_left, grad_point, _) = fee.mine, lef.mine
        (grad_proj, grad_out, _), (grad_gated, grad_conv) = pro.mine, lat.mine[:2]
        smalls = [
            item.reshape(-1) if item.shape[0] == 1 else item for item in lat.mine[2:-1]
        ]
    else:

        def whole(keep, send, offset, rows, columns):
            both = [
                jnp.stack([opened(item, 2 * at, 2, offset, rows, columns) for at in range(pieces)])
                for item in (keep, send)
            ]
            return finish_inner(both[0], both[1], mp_first)

        def shared(keep, send, offset, rows, columns):
            both = [opened(item, 0, 4, offset, rows, columns) for item in (keep, send)]
            return finish_shared(both[0], both[1], mp_first)

        eighth = width // 8
        grad_shrink = whole(feed_keep, feed_send, 0, local // 4, width)
        grad_expand = whole(
            feed_keep, feed_send, width * local // 1024, width // 4, local
        )
        grad_left = whole(left_keep, left_send, 0, width // 4, local)
        grad_point = whole(left_keep, left_send, width * local // 1024, local // 4, channels)
        grad_proj = shared(proj_keep, proj_send, 0, eighth, 3 * width)
        grad_out = shared(proj_keep, proj_send, 6 * eighth, eighth, width)
        grad_gated = shared(last_keep, last_send, 0, eighth, 2 * width)
        grad_conv = jnp.stack(
            [shared(last_keep, last_send, (4 + at) * eighth, eighth, channels) for at in range(3)]
        )
        chunks = [wide_sums[:, at : at + local] for at in range(0, inner, local)]
        for bit in mp_bits:
            count = len(chunks) // 2
            moved = [swap(item, "mp", bit) for item in chunks[count:]]
            chunks = [one + two for one, two in zip(chunks[:count], moved)]
            fixed = fixed + swap(fixed, "mp", bit)
        wide_total = chunks[0]
        for bit in bits_of("dp"):
            fixed = fixed + swap(fixed, "dp", bit)
            wide_total = wide_total + swap(wide_total, "dp", bit)
        smalls = [
            fixed[0:8].reshape(4, 2, width),
            fixed[8:10].reshape(2 * width),
            wide_total[0],
            fixed[14, :channels],
            wide_total[2:4],
            wide_total[4:13],
            fixed[14, channels:],
            fixed[10:12],
            fixed[12],
            wide_total[1],
            fixed[13],
        ]
    return (
        cell_output,
        input_grad,
        smalls[0],
        grad_gated,
        smalls[1],
        grad_left,
        smalls[2],
        grad_conv,
        smalls[3],
        smalls[4],
        smalls[5],
        grad_point,
        smalls[6],
        grad_proj,
        smalls[7],
        grad_out,
        smalls[8],
        grad_expand,
        smalls[9],
        grad_shrink,
        smalls[10],
    )


def solution(mesh):
    return jax.shard_map(
        body,
        mesh=mesh,
        in_specs=(
            P(("dp", "mp"), None),
            P(("dp", "mp")),
            P(("dp", "mp"), None),
            P(),
            P(),
            P(),
            P(None, "mp"),
            P("mp"),
            P(),
            P(),
            P(None, "mp"),
            P(None, "mp"),
            P("mp", None),
            P(),
            P(),
            P(),
            P(),
            P(),
            P(None, "mp"),
            P("mp"),
            P("mp", None),
            P(),
        ),
        out_specs=(
            P(("dp", "mp"), None),
            P(("dp", "mp"), None),
            P(),
            P(),
            P(),
            P(None, "mp"),
            P("mp"),
            P(),
            P(),
            P(None, "mp"),
            P(None, "mp"),
            P("mp", None),
            P(),
            P(),
            P(),
            P(),
            P(),
            P(None, "mp"),
            P("mp"),
            P("mp", None),
            P(),
        ),
        check_vma=False,
    )
```

```python
import jax
import jax.numpy as jnp
from jax import lax
from jax.experimental import pallas as pl
from jax.experimental.pallas import tpu as pltpu
from jax.sharding import PartitionSpec as P

HEADS = 8
SEQ = 256
EPS = 1e-06
NEGATIVE = -1000000000.0
LOW = jnp.bfloat16
F32 = jnp.float32
STEP = 64
LIMIT = 24 * 2**20
SCALE = 4
EARLY = 0.001
ADV = 20 * 10**9


def as_low(values):
    return values.astype(LOW)


def dot(left, right):
    return jnp.dot(left, right, preferred_element_type=F32)


def dot_left(left, right):
    return lax.dot_general(left, right, (((0,), (0,)), ((), ())), preferred_element_type=F32)


def dot_right(left, right):
    return lax.dot_general(left, right, (((1,), (1,)), ((), ())), preferred_element_type=F32)


def swap(values, axis, bit):
    count = lax.axis_size(axis)
    return lax.ppermute(values, axis, [(at, at ^ bit) for at in range(count)])


def bit_of(axis, bit):
    return (lax.axis_index(axis) // bit) % 2


def bits_of(axis):
    bits, bit = [], 1
    while bit < lax.axis_size(axis):
        bits.append(bit)
        bit *= 2
    return bits


def add_low(first, second):
    return as_low(first.astype(F32) + second.astype(F32))


def split(values, own):
    half = values.shape[0] // 2
    mine = lax.dynamic_slice_in_dim(values, own * half, half, 0)
    other = lax.dynamic_slice_in_dim(values, (1 - own) * half, half, 0)
    return mine, other


def join(mine, other, own):
    swapped = own == 1
    return jnp.concatenate(
        [jnp.where(swapped, other, mine), jnp.where(swapped, mine, other)], 0
    )


def sum_shared(values, order):
    held = []
    steps = [("dp", 1)] + order
    for axis, bit in steps[:-1]:
        own = bit_of(axis, bit)
        mine, other = split(values, own)
        values = add_low(mine, swap(other, axis, bit))
        held.append((axis, bit, own))
    axis, bit = steps[-1]
    values = add_low(values, swap(values, axis, bit))
    for axis, bit, own in reversed(held):
        values = join(values, swap(values, axis, bit), own)
    return values.astype(F32)


def sum_inner(pieces, order):
    held = []
    steps = [("dp", 1)] + order
    for axis, bit in steps[:-1]:
        if axis == "mp":
            keep_count = len(pieces) // 2
            moved = [swap(item, axis, bit) for item in pieces[keep_count:]]
            pieces = [add_low(one, two) for one, two in zip(pieces[:keep_count], moved)]
            continue
        own = bit_of(axis, bit)
        parts = [split(item, own) for item in pieces]
        pieces = [add_low(mine, swap(other, axis, bit)) for mine, other in parts]
        held.append((axis, bit, own))
    axis, bit = steps[-1]
    values = add_low(pieces[0], swap(pieces[0], axis, bit))
    for axis, bit, own in reversed(held):
        values = join(values, swap(values, axis, bit), own)
    return values.astype(F32)


def sigmoid(values):
    return 0.5 * jnp.tanh(0.5 * values) + 0.5


def spans(total, step):
    return [slice(at, at + step) for at in range(0, total, step)]


def at_lane(start, size):
    return pl.ds(pl.multiple_of(start, 128), size)


def normalize(values):
    width = values.shape[1]
    centre = jnp.sum(values, -1, keepdims=True) * (1.0 / width)
    centered = values - centre
    variance = jnp.sum(centered * centered, -1, keepdims=True) * (1.0 / width)
    rstd = lax.rsqrt(variance + EPS)
    return centered * rstd, rstd


def normalize_back(grad, normed, rstd, gain):
    width = grad.shape[1]
    scaled = grad * gain
    first = jnp.sum(scaled, -1, keepdims=True) * (1.0 / width)
    second = jnp.sum(scaled * normed, -1, keepdims=True) * (1.0 / width)
    return rstd * (scaled - first - normed * second)


def columns_sum(values):
    return jnp.sum(values, 0, keepdims=True)


def eighths_sum(values):
    return jnp.sum(values.reshape(-1, 8, values.shape[1]), 0)


def low_columns_sum(values):
    ones = jnp.ones((16, values.shape[0]), LOW)
    return dot(ones, values)[0:1]


def place(local):
    dp, mp = lax.axis_index("dp"), lax.axis_index("mp")
    return dp % 2, mp * local, None, mp % 2, dp // 2 % 2, dp // 4 % 2


class Chain:
    def __init__(self, local):
        self.link = None
        self.local = local

    def run(self, kernel, outs, ins, scratch, flops, placed=0):
        ins = list(ins)
        specs = [
            pl.BlockSpec(memory_space=pltpu.SMEM if item.dtype == jnp.int32 else pltpu.VMEM)
            for item in ins
        ]
        count = len(ins)
        moved = sum(item.size * item.dtype.itemsize for item in ins + list(outs))
        linked = self.link is not None
        if linked:
            ins.append(self.link)
            specs.append(pl.BlockSpec(memory_space=pl.ANY))

        def call(*refs):
            kernel(place(self.local), *(refs[:count] + refs[count + 1 :] if linked else refs))

        results = pl.pallas_call(
            call,
            out_shape=outs,
            in_specs=specs,
            out_specs=[
                pl.BlockSpec(memory_space=pltpu.HBM if at < placed else pltpu.VMEM)
                for at in range(len(outs))
            ],
            scratch_shapes=scratch,
            compiler_params=pltpu.CompilerParams(vmem_limit_bytes=LIMIT),
            cost_estimate=pl.CostEstimate(
                flops=flops, bytes_accessed=moved + flops // 50, transcendentals=0
            ),
        )(*ins)
        self.link = min(results, key=lambda item: item.size)
        return results


def put(out, first, count, offset, values):
    rows = values.shape[0] // count
    low = as_low(values)
    for quarter in range(count):
        for part in range(values.shape[1] // 256):
            at = offset + part * rows
            out[first + quarter, at : at + rows] = low[
                quarter * rows : (quarter + 1) * rows, part * 256 : (part + 1) * 256
            ]


def shaped(shape, kind):
    return jax.ShapeDtypeStruct(shape, kind)


def pre_kernel(
    info, lengths, left, own, x_ref, gated_w, conv_w, norms, gated_b, conv_b, point_b, project_b, output_b, shrink_b,
    a1, values, gates, x1, a2, right_pre, vec, kept, valid, mixed, slope, total_ref, square, right
):
    width = x_ref.shape[1]
    channels = right.shape[1]
    length = lengths[0]
    for ref, axis in ((kept, 0), (valid, 1)):
        spots = lax.broadcasted_iota(jnp.int32, ref.shape, axis)
        ref[...] = jnp.where(spots < length, 1.0, 0.0).astype(F32)
    vec[...] = jnp.zeros_like(vec)
    for at in range(4):
        vec[2 * at : 2 * at + 2] = norms[at].astype(F32)
    for row, item in ((8, gated_b.at[0:width]), (9, gated_b.at[width:]), (13, output_b), (14, shrink_b)):
        vec[row : row + 1] = item[...].astype(F32).reshape(1, width)
    vec[10:11, 0:channels] = conv_b[...].astype(F32).reshape(1, channels)
    vec[10:11, channels:] = point_b[...].astype(F32).reshape(1, channels)
    vec[11:13] = project_b[...].astype(F32)
    for row in spans(SEQ, STEP):
        normed, _ = normalize(x_ref[row].astype(F32))
        a1[row] = as_low(normed * vec[0:1] + vec[1:2])
    for col in spans(width, 256):
        gate_col = slice(col.start + width, col.stop + width)
        value = dot(a1[...], gated_w[:, col]) + vec[8:9, col]
        gate = sigmoid(dot(a1[...], gated_w[:, gate_col]) + vec[9:10, col])
        values[:, col] = value
        gates[:, col] = gate
        x1[:, col] = x_ref[:, col].astype(F32) + value * gate
    for row in spans(SEQ, STEP):
        normed, _ = normalize(x1[row])
        a2[row] = as_low((normed * vec[2:3] + vec[3:4]) * kept[row, 0:1])
    rows = lax.broadcasted_iota(jnp.int32, right_pre.shape, 0)
    first = jnp.where(rows == 0, 0.0, pltpu.roll(dot(a2[...], conv_w[0]), 1, 0))
    last = jnp.where(rows == SEQ - 1, 0.0, pltpu.roll(dot(a2[...], conv_w[2]), SEQ - 1, 0))
    total = first + dot(a2[...], conv_w[1]) + last + vec[10:11, 0 : right_pre.shape[1]]
    right_pre[...] = total
    right[...] = as_low(total * sigmoid(total))
    total_ref[...] = jnp.zeros_like(total_ref)
    square[...] = jnp.zeros_like(square)
    right_rows = right[...].astype(F32)
    left_piece(a2, left, (own, 0), right_rows, info[1], 0, mixed, slope, total_ref, square)


def unpack(refs, counts):
    groups, at = [], 0
    for count in counts:
        groups.append(refs[at : at + count])
        at += count
    return groups


def places(info, count):
    core, y, near = info[0], info[4], info[5]
    if count == 2:
        return [core, 1 - core]
    mine = (1 - core) * y + core * near
    theirs = (1 - core) * near + core * y
    return [2 * core + mine, 2 * core + 1 - mine, 2 - 2 * core + theirs, 3 - 2 * core - theirs]


def assemble(info, target, blocks, offset):
    rows = target.shape[0] // len(blocks)
    for spot, block in zip(places(info, len(blocks)), blocks):
        here = pl.ds(pl.multiple_of(spot * rows, 16), rows)
        for part in range(target.shape[1] // 256):
            at = offset + part * rows
            target[here, part * 256 : (part + 1) * 256] = block[at : at + rows]


def vectors_of(own, blocks, per_piece, offset):
    found = [(own, 0)]
    for at in range(0, len(blocks), per_piece):
        found.append((blocks[at], offset))
    return found


def rows_of(vectors, index, lanes):
    ref, offset = vectors
    return ref[pl.ds(pl.multiple_of(offset + index * 16, 16), 16), lanes].astype(F32)


def left_piece(a2, left, vectors, right_rows, offset, base, mixed, slope, total, square):
    local = left.shape[1]
    for col in spans(local, 256):
        pre = dot(a2[...], left[:, col])
        pre = pre + rows_of(vectors, col.start // 256, slice(0, 256))[0:1]
        sigma = sigmoid(pre)
        at = base + col.start
        slope[:, at : at + 256] = as_low(sigma * (1.0 + pre * (1.0 - sigma)))
        value = pre * sigma + right_rows * jnp.where(offset == at, 1.0, 0.0)
        mixed[:, col] = value
        total[...] += value[:, 0:128] + value[:, 128:256]
        squared = value * value
        square[...] += squared[:, 0:128] + squared[:, 128:256]


def inner_forward_kernel(pieces, per, refs):
    info, refs = refs[0], refs[1:]
    (a2, right, mixed_own, slope_own, total_own, square_own, own, keep), packed, outs, scratch = unpack(
        refs, [8, per * (pieces - 1), 5, 6]
    )
    normed_ref, slope_ref, depth, rstd_ref, left_rest = outs
    mixed, total, square, centre_ref, padded, padded_two = scratch
    local = mixed_own.shape[1]
    inner = local * pieces
    skipped = a2.shape[1] * local // (256 * per) + local // per
    wide = vectors_of(own, packed, per, skipped)
    right_rows = right[...].astype(F32)
    total[...] = total_own[...]
    square[...] = square_own[...]
    slope_ref[:, 0:local] = slope_own[...]
    for piece in range(1, pieces):
        rest = left_rest.at[piece - 1]
        assemble(info, rest, packed[(piece - 1) * per : piece * per], 0)
        left_piece(
            a2, rest, wide[piece], right_rows, info[1], piece * local,
            mixed.at[piece - 1], slope_ref, total, square,
        )
    centre = jnp.sum(total[...], 1, keepdims=True) * (1.0 / inner)
    variance = jnp.sum(square[...], 1, keepdims=True) * (1.0 / inner) - centre * centre
    rstd = lax.rsqrt(variance + EPS)
    centre_ref[...] = jnp.broadcast_to(centre, centre_ref.shape)
    rstd_ref[...] = jnp.broadcast_to(rstd, rstd_ref.shape)
    for pad in (padded, padded_two):
        pad[0:8] = jnp.zeros((8, 128), F32)
        pad[SEQ + 8 : SEQ + 16] = jnp.zeros((8, 128), F32)
    kept = keep[:, 0:1]
    for piece in range(pieces):

        def one(index, part, pad):
            here = at_lane(piece * local + index * 256 + part, 128)
            vectors = rows_of(wide[piece], index, slice(part, part + 128))
            source = mixed_own if piece == 0 else mixed.at[piece - 1]
            value = source[:, at_lane(index * 256 + part, 128)]
            normed = (value - centre_ref[...]) * rstd_ref[...]
            normed_ref[:, here] = as_low(normed)
            pad[8 : SEQ + 8] = (normed * vectors[2:3] + vectors[3:4]) * kept
            result = pad[4 : SEQ + 4] * vectors[4:5]
            for tap in range(1, 9):
                result = result + pad[4 + tap : SEQ + 4 + tap] * vectors[4 + tap : 5 + tap]
            depth[:, here] = as_low(result)

        def step(index, carry):
            one(index, 0, padded)
            one(index, 128, padded_two)
            return carry

        lax.fori_loop(0, local // 256, step, 0)


def masked_scores(queries, keys, valid, scale):
    return jnp.where(valid, dot_right(queries, keys) * scale, NEGATIVE)


def attention_forward_kernel(pieces, per, refs):
    (info, x1, depth, point, vec, project_w, output_w, mask), packed, outs = unpack(
        refs, [8, per * (pieces - 1), 8]
    )
    x2, a4, qkv, lse, attended, x3, a5, point_rest = outs
    width = x2.shape[1]
    local, channels = point.shape
    sep = dot(depth[:, 0:local], point[...])
    for piece in range(1, pieces):
        blocks = packed[(piece - 1) * per : piece * per]
        assemble(info, point_rest.at[piece - 1], blocks, width * local // (256 * per))
        sep = sep + dot(depth[:, piece * local : (piece + 1) * local], point_rest[piece - 1])
    x2[:, 0:channels] = x1[:, 0:channels] + sep + vec[10:11, channels : 2 * channels]
    x2[:, channels:width] = x1[:, channels:width]
    for row in spans(SEQ, STEP):
        normed, _ = normalize(x2[row])
        a4[row] = as_low(normed * vec[4:5] + vec[5:6])
    for col in spans(3 * width, 256):
        part = dot(a4[...], project_w[:, col])
        if col.start < width:
            part = part + vec[11:12, col]
        elif col.start >= 2 * width:
            part = part + vec[12:13, col.start - 2 * width : col.stop - 2 * width]
        qkv[:, col] = as_low(part)
    scale = (width // HEADS) ** (-0.5)
    lanes = lax.broadcasted_iota(jnp.int32, (SEQ, 128), 1)
    valid = jnp.broadcast_to(mask[0:1], (SEQ, SEQ)) > 0.5
    logs = jnp.zeros((SEQ, 128), F32)
    for pair in range(width // 128):
        at = pair * 128
        queries = qkv[:, at : at + 128]
        keys = qkv[:, width + at : width + at + 128]
        vals = qkv[:, 2 * width + at : 2 * width + at + 128]
        mixed = []
        for side in range(2):
            mine = (lanes < 64) if side == 0 else (lanes >= 64)
            scores = masked_scores(jnp.where(mine, queries, 0), keys, valid, scale)
            highest = jnp.max(scores, -1, keepdims=True)
            weights = jnp.exp(scores - highest)
            total = jnp.sum(weights, -1, keepdims=True)
            mixed.append(dot(as_low(weights * (1.0 / total)), vals))
            logs = jnp.where(lanes == 2 * pair + side, highest + jnp.log(total), logs)
        attended[:, at : at + 128] = as_low(jnp.where(lanes < 64, mixed[0], mixed[1]))
    lse[...] = logs
    x3[...] = x2[...] + dot(attended[...], output_w[...]) + vec[13:14]
    for row in spans(SEQ, STEP):
        normed, _ = normalize(x3[row])
        a5[row] = as_low(normed * vec[6:7] + vec[7:8])


def feed_piece(a5, top, expand, shrink, vectors, hidden, slope, d_expand):
    local = expand.shape[1]
    for col in spans(local, 256):
        pre = dot(a5[...], expand[:, col])
        pre = pre + rows_of(vectors, col.start // 256, slice(0, 256))[1:2]
        sigma = sigmoid(pre)
        hidden[:, col] = as_low(pre * sigma)
        slope[:, col] = sigma * (1.0 + pre * (1.0 - sigma))
    part = dot(hidden[...], shrink[...])
    for row in spans(local, 256):
        d_expand[:, row] = as_low(dot_right(top[...], shrink[row]) * slope[:, row])
    return part


def feed_grads(core, a5, top, hidden, d_expand, keep, send, first):
    local = hidden.shape[1]
    half, rows = a5.shape[1] // 2, local // 2
    for side, out in ((1 - core, send), (core, keep)):
        put(out, first, 2, 0, dot_left(hidden[:, at_lane(side * rows, rows)], top[...]))
        grad = dot_left(a5[:, at_lane(side * half, half)], d_expand[...])
        put(out, first, 2, a5.shape[1] * local // 1024, grad)


def feed_own_kernel(
    info, a5, top, expand, shrink, own, keep, send, shrunk, d_a5, grad_bias, hidden, slope, d_expand
):
    shrunk[...] = feed_piece(a5, top, expand, shrink, (own, 0), hidden, slope, d_expand)
    feed_grads(info[0], a5, top, hidden, d_expand, keep, send, 0)
    grad_bias[...] = jnp.broadcast_to(low_columns_sum(d_expand[...]), grad_bias.shape)
    d_a5[...] = dot_right(d_expand[...], expand[...])


def feed_kernel(pieces, per, refs):
    info, refs = refs[0], refs[1:]
    (a5, x3, top, vec, keep_own, send_own, shrunk_own, d_a5_own, bias_own), first, packed, outs, scratch = unpack(
        refs, [9, per * (pieces - 1), per * (pieces - 1), 6, 7]
    )
    output, keep, send, dx3, fixed, grad_bias = outs
    hidden, slope, d_expand, shrunk, d_a5, expand, shrink = scratch
    local, width = shrink.shape
    wide = vectors_of(None, first, per, width * local // (256 * per) + local // per)
    keep[0:2] = keep_own[...]
    send[0:2] = send_own[...]
    shrunk[...] = shrunk_own[...]
    d_a5[...] = d_a5_own[...]
    grad_bias[:, 0:local] = bias_own[...]
    for piece in range(1, pieces):
        blocks = packed[(piece - 1) * per : piece * per]
        assemble(info, expand, blocks, 0)
        assemble(info, shrink, blocks, width * local // (256 * per))
        shrunk[...] += feed_piece(
            a5, top, expand, shrink, wide[piece], hidden, slope, d_expand
        )
        feed_grads(info[0], a5, top, hidden, d_expand, keep, send, 2 * piece)
        cols = slice(piece * local, (piece + 1) * local)
        grad_bias[:, cols] = jnp.broadcast_to(low_columns_sum(d_expand[...]), (8, local))
        d_a5[...] += dot_right(d_expand[...], expand[...])
    for row in spans(SEQ, STEP):
        output[row] = as_low(x3[row] + shrunk[row] + vec[14:15])
    fixed[...] = jnp.zeros_like(fixed)
    for row in spans(SEQ, STEP):
        normed, rstd = normalize(x3[row])
        grad = d_a5[row]
        dx3[row] = top[row].astype(F32) + normalize_back(grad, normed, rstd, vec[6:7])
        fixed[6:7] += columns_sum(grad * normed)
        fixed[7:8] += columns_sum(grad)
    fixed[13:14] = low_columns_sum(top[...])


def attention_backward_kernel(
    info, dx3, attended, output_w, qkv, lse, mask, d_out, d_proj, d_att
):
    width = dx3.shape[1]
    d_out[...] = as_low(dx3[...])
    d_att[...] = as_low(dot_right(d_out[...], output_w[...]))
    scale = (width // HEADS) ** (-0.5)
    lanes = lax.broadcasted_iota(jnp.int32, (SEQ, 128), 1)
    valid = jnp.broadcast_to(mask[0:1], (SEQ, SEQ)) > 0.5
    for pair in range(width // 128):
        at = pair * 128
        queries = qkv[:, at : at + 128]
        keys = qkv[:, width + at : width + at + 128]
        vals = qkv[:, 2 * width + at : 2 * width + at + 128]
        grads = d_att[:, at : at + 128]
        parts = []
        for side in range(2):
            head = 2 * pair + side
            mine = (lanes < 64) if side == 0 else (lanes >= 64)
            scores = masked_scores(jnp.where(mine, queries, 0), keys, valid, scale)
            probs = jnp.exp(scores - lse[:, head : head + 1])
            d_vals = dot_left(as_low(probs), grads)
            d_probs = dot_right(jnp.where(mine, grads, 0), vals)
            weighted = jnp.sum(d_probs * probs, -1, keepdims=True)
            d_scores = as_low(probs * (d_probs - weighted))
            parts.append((dot(d_scores, keys) * scale, dot_left(d_scores, queries) * scale, d_vals))
        for kind in range(3):
            here = slice(kind * width + at, kind * width + at + 128)
            d_proj[:, here] = as_low(jnp.where(lanes < 64, parts[0][kind], parts[1][kind]))


def project_backward_kernel(
    info, dx3, attended, a4, d_out, d_proj, project_w, x2, vec, before, send, keep, dx2, d_sep, fixed
):
    width = x2.shape[1]
    half = width // 2
    core = info[0]
    fixed[...] = before[...]
    for side, out in ((1 - core, send), (core, keep)):
        here = at_lane(side * half, half)
        put(out, 0, 4, 0, dot_left(a4[:, here], d_proj[...]))
        put(out, 0, 4, 3 * width * half // 1024, dot_left(attended[:, here], d_out[...]))
    fixed[12:13] = low_columns_sum(d_out[...])
    fixed[10:11] = low_columns_sum(d_proj[:, :width])
    fixed[11:12] = low_columns_sum(d_proj[:, 2 * width :])
    dx2[...] = dot_right(d_proj[...], project_w[...])
    for row in spans(SEQ, STEP):
        normed, rstd = normalize(x2[row])
        grad = dx2[row]
        dx2[row] = dx3[row] + normalize_back(grad, normed, rstd, vec[4:5])
        fixed[4:5] += columns_sum(grad * normed)
        fixed[5:6] += columns_sum(grad)
    channels = d_sep.shape[1]
    d_sep[...] = as_low(dx2[:, :channels])
    fixed[14:15, channels : 2 * channels] = low_columns_sum(d_sep[...])


def inner_backward_kernel(pieces, per, refs):
    info, refs = refs[0], refs[1:]
    (
        (d_sep, depth, normed_ref, slope_ref, rstd_ref, a2, bias_before, point, point_rest),
        (left, left_rest, own, keep_mask),
        packed,
        outs,
        scratch,
    ) = unpack(refs, [9, 4, per * (pieces - 1), 5, 7])
    keep, send, d_a2, d_right, grads = outs
    d_depth, padded, padded_two, d_left, first_ref, second_ref, sums = scratch
    local = left.shape[1]
    inner = local * pieces
    core, offset = info[0], info[1]
    rows = local // 2
    half = a2.shape[1] // 2
    wide = vectors_of(own, packed, per, a2.shape[1] * local // (256 * per) + local // per)
    for piece in range(pieces):
        weights = point if piece == 0 else point_rest.at[piece - 1]
        for row in spans(local, 256):
            back = dot_right(d_sep[...], weights[row])
            index = (piece * local + row.start) // 128
            d_depth[index] = back[:, 0:128]
            d_depth[index + 1] = back[:, 128:256]
    first_ref[...] = jnp.zeros_like(first_ref)
    second_ref[...] = jnp.zeros_like(second_ref)
    for pad in (padded, padded_two):
        pad[0:8] = jnp.zeros((8, 128), F32)
        pad[SEQ + 8 : SEQ + 16] = jnp.zeros((8, 128), F32)
    grads[...] = jnp.zeros_like(grads)
    grads[1:2] = bias_before[0:1]
    kept = keep_mask[:, 0:1]
    for piece in range(pieces):

        def one(pair, part, pad):
            here = at_lane(piece * local + pair * 256 + part, 128)
            index = piece * (local // 128) + 2 * pair + part // 128
            vectors = rows_of(wide[piece], pair, slice(part, part + 128))
            normed = normed_ref[:, here].astype(F32)
            normal = (normed * vectors[2:3] + vectors[3:4]) * kept
            pad[8 : SEQ + 8] = d_depth[index]
            result = pad[12 : SEQ + 12] * vectors[4:5]
            sums[2, :, here] = eighths_sum(normal * pad[12 : SEQ + 12])
            for tap in range(1, 9):
                shifted = pad[12 - tap : SEQ + 12 - tap]
                result = result + shifted * vectors[4 + tap : 5 + tap]
                sums[2 + tap, :, here] = eighths_sum(normal * shifted)
            result = result * kept
            sums[0, :, here] = eighths_sum(result * normed)
            sums[1, :, here] = eighths_sum(result)
            scaled = result * vectors[2:3]
            first_ref[...] += scaled
            second_ref[...] += scaled * normed
            d_depth[index] = scaled

        def step(index, carry):
            one(index, 0, padded)
            one(index, 128, padded_two)
            return carry

        lax.fori_loop(0, local // 256, step, 0)
    for col in spans(inner, 512):
        grads[2:13, col] = jnp.sum(sums[:, :, col], 1)
    first_ref[...] = jnp.broadcast_to(
        jnp.sum(first_ref[...], 1, keepdims=True) * (1.0 / inner), first_ref.shape
    )
    second_ref[...] = jnp.broadcast_to(
        jnp.sum(second_ref[...], 1, keepdims=True) * (1.0 / inner), second_ref.shape
    )

    def back(index, carry):
        here = at_lane(index * 128, 128)
        normed = normed_ref[:, here].astype(F32)
        d_mixed = rstd_ref[...] * (
            d_depth[index] - first_ref[...] - normed * second_ref[...]
        )
        d_depth[index] = d_mixed
        d_left[:, here] = as_low(d_mixed * slope_ref[:, here].astype(F32))
        return carry

    lax.fori_loop(0, inner // 128, back, 0)
    for part in range(d_right.shape[1] // 128):
        d_right[:, part * 128 : (part + 1) * 128] = d_depth[offset // 128 + part]
    for piece in range(pieces):
        base = piece * local
        cols = slice(base, base + local)
        for side, out in ((1 - core, send), (core, keep)):
            grad = dot_left(a2[:, at_lane(side * half, half)], d_left[:, cols])
            put(out, 2 * piece, 2, 0, grad)
            grad = dot_left(depth[:, at_lane(base + side * rows, rows)], d_sep[...])
            put(out, 2 * piece, 2, half * local // 512, grad)
        grads[0:1, cols] = low_columns_sum(d_left[:, cols])
        if piece == 0:
            d_a2[...] = dot_right(d_left[:, cols], left[...])
        else:
            d_a2[...] += dot_right(d_left[:, cols], left_rest[piece - 1])


def last_kernel(
    info, d_a2_left, d_right, right_pre, conv_w, a2, x1, dx2, values, gates, a1, gated_w, x_ref, vec, kept, before, wide_sums,
    send, keep, input_grad, fixed, shifted, d_a2, d_gated, rows_ref
):
    width = x1.shape[1]
    half = width // 2
    channels = right_pre.shape[1]
    core = info[0]
    fixed[...] = before[...]
    pre = right_pre[...]
    sigma = sigmoid(pre)
    low = as_low(d_right[...] * (sigma * (1.0 + pre * (1.0 - sigma))))
    fixed[14:15, 0:channels] = low_columns_sum(low)
    wide = low.astype(F32)
    rows = lax.broadcasted_iota(jnp.int32, wide.shape, 0)
    shifted[:, 0:channels] = as_low(
        jnp.where(rows == SEQ - 1, 0.0, pltpu.roll(wide, SEQ - 1, 0))
    )
    shifted[:, channels : 2 * channels] = low
    shifted[:, 2 * channels :] = as_low(jnp.where(rows == 0, 0.0, pltpu.roll(wide, 1, 0)))
    total = d_a2_left[...]
    for tap in range(3):
        total = total + dot_right(shifted[:, tap * channels : (tap + 1) * channels], conv_w[tap])
    d_a2[...] = total
    for row in spans(SEQ, STEP):
        normed, rstd = normalize(x1[row])
        grad = d_a2[row] * kept[row, 0:1]
        fixed[2:3] += columns_sum(grad * normed)
        fixed[3:4] += columns_sum(grad)
        dx1 = dx2[row] + normalize_back(grad, normed, rstd, vec[2:3])
        input_grad[row] = dx1
        gate = gates[row]
        scaled = dx1 * gate
        d_gated[row, 0:width] = as_low(scaled)
        d_gated[row, width:] = as_low(scaled * values[row] * (1.0 - gate))
    for side, out in ((1 - core, send), (core, keep)):
        here = at_lane(side * half, half)
        put(out, 0, 4, 0, dot_left(a1[:, here], d_gated[...]))
        put(out, 0, 4, half * width // 512, dot_left(a2[:, here], shifted[...]))
    sums = low_columns_sum(d_gated[...])
    fixed[8:9] = sums[:, 0:width]
    fixed[9:10] = sums[:, width:]
    d_a2[...] = dot_right(d_gated[...], gated_w[...])
    for row in spans(SEQ, STEP):
        normed, rstd = normalize(x_ref[row].astype(F32))
        grad = d_a2[row]
        fixed[0:1] += columns_sum(grad * normed)
        fixed[1:2] += columns_sum(grad)
        input_grad[row] += normalize_back(grad, normed, rstd, vec[0:1])
    pack_small(info, wide_sums, fixed, send, keep, rows_ref)


def pack_small(info, wide, fixed, send, keep, rows_ref):
    if rows_ref is None:
        return
    pieces = lax.axis_size("mp")
    local = wide.shape[1] // pieces
    parts = local // 256
    rows_ref[...] = jnp.zeros_like(rows_ref)
    for piece in range(pieces):
        owner = jnp.bitwise_xor(info[1] // local, piece)
        for part in range(parts):
            spot = pl.multiple_of((owner * parts + part) * 16, 16)
            at = piece * local + part * 256
            rows_ref[pl.ds(spot, 16)] = wide[:, at : at + 256]
    base = wide.shape[1] // 16
    for part in range(fixed.shape[1] // 256):
        rows_ref[base + part * 16 : base + (part + 1) * 16] = fixed[:, part * 256 : (part + 1) * 256]
    count = rows_ref.shape[0] // 2
    offset = send.shape[1] - count // 4
    for side, out in ((1 - info[0], send), (info[0], keep)):
        put(out, 0, 4, offset, rows_ref[pl.ds(pl.multiple_of(side * count, 16), count)])


def own_place(count):
    core = lax.axis_index("dp") % 2
    if count == 2:
        return core
    y = lax.axis_index("dp") // 2 % 2
    near = lax.axis_index("dp") // 4 % 2
    return 2 * core + (1 - core) * y + core * near


def cut(weights, vectors, per, link):
    shapes = [(item.shape[0] // per, item.shape[1]) for item in weights]
    total = sum(rows * columns // 256 for rows, columns in shapes)
    local = weights[0].shape[1]
    small = local // 16 if vectors else 0
    chained = [] if link is None else [link]

    def kernel(*refs):
        refs = list(refs)
        sources = [refs.pop(0) for _ in weights]
        small_in = [refs.pop(0) for _ in vectors]
        for _ in chained:
            refs.pop(0)
        packed = refs.pop(0)
        own = refs.pop(0) if vectors else None
        sems, held = refs
        place = own_place(per)
        copies = []
        offset = 0
        for source, (rows, columns) in zip(sources, shapes):
            here = pl.ds(pl.multiple_of(place * rows, 16), rows)
            for part in range(columns // 256):
                copy = pltpu.make_async_copy(
                    source.at[here, pl.ds(part * 256, 256)],
                    packed.at[pl.ds(offset, rows)],
                    sems.at[len(copies)],
                )
                copy.start()
                copies.append(copy)
                offset += rows
        if vectors:
            held[...] = jnp.zeros_like(held)
            for part in range(local // 256):
                lanes = slice(part * 256, (part + 1) * 256)
                row = 0
                for item in small_in:
                    count = item.shape[0] if len(item.shape) == 2 else 1
                    held[row : row + count] = item[..., lanes].astype(F32).reshape(count, 256)
                    row += count
                chunk = as_low(held[...])
                own[part * 16 : (part + 1) * 16] = chunk
                packed[total + part * 16 : total + (part + 1) * 16] = chunk
        for copy in copies:
            copy.wait()

    outs = [shaped((total + small, 256), LOW)]
    if vectors:
        outs.append(shaped((small, 256), LOW))
    return pl.pallas_call(
        kernel,
        out_shape=outs,
        in_specs=[pl.BlockSpec(memory_space=pl.ANY) for _ in weights]
        + [pl.BlockSpec(memory_space=pltpu.VMEM) for _ in vectors]
        + [pl.BlockSpec(memory_space=pl.ANY) for _ in chained],
        out_specs=[pl.BlockSpec(memory_space=pltpu.VMEM) for _ in outs],
        scratch_shapes=[
            pltpu.SemaphoreType.DMA((sum(columns // 256 for _, columns in shapes),)),
            pltpu.VMEM((16, 256), F32),
        ],
    )(*weights, *vectors, *chained)


def flat_swap(values, partner):
    count = lax.axis_size("dp") * lax.axis_size("mp")
    return lax.ppermute(values, ("dp", "mp"), [(at, partner(at)) for at in range(count)])


PARTNERS = {
    "core": lambda at: at ^ 2,
    "first": lambda at: at ^ (4 if at & 2 else 1),
    "second": lambda at: at ^ (1 if at & 2 else 4),
    "x": lambda at: at ^ 1,
    "y": lambda at: at ^ 4,
    "near": lambda at: at ^ 8,
    "far": lambda at: at ^ 16,
    "hop": lambda at: at ^ (8 if at & 2 else 4),
}
INNER_STEPS = [
    ("quarter", "first"),
    ("half_mix", "second"),
    ("half_near", "near"),
    ("sum", "far"),
    ("sum", "near"),
    ("join_near", "y"),
    ("join_y", "core"),
    ("final", None),
]
SHARED_STEPS = [
    ("quarter", "first"),
    ("half_mix", "second"),
    ("half_near", "near"),
    ("sum", "far"),
    ("sum", "near"),
    ("join_near", "second"),
    ("join_mix", "first"),
    ("spread", "core"),
    ("final", None),
]


PLAN = (
    "p",
    "a",
    "d",
    "p",
    "a",
    "d",
    "c",
    "d",
    "p",
    "a",
    "c",
    "d",
    "ac",
    "d",
    "p",
    "c",
    "d",
    "p",
    "d",
    "c",
    "p",
    "a",
    "d",
    "c",
    "!d",
    "p",
    "!a",
    "!p",
    "c",
    "!c",
)


class Stream:
    def __init__(self, inner, mine, other, parts):
        self.inner = inner
        self.mine = mine
        self.flight = flat_swap(other, PARTNERS["core"])
        self.steps = list(INNER_STEPS if inner else SHARED_STEPS)
        self.parts = parts


def advance_kernel(jobs, refs):
    info, refs = refs[0], refs[1:]
    core, y, near = info[0], info[4], info[5]
    ins, outs = list(refs[: 2 * len(jobs)]), list(refs[2 * len(jobs) :])
    for inner, step, parts in jobs:
        mine, flight = ins.pop(0), ins.pop(0)
        x = 0 if inner else info[3]
        mix = core * x + (1 - core) * y

        def added(spot):
            return as_low(mine[spot].astype(F32) + flight[spot].astype(F32))

        if step == "quarter":
            keep, send = outs.pop(0), outs.pop(0)
            for at in range(2):
                send[at] = added(core * (2 * at + 1 - y) + (1 - core) * (2 * (1 - x) + at))
                keep[at] = added(core * (2 * at + y) + (1 - core) * (2 * x + at))
        elif step == "half_mix":
            keep, send = outs.pop(0), outs.pop(0)
            send[0] = added(1 - mix)
            keep[0] = added(mix)
        elif step == "half_near":
            keep, send = outs.pop(0), outs.pop(0)
            rows = keep.shape[1]
            for out, side in ((send, 1 - near), (keep, near)):
                here = pl.ds(pl.multiple_of(side * rows, 16), rows)
                out[0] = as_low(mine[0, here].astype(F32) + flight[0, here].astype(F32))
        elif step == "sum":
            outs.pop(0)[0] = added(0)
        elif step == "join_near":
            out = outs.pop(0)
            rows = mine.shape[1]
            out[0, pl.ds(pl.multiple_of(near * rows, 16), rows)] = mine[0]
            out[0, pl.ds(pl.multiple_of((1 - near) * rows, 16), rows)] = flight[0]
        elif step in ("join_y", "join_mix"):
            out = outs.pop(0)
            side = y if step == "join_y" else mix
            out[side] = mine[0]
            out[1 - side] = flight[0]
        elif step == "spread":
            out = outs.pop(0)
            for at in range(2):
                out[core * (2 * at + y) + (1 - core) * (2 * x + at)] = mine[at]
                out[core * (2 * at + 1 - y) + (1 - core) * (2 * (1 - x) + at)] = flight[at]


def finish_kernel(parts, small, refs):
    info, mine, flight, refs = refs[0], refs[1], refs[2], list(refs[3:])
    core = info[0]
    outs = [refs.pop(0) for _ in parts]
    smalls = [refs.pop(0) for _ in range(11)] if small else []
    link = refs.pop(0)
    link[...] = jnp.zeros_like(link)
    held = [refs.pop(0) for _ in parts]
    sems = refs.pop(0)
    copies = []
    quarters = mine.shape[0]
    for at, (offset, rows, shape) in enumerate(parts):
        target, columns, deep = held[at], shape[-1] // 256, len(shape) == 3
        for half, (source, side) in enumerate(((mine, core), (flight, 1 - core))):
            for quarter in range(quarters):
                here = slice(quarter * rows, (quarter + 1) * rows)
                for part in range(columns * (shape[0] if deep else 1)):
                    row = offset + part * rows
                    block = source[quarter, row : row + rows].astype(F32)
                    if deep:
                        target[half, part, here] = block
                    else:
                        target[half, here, part * 256 : (part + 1) * 256] = block
            spot = pl.ds(pl.multiple_of(side * quarters * rows, 16), quarters * rows)
            spot = (slice(None), spot) if deep else (spot,)
            copies.append(
                pltpu.make_async_copy(target.at[half], outs[at].at[spot], sems.at[len(copies)])
            )
            copies[-1].start()
    if small:
        total = refs.pop(0)
        offset, rows = small
        for source, side in ((mine, core), (flight, 1 - core)):
            for quarter in range(mine.shape[0]):
                spot = (side * mine.shape[0] + quarter) * rows
                total[pl.ds(pl.multiple_of(spot, 16), rows)] = source[
                    quarter, offset : offset + rows
                ].astype(F32)
        norm, gated, left, conv, inner, depth, point, project, output, expand, shrink = smalls
        local, width = left.shape[-1], output.shape[-1]
        for part in range(local // 256):
            lanes = slice(part * 256, (part + 1) * 256)
            spot = (info[1] // local * (local // 256) + part) * 16
            block = total[pl.ds(pl.multiple_of(spot, 16), 16)]
            left[:, lanes] = block[0:1]
            expand[:, lanes] = block[1:2]
            inner[:, lanes] = block[2:4]
            depth[:, lanes] = block[4:13]
        for part in range(width // 256):
            lanes = slice(part * 256, (part + 1) * 256)
            base = local * 2 // 16 + part * 16
            block = total[base : base + 16]
            for at in range(4):
                norm[at, :, lanes] = block[2 * at : 2 * at + 2]
            gated[:, lanes] = block[8:9]
            gated[:, width + part * 256 : width + (part + 1) * 256] = block[9:10]
            project[:, lanes] = block[10:12]
            output[:, lanes] = block[12:13]
            shrink[:, lanes] = block[13:14]
            (conv if part == 0 else point)[...] = block[14:15]
    for copy in copies:
        copy.wait()


def finish(chain, stream, small):
    parts = stream.parts
    shapes = [shaped(shape, F32) for _, _, shape in parts]
    scratch = [
        pltpu.VMEM((2,) + shape[:-2] + (shape[-2] // 2, shape[-1]), F32) for _, _, shape in parts
    ]
    scratch.append(pltpu.SemaphoreType.DMA((2 * len(parts),)))
    names = []
    if small:
        scratch.append(pltpu.VMEM((256, 256), F32))
        names = [shaped(shape, F32) for shape in small[1]]
    stream.mine = chain.run(
        lambda *refs: finish_kernel(parts, small[0] if small else None, refs),
        shapes + names + [shaped((8, 128), F32)],
        [stream.mine, stream.flight],
        scratch,
        ADV,
        len(parts),
    )


def advance(chain, streams):
    jobs, ins, outs = [], [], []
    for stream in streams:
        step = stream.steps[0][0]
        jobs.append((stream.inner, step, stream.parts))
        ins += [stream.mine, stream.flight]
        lead, rows, columns = stream.mine.shape
        if step in ("quarter", "half_mix"):
            outs += [shaped((lead // 2, rows, columns), LOW)] * 2
        elif step == "half_near":
            outs += [shaped((lead, rows // 2, columns), LOW)] * 2
        elif step == "sum":
            outs.append(shaped((lead, rows, columns), LOW))
        elif step == "join_near":
            outs.append(shaped((lead, rows * 2, columns), LOW))
        else:
            outs.append(shaped((lead * 2, rows, columns), LOW))
    results = list(chain.run(lambda *refs: advance_kernel(jobs, refs), outs, ins, [], ADV))
    for stream in streams:
        step, partner = stream.steps.pop(0)
        stream.mine = results.pop(0)
        if step in ("quarter", "half_mix", "half_near"):
            stream.flight = flat_swap(results.pop(0), PARTNERS[partner])
        else:
            stream.flight = flat_swap(stream.mine, PARTNERS[partner])


def opened(packed, first, count, offset, rows, columns):
    parts = [
        packed[first : first + count, offset + at * rows : offset + (at + 1) * rows]
        for at in range(columns // 256)
    ]
    return jnp.concatenate(parts, 2).reshape(count * rows, columns)


class Weights:
    def __init__(self, packed, per):
        pieces = [packed]
        for bit in bits_of("mp"):
            pieces = pieces + [swap(item, "mp", bit) for item in pieces]
        self.blocks = [[item] for item in pieces[1:]]
        self.per = per

    def hop(self, after):
        if self.per == 4:
            for blocks in self.blocks:
                blocks[0], _ = lax.optimization_barrier((blocks[0], after))
                blocks.append(flat_swap(blocks[0], PARTNERS["hop"]))

    def share(self, after):
        found = []
        for blocks in self.blocks:
            held = [lax.optimization_barrier((item, after))[0] for item in blocks]
            found += held + [swap(item, "dp", 1) for item in held]
        return found


def finish_shared(mine, other, order):
    own = bit_of("dp", 1)
    values = add_low(mine, swap(other, "dp", 1))
    held = [("dp", 1, own)]
    for axis, bit in order[:-1]:
        own = bit_of(axis, bit)
        mine, other = split(values, own)
        values = add_low(mine, swap(other, axis, bit))
        held.append((axis, bit, own))
    axis, bit = order[-1]
    values = add_low(values, swap(values, axis, bit))
    for axis, bit, own in reversed(held):
        values = join(values, swap(values, axis, bit), own)
    return values.astype(F32)


def finish_inner(mine, other, order):
    values = add_low(mine, swap(other, "dp", 1))
    pieces = [values[at] for at in range(values.shape[0])]
    held = [("dp", 1, bit_of("dp", 1))]
    for axis, bit in order[:-1]:
        if axis == "mp":
            keep_count = len(pieces) // 2
            moved = [swap(item, axis, bit) for item in pieces[keep_count:]]
            pieces = [add_low(one, two) for one, two in zip(pieces[:keep_count], moved)]
            continue
        own = bit_of(axis, bit)
        parts = [split(item, own) for item in pieces]
        pieces = [add_low(mine, swap(other, axis, bit)) for mine, other in parts]
        held.append((axis, bit, own))
    axis, bit = order[-1]
    values = add_low(pieces[0], swap(pieces[0], axis, bit))
    for axis, bit, own in reversed(held):
        values = join(values, swap(values, axis, bit), own)
    return values.astype(F32)


def body(
    cell_input,
    lengths,
    out_grad,
    norm_params,
    gated_weight,
    gated_bias,
    left_weight,
    left_bias,
    conv_weight,
    conv_bias,
    inner_norm,
    depth_weight,
    point_weight,
    point_bias,
    project_weight,
    project_bias,
    output_weight,
    output_bias,
    expand_weight,
    expand_bias,
    shrink_weight,
    shrink_bias,
):
    width = cell_input.shape[1]
    channels = conv_weight.shape[2]
    local = left_weight.shape[1]
    pieces = lax.axis_size("mp")
    inner = local * pieces
    tokens = cell_input.shape[0]
    assert tokens == SEQ
    tuned = lax.axis_size("dp") == 16 and pieces == 2
    mp_bits = bits_of("mp")[::-1]
    dp_bits = bits_of("dp")[1:]
    mp_first = [("mp", bit) for bit in mp_bits] + [("dp", bit) for bit in dp_bits]
    core = bit_of("dp", 1)
    chain = Chain(local)

    def inner_rows(size):
        return (2 * pieces, size // 1024, 256)


    per = 4 if tuned else 2
    vectors = [left_bias, expand_bias, inner_norm, depth_weight]
    packed, own = cut([left_weight, point_weight], vectors, per, None)
    early = Weights(packed, per)
    (packed,) = cut([expand_weight, shrink_weight], [], per, own)
    late = Weights(packed, per)
    chain.link = packed
    a1, values, gates, x1, a2, right_pre, vec, kept, valid, *parts, right = chain.run(
        pre_kernel,
        [
            shaped((tokens, width), LOW),
            shaped((tokens, width), F32),
            shaped((tokens, width), F32),
            shaped((tokens, width), F32),
            shaped((tokens, width), LOW),
            shaped((tokens, channels), F32),
            shaped((16, width), F32),
            shaped((tokens, 128), F32),
            shaped((8, tokens), F32),
            shaped((tokens, local), F32),
            shaped((tokens, local), LOW),
            shaped((tokens, 128), F32),
            shaped((tokens, 128), F32),
            shaped((tokens, channels), LOW),
        ],
        [
            lengths,
            left_weight,
            own,
            cell_input,
            gated_weight,
            conv_weight,
            norm_params,
            gated_bias,
            conv_bias,
            point_bias,
            project_bias,
            output_bias,
            shrink_bias,
        ],
        [],
        int(2.2e9 * EARLY),
    )
    early.hop(right)
    early_blocks = early.share(right)
    normed, slope, depth, rstd, left_rest = chain.run(
        lambda *refs: inner_forward_kernel(pieces, per, refs),
        [
            shaped((tokens, inner), LOW),
            shaped((tokens, inner), LOW),
            shaped((tokens, inner), LOW),
            shaped((tokens, 128), F32),
            shaped((pieces - 1, width, local), LOW),
        ],
        [a2, right, *parts, own, kept] + early_blocks,
        [
            pltpu.VMEM((pieces - 1, tokens, local), F32),
            pltpu.VMEM((tokens, 128), F32),
            pltpu.VMEM((tokens, 128), F32),
            pltpu.VMEM((tokens, 128), F32),
            pltpu.VMEM((tokens + 16, 128), F32),
            pltpu.VMEM((tokens + 16, 128), F32),
        ],
        int(6.5e9 * EARLY),
    )
    late.hop(rstd)
    x2, a4, qkv, lse, attended, x3, a5, point_rest = chain.run(
        lambda *refs: attention_forward_kernel(pieces, per, refs),
        [
            shaped((tokens, width), F32),
            shaped((tokens, width), LOW),
            shaped((tokens, 3 * width), LOW),
            shaped((tokens, 128), F32),
            shaped((tokens, width), LOW),
            shaped((tokens, width), F32),
            shaped((tokens, width), LOW),
            shaped((pieces - 1, local, channels), LOW),
        ],
        [x1, depth, point_weight, vec, project_weight, output_weight, valid]
        + early_blocks,
        [],
        int(4.4e9 * EARLY),
    )
    keep_own, send_own, shrunk_own, d_a5_own, bias_own = chain.run(
        feed_own_kernel,
        [
            shaped((2, 2 * local * width // 1024, 256), LOW),
            shaped((2, 2 * local * width // 1024, 256), LOW),
            shaped((tokens, width), F32),
            shaped((tokens, width), F32),
            shaped((8, local), F32),
        ],
        [a5, out_grad, expand_weight, shrink_weight, own],
        [
            pltpu.VMEM((tokens, local), LOW),
            pltpu.VMEM((tokens, local), F32),
            pltpu.VMEM((tokens, local), LOW),
        ],
        int(3e9 * EARLY),
    )
    late_blocks = late.share(bias_own)
    cell_output, feed_keep, feed_send, dx3, fixed, expand_sum = chain.run(
        lambda *refs: feed_kernel(pieces, per, refs),
        [
            shaped((tokens, width), LOW),
            shaped(inner_rows(2 * local * width), LOW),
            shaped(inner_rows(2 * local * width), LOW),
            shaped((tokens, width), F32),
            shaped((16, width), F32),
            shaped((8, inner), F32),
        ],
        [a5, x3, out_grad, vec, keep_own, send_own, shrunk_own, d_a5_own, bias_own]
        + early_blocks
        + late_blocks,
        [
            pltpu.VMEM((tokens, local), LOW),
            pltpu.VMEM((tokens, local), F32),
            pltpu.VMEM((tokens, local), LOW),
            pltpu.VMEM((tokens, width), F32),
            pltpu.VMEM((tokens, width), F32),
            pltpu.VMEM((width, local), LOW),
            pltpu.VMEM((local, width), LOW),
        ],
        int(8e9 * SCALE),
    )
    if tuned:
        fee = Stream(
            True,
            feed_keep,
            feed_send,
            [
                (0, local // 4, (local, width)),
                (width * local // 1024, width // 4, (width, local)),
            ],
        )
    d_out, d_proj = chain.run(
        attention_backward_kernel,
        [shaped((tokens, width), LOW), shaped((tokens, 3 * width), LOW)],
        [dx3, attended, output_weight, qkv, lse, valid],
        [pltpu.VMEM((tokens, width), LOW)],
        int(5e9 * SCALE),
    )
    if tuned:
        advance(chain, [fee])
    proj_send, proj_keep, dx2, d_sep, fixed = chain.run(
        project_backward_kernel,
        [
            shaped((4, width * width // 512, 256), LOW),
            shaped((4, width * width // 512, 256), LOW),
            shaped((tokens, width), F32),
            shaped((tokens, channels), LOW),
            shaped((16, width), F32),
        ],
        [dx3, attended, a4, d_out, d_proj, project_weight, x2, vec, fixed],
        [],
        int(3e9 * SCALE),
    )
    if tuned:
        pro = Stream(
            False,
            proj_keep,
            proj_send,
            [
                (0, width // 8, (width, 3 * width)),
                (3 * width * width // 2048, width // 8, (width, width)),
            ],
        )
        advance(chain, [pro])
    left_keep, left_send, d_a2, d_right, wide_sums = chain.run(
        lambda *refs: inner_backward_kernel(pieces, per, refs),
        [
            shaped(inner_rows(local * (width + channels)), LOW),
            shaped(inner_rows(local * (width + channels)), LOW),
            shaped((tokens, width), F32),
            shaped((tokens, channels), F32),
            shaped((16, inner), F32),
        ],
        [
            d_sep,
            depth,
            normed,
            slope,
            rstd,
            a2,
            expand_sum,
            point_weight,
            point_rest,
            left_weight,
            left_rest,
            own,
            kept,
        ]
        + early_blocks,
        [
            pltpu.VMEM((inner // 128, tokens, 128), F32),
            pltpu.VMEM((tokens + 16, 128), F32),
            pltpu.VMEM((tokens + 16, 128), F32),
            pltpu.VMEM((tokens, inner), LOW),
            pltpu.VMEM((tokens, 128), F32),
            pltpu.VMEM((tokens, 128), F32),
            pltpu.VMEM((11, 8, inner), F32),
        ],
        int(11.5e9 * SCALE),
    )
    if tuned:
        lef = Stream(
            True,
            left_keep,
            left_send,
            [
                (0, width // 4, (width, local)),
                (width * local // 1024, local // 4, (local, channels)),
            ],
        )
        advance(chain, [fee])
    small = 32 if tuned else 0
    last_rows = width * (2 * width + 3 * channels) // 2048 + small
    last_send, last_keep, input_grad, fixed = chain.run(
        last_kernel if tuned else lambda *refs: last_kernel(*refs, None),
        [
            shaped((4, last_rows, 256), LOW),
            shaped((4, last_rows, 256), LOW),
            shaped((tokens, width), F32),
            shaped((16, width), F32),
        ],
        [
            d_a2,
            d_right,
            right_pre,
            conv_weight,
            a2,
            x1,
            dx2,
            values,
            gates,
            a1,
            gated_weight,
            cell_input,
            vec,
            kept,
            fixed,
            wide_sums,
        ],
        [
            pltpu.VMEM((tokens, 3 * channels), LOW),
            pltpu.VMEM((tokens, width), F32),
            pltpu.VMEM((tokens, 2 * width), LOW),
        ]
        + ([pltpu.VMEM((8 * small, 256), F32)] if tuned else []),
        int(4.0e9 * SCALE),
    )
    if tuned:
        lat = Stream(
            False,
            last_keep,
            last_send,
            [
                (0, width // 8, (width, 2 * width)),
                (width * width // 1024, width // 8, (3, width, channels)),
            ],
        )
        groups = {"a": [fee], "p": [pro], "c": [lef], "d": [lat]}
        small_shapes = [
            (4, 2, width),
            (1, 2 * width),
            (1, local),
            (1, channels),
            (2, local),
            (9, local),
            (1, channels),
            (2, width),
            (1, width),
            (1, local),
            (1, width),
        ]
        small_part = ((last_rows - small, small), small_shapes)
        for names in PLAN:
            if names[0] == "!":
                stream = groups[names[1]][0]
                finish(chain, stream, small_part if names == "!d" else None)
            else:
                advance(chain, [groups[name][0] for name in names])
        (grad_shrink, grad_expand, _), (grad_left, grad_point, _) = fee.mine, lef.mine
        (grad_proj, grad_out, _), (grad_gated, grad_conv) = pro.mine, lat.mine[:2]
        smalls = [
            item.reshape(-1) if item.shape[0] == 1 else item for item in lat.mine[2:-1]
        ]
    else:

        def whole(keep, send, offset, rows, columns):
            both = [
                jnp.stack([opened(item, 2 * at, 2, offset, rows, columns) for at in range(pieces)])
                for item in (keep, send)
            ]
            return finish_inner(both[0], both[1], mp_first)

        def shared(keep, send, offset, rows, columns):
            both = [opened(item, 0, 4, offset, rows, columns) for item in (keep, send)]
            return finish_shared(both[0], both[1], mp_first)

        eighth = width // 8
        grad_shrink = whole(feed_keep, feed_send, 0, local // 4, width)
        grad_expand = whole(
            feed_keep, feed_send, width * local // 1024, width // 4, local
        )
        grad_left = whole(left_keep, left_send, 0, width // 4, local)
        grad_point = whole(left_keep, left_send, width * local // 1024, local // 4, channels)
        grad_proj = shared(proj_keep, proj_send, 0, eighth, 3 * width)
        grad_out = shared(proj_keep, proj_send, 6 * eighth, eighth, width)
        grad_gated = shared(last_keep, last_send, 0, eighth, 2 * width)
        grad_conv = jnp.stack(
            [shared(last_keep, last_send, (4 + at) * eighth, eighth, channels) for at in range(3)]
        )
        chunks = [wide_sums[:, at : at + local] for at in range(0, inner, local)]
        for bit in mp_bits:
            count = len(chunks) // 2
            moved = [swap(item, "mp", bit) for item in chunks[count:]]
            chunks = [one + two for one, two in zip(chunks[:count], moved)]
            fixed = fixed + swap(fixed, "mp", bit)
        wide_total = chunks[0]
        for bit in bits_of("dp"):
            fixed = fixed + swap(fixed, "dp", bit)
            wide_total = wide_total + swap(wide_total, "dp", bit)
        smalls = [
            fixed[0:8].reshape(4, 2, width),
            fixed[8:10].reshape(2 * width),
            wide_total[0],
            fixed[14, :channels],
            wide_total[2:4],
            wide_total[4:13],
            fixed[14, channels:],
            fixed[10:12],
            fixed[12],
            wide_total[1],
            fixed[13],
        ]
    return (
        cell_output,
        input_grad,
        smalls[0],
        grad_gated,
        smalls[1],
        grad_left,
        smalls[2],
        grad_conv,
        smalls[3],
        smalls[4],
        smalls[5],
        grad_point,
        smalls[6],
        grad_proj,
        smalls[7],
        grad_out,
        smalls[8],
        grad_expand,
        smalls[9],
        grad_shrink,
        smalls[10],
    )


def solution(mesh):
    return jax.shard_map(
        body,
        mesh=mesh,
        in_specs=(
            P(("dp", "mp"), None),
            P(("dp", "mp")),
            P(("dp", "mp"), None),
            P(),
            P(),
            P(),
            P(None, "mp"),
            P("mp"),
            P(),
            P(),
            P(None, "mp"),
            P(None, "mp"),
            P("mp", None),
            P(),
            P(),
            P(),
            P(),
            P(),
            P(None, "mp"),
            P("mp"),
            P("mp", None),
            P(),
        ),
        out_specs=(
            P(("dp", "mp"), None),
            P(("dp", "mp"), None),
            P(),
            P(),
            P(),
            P(None, "mp"),
            P("mp"),
            P(),
            P(),
            P(None, "mp"),
            P(None, "mp"),
            P("mp", None),
            P(),
            P(),
            P(),
            P(),
            P(),
            P(None, "mp"),
            P("mp"),
            P("mp", None),
            P(),
        ),
        check_vma=False,
    )
```

```python
import jax
import jax.numpy as jnp
from jax import lax
from jax.experimental import pallas as pl
from jax.experimental.pallas import tpu as pltpu
from jax.sharding import PartitionSpec as P

HEADS = 8
SEQ = 256
EPS = 1e-06
NEGATIVE = -1000000000.0
LOW = jnp.bfloat16
F32 = jnp.float32
STEP = 64
LIMIT = 24 * 2**20
SCALE = 4
EARLY = 0.001
ADV = 20 * 10**9


def as_low(values):
    return values.astype(LOW)


def dot(left, right):
    return jnp.dot(left, right, preferred_element_type=F32)


def dot_left(left, right):
    return lax.dot_general(left, right, (((0,), (0,)), ((), ())), preferred_element_type=F32)


def dot_right(left, right):
    return lax.dot_general(left, right, (((1,), (1,)), ((), ())), preferred_element_type=F32)


def swap(values, axis, bit):
    count = lax.axis_size(axis)
    return lax.ppermute(values, axis, [(at, at ^ bit) for at in range(count)])


def bit_of(axis, bit):
    return (lax.axis_index(axis) // bit) % 2


def bits_of(axis):
    bits, bit = [], 1
    while bit < lax.axis_size(axis):
        bits.append(bit)
        bit *= 2
    return bits


def add_low(first, second):
    return as_low(first.astype(F32) + second.astype(F32))


def split(values, own):
    half = values.shape[0] // 2
    mine = lax.dynamic_slice_in_dim(values, own * half, half, 0)
    other = lax.dynamic_slice_in_dim(values, (1 - own) * half, half, 0)
    return mine, other


def join(mine, other, own):
    swapped = own == 1
    return jnp.concatenate(
        [jnp.where(swapped, other, mine), jnp.where(swapped, mine, other)], 0
    )


def sum_shared(values, order):
    held = []
    steps = [("dp", 1)] + order
    for axis, bit in steps[:-1]:
        own = bit_of(axis, bit)
        mine, other = split(values, own)
        values = add_low(mine, swap(other, axis, bit))
        held.append((axis, bit, own))
    axis, bit = steps[-1]
    values = add_low(values, swap(values, axis, bit))
    for axis, bit, own in reversed(held):
        values = join(values, swap(values, axis, bit), own)
    return values.astype(F32)


def sum_inner(pieces, order):
    held = []
    steps = [("dp", 1)] + order
    for axis, bit in steps[:-1]:
        if axis == "mp":
            keep_count = len(pieces) // 2
            moved = [swap(item, axis, bit) for item in pieces[keep_count:]]
            pieces = [add_low(one, two) for one, two in zip(pieces[:keep_count], moved)]
            continue
        own = bit_of(axis, bit)
        parts = [split(item, own) for item in pieces]
        pieces = [add_low(mine, swap(other, axis, bit)) for mine, other in parts]
        held.append((axis, bit, own))
    axis, bit = steps[-1]
    values = add_low(pieces[0], swap(pieces[0], axis, bit))
    for axis, bit, own in reversed(held):
        values = join(values, swap(values, axis, bit), own)
    return values.astype(F32)


def sigmoid(values):
    return 0.5 * jnp.tanh(0.5 * values) + 0.5


def spans(total, step):
    return [slice(at, at + step) for at in range(0, total, step)]


def at_lane(start, size):
    return pl.ds(pl.multiple_of(start, 128), size)


def normalize(values):
    width = values.shape[1]
    centre = jnp.sum(values, -1, keepdims=True) * (1.0 / width)
    centered = values - centre
    variance = jnp.sum(centered * centered, -1, keepdims=True) * (1.0 / width)
    rstd = lax.rsqrt(variance + EPS)
    return centered * rstd, rstd


def normalize_back(grad, normed, rstd, gain):
    width = grad.shape[1]
    scaled = grad * gain
    first = jnp.sum(scaled, -1, keepdims=True) * (1.0 / width)
    second = jnp.sum(scaled * normed, -1, keepdims=True) * (1.0 / width)
    return rstd * (scaled - first - normed * second)


def columns_sum(values):
    return jnp.sum(values, 0, keepdims=True)


def eighths_sum(values):
    return jnp.sum(values.reshape(-1, 8, values.shape[1]), 0)


def low_columns_sum(values):
    ones = jnp.ones((16, values.shape[0]), LOW)
    return dot(ones, values)[0:1]


def place(local):
    dp, mp = lax.axis_index("dp"), lax.axis_index("mp")
    return dp % 2, mp * local, None, mp % 2, dp // 2 % 2, dp // 4 % 2


class Chain:
    def __init__(self, local):
        self.link = None
        self.local = local

    def run(self, kernel, outs, ins, scratch, flops, placed=0):
        ins = list(ins)
        specs = [
            pl.BlockSpec(memory_space=pltpu.SMEM if item.dtype == jnp.int32 else pltpu.VMEM)
            for item in ins
        ]
        count = len(ins)
        moved = sum(item.size * item.dtype.itemsize for item in ins + list(outs))
        linked = self.link is not None
        if linked:
            ins.append(self.link)
            specs.append(pl.BlockSpec(memory_space=pl.ANY))

        def call(*refs):
            kernel(place(self.local), *(refs[:count] + refs[count + 1 :] if linked else refs))

        results = pl.pallas_call(
            call,
            out_shape=outs,
            in_specs=specs,
            out_specs=[
                pl.BlockSpec(memory_space=pltpu.HBM if at < placed else pltpu.VMEM)
                for at in range(len(outs))
            ],
            scratch_shapes=scratch,
            compiler_params=pltpu.CompilerParams(vmem_limit_bytes=LIMIT),
            cost_estimate=pl.CostEstimate(
                flops=flops, bytes_accessed=moved + flops // 50, transcendentals=0
            ),
        )(*ins)
        self.link = min(results, key=lambda item: item.size)
        return results


def put(out, first, count, offset, values):
    rows = values.shape[0] // count
    low = as_low(values)
    for quarter in range(count):
        for part in range(values.shape[1] // 256):
            at = offset + part * rows
            out[first + quarter, at : at + rows] = low[
                quarter * rows : (quarter + 1) * rows, part * 256 : (part + 1) * 256
            ]


def shaped(shape, kind):
    return jax.ShapeDtypeStruct(shape, kind)


def pre_kernel(
    info, lengths, left, own, x_ref, gated_w, conv_w, norms, gated_b, conv_b, point_b, project_b, output_b, shrink_b,
    a1, values, gates, x1, a2, right_pre, vec, kept, valid, mixed, slope, total_ref, square, right
):
    width = x_ref.shape[1]
    channels = right.shape[1]
    length = lengths[0]
    for ref, axis in ((kept, 0), (valid, 1)):
        spots = lax.broadcasted_iota(jnp.int32, ref.shape, axis)
        ref[...] = jnp.where(spots < length, 1.0, 0.0).astype(F32)
    vec[...] = jnp.zeros_like(vec)
    for at in range(4):
        vec[2 * at : 2 * at + 2] = norms[at].astype(F32)
    for row, item in ((8, gated_b.at[0:width]), (9, gated_b.at[width:]), (13, output_b), (14, shrink_b)):
        vec[row : row + 1] = item[...].astype(F32).reshape(1, width)
    vec[10:11, 0:channels] = conv_b[...].astype(F32).reshape(1, channels)
    vec[10:11, channels:] = point_b[...].astype(F32).reshape(1, channels)
    vec[11:13] = project_b[...].astype(F32)
    for row in spans(SEQ, STEP):
        normed, _ = normalize(x_ref[row].astype(F32))
        a1[row] = as_low(normed * vec[0:1] + vec[1:2])
    for col in spans(width, 256):
        gate_col = slice(col.start + width, col.stop + width)
        value = dot(a1[...], gated_w[:, col]) + vec[8:9, col]
        gate = sigmoid(dot(a1[...], gated_w[:, gate_col]) + vec[9:10, col])
        values[:, col] = value
        gates[:, col] = gate
        x1[:, col] = x_ref[:, col].astype(F32) + value * gate
    for row in spans(SEQ, STEP):
        normed, _ = normalize(x1[row])
        a2[row] = as_low((normed * vec[2:3] + vec[3:4]) * kept[row, 0:1])
    rows = lax.broadcasted_iota(jnp.int32, right_pre.shape, 0)
    first = jnp.where(rows == 0, 0.0, pltpu.roll(dot(a2[...], conv_w[0]), 1, 0))
    last = jnp.where(rows == SEQ - 1, 0.0, pltpu.roll(dot(a2[...], conv_w[2]), SEQ - 1, 0))
    total = first + dot(a2[...], conv_w[1]) + last + vec[10:11, 0 : right_pre.shape[1]]
    right_pre[...] = total
    right[...] = as_low(total * sigmoid(total))
    total_ref[...] = jnp.zeros_like(total_ref)
    square[...] = jnp.zeros_like(square)
    right_rows = right[...].astype(F32)
    left_piece(a2, left, (own, 0), right_rows, info[1], 0, mixed, slope, total_ref, square)


def unpack(refs, counts):
    groups, at = [], 0
    for count in counts:
        groups.append(refs[at : at + count])
        at += count
    return groups


def places(info, count):
    core, y, near = info[0], info[4], info[5]
    if count == 2:
        return [core, 1 - core]
    mine = (1 - core) * y + core * near
    theirs = (1 - core) * near + core * y
    return [2 * core + mine, 2 * core + 1 - mine, 2 - 2 * core + theirs, 3 - 2 * core - theirs]


def assemble(info, target, blocks, offset):
    rows = target.shape[0] // len(blocks)
    for spot, block in zip(places(info, len(blocks)), blocks):
        here = pl.ds(pl.multiple_of(spot * rows, 16), rows)
        for part in range(target.shape[1] // 256):
            at = offset + part * rows
            target[here, part * 256 : (part + 1) * 256] = block[at : at + rows]


def vectors_of(own, blocks, per_piece, offset):
    found = [(own, 0)]
    for at in range(0, len(blocks), per_piece):
        found.append((blocks[at], offset))
    return found


def rows_of(vectors, index, lanes):
    ref, offset = vectors
    return ref[pl.ds(pl.multiple_of(offset + index * 16, 16), 16), lanes].astype(F32)


def left_piece(a2, left, vectors, right_rows, offset, base, mixed, slope, total, square):
    local = left.shape[1]
    for col in spans(local, 256):
        pre = dot(a2[...], left[:, col])
        pre = pre + rows_of(vectors, col.start // 256, slice(0, 256))[0:1]
        sigma = sigmoid(pre)
        at = base + col.start
        slope[:, at : at + 256] = as_low(sigma * (1.0 + pre * (1.0 - sigma)))
        value = pre * sigma + right_rows * jnp.where(offset == at, 1.0, 0.0)
        mixed[:, col] = value
        total[...] += value[:, 0:128] + value[:, 128:256]
        squared = value * value
        square[...] += squared[:, 0:128] + squared[:, 128:256]


def inner_forward_kernel(pieces, per, refs):
    info, refs = refs[0], refs[1:]
    (a2, right, mixed_own, slope_own, total_own, square_own, own, keep), packed, outs, scratch = unpack(
        refs, [8, per * (pieces - 1), 5, 6]
    )
    normed_ref, slope_ref, depth, rstd_ref, left_rest = outs
    mixed, total, square, centre_ref, padded, padded_two = scratch
    local = mixed_own.shape[1]
    inner = local * pieces
    skipped = a2.shape[1] * local // (256 * per) + local // per
    wide = vectors_of(own, packed, per, skipped)
    right_rows = right[...].astype(F32)
    total[...] = total_own[...]
    square[...] = square_own[...]
    slope_ref[:, 0:local] = slope_own[...]
    for piece in range(1, pieces):
        rest = left_rest.at[piece - 1]
        assemble(info, rest, packed[(piece - 1) * per : piece * per], 0)
        left_piece(
            a2, rest, wide[piece], right_rows, info[1], piece * local,
            mixed.at[piece - 1], slope_ref, total, square,
        )
    centre = jnp.sum(total[...], 1, keepdims=True) * (1.0 / inner)
    variance = jnp.sum(square[...], 1, keepdims=True) * (1.0 / inner) - centre * centre
    rstd = lax.rsqrt(variance + EPS)
    centre_ref[...] = jnp.broadcast_to(centre, centre_ref.shape)
    rstd_ref[...] = jnp.broadcast_to(rstd, rstd_ref.shape)
    for pad in (padded, padded_two):
        pad[0:8] = jnp.zeros((8, 128), F32)
        pad[SEQ + 8 : SEQ + 16] = jnp.zeros((8, 128), F32)
    kept = keep[:, 0:1]
    for piece in range(pieces):

        def one(index, part, pad):
            here = at_lane(piece * local + index * 256 + part, 128)
            vectors = rows_of(wide[piece], index, slice(part, part + 128))
            source = mixed_own if piece == 0 else mixed.at[piece - 1]
            value = source[:, at_lane(index * 256 + part, 128)]
            normed = (value - centre_ref[...]) * rstd_ref[...]
            normed_ref[:, here] = as_low(normed)
            pad[8 : SEQ + 8] = (normed * vectors[2:3] + vectors[3:4]) * kept
            result = pad[4 : SEQ + 4] * vectors[4:5]
            for tap in range(1, 9):
                result = result + pad[4 + tap : SEQ + 4 + tap] * vectors[4 + tap : 5 + tap]
            depth[:, here] = as_low(result)

        def step(index, carry):
            one(index, 0, padded)
            one(index, 128, padded_two)
            return carry

        lax.fori_loop(0, local // 256, step, 0)


def masked_scores(queries, keys, valid, scale):
    return jnp.where(valid, dot_right(queries, keys) * scale, NEGATIVE)


def attention_forward_kernel(pieces, per, refs):
    (info, x1, depth, point, vec, project_w, output_w, mask), packed, outs = unpack(
        refs, [8, per * (pieces - 1), 8]
    )
    x2, a4, qkv, lse, attended, x3, a5, point_rest = outs
    width = x2.shape[1]
    local, channels = point.shape
    sep = dot(depth[:, 0:local], point[...])
    for piece in range(1, pieces):
        blocks = packed[(piece - 1) * per : piece * per]
        assemble(info, point_rest.at[piece - 1], blocks, width * local // (256 * per))
        sep = sep + dot(depth[:, piece * local : (piece + 1) * local], point_rest[piece - 1])
    x2[:, 0:channels] = x1[:, 0:channels] + sep + vec[10:11, channels : 2 * channels]
    x2[:, channels:width] = x1[:, channels:width]
    for row in spans(SEQ, STEP):
        normed, _ = normalize(x2[row])
        a4[row] = as_low(normed * vec[4:5] + vec[5:6])
    for col in spans(3 * width, 256):
        part = dot(a4[...], project_w[:, col])
        if col.start < width:
            part = part + vec[11:12, col]
        elif col.start >= 2 * width:
            part = part + vec[12:13, col.start - 2 * width : col.stop - 2 * width]
        qkv[:, col] = as_low(part)
    scale = (width // HEADS) ** (-0.5)
    lanes = lax.broadcasted_iota(jnp.int32, (SEQ, 128), 1)
    valid = jnp.broadcast_to(mask[0:1], (SEQ, SEQ)) > 0.5
    logs = jnp.zeros((SEQ, 128), F32)
    for pair in range(width // 128):
        at = pair * 128
        queries = qkv[:, at : at + 128]
        keys = qkv[:, width + at : width + at + 128]
        vals = qkv[:, 2 * width + at : 2 * width + at + 128]
        mixed = []
        for side in range(2):
            mine = (lanes < 64) if side == 0 else (lanes >= 64)
            scores = masked_scores(jnp.where(mine, queries, 0), keys, valid, scale)
            highest = jnp.max(scores, -1, keepdims=True)
            weights = jnp.exp(scores - highest)
            total = jnp.sum(weights, -1, keepdims=True)
            mixed.append(dot(as_low(weights * (1.0 / total)), vals))
            logs = jnp.where(lanes == 2 * pair + side, highest + jnp.log(total), logs)
        attended[:, at : at + 128] = as_low(jnp.where(lanes < 64, mixed[0], mixed[1]))
    lse[...] = logs
    x3[...] = x2[...] + dot(attended[...], output_w[...]) + vec[13:14]
    for row in spans(SEQ, STEP):
        normed, _ = normalize(x3[row])
        a5[row] = as_low(normed * vec[6:7] + vec[7:8])


def feed_piece(a5, top, expand, shrink, vectors, hidden, slope, d_expand):
    local = expand.shape[1]
    for col in spans(local, 256):
        pre = dot(a5[...], expand[:, col])
        pre = pre + rows_of(vectors, col.start // 256, slice(0, 256))[1:2]
        sigma = sigmoid(pre)
        hidden[:, col] = as_low(pre * sigma)
        slope[:, col] = sigma * (1.0 + pre * (1.0 - sigma))
    part = dot(hidden[...], shrink[...])
    for row in spans(local, 256):
        d_expand[:, row] = as_low(dot_right(top[...], shrink[row]) * slope[:, row])
    return part


def feed_grads(core, a5, top, hidden, d_expand, keep, send, first):
    local = hidden.shape[1]
    half, rows = a5.shape[1] // 2, local // 2
    for side, out in ((1 - core, send), (core, keep)):
        put(out, first, 2, 0, dot_left(hidden[:, at_lane(side * rows, rows)], top[...]))
        grad = dot_left(a5[:, at_lane(side * half, half)], d_expand[...])
        put(out, first, 2, a5.shape[1] * local // 1024, grad)


def feed_own_kernel(
    info, a5, top, expand, shrink, own, keep, send, shrunk, d_a5, grad_bias, hidden, slope, d_expand
):
    shrunk[...] = feed_piece(a5, top, expand, shrink, (own, 0), hidden, slope, d_expand)
    feed_grads(info[0], a5, top, hidden, d_expand, keep, send, 0)
    grad_bias[...] = jnp.broadcast_to(low_columns_sum(d_expand[...]), grad_bias.shape)
    d_a5[...] = dot_right(d_expand[...], expand[...])


def feed_kernel(pieces, per, refs):
    info, refs = refs[0], refs[1:]
    (a5, x3, top, vec, keep_own, send_own, shrunk_own, d_a5_own, bias_own), first, packed, outs, scratch = unpack(
        refs, [9, per * (pieces - 1), per * (pieces - 1), 6, 7]
    )
    output, keep, send, dx3, fixed, grad_bias = outs
    hidden, slope, d_expand, shrunk, d_a5, expand, shrink = scratch
    local, width = shrink.shape
    wide = vectors_of(None, first, per, width * local // (256 * per) + local // per)
    keep[0:2] = keep_own[...]
    send[0:2] = send_own[...]
    shrunk[...] = shrunk_own[...]
    d_a5[...] = d_a5_own[...]
    grad_bias[:, 0:local] = bias_own[...]
    for piece in range(1, pieces):
        blocks = packed[(piece - 1) * per : piece * per]
        assemble(info, expand, blocks, 0)
        assemble(info, shrink, blocks, width * local // (256 * per))
        shrunk[...] += feed_piece(
            a5, top, expand, shrink, wide[piece], hidden, slope, d_expand
        )
        feed_grads(info[0], a5, top, hidden, d_expand, keep, send, 2 * piece)
        cols = slice(piece * local, (piece + 1) * local)
        grad_bias[:, cols] = jnp.broadcast_to(low_columns_sum(d_expand[...]), (8, local))
        d_a5[...] += dot_right(d_expand[...], expand[...])
    for row in spans(SEQ, STEP):
        output[row] = as_low(x3[row] + shrunk[row] + vec[14:15])
    fixed[...] = jnp.zeros_like(fixed)
    for row in spans(SEQ, STEP):
        normed, rstd = normalize(x3[row])
        grad = d_a5[row]
        dx3[row] = top[row].astype(F32) + normalize_back(grad, normed, rstd, vec[6:7])
        fixed[6:7] += columns_sum(grad * normed)
        fixed[7:8] += columns_sum(grad)
    fixed[13:14] = low_columns_sum(top[...])


def attention_backward_kernel(
    info, dx3, attended, output_w, qkv, lse, mask, d_out, d_proj, d_att
):
    width = dx3.shape[1]
    d_out[...] = as_low(dx3[...])
    d_att[...] = as_low(dot_right(d_out[...], output_w[...]))
    scale = (width // HEADS) ** (-0.5)
    lanes = lax.broadcasted_iota(jnp.int32, (SEQ, 128), 1)
    valid = jnp.broadcast_to(mask[0:1], (SEQ, SEQ)) > 0.5
    for pair in range(width // 128):
        at = pair * 128
        queries = qkv[:, at : at + 128]
        keys = qkv[:, width + at : width + at + 128]
        vals = qkv[:, 2 * width + at : 2 * width + at + 128]
        grads = d_att[:, at : at + 128]
        parts = []
        for side in range(2):
            head = 2 * pair + side
            mine = (lanes < 64) if side == 0 else (lanes >= 64)
            scores = masked_scores(jnp.where(mine, queries, 0), keys, valid, scale)
            probs = jnp.exp(scores - lse[:, head : head + 1])
            d_vals = dot_left(as_low(probs), grads)
            d_probs = dot_right(jnp.where(mine, grads, 0), vals)
            weighted = jnp.sum(d_probs * probs, -1, keepdims=True)
            d_scores = as_low(probs * (d_probs - weighted))
            parts.append((dot(d_scores, keys) * scale, dot_left(d_scores, queries) * scale, d_vals))
        for kind in range(3):
            here = slice(kind * width + at, kind * width + at + 128)
            d_proj[:, here] = as_low(jnp.where(lanes < 64, parts[0][kind], parts[1][kind]))


def project_backward_kernel(
    info, dx3, attended, a4, d_out, d_proj, project_w, x2, vec, before, send, keep, dx2, d_sep, fixed
):
    width = x2.shape[1]
    half = width // 2
    core = info[0]
    fixed[...] = before[...]
    for side, out in ((1 - core, send), (core, keep)):
        here = at_lane(side * half, half)
        put(out, 0, 4, 0, dot_left(a4[:, here], d_proj[...]))
        put(out, 0, 4, 3 * width * half // 1024, dot_left(attended[:, here], d_out[...]))
    fixed[12:13] = low_columns_sum(d_out[...])
    fixed[10:11] = low_columns_sum(d_proj[:, :width])
    fixed[11:12] = low_columns_sum(d_proj[:, 2 * width :])
    dx2[...] = dot_right(d_proj[...], project_w[...])
    for row in spans(SEQ, STEP):
        normed, rstd = normalize(x2[row])
        grad = dx2[row]
        dx2[row] = dx3[row] + normalize_back(grad, normed, rstd, vec[4:5])
        fixed[4:5] += columns_sum(grad * normed)
        fixed[5:6] += columns_sum(grad)
    channels = d_sep.shape[1]
    d_sep[...] = as_low(dx2[:, :channels])
    fixed[14:15, channels : 2 * channels] = low_columns_sum(d_sep[...])


def inner_backward_kernel(pieces, per, refs):
    info, refs = refs[0], refs[1:]
    (
        (d_sep, depth, normed_ref, slope_ref, rstd_ref, a2, bias_before, point, point_rest),
        (left, left_rest, own, keep_mask),
        packed,
        outs,
        scratch,
    ) = unpack(refs, [9, 4, per * (pieces - 1), 5, 7])
    keep, send, d_a2, d_right, grads = outs
    d_depth, padded, padded_two, d_left, first_ref, second_ref, sums = scratch
    local = left.shape[1]
    inner = local * pieces
    core, offset = info[0], info[1]
    rows = local // 2
    half = a2.shape[1] // 2
    wide = vectors_of(own, packed, per, a2.shape[1] * local // (256 * per) + local // per)
    for piece in range(pieces):
        weights = point if piece == 0 else point_rest.at[piece - 1]
        for row in spans(local, 256):
            back = dot_right(d_sep[...], weights[row])
            index = (piece * local + row.start) // 128
            d_depth[index] = back[:, 0:128]
            d_depth[index + 1] = back[:, 128:256]
    first_ref[...] = jnp.zeros_like(first_ref)
    second_ref[...] = jnp.zeros_like(second_ref)
    for pad in (padded, padded_two):
        pad[0:8] = jnp.zeros((8, 128), F32)
        pad[SEQ + 8 : SEQ + 16] = jnp.zeros((8, 128), F32)
    grads[...] = jnp.zeros_like(grads)
    grads[1:2] = bias_before[0:1]
    kept = keep_mask[:, 0:1]
    for piece in range(pieces):

        def one(pair, part, pad):
            here = at_lane(piece * local + pair * 256 + part, 128)
            index = piece * (local // 128) + 2 * pair + part // 128
            vectors = rows_of(wide[piece], pair, slice(part, part + 128))
            normed = normed_ref[:, here].astype(F32)
            normal = (normed * vectors[2:3] + vectors[3:4]) * kept
            pad[8 : SEQ + 8] = d_depth[index]
            result = pad[12 : SEQ + 12] * vectors[4:5]
            sums[2, :, here] = eighths_sum(normal * pad[12 : SEQ + 12])
            for tap in range(1, 9):
                shifted = pad[12 - tap : SEQ + 12 - tap]
                result = result + shifted * vectors[4 + tap : 5 + tap]
                sums[2 + tap, :, here] = eighths_sum(normal * shifted)
            result = result * kept
            sums[0, :, here] = eighths_sum(result * normed)
            sums[1, :, here] = eighths_sum(result)
            scaled = result * vectors[2:3]
            first_ref[...] += scaled
            second_ref[...] += scaled * normed
            d_depth[index] = scaled

        def step(index, carry):
            one(index, 0, padded)
            one(index, 128, padded_two)
            return carry

        lax.fori_loop(0, local // 256, step, 0)
    for col in spans(inner, 512):
        grads[2:13, col] = jnp.sum(sums[:, :, col], 1)
    first_ref[...] = jnp.broadcast_to(
        jnp.sum(first_ref[...], 1, keepdims=True) * (1.0 / inner), first_ref.shape
    )
    second_ref[...] = jnp.broadcast_to(
        jnp.sum(second_ref[...], 1, keepdims=True) * (1.0 / inner), second_ref.shape
    )

    def back(index, carry):
        here = at_lane(index * 128, 128)
        normed = normed_ref[:, here].astype(F32)
        d_mixed = rstd_ref[...] * (
            d_depth[index] - first_ref[...] - normed * second_ref[...]
        )
        d_depth[index] = d_mixed
        d_left[:, here] = as_low(d_mixed * slope_ref[:, here].astype(F32))
        return carry

    lax.fori_loop(0, inner // 128, back, 0)
    for part in range(d_right.shape[1] // 128):
        d_right[:, part * 128 : (part + 1) * 128] = d_depth[offset // 128 + part]
    for piece in range(pieces):
        base = piece * local
        cols = slice(base, base + local)
        for side, out in ((1 - core, send), (core, keep)):
            grad = dot_left(a2[:, at_lane(side * half, half)], d_left[:, cols])
            put(out, 2 * piece, 2, 0, grad)
            grad = dot_left(depth[:, at_lane(base + side * rows, rows)], d_sep[...])
            put(out, 2 * piece, 2, half * local // 512, grad)
        grads[0:1, cols] = low_columns_sum(d_left[:, cols])
        if piece == 0:
            d_a2[...] = dot_right(d_left[:, cols], left[...])
        else:
            d_a2[...] += dot_right(d_left[:, cols], left_rest[piece - 1])


def last_kernel(
    info, d_a2_left, d_right, right_pre, conv_w, a2, x1, dx2, values, gates, a1, gated_w, x_ref, vec, kept, before, wide_sums,
    send, keep, input_grad, fixed, shifted, d_a2, d_gated, rows_ref
):
    width = x1.shape[1]
    half = width // 2
    channels = right_pre.shape[1]
    core = info[0]
    fixed[...] = before[...]
    pre = right_pre[...]
    sigma = sigmoid(pre)
    low = as_low(d_right[...] * (sigma * (1.0 + pre * (1.0 - sigma))))
    fixed[14:15, 0:channels] = low_columns_sum(low)
    wide = low.astype(F32)
    rows = lax.broadcasted_iota(jnp.int32, wide.shape, 0)
    shifted[:, 0:channels] = as_low(
        jnp.where(rows == SEQ - 1, 0.0, pltpu.roll(wide, SEQ - 1, 0))
    )
    shifted[:, channels : 2 * channels] = low
    shifted[:, 2 * channels :] = as_low(jnp.where(rows == 0, 0.0, pltpu.roll(wide, 1, 0)))
    total = d_a2_left[...]
    for tap in range(3):
        total = total + dot_right(shifted[:, tap * channels : (tap + 1) * channels], conv_w[tap])
    d_a2[...] = total
    for row in spans(SEQ, STEP):
        normed, rstd = normalize(x1[row])
        grad = d_a2[row] * kept[row, 0:1]
        fixed[2:3] += columns_sum(grad * normed)
        fixed[3:4] += columns_sum(grad)
        dx1 = dx2[row] + normalize_back(grad, normed, rstd, vec[2:3])
        input_grad[row] = dx1
        gate = gates[row]
        scaled = dx1 * gate
        d_gated[row, 0:width] = as_low(scaled)
        d_gated[row, width:] = as_low(scaled * values[row] * (1.0 - gate))
    for side, out in ((1 - core, send), (core, keep)):
        here = at_lane(side * half, half)
        put(out, 0, 4, 0, dot_left(a1[:, here], d_gated[...]))
        put(out, 0, 4, half * width // 512, dot_left(a2[:, here], shifted[...]))
    sums = low_columns_sum(d_gated[...])
    fixed[8:9] = sums[:, 0:width]
    fixed[9:10] = sums[:, width:]
    d_a2[...] = dot_right(d_gated[...], gated_w[...])
    for row in spans(SEQ, STEP):
        normed, rstd = normalize(x_ref[row].astype(F32))
        grad = d_a2[row]
        fixed[0:1] += columns_sum(grad * normed)
        fixed[1:2] += columns_sum(grad)
        input_grad[row] += normalize_back(grad, normed, rstd, vec[0:1])
    pack_small(info, wide_sums, fixed, send, keep, rows_ref)


def pack_small(info, wide, fixed, send, keep, rows_ref):
    if rows_ref is None:
        return
    pieces = lax.axis_size("mp")
    local = wide.shape[1] // pieces
    parts = local // 256
    rows_ref[...] = jnp.zeros_like(rows_ref)
    for piece in range(pieces):
        owner = jnp.bitwise_xor(info[1] // local, piece)
        for part in range(parts):
            spot = pl.multiple_of((owner * parts + part) * 16, 16)
            at = piece * local + part * 256
            rows_ref[pl.ds(spot, 16)] = wide[:, at : at + 256]
    base = wide.shape[1] // 16
    for part in range(fixed.shape[1] // 256):
        rows_ref[base + part * 16 : base + (part + 1) * 16] = fixed[:, part * 256 : (part + 1) * 256]
    count = rows_ref.shape[0] // 2
    offset = send.shape[1] - count // 4
    for side, out in ((1 - info[0], send), (info[0], keep)):
        put(out, 0, 4, offset, rows_ref[pl.ds(pl.multiple_of(side * count, 16), count)])


def own_place(count):
    core = lax.axis_index("dp") % 2
    if count == 2:
        return core
    y = lax.axis_index("dp") // 2 % 2
    near = lax.axis_index("dp") // 4 % 2
    return 2 * core + (1 - core) * y + core * near


def cut(weights, vectors, per, link):
    shapes = [(item.shape[0] // per, item.shape[1]) for item in weights]
    total = sum(rows * columns // 256 for rows, columns in shapes)
    local = weights[0].shape[1]
    small = local // 16 if vectors else 0
    chained = [] if link is None else [link]

    def kernel(*refs):
        refs = list(refs)
        sources = [refs.pop(0) for _ in weights]
        small_in = [refs.pop(0) for _ in vectors]
        for _ in chained:
            refs.pop(0)
        packed = refs.pop(0)
        own = refs.pop(0) if vectors else None
        sems, held = refs
        place = own_place(per)
        copies = []
        offset = 0
        for source, (rows, columns) in zip(sources, shapes):
            here = pl.ds(pl.multiple_of(place * rows, 16), rows)
            for part in range(columns // 256):
                copy = pltpu.make_async_copy(
                    source.at[here, pl.ds(part * 256, 256)],
                    packed.at[pl.ds(offset, rows)],
                    sems.at[len(copies)],
                )
                copy.start()
                copies.append(copy)
                offset += rows
        if vectors:
            held[...] = jnp.zeros_like(held)
            for part in range(local // 256):
                lanes = slice(part * 256, (part + 1) * 256)
                row = 0
                for item in small_in:
                    count = item.shape[0] if len(item.shape) == 2 else 1
                    held[row : row + count] = item[..., lanes].astype(F32).reshape(count, 256)
                    row += count
                chunk = as_low(held[...])
                own[part * 16 : (part + 1) * 16] = chunk
                packed[total + part * 16 : total + (part + 1) * 16] = chunk
        for copy in copies:
            copy.wait()

    outs = [shaped((total + small, 256), LOW)]
    if vectors:
        outs.append(shaped((small, 256), LOW))
    return pl.pallas_call(
        kernel,
        out_shape=outs,
        in_specs=[pl.BlockSpec(memory_space=pl.ANY) for _ in weights]
        + [pl.BlockSpec(memory_space=pltpu.VMEM) for _ in vectors]
        + [pl.BlockSpec(memory_space=pl.ANY) for _ in chained],
        out_specs=[pl.BlockSpec(memory_space=pltpu.VMEM) for _ in outs],
        scratch_shapes=[
            pltpu.SemaphoreType.DMA((sum(columns // 256 for _, columns in shapes),)),
            pltpu.VMEM((16, 256), F32),
        ],
    )(*weights, *vectors, *chained)


def flat_swap(values, partner):
    count = lax.axis_size("dp") * lax.axis_size("mp")
    return lax.ppermute(values, ("dp", "mp"), [(at, partner(at)) for at in range(count)])


PARTNERS = {
    "core": lambda at: at ^ 2,
    "first": lambda at: at ^ (4 if at & 2 else 1),
    "second": lambda at: at ^ (1 if at & 2 else 4),
    "x": lambda at: at ^ 1,
    "y": lambda at: at ^ 4,
    "near": lambda at: at ^ 8,
    "far": lambda at: at ^ 16,
    "hop": lambda at: at ^ (8 if at & 2 else 4),
}
LENGTH_FIRST_STEPS = [
    ("half_near", "near"),
    ("quarter", "first"),
    ("half_mix", "second"),
    ("sum", "far"),
    ("sum", "second"),
    ("join_mix", "first"),
    ("spread", "near"),
    ("join_near", "core"),
    ("final", None),
]
INNER_STEPS = [
    ("quarter", "first"),
    ("half_mix", "second"),
    ("half_near", "near"),
    ("sum", "far"),
    ("sum", "near"),
    ("join_near", "y"),
    ("join_y", "core"),
    ("final", None),
]
SHARED_STEPS = [
    ("quarter", "first"),
    ("half_mix", "second"),
    ("half_near", "near"),
    ("sum", "far"),
    ("sum", "near"),
    ("join_near", "second"),
    ("join_mix", "first"),
    ("spread", "core"),
    ("final", None),
]


PLAN = (
    "p",
    "d",
    "a",
    "p",
    "c",
    "a",
    "d",
    "d",
    "p",
    "a",
    "c",
    "d",
    "a",
    "c",
    "dp",
    "c",
    "d",
    "p",
    "d",
    "c",
    "p",
    "a",
    "d",
    "c",
    "!d",
    "p",
    "!a",
    "!p",
    "c",
    "!c",
)


class Stream:
    def __init__(self, inner, mine, other, parts, steps=None):
        self.inner = inner
        self.mine = mine
        self.flight = flat_swap(other, PARTNERS["core"])
        self.steps = list(steps or (INNER_STEPS if inner else SHARED_STEPS))
        self.parts = parts


def advance_kernel(jobs, refs):
    info, refs = refs[0], refs[1:]
    core, y, near = info[0], info[4], info[5]
    ins, outs = list(refs[: 2 * len(jobs)]), list(refs[2 * len(jobs) :])
    for inner, step, parts in jobs:
        mine, flight = ins.pop(0), ins.pop(0)
        x = 0 if inner else info[3]
        mix = core * x + (1 - core) * y

        def added(spot):
            return as_low(mine[spot].astype(F32) + flight[spot].astype(F32))

        if step == "quarter":
            keep, send = outs.pop(0), outs.pop(0)
            for at in range(2):
                send[at] = added(core * (2 * at + 1 - y) + (1 - core) * (2 * (1 - x) + at))
                keep[at] = added(core * (2 * at + y) + (1 - core) * (2 * x + at))
        elif step == "half_mix":
            keep, send = outs.pop(0), outs.pop(0)
            send[0] = added(1 - mix)
            keep[0] = added(mix)
        elif step == "half_near":
            keep, send = outs.pop(0), outs.pop(0)
            rows = keep.shape[1]
            for out, side in ((send, 1 - near), (keep, near)):
                here = pl.ds(pl.multiple_of(side * rows, 16), rows)
                for at in range(keep.shape[0]):
                    out[at] = as_low(mine[at, here].astype(F32) + flight[at, here].astype(F32))
        elif step == "sum":
            outs.pop(0)[0] = added(0)
        elif step == "join_near":
            out = outs.pop(0)
            rows = mine.shape[1]
            for source, side in ((mine, near), (flight, 1 - near)):
                for at in range(mine.shape[0]):
                    out[at, pl.ds(pl.multiple_of(side * rows, 16), rows)] = source[at]
        elif step in ("join_y", "join_mix"):
            out = outs.pop(0)
            side = y if step == "join_y" else mix
            out[side] = mine[0]
            out[1 - side] = flight[0]
        elif step == "spread":
            out = outs.pop(0)
            for at in range(2):
                out[core * (2 * at + y) + (1 - core) * (2 * x + at)] = mine[at]
                out[core * (2 * at + 1 - y) + (1 - core) * (2 * (1 - x) + at)] = flight[at]


def finish_kernel(parts, small, refs):
    info, mine, flight, refs = refs[0], refs[1], refs[2], list(refs[3:])
    core = info[0]
    outs = [refs.pop(0) for _ in parts]
    smalls = [refs.pop(0) for _ in range(11)] if small else []
    link = refs.pop(0)
    link[...] = jnp.zeros_like(link)
    held = [refs.pop(0) for _ in parts]
    sems = refs.pop(0)
    copies = []
    quarters = mine.shape[0]
    for at, (offset, rows, shape) in enumerate(parts):
        target, columns, deep = held[at], shape[-1] // 256, len(shape) == 3
        for half, (source, side) in enumerate(((mine, core), (flight, 1 - core))):
            for quarter in range(quarters):
                here = slice(quarter * rows, (quarter + 1) * rows)
                for part in range(columns * (shape[0] if deep else 1)):
                    row = offset + part * rows
                    block = source[quarter, row : row + rows].astype(F32)
                    if deep:
                        target[half, part, here] = block
                    else:
                        target[half, here, part * 256 : (part + 1) * 256] = block
            spot = pl.ds(pl.multiple_of(side * quarters * rows, 16), quarters * rows)
            spot = (slice(None), spot) if deep else (spot,)
            copies.append(
                pltpu.make_async_copy(target.at[half], outs[at].at[spot], sems.at[len(copies)])
            )
            copies[-1].start()
    if small:
        total = refs.pop(0)
        offset, rows = small
        for source, side in ((mine, core), (flight, 1 - core)):
            for quarter in range(mine.shape[0]):
                spot = (side * mine.shape[0] + quarter) * rows
                total[pl.ds(pl.multiple_of(spot, 16), rows)] = source[
                    quarter, offset : offset + rows
                ].astype(F32)
        norm, gated, left, conv, inner, depth, point, project, output, expand, shrink = smalls
        local, width = left.shape[-1], output.shape[-1]
        for part in range(local // 256):
            lanes = slice(part * 256, (part + 1) * 256)
            spot = (info[1] // local * (local // 256) + part) * 16
            block = total[pl.ds(pl.multiple_of(spot, 16), 16)]
            left[:, lanes] = block[0:1]
            expand[:, lanes] = block[1:2]
            inner[:, lanes] = block[2:4]
            depth[:, lanes] = block[4:13]
        for part in range(width // 256):
            lanes = slice(part * 256, (part + 1) * 256)
            base = local * 2 // 16 + part * 16
            block = total[base : base + 16]
            for at in range(4):
                norm[at, :, lanes] = block[2 * at : 2 * at + 2]
            gated[:, lanes] = block[8:9]
            gated[:, width + part * 256 : width + (part + 1) * 256] = block[9:10]
            project[:, lanes] = block[10:12]
            output[:, lanes] = block[12:13]
            shrink[:, lanes] = block[13:14]
            (conv if part == 0 else point)[...] = block[14:15]
    for copy in copies:
        copy.wait()


def finish(chain, stream, small):
    parts = stream.parts
    shapes = [shaped(shape, F32) for _, _, shape in parts]
    scratch = [
        pltpu.VMEM((2,) + shape[:-2] + (shape[-2] // 2, shape[-1]), F32) for _, _, shape in parts
    ]
    scratch.append(pltpu.SemaphoreType.DMA((2 * len(parts),)))
    names = []
    if small:
        scratch.append(pltpu.VMEM((256, 256), F32))
        names = [shaped(shape, F32) for shape in small[1]]
    stream.mine = chain.run(
        lambda *refs: finish_kernel(parts, small[0] if small else None, refs),
        shapes + names + [shaped((8, 128), F32)],
        [stream.mine, stream.flight],
        scratch,
        ADV,
        len(parts),
    )


def advance(chain, streams):
    jobs, ins, outs = [], [], []
    for stream in streams:
        step = stream.steps[0][0]
        jobs.append((stream.inner, step, stream.parts))
        ins += [stream.mine, stream.flight]
        lead, rows, columns = stream.mine.shape
        if step in ("quarter", "half_mix"):
            outs += [shaped((lead // 2, rows, columns), LOW)] * 2
        elif step == "half_near":
            outs += [shaped((lead, rows // 2, columns), LOW)] * 2
        elif step == "sum":
            outs.append(shaped((lead, rows, columns), LOW))
        elif step == "join_near":
            outs.append(shaped((lead, rows * 2, columns), LOW))
        else:
            outs.append(shaped((lead * 2, rows, columns), LOW))
    results = list(chain.run(lambda *refs: advance_kernel(jobs, refs), outs, ins, [], ADV))
    for stream in streams:
        step, partner = stream.steps.pop(0)
        stream.mine = results.pop(0)
        if step in ("quarter", "half_mix", "half_near"):
            stream.flight = flat_swap(results.pop(0), PARTNERS[partner])
        else:
            stream.flight = flat_swap(stream.mine, PARTNERS[partner])


def opened(packed, first, count, offset, rows, columns):
    parts = [
        packed[first : first + count, offset + at * rows : offset + (at + 1) * rows]
        for at in range(columns // 256)
    ]
    return jnp.concatenate(parts, 2).reshape(count * rows, columns)


class Weights:
    def __init__(self, packed, per):
        pieces = [packed]
        for bit in bits_of("mp"):
            pieces = pieces + [swap(item, "mp", bit) for item in pieces]
        self.blocks = [[item] for item in pieces[1:]]
        self.per = per

    def hop(self, after):
        if self.per == 4:
            for blocks in self.blocks:
                blocks[0], _ = lax.optimization_barrier((blocks[0], after))
                blocks.append(flat_swap(blocks[0], PARTNERS["hop"]))

    def share(self, after):
        found = []
        for blocks in self.blocks:
            held = [lax.optimization_barrier((item, after))[0] for item in blocks]
            found += held + [swap(item, "dp", 1) for item in held]
        return found


def finish_shared(mine, other, order):
    own = bit_of("dp", 1)
    values = add_low(mine, swap(other, "dp", 1))
    held = [("dp", 1, own)]
    for axis, bit in order[:-1]:
        own = bit_of(axis, bit)
        mine, other = split(values, own)
        values = add_low(mine, swap(other, axis, bit))
        held.append((axis, bit, own))
    axis, bit = order[-1]
    values = add_low(values, swap(values, axis, bit))
    for axis, bit, own in reversed(held):
        values = join(values, swap(values, axis, bit), own)
    return values.astype(F32)


def finish_inner(mine, other, order):
    values = add_low(mine, swap(other, "dp", 1))
    pieces = [values[at] for at in range(values.shape[0])]
    held = [("dp", 1, bit_of("dp", 1))]
    for axis, bit in order[:-1]:
        if axis == "mp":
            keep_count = len(pieces) // 2
            moved = [swap(item, axis, bit) for item in pieces[keep_count:]]
            pieces = [add_low(one, two) for one, two in zip(pieces[:keep_count], moved)]
            continue
        own = bit_of(axis, bit)
        parts = [split(item, own) for item in pieces]
        pieces = [add_low(mine, swap(other, axis, bit)) for mine, other in parts]
        held.append((axis, bit, own))
    axis, bit = order[-1]
    values = add_low(pieces[0], swap(pieces[0], axis, bit))
    for axis, bit, own in reversed(held):
        values = join(values, swap(values, axis, bit), own)
    return values.astype(F32)


def body(
    cell_input,
    lengths,
    out_grad,
    norm_params,
    gated_weight,
    gated_bias,
    left_weight,
    left_bias,
    conv_weight,
    conv_bias,
    inner_norm,
    depth_weight,
    point_weight,
    point_bias,
    project_weight,
    project_bias,
    output_weight,
    output_bias,
    expand_weight,
    expand_bias,
    shrink_weight,
    shrink_bias,
):
    width = cell_input.shape[1]
    channels = conv_weight.shape[2]
    local = left_weight.shape[1]
    pieces = lax.axis_size("mp")
    inner = local * pieces
    tokens = cell_input.shape[0]
    assert tokens == SEQ
    tuned = lax.axis_size("dp") == 16 and pieces == 2
    mp_bits = bits_of("mp")[::-1]
    dp_bits = bits_of("dp")[1:]
    mp_first = [("mp", bit) for bit in mp_bits] + [("dp", bit) for bit in dp_bits]
    core = bit_of("dp", 1)
    chain = Chain(local)

    def inner_rows(size):
        return (2 * pieces, size // 1024, 256)


    per = 4 if tuned else 2
    vectors = [left_bias, expand_bias, inner_norm, depth_weight]
    packed, own = cut([left_weight, point_weight], vectors, per, None)
    early = Weights(packed, per)
    (packed,) = cut([expand_weight, shrink_weight], [], per, own)
    late = Weights(packed, per)
    chain.link = packed
    a1, values, gates, x1, a2, right_pre, vec, kept, valid, *parts, right = chain.run(
        pre_kernel,
        [
            shaped((tokens, width), LOW),
            shaped((tokens, width), F32),
            shaped((tokens, width), F32),
            shaped((tokens, width), F32),
            shaped((tokens, width), LOW),
            shaped((tokens, channels), F32),
            shaped((16, width), F32),
            shaped((tokens, 128), F32),
            shaped((8, tokens), F32),
            shaped((tokens, local), F32),
            shaped((tokens, local), LOW),
            shaped((tokens, 128), F32),
            shaped((tokens, 128), F32),
            shaped((tokens, channels), LOW),
        ],
        [
            lengths,
            left_weight,
            own,
            cell_input,
            gated_weight,
            conv_weight,
            norm_params,
            gated_bias,
            conv_bias,
            point_bias,
            project_bias,
            output_bias,
            shrink_bias,
        ],
        [],
        int(2.2e9 * EARLY),
    )
    early.hop(right)
    early_blocks = early.share(right)
    normed, slope, depth, rstd, left_rest = chain.run(
        lambda *refs: inner_forward_kernel(pieces, per, refs),
        [
            shaped((tokens, inner), LOW),
            shaped((tokens, inner), LOW),
            shaped((tokens, inner), LOW),
            shaped((tokens, 128), F32),
            shaped((pieces - 1, width, local), LOW),
        ],
        [a2, right, *parts, own, kept] + early_blocks,
        [
            pltpu.VMEM((pieces - 1, tokens, local), F32),
            pltpu.VMEM((tokens, 128), F32),
            pltpu.VMEM((tokens, 128), F32),
            pltpu.VMEM((tokens, 128), F32),
            pltpu.VMEM((tokens + 16, 128), F32),
            pltpu.VMEM((tokens + 16, 128), F32),
        ],
        int(6.5e9 * EARLY),
    )
    late.hop(rstd)
    x2, a4, qkv, lse, attended, x3, a5, point_rest = chain.run(
        lambda *refs: attention_forward_kernel(pieces, per, refs),
        [
            shaped((tokens, width), F32),
            shaped((tokens, width), LOW),
            shaped((tokens, 3 * width), LOW),
            shaped((tokens, 128), F32),
            shaped((tokens, width), LOW),
            shaped((tokens, width), F32),
            shaped((tokens, width), LOW),
            shaped((pieces - 1, local, channels), LOW),
        ],
        [x1, depth, point_weight, vec, project_weight, output_weight, valid]
        + early_blocks,
        [],
        int(4.4e9 * EARLY),
    )
    keep_own, send_own, shrunk_own, d_a5_own, bias_own = chain.run(
        feed_own_kernel,
        [
            shaped((2, 2 * local * width // 1024, 256), LOW),
            shaped((2, 2 * local * width // 1024, 256), LOW),
            shaped((tokens, width), F32),
            shaped((tokens, width), F32),
            shaped((8, local), F32),
        ],
        [a5, out_grad, expand_weight, shrink_weight, own],
        [
            pltpu.VMEM((tokens, local), LOW),
            pltpu.VMEM((tokens, local), F32),
            pltpu.VMEM((tokens, local), LOW),
        ],
        int(3e9 * EARLY),
    )
    late_blocks = late.share(bias_own)
    cell_output, feed_keep, feed_send, dx3, fixed, expand_sum = chain.run(
        lambda *refs: feed_kernel(pieces, per, refs),
        [
            shaped((tokens, width), LOW),
            shaped(inner_rows(2 * local * width), LOW),
            shaped(inner_rows(2 * local * width), LOW),
            shaped((tokens, width), F32),
            shaped((16, width), F32),
            shaped((8, inner), F32),
        ],
        [a5, x3, out_grad, vec, keep_own, send_own, shrunk_own, d_a5_own, bias_own]
        + early_blocks
        + late_blocks,
        [
            pltpu.VMEM((tokens, local), LOW),
            pltpu.VMEM((tokens, local), F32),
            pltpu.VMEM((tokens, local), LOW),
            pltpu.VMEM((tokens, width), F32),
            pltpu.VMEM((tokens, width), F32),
            pltpu.VMEM((width, local), LOW),
            pltpu.VMEM((local, width), LOW),
        ],
        int(8e9 * SCALE),
    )
    if tuned:
        fee = Stream(
            True,
            feed_keep,
            feed_send,
            [
                (0, local // 4, (local, width)),
                (width * local // 1024, width // 4, (width, local)),
            ],
        )
    d_out, d_proj = chain.run(
        attention_backward_kernel,
        [shaped((tokens, width), LOW), shaped((tokens, 3 * width), LOW)],
        [dx3, attended, output_weight, qkv, lse, valid],
        [pltpu.VMEM((tokens, width), LOW)],
        int(5e9 * SCALE),
    )
    if tuned:
        advance(chain, [fee])
    proj_send, proj_keep, dx2, d_sep, fixed = chain.run(
        project_backward_kernel,
        [
            shaped((4, width * width // 512, 256), LOW),
            shaped((4, width * width // 512, 256), LOW),
            shaped((tokens, width), F32),
            shaped((tokens, channels), LOW),
            shaped((16, width), F32),
        ],
        [dx3, attended, a4, d_out, d_proj, project_weight, x2, vec, fixed],
        [],
        int(3e9 * SCALE),
    )
    if tuned:
        pro = Stream(
            False,
            proj_keep,
            proj_send,
            [
                (0, width // 8, (width, 3 * width)),
                (3 * width * width // 2048, width // 8, (width, width)),
            ],
            LENGTH_FIRST_STEPS,
        )
        advance(chain, [pro])
    left_keep, left_send, d_a2, d_right, wide_sums = chain.run(
        lambda *refs: inner_backward_kernel(pieces, per, refs),
        [
            shaped(inner_rows(local * (width + channels)), LOW),
            shaped(inner_rows(local * (width + channels)), LOW),
            shaped((tokens, width), F32),
            shaped((tokens, channels), F32),
            shaped((16, inner), F32),
        ],
        [
            d_sep,
            depth,
            normed,
            slope,
            rstd,
            a2,
            expand_sum,
            point_weight,
            point_rest,
            left_weight,
            left_rest,
            own,
            kept,
        ]
        + early_blocks,
        [
            pltpu.VMEM((inner // 128, tokens, 128), F32),
            pltpu.VMEM((tokens + 16, 128), F32),
            pltpu.VMEM((tokens + 16, 128), F32),
            pltpu.VMEM((tokens, inner), LOW),
            pltpu.VMEM((tokens, 128), F32),
            pltpu.VMEM((tokens, 128), F32),
            pltpu.VMEM((11, 8, inner), F32),
        ],
        int(11.5e9 * SCALE),
    )
    if tuned:
        lef = Stream(
            True,
            left_keep,
            left_send,
            [
                (0, width // 4, (width, local)),
                (width * local // 1024, local // 4, (local, channels)),
            ],
        )
        advance(chain, [fee])
    small = 32 if tuned else 0
    last_rows = width * (2 * width + 3 * channels) // 2048 + small
    last_send, last_keep, input_grad, fixed = chain.run(
        last_kernel if tuned else lambda *refs: last_kernel(*refs, None),
        [
            shaped((4, last_rows, 256), LOW),
            shaped((4, last_rows, 256), LOW),
            shaped((tokens, width), F32),
            shaped((16, width), F32),
        ],
        [
            d_a2,
            d_right,
            right_pre,
            conv_weight,
            a2,
            x1,
            dx2,
            values,
            gates,
            a1,
            gated_weight,
            cell_input,
            vec,
            kept,
            fixed,
            wide_sums,
        ],
        [
            pltpu.VMEM((tokens, 3 * channels), LOW),
            pltpu.VMEM((tokens, width), F32),
            pltpu.VMEM((tokens, 2 * width), LOW),
        ]
        + ([pltpu.VMEM((8 * small, 256), F32)] if tuned else []),
        int(4.0e9 * SCALE),
    )
    if tuned:
        lat = Stream(
            False,
            last_keep,
            last_send,
            [
                (0, width // 8, (width, 2 * width)),
                (width * width // 1024, width // 8, (3, width, channels)),
            ],
        )
        groups = {"a": [fee], "p": [pro], "c": [lef], "d": [lat]}
        small_shapes = [
            (4, 2, width),
            (1, 2 * width),
            (1, local),
            (1, channels),
            (2, local),
            (9, local),
            (1, channels),
            (2, width),
            (1, width),
            (1, local),
            (1, width),
        ]
        small_part = ((last_rows - small, small), small_shapes)
        for names in PLAN:
            if names[0] == "!":
                stream = groups[names[1]][0]
                finish(chain, stream, small_part if names == "!d" else None)
            else:
                advance(chain, [groups[name][0] for name in names])
        (grad_shrink, grad_expand, _), (grad_left, grad_point, _) = fee.mine, lef.mine
        (grad_proj, grad_out, _), (grad_gated, grad_conv) = pro.mine, lat.mine[:2]
        smalls = [
            item.reshape(-1) if item.shape[0] == 1 else item for item in lat.mine[2:-1]
        ]
    else:

        def whole(keep, send, offset, rows, columns):
            both = [
                jnp.stack([opened(item, 2 * at, 2, offset, rows, columns) for at in range(pieces)])
                for item in (keep, send)
            ]
            return finish_inner(both[0], both[1], mp_first)

        def shared(keep, send, offset, rows, columns):
            both = [opened(item, 0, 4, offset, rows, columns) for item in (keep, send)]
            return finish_shared(both[0], both[1], mp_first)

        eighth = width // 8
        grad_shrink = whole(feed_keep, feed_send, 0, local // 4, width)
        grad_expand = whole(
            feed_keep, feed_send, width * local // 1024, width // 4, local
        )
        grad_left = whole(left_keep, left_send, 0, width // 4, local)
        grad_point = whole(left_keep, left_send, width * local // 1024, local // 4, channels)
        grad_proj = shared(proj_keep, proj_send, 0, eighth, 3 * width)
        grad_out = shared(proj_keep, proj_send, 6 * eighth, eighth, width)
        grad_gated = shared(last_keep, last_send, 0, eighth, 2 * width)
        grad_conv = jnp.stack(
            [shared(last_keep, last_send, (4 + at) * eighth, eighth, channels) for at in range(3)]
        )
        chunks = [wide_sums[:, at : at + local] for at in range(0, inner, local)]
        for bit in mp_bits:
            count = len(chunks) // 2
            moved = [swap(item, "mp", bit) for item in chunks[count:]]
            chunks = [one + two for one, two in zip(chunks[:count], moved)]
            fixed = fixed + swap(fixed, "mp", bit)
        wide_total = chunks[0]
        for bit in bits_of("dp"):
            fixed = fixed + swap(fixed, "dp", bit)
            wide_total = wide_total + swap(wide_total, "dp", bit)
        smalls = [
            fixed[0:8].reshape(4, 2, width),
            fixed[8:10].reshape(2 * width),
            wide_total[0],
            fixed[14, :channels],
            wide_total[2:4],
            wide_total[4:13],
            fixed[14, channels:],
            fixed[10:12],
            fixed[12],
            wide_total[1],
            fixed[13],
        ]
    return (
        cell_output,
        input_grad,
        smalls[0],
        grad_gated,
        smalls[1],
        grad_left,
        smalls[2],
        grad_conv,
        smalls[3],
        smalls[4],
        smalls[5],
        grad_point,
        smalls[6],
        grad_proj,
        smalls[7],
        grad_out,
        smalls[8],
        grad_expand,
        smalls[9],
        grad_shrink,
        smalls[10],
    )


def solution(mesh):
    return jax.shard_map(
        body,
        mesh=mesh,
        in_specs=(
            P(("dp", "mp"), None),
            P(("dp", "mp")),
            P(("dp", "mp"), None),
            P(),
            P(),
            P(),
            P(None, "mp"),
            P("mp"),
            P(),
            P(),
            P(None, "mp"),
            P(None, "mp"),
            P("mp", None),
            P(),
            P(),
            P(),
            P(),
            P(),
            P(None, "mp"),
            P("mp"),
            P("mp", None),
            P(),
        ),
        out_specs=(
            P(("dp", "mp"), None),
            P(("dp", "mp"), None),
            P(),
            P(),
            P(),
            P(None, "mp"),
            P("mp"),
            P(),
            P(),
            P(None, "mp"),
            P(None, "mp"),
            P("mp", None),
            P(),
            P(),
            P(),
            P(),
            P(),
            P(None, "mp"),
            P("mp"),
            P("mp", None),
            P(),
        ),
        check_vma=False,
    )
```

```python
import jax
import jax.numpy as jnp
from jax import lax
from jax.experimental import pallas as pl
from jax.experimental.pallas import tpu as pltpu
from jax.sharding import PartitionSpec as P

HEADS = 8
SEQ = 256
EPS = 1e-06
NEGATIVE = -1000000000.0
LOW = jnp.bfloat16
F32 = jnp.float32
STEP = 64
LIMIT = 24 * 2**20
SCALE = 4
EARLY = 0.001
ADV = 20 * 10**9


def as_low(values):
    return values.astype(LOW)


def dot(left, right):
    return jnp.dot(left, right, preferred_element_type=F32)


def dot_left(left, right):
    return lax.dot_general(left, right, (((0,), (0,)), ((), ())), preferred_element_type=F32)


def dot_right(left, right):
    return lax.dot_general(left, right, (((1,), (1,)), ((), ())), preferred_element_type=F32)


def swap(values, axis, bit):
    count = lax.axis_size(axis)
    return lax.ppermute(values, axis, [(at, at ^ bit) for at in range(count)])


def bit_of(axis, bit):
    return (lax.axis_index(axis) // bit) % 2


def bits_of(axis):
    bits, bit = [], 1
    while bit < lax.axis_size(axis):
        bits.append(bit)
        bit *= 2
    return bits


def add_low(first, second):
    return as_low(first.astype(F32) + second.astype(F32))


def split(values, own):
    half = values.shape[0] // 2
    mine = lax.dynamic_slice_in_dim(values, own * half, half, 0)
    other = lax.dynamic_slice_in_dim(values, (1 - own) * half, half, 0)
    return mine, other


def join(mine, other, own):
    swapped = own == 1
    return jnp.concatenate(
        [jnp.where(swapped, other, mine), jnp.where(swapped, mine, other)], 0
    )


def sum_shared(values, order):
    held = []
    steps = [("dp", 1)] + order
    for axis, bit in steps[:-1]:
        own = bit_of(axis, bit)
        mine, other = split(values, own)
        values = add_low(mine, swap(other, axis, bit))
        held.append((axis, bit, own))
    axis, bit = steps[-1]
    values = add_low(values, swap(values, axis, bit))
    for axis, bit, own in reversed(held):
        values = join(values, swap(values, axis, bit), own)
    return values.astype(F32)


def sum_inner(pieces, order):
    held = []
    steps = [("dp", 1)] + order
    for axis, bit in steps[:-1]:
        if axis == "mp":
            keep_count = len(pieces) // 2
            moved = [swap(item, axis, bit) for item in pieces[keep_count:]]
            pieces = [add_low(one, two) for one, two in zip(pieces[:keep_count], moved)]
            continue
        own = bit_of(axis, bit)
        parts = [split(item, own) for item in pieces]
        pieces = [add_low(mine, swap(other, axis, bit)) for mine, other in parts]
        held.append((axis, bit, own))
    axis, bit = steps[-1]
    values = add_low(pieces[0], swap(pieces[0], axis, bit))
    for axis, bit, own in reversed(held):
        values = join(values, swap(values, axis, bit), own)
    return values.astype(F32)


def sigmoid(values):
    return 0.5 * jnp.tanh(0.5 * values) + 0.5


def spans(total, step):
    return [slice(at, at + step) for at in range(0, total, step)]


def at_lane(start, size):
    return pl.ds(pl.multiple_of(start, 128), size)


def normalize(values):
    width = values.shape[1]
    centre = jnp.sum(values, -1, keepdims=True) * (1.0 / width)
    centered = values - centre
    variance = jnp.sum(centered * centered, -1, keepdims=True) * (1.0 / width)
    rstd = lax.rsqrt(variance + EPS)
    return centered * rstd, rstd


def normalize_back(grad, normed, rstd, gain):
    width = grad.shape[1]
    scaled = grad * gain
    first = jnp.sum(scaled, -1, keepdims=True) * (1.0 / width)
    second = jnp.sum(scaled * normed, -1, keepdims=True) * (1.0 / width)
    return rstd * (scaled - first - normed * second)


def columns_sum(values):
    return jnp.sum(values, 0, keepdims=True)


def eighths_sum(values):
    return jnp.sum(values.reshape(-1, 8, values.shape[1]), 0)


def low_columns_sum(values):
    ones = jnp.ones((16, values.shape[0]), LOW)
    return dot(ones, values)[0:1]


def place(local):
    dp, mp = lax.axis_index("dp"), lax.axis_index("mp")
    return dp % 2, mp * local, None, mp % 2, dp // 2 % 2, dp // 4 % 2


class Chain:
    def __init__(self, local):
        self.link = None
        self.local = local

    def run(self, kernel, outs, ins, scratch, flops, placed=0):
        ins = list(ins)
        specs = [
            pl.BlockSpec(memory_space=pltpu.SMEM if item.dtype == jnp.int32 else pltpu.VMEM)
            for item in ins
        ]
        count = len(ins)
        moved = sum(item.size * item.dtype.itemsize for item in ins + list(outs))
        linked = self.link is not None
        if linked:
            ins.append(self.link)
            specs.append(pl.BlockSpec(memory_space=pl.ANY))

        def call(*refs):
            kernel(place(self.local), *(refs[:count] + refs[count + 1 :] if linked else refs))

        results = pl.pallas_call(
            call,
            out_shape=outs,
            in_specs=specs,
            out_specs=[
                pl.BlockSpec(memory_space=pltpu.HBM if at < placed else pltpu.VMEM)
                for at in range(len(outs))
            ],
            scratch_shapes=scratch,
            compiler_params=pltpu.CompilerParams(vmem_limit_bytes=LIMIT),
            cost_estimate=pl.CostEstimate(
                flops=flops, bytes_accessed=moved + flops // 50, transcendentals=0
            ),
        )(*ins)
        self.link = min(results, key=lambda item: item.size)
        return results


def put(out, first, count, offset, values):
    rows = values.shape[0] // count
    low = as_low(values)
    for quarter in range(count):
        for part in range(values.shape[1] // 256):
            at = offset + part * rows
            out[first + quarter, at : at + rows] = low[
                quarter * rows : (quarter + 1) * rows, part * 256 : (part + 1) * 256
            ]


def shaped(shape, kind):
    return jax.ShapeDtypeStruct(shape, kind)


def pre_kernel(
    info, lengths, left, own, x_ref, gated_w, conv_w, norms, gated_b, conv_b, point_b, project_b, output_b, shrink_b,
    a1, values, gates, x1, a2, right_pre, vec, kept, valid, mixed, slope, total_ref, square, right
):
    width = x_ref.shape[1]
    channels = right.shape[1]
    length = lengths[0]
    for ref, axis in ((kept, 0), (valid, 1)):
        spots = lax.broadcasted_iota(jnp.int32, ref.shape, axis)
        ref[...] = jnp.where(spots < length, 1.0, 0.0).astype(F32)
    vec[...] = jnp.zeros_like(vec)
    for at in range(4):
        vec[2 * at : 2 * at + 2] = norms[at].astype(F32)
    for row, item in ((8, gated_b.at[0:width]), (9, gated_b.at[width:]), (13, output_b), (14, shrink_b)):
        vec[row : row + 1] = item[...].astype(F32).reshape(1, width)
    vec[10:11, 0:channels] = conv_b[...].astype(F32).reshape(1, channels)
    vec[10:11, channels:] = point_b[...].astype(F32).reshape(1, channels)
    vec[11:13] = project_b[...].astype(F32)
    for row in spans(SEQ, STEP):
        normed, _ = normalize(x_ref[row].astype(F32))
        a1[row] = as_low(normed * vec[0:1] + vec[1:2])
    for col in spans(width, 256):
        gate_col = slice(col.start + width, col.stop + width)
        value = dot(a1[...], gated_w[:, col]) + vec[8:9, col]
        gate = sigmoid(dot(a1[...], gated_w[:, gate_col]) + vec[9:10, col])
        values[:, col] = value
        gates[:, col] = gate
        x1[:, col] = x_ref[:, col].astype(F32) + value * gate
    for row in spans(SEQ, STEP):
        normed, _ = normalize(x1[row])
        a2[row] = as_low((normed * vec[2:3] + vec[3:4]) * kept[row, 0:1])
    rows = lax.broadcasted_iota(jnp.int32, right_pre.shape, 0)
    first = jnp.where(rows == 0, 0.0, pltpu.roll(dot(a2[...], conv_w[0]), 1, 0))
    last = jnp.where(rows == SEQ - 1, 0.0, pltpu.roll(dot(a2[...], conv_w[2]), SEQ - 1, 0))
    total = first + dot(a2[...], conv_w[1]) + last + vec[10:11, 0 : right_pre.shape[1]]
    right_pre[...] = total
    right[...] = as_low(total * sigmoid(total))
    total_ref[...] = jnp.zeros_like(total_ref)
    square[...] = jnp.zeros_like(square)
    right_rows = right[...].astype(F32)
    left_piece(a2, left, (own, 0), right_rows, info[1], 0, mixed, slope, total_ref, square)


def unpack(refs, counts):
    groups, at = [], 0
    for count in counts:
        groups.append(refs[at : at + count])
        at += count
    return groups


def places(info, count):
    core, y, near = info[0], info[4], info[5]
    if count == 2:
        return [core, 1 - core]
    mine = (1 - core) * y + core * near
    theirs = (1 - core) * near + core * y
    return [2 * core + mine, 2 * core + 1 - mine, 2 - 2 * core + theirs, 3 - 2 * core - theirs]


def assemble(info, target, blocks, offset):
    rows = target.shape[0] // len(blocks)
    for spot, block in zip(places(info, len(blocks)), blocks):
        here = pl.ds(pl.multiple_of(spot * rows, 16), rows)
        for part in range(target.shape[1] // 256):
            at = offset + part * rows
            target[here, part * 256 : (part + 1) * 256] = block[at : at + rows]


def vectors_of(own, blocks, per_piece, offset):
    found = [(own, 0)]
    for at in range(0, len(blocks), per_piece):
        found.append((blocks[at], offset))
    return found


def rows_of(vectors, index, lanes):
    ref, offset = vectors
    return ref[pl.ds(pl.multiple_of(offset + index * 16, 16), 16), lanes].astype(F32)


def left_piece(a2, left, vectors, right_rows, offset, base, mixed, slope, total, square):
    local = left.shape[1]
    for col in spans(local, 256):
        pre = dot(a2[...], left[:, col])
        pre = pre + rows_of(vectors, col.start // 256, slice(0, 256))[0:1]
        sigma = sigmoid(pre)
        at = base + col.start
        slope[:, at : at + 256] = as_low(sigma * (1.0 + pre * (1.0 - sigma)))
        value = pre * sigma + right_rows * jnp.where(offset == at, 1.0, 0.0)
        mixed[:, col] = value
        total[...] += value[:, 0:128] + value[:, 128:256]
        squared = value * value
        square[...] += squared[:, 0:128] + squared[:, 128:256]


def inner_forward_kernel(pieces, per, refs):
    info, refs = refs[0], refs[1:]
    (a2, right, mixed_own, slope_own, total_own, square_own, own, keep), packed, outs, scratch = unpack(
        refs, [8, per * (pieces - 1), 5, 6]
    )
    normed_ref, slope_ref, depth, rstd_ref, left_rest = outs
    mixed, total, square, centre_ref, padded, padded_two = scratch
    local = mixed_own.shape[1]
    inner = local * pieces
    skipped = a2.shape[1] * local // (256 * per) + local // per
    wide = vectors_of(own, packed, per, skipped)
    right_rows = right[...].astype(F32)
    total[...] = total_own[...]
    square[...] = square_own[...]
    slope_ref[:, 0:local] = slope_own[...]
    for piece in range(1, pieces):
        rest = left_rest.at[piece - 1]
        assemble(info, rest, packed[(piece - 1) * per : piece * per], 0)
        left_piece(
            a2, rest, wide[piece], right_rows, info[1], piece * local,
            mixed.at[piece - 1], slope_ref, total, square,
        )
    centre = jnp.sum(total[...], 1, keepdims=True) * (1.0 / inner)
    variance = jnp.sum(square[...], 1, keepdims=True) * (1.0 / inner) - centre * centre
    rstd = lax.rsqrt(variance + EPS)
    centre_ref[...] = jnp.broadcast_to(centre, centre_ref.shape)
    rstd_ref[...] = jnp.broadcast_to(rstd, rstd_ref.shape)
    for pad in (padded, padded_two):
        pad[0:8] = jnp.zeros((8, 128), F32)
        pad[SEQ + 8 : SEQ + 16] = jnp.zeros((8, 128), F32)
    kept = keep[:, 0:1]
    for piece in range(pieces):

        def one(index, part, pad):
            here = at_lane(piece * local + index * 256 + part, 128)
            vectors = rows_of(wide[piece], index, slice(part, part + 128))
            source = mixed_own if piece == 0 else mixed.at[piece - 1]
            value = source[:, at_lane(index * 256 + part, 128)]
            normed = (value - centre_ref[...]) * rstd_ref[...]
            normed_ref[:, here] = as_low(normed)
            pad[8 : SEQ + 8] = (normed * vectors[2:3] + vectors[3:4]) * kept
            result = pad[4 : SEQ + 4] * vectors[4:5]
            for tap in range(1, 9):
                result = result + pad[4 + tap : SEQ + 4 + tap] * vectors[4 + tap : 5 + tap]
            depth[:, here] = as_low(result)

        def step(index, carry):
            one(index, 0, padded)
            one(index, 128, padded_two)
            return carry

        lax.fori_loop(0, local // 256, step, 0)


def masked_scores(queries, keys, valid, scale):
    return jnp.where(valid, dot_right(queries, keys) * scale, NEGATIVE)


def attention_forward_kernel(pieces, per, refs):
    (info, x1, depth, point, vec, project_w, output_w, mask), packed, outs = unpack(
        refs, [8, per * (pieces - 1), 8]
    )
    x2, a4, qkv, lse, attended, x3, a5, point_rest = outs
    width = x2.shape[1]
    local, channels = point.shape
    sep = dot(depth[:, 0:local], point[...])
    for piece in range(1, pieces):
        blocks = packed[(piece - 1) * per : piece * per]
        assemble(info, point_rest.at[piece - 1], blocks, width * local // (256 * per))
        sep = sep + dot(depth[:, piece * local : (piece + 1) * local], point_rest[piece - 1])
    x2[:, 0:channels] = x1[:, 0:channels] + sep + vec[10:11, channels : 2 * channels]
    x2[:, channels:width] = x1[:, channels:width]
    for row in spans(SEQ, STEP):
        normed, _ = normalize(x2[row])
        a4[row] = as_low(normed * vec[4:5] + vec[5:6])
    for col in spans(3 * width, 256):
        part = dot(a4[...], project_w[:, col])
        if col.start < width:
            part = part + vec[11:12, col]
        elif col.start >= 2 * width:
            part = part + vec[12:13, col.start - 2 * width : col.stop - 2 * width]
        qkv[:, col] = as_low(part)
    scale = (width // HEADS) ** (-0.5)
    lanes = lax.broadcasted_iota(jnp.int32, (SEQ, 128), 1)
    valid = jnp.broadcast_to(mask[0:1], (SEQ, SEQ)) > 0.5
    logs = jnp.zeros((SEQ, 128), F32)
    for pair in range(width // 128):
        at = pair * 128
        queries = qkv[:, at : at + 128]
        keys = qkv[:, width + at : width + at + 128]
        vals = qkv[:, 2 * width + at : 2 * width + at + 128]
        mixed = []
        for side in range(2):
            mine = (lanes < 64) if side == 0 else (lanes >= 64)
            scores = masked_scores(jnp.where(mine, queries, 0), keys, valid, scale)
            highest = jnp.max(scores, -1, keepdims=True)
            weights = jnp.exp(scores - highest)
            total = jnp.sum(weights, -1, keepdims=True)
            mixed.append(dot(as_low(weights * (1.0 / total)), vals))
            logs = jnp.where(lanes == 2 * pair + side, highest + jnp.log(total), logs)
        attended[:, at : at + 128] = as_low(jnp.where(lanes < 64, mixed[0], mixed[1]))
    lse[...] = logs
    x3[...] = x2[...] + dot(attended[...], output_w[...]) + vec[13:14]
    for row in spans(SEQ, STEP):
        normed, _ = normalize(x3[row])
        a5[row] = as_low(normed * vec[6:7] + vec[7:8])


def feed_piece(a5, top, expand, shrink, vectors, hidden, slope, d_expand):
    local = expand.shape[1]
    for col in spans(local, 256):
        pre = dot(a5[...], expand[:, col])
        pre = pre + rows_of(vectors, col.start // 256, slice(0, 256))[1:2]
        sigma = sigmoid(pre)
        hidden[:, col] = as_low(pre * sigma)
        slope[:, col] = sigma * (1.0 + pre * (1.0 - sigma))
    part = dot(hidden[...], shrink[...])
    for row in spans(local, 256):
        d_expand[:, row] = as_low(dot_right(top[...], shrink[row]) * slope[:, row])
    return part


def feed_grads(core, a5, top, hidden, d_expand, keep, send, first):
    local = hidden.shape[1]
    half, rows = a5.shape[1] // 2, local // 2
    for side, out in ((1 - core, send), (core, keep)):
        put(out, first, 2, 0, dot_left(hidden[:, at_lane(side * rows, rows)], top[...]))
        grad = dot_left(a5[:, at_lane(side * half, half)], d_expand[...])
        put(out, first, 2, a5.shape[1] * local // 1024, grad)


def feed_own_kernel(
    info, a5, top, expand, shrink, own, keep, send, shrunk, d_a5, grad_bias, hidden, slope, d_expand
):
    shrunk[...] = feed_piece(a5, top, expand, shrink, (own, 0), hidden, slope, d_expand)
    feed_grads(info[0], a5, top, hidden, d_expand, keep, send, 0)
    grad_bias[...] = jnp.broadcast_to(low_columns_sum(d_expand[...]), grad_bias.shape)
    d_a5[...] = dot_right(d_expand[...], expand[...])


def feed_kernel(pieces, per, refs):
    info, refs = refs[0], refs[1:]
    (a5, x3, top, vec, keep_own, send_own, shrunk_own, d_a5_own, bias_own), first, packed, outs, scratch = unpack(
        refs, [9, per * (pieces - 1), per * (pieces - 1), 6, 7]
    )
    output, keep, send, dx3, fixed, grad_bias = outs
    hidden, slope, d_expand, shrunk, d_a5, expand, shrink = scratch
    local, width = shrink.shape
    wide = vectors_of(None, first, per, width * local // (256 * per) + local // per)
    keep[0:2] = keep_own[...]
    send[0:2] = send_own[...]
    shrunk[...] = shrunk_own[...]
    d_a5[...] = d_a5_own[...]
    grad_bias[:, 0:local] = bias_own[...]
    for piece in range(1, pieces):
        blocks = packed[(piece - 1) * per : piece * per]
        assemble(info, expand, blocks, 0)
        assemble(info, shrink, blocks, width * local // (256 * per))
        shrunk[...] += feed_piece(
            a5, top, expand, shrink, wide[piece], hidden, slope, d_expand
        )
        feed_grads(info[0], a5, top, hidden, d_expand, keep, send, 2 * piece)
        cols = slice(piece * local, (piece + 1) * local)
        grad_bias[:, cols] = jnp.broadcast_to(low_columns_sum(d_expand[...]), (8, local))
        d_a5[...] += dot_right(d_expand[...], expand[...])
    for row in spans(SEQ, STEP):
        output[row] = as_low(x3[row] + shrunk[row] + vec[14:15])
    fixed[...] = jnp.zeros_like(fixed)
    for row in spans(SEQ, STEP):
        normed, rstd = normalize(x3[row])
        grad = d_a5[row]
        dx3[row] = top[row].astype(F32) + normalize_back(grad, normed, rstd, vec[6:7])
        fixed[6:7] += columns_sum(grad * normed)
        fixed[7:8] += columns_sum(grad)
    fixed[13:14] = low_columns_sum(top[...])


def attention_backward_kernel(
    info, dx3, attended, output_w, qkv, lse, mask, d_out, d_proj, d_att
):
    width = dx3.shape[1]
    d_out[...] = as_low(dx3[...])
    d_att[...] = as_low(dot_right(d_out[...], output_w[...]))
    scale = (width // HEADS) ** (-0.5)
    lanes = lax.broadcasted_iota(jnp.int32, (SEQ, 128), 1)
    valid = jnp.broadcast_to(mask[0:1], (SEQ, SEQ)) > 0.5
    for pair in range(width // 128):
        at = pair * 128
        queries = qkv[:, at : at + 128]
        keys = qkv[:, width + at : width + at + 128]
        vals = qkv[:, 2 * width + at : 2 * width + at + 128]
        grads = d_att[:, at : at + 128]
        parts = []
        for side in range(2):
            head = 2 * pair + side
            mine = (lanes < 64) if side == 0 else (lanes >= 64)
            scores = masked_scores(jnp.where(mine, queries, 0), keys, valid, scale)
            probs = jnp.exp(scores - lse[:, head : head + 1])
            d_vals = dot_left(as_low(probs), grads)
            d_probs = dot_right(jnp.where(mine, grads, 0), vals)
            weighted = jnp.sum(d_probs * probs, -1, keepdims=True)
            d_scores = as_low(probs * (d_probs - weighted))
            parts.append((dot(d_scores, keys) * scale, dot_left(d_scores, queries) * scale, d_vals))
        for kind in range(3):
            here = slice(kind * width + at, kind * width + at + 128)
            d_proj[:, here] = as_low(jnp.where(lanes < 64, parts[0][kind], parts[1][kind]))


def project_backward_kernel(
    info, dx3, attended, a4, d_out, d_proj, project_w, x2, vec, before, send, keep, dx2, d_sep, fixed
):
    width = x2.shape[1]
    half = width // 2
    core = info[0]
    fixed[...] = before[...]
    for side, out in ((1 - core, send), (core, keep)):
        here = at_lane(side * half, half)
        put(out, 0, 4, 0, dot_left(a4[:, here], d_proj[...]))
        put(out, 0, 4, 3 * width * half // 1024, dot_left(attended[:, here], d_out[...]))
    fixed[12:13] = low_columns_sum(d_out[...])
    fixed[10:11] = low_columns_sum(d_proj[:, :width])
    fixed[11:12] = low_columns_sum(d_proj[:, 2 * width :])
    dx2[...] = dot_right(d_proj[...], project_w[...])
    for row in spans(SEQ, STEP):
        normed, rstd = normalize(x2[row])
        grad = dx2[row]
        dx2[row] = dx3[row] + normalize_back(grad, normed, rstd, vec[4:5])
        fixed[4:5] += columns_sum(grad * normed)
        fixed[5:6] += columns_sum(grad)
    channels = d_sep.shape[1]
    d_sep[...] = as_low(dx2[:, :channels])
    fixed[14:15, channels : 2 * channels] = low_columns_sum(d_sep[...])


def inner_backward_kernel(pieces, per, refs):
    info, refs = refs[0], refs[1:]
    (
        (d_sep, depth, normed_ref, slope_ref, rstd_ref, a2, bias_before, point, point_rest),
        (left, left_rest, own, keep_mask),
        packed,
        outs,
        scratch,
    ) = unpack(refs, [9, 4, per * (pieces - 1), 5, 7])
    keep, send, d_a2, d_right, grads = outs
    d_depth, padded, padded_two, d_left, first_ref, second_ref, sums = scratch
    local = left.shape[1]
    inner = local * pieces
    core, offset = info[0], info[1]
    rows = local // 2
    half = a2.shape[1] // 2
    wide = vectors_of(own, packed, per, a2.shape[1] * local // (256 * per) + local // per)
    for piece in range(pieces):
        weights = point if piece == 0 else point_rest.at[piece - 1]
        for row in spans(local, 256):
            back = dot_right(d_sep[...], weights[row])
            index = (piece * local + row.start) // 128
            d_depth[index] = back[:, 0:128]
            d_depth[index + 1] = back[:, 128:256]
    first_ref[...] = jnp.zeros_like(first_ref)
    second_ref[...] = jnp.zeros_like(second_ref)
    for pad in (padded, padded_two):
        pad[0:8] = jnp.zeros((8, 128), F32)
        pad[SEQ + 8 : SEQ + 16] = jnp.zeros((8, 128), F32)
    grads[...] = jnp.zeros_like(grads)
    grads[1:2] = bias_before[0:1]
    kept = keep_mask[:, 0:1]
    for piece in range(pieces):

        def one(pair, part, pad):
            here = at_lane(piece * local + pair * 256 + part, 128)
            index = piece * (local // 128) + 2 * pair + part // 128
            vectors = rows_of(wide[piece], pair, slice(part, part + 128))
            normed = normed_ref[:, here].astype(F32)
            normal = (normed * vectors[2:3] + vectors[3:4]) * kept
            pad[8 : SEQ + 8] = d_depth[index]
            result = pad[12 : SEQ + 12] * vectors[4:5]
            sums[2, :, here] = eighths_sum(normal * pad[12 : SEQ + 12])
            for tap in range(1, 9):
                shifted = pad[12 - tap : SEQ + 12 - tap]
                result = result + shifted * vectors[4 + tap : 5 + tap]
                sums[2 + tap, :, here] = eighths_sum(normal * shifted)
            result = result * kept
            sums[0, :, here] = eighths_sum(result * normed)
            sums[1, :, here] = eighths_sum(result)
            scaled = result * vectors[2:3]
            first_ref[...] += scaled
            second_ref[...] += scaled * normed
            d_depth[index] = scaled

        def step(index, carry):
            one(index, 0, padded)
            one(index, 128, padded_two)
            return carry

        lax.fori_loop(0, local // 256, step, 0)
    for col in spans(inner, 512):
        grads[2:13, col] = jnp.sum(sums[:, :, col], 1)
    first_ref[...] = jnp.broadcast_to(
        jnp.sum(first_ref[...], 1, keepdims=True) * (1.0 / inner), first_ref.shape
    )
    second_ref[...] = jnp.broadcast_to(
        jnp.sum(second_ref[...], 1, keepdims=True) * (1.0 / inner), second_ref.shape
    )

    def back(index, carry):
        here = at_lane(index * 128, 128)
        normed = normed_ref[:, here].astype(F32)
        d_mixed = rstd_ref[...] * (
            d_depth[index] - first_ref[...] - normed * second_ref[...]
        )
        d_depth[index] = d_mixed
        d_left[:, here] = as_low(d_mixed * slope_ref[:, here].astype(F32))
        return carry

    lax.fori_loop(0, inner // 128, back, 0)
    for part in range(d_right.shape[1] // 128):
        d_right[:, part * 128 : (part + 1) * 128] = d_depth[offset // 128 + part]
    for piece in range(pieces):
        base = piece * local
        cols = slice(base, base + local)
        for side, out in ((1 - core, send), (core, keep)):
            grad = dot_left(a2[:, at_lane(side * half, half)], d_left[:, cols])
            put(out, 2 * piece, 2, 0, grad)
            grad = dot_left(depth[:, at_lane(base + side * rows, rows)], d_sep[...])
            put(out, 2 * piece, 2, half * local // 512, grad)
        grads[0:1, cols] = low_columns_sum(d_left[:, cols])
        if piece == 0:
            d_a2[...] = dot_right(d_left[:, cols], left[...])
        else:
            d_a2[...] += dot_right(d_left[:, cols], left_rest[piece - 1])


def last_kernel(
    info, d_a2_left, d_right, right_pre, conv_w, a2, x1, dx2, values, gates, a1, gated_w, x_ref, vec, kept, before, wide_sums,
    send, keep, input_grad, fixed, shifted, d_a2, d_gated, rows_ref
):
    width = x1.shape[1]
    half = width // 2
    channels = right_pre.shape[1]
    core = info[0]
    fixed[...] = before[...]
    pre = right_pre[...]
    sigma = sigmoid(pre)
    low = as_low(d_right[...] * (sigma * (1.0 + pre * (1.0 - sigma))))
    fixed[14:15, 0:channels] = low_columns_sum(low)
    wide = low.astype(F32)
    rows = lax.broadcasted_iota(jnp.int32, wide.shape, 0)
    shifted[:, 0:channels] = as_low(
        jnp.where(rows == SEQ - 1, 0.0, pltpu.roll(wide, SEQ - 1, 0))
    )
    shifted[:, channels : 2 * channels] = low
    shifted[:, 2 * channels :] = as_low(jnp.where(rows == 0, 0.0, pltpu.roll(wide, 1, 0)))
    total = d_a2_left[...]
    for tap in range(3):
        total = total + dot_right(shifted[:, tap * channels : (tap + 1) * channels], conv_w[tap])
    d_a2[...] = total
    for row in spans(SEQ, STEP):
        normed, rstd = normalize(x1[row])
        grad = d_a2[row] * kept[row, 0:1]
        fixed[2:3] += columns_sum(grad * normed)
        fixed[3:4] += columns_sum(grad)
        dx1 = dx2[row] + normalize_back(grad, normed, rstd, vec[2:3])
        input_grad[row] = dx1
        gate = gates[row]
        scaled = dx1 * gate
        d_gated[row, 0:width] = as_low(scaled)
        d_gated[row, width:] = as_low(scaled * values[row] * (1.0 - gate))
    for side, out in ((1 - core, send), (core, keep)):
        here = at_lane(side * half, half)
        put(out, 0, 4, 0, dot_left(a1[:, here], d_gated[...]))
        put(out, 0, 4, half * width // 512, dot_left(a2[:, here], shifted[...]))
    sums = low_columns_sum(d_gated[...])
    fixed[8:9] = sums[:, 0:width]
    fixed[9:10] = sums[:, width:]
    d_a2[...] = dot_right(d_gated[...], gated_w[...])
    for row in spans(SEQ, STEP):
        normed, rstd = normalize(x_ref[row].astype(F32))
        grad = d_a2[row]
        fixed[0:1] += columns_sum(grad * normed)
        fixed[1:2] += columns_sum(grad)
        input_grad[row] += normalize_back(grad, normed, rstd, vec[0:1])
    pack_small(info, wide_sums, fixed, send, keep, rows_ref)


def pack_small(info, wide, fixed, send, keep, rows_ref):
    if rows_ref is None:
        return
    pieces = lax.axis_size("mp")
    local = wide.shape[1] // pieces
    parts = local // 256
    rows_ref[...] = jnp.zeros_like(rows_ref)
    for piece in range(pieces):
        owner = jnp.bitwise_xor(info[1] // local, piece)
        for part in range(parts):
            spot = pl.multiple_of((owner * parts + part) * 16, 16)
            at = piece * local + part * 256
            rows_ref[pl.ds(spot, 16)] = wide[:, at : at + 256]
    base = wide.shape[1] // 16
    for part in range(fixed.shape[1] // 256):
        rows_ref[base + part * 16 : base + (part + 1) * 16] = fixed[:, part * 256 : (part + 1) * 256]
    count = rows_ref.shape[0] // 2
    offset = send.shape[1] - count // 4
    for side, out in ((1 - info[0], send), (info[0], keep)):
        put(out, 0, 4, offset, rows_ref[pl.ds(pl.multiple_of(side * count, 16), count)])


def own_place(count):
    core = lax.axis_index("dp") % 2
    if count == 2:
        return core
    y = lax.axis_index("dp") // 2 % 2
    near = lax.axis_index("dp") // 4 % 2
    return 2 * core + (1 - core) * y + core * near


def cut(weights, vectors, per, link):
    shapes = [(item.shape[0] // per, item.shape[1]) for item in weights]
    total = sum(rows * columns // 256 for rows, columns in shapes)
    local = weights[0].shape[1]
    small = local // 16 if vectors else 0
    chained = [] if link is None else [link]

    def kernel(*refs):
        refs = list(refs)
        sources = [refs.pop(0) for _ in weights]
        small_in = [refs.pop(0) for _ in vectors]
        for _ in chained:
            refs.pop(0)
        packed = refs.pop(0)
        own = refs.pop(0) if vectors else None
        sems, held = refs
        place = own_place(per)
        copies = []
        offset = 0
        for source, (rows, columns) in zip(sources, shapes):
            here = pl.ds(pl.multiple_of(place * rows, 16), rows)
            for part in range(columns // 256):
                copy = pltpu.make_async_copy(
                    source.at[here, pl.ds(part * 256, 256)],
                    packed.at[pl.ds(offset, rows)],
                    sems.at[len(copies)],
                )
                copy.start()
                copies.append(copy)
                offset += rows
        if vectors:
            held[...] = jnp.zeros_like(held)
            for part in range(local // 256):
                lanes = slice(part * 256, (part + 1) * 256)
                row = 0
                for item in small_in:
                    count = item.shape[0] if len(item.shape) == 2 else 1
                    held[row : row + count] = item[..., lanes].astype(F32).reshape(count, 256)
                    row += count
                chunk = as_low(held[...])
                own[part * 16 : (part + 1) * 16] = chunk
                packed[total + part * 16 : total + (part + 1) * 16] = chunk
        for copy in copies:
            copy.wait()

    outs = [shaped((total + small, 256), LOW)]
    if vectors:
        outs.append(shaped((small, 256), LOW))
    return pl.pallas_call(
        kernel,
        out_shape=outs,
        in_specs=[pl.BlockSpec(memory_space=pl.ANY) for _ in weights]
        + [pl.BlockSpec(memory_space=pltpu.VMEM) for _ in vectors]
        + [pl.BlockSpec(memory_space=pl.ANY) for _ in chained],
        out_specs=[pl.BlockSpec(memory_space=pltpu.VMEM) for _ in outs],
        scratch_shapes=[
            pltpu.SemaphoreType.DMA((sum(columns // 256 for _, columns in shapes),)),
            pltpu.VMEM((16, 256), F32),
        ],
    )(*weights, *vectors, *chained)


def flat_swap(values, partner):
    count = lax.axis_size("dp") * lax.axis_size("mp")
    return lax.ppermute(values, ("dp", "mp"), [(at, partner(at)) for at in range(count)])


PARTNERS = {
    "core": lambda at: at ^ 2,
    "first": lambda at: at ^ (4 if at & 2 else 1),
    "second": lambda at: at ^ (1 if at & 2 else 4),
    "x": lambda at: at ^ 1,
    "y": lambda at: at ^ 4,
    "near": lambda at: at ^ 8,
    "far": lambda at: at ^ 16,
    "hop": lambda at: at ^ (8 if at & 2 else 4),
}
LENGTH_FIRST_STEPS = [
    ("half_near", "near"),
    ("quarter", "first"),
    ("half_mix", "second"),
    ("sum", "far"),
    ("sum", "second"),
    ("join_mix", "first"),
    ("spread", "near"),
    ("join_near", "core"),
    ("final", None),
]
INNER_STEPS = [
    ("quarter", "first"),
    ("half_mix", "second"),
    ("half_near", "near"),
    ("sum", "far"),
    ("sum", "near"),
    ("join_near", "y"),
    ("join_y", "core"),
    ("final", None),
]
SHARED_STEPS = [
    ("quarter", "first"),
    ("half_mix", "second"),
    ("half_near", "near"),
    ("sum", "far"),
    ("sum", "near"),
    ("join_near", "second"),
    ("join_mix", "first"),
    ("spread", "core"),
    ("final", None),
]


PLAN = (
    "p",
    "d",
    "a",
    "p",
    "c",
    "a",
    "d",
    "d",
    "p",
    "a",
    "c",
    "d",
    "a",
    "c",
    "dp",
    "c",
    "d",
    "p",
    "d",
    "c",
    "p",
    "a",
    "d",
    "c",
    "!d",
    "p",
    "!a",
    "!p",
    "c",
    "!c",
)


class Stream:
    def __init__(self, inner, mine, other, parts, steps=None):
        self.inner = inner
        self.mine = mine
        self.flight = flat_swap(other, PARTNERS["core"])
        self.steps = list(steps or (INNER_STEPS if inner else SHARED_STEPS))
        self.parts = parts


def advance_kernel(jobs, refs):
    info, refs = refs[0], refs[1:]
    core, y, near = info[0], info[4], info[5]
    ins, outs = list(refs[: 2 * len(jobs)]), list(refs[2 * len(jobs) :])
    for inner, step, parts in jobs:
        mine, flight = ins.pop(0), ins.pop(0)
        x = 0 if inner else info[3]
        mix = core * x + (1 - core) * y

        def added(spot):
            return as_low(mine[spot].astype(F32) + flight[spot].astype(F32))

        if step == "quarter":
            keep, send = outs.pop(0), outs.pop(0)
            for at in range(2):
                send[at] = added(core * (2 * at + 1 - y) + (1 - core) * (2 * (1 - x) + at))
                keep[at] = added(core * (2 * at + y) + (1 - core) * (2 * x + at))
        elif step == "half_mix":
            keep, send = outs.pop(0), outs.pop(0)
            send[0] = added(1 - mix)
            keep[0] = added(mix)
        elif step == "half_near":
            keep, send = outs.pop(0), outs.pop(0)
            rows = keep.shape[1]
            for out, side in ((send, 1 - near), (keep, near)):
                here = pl.ds(pl.multiple_of(side * rows, 16), rows)
                for at in range(keep.shape[0]):
                    out[at] = as_low(mine[at, here].astype(F32) + flight[at, here].astype(F32))
        elif step == "sum":
            outs.pop(0)[0] = added(0)
        elif step == "join_near":
            out = outs.pop(0)
            rows = mine.shape[1]
            for source, side in ((mine, near), (flight, 1 - near)):
                for at in range(mine.shape[0]):
                    out[at, pl.ds(pl.multiple_of(side * rows, 16), rows)] = source[at]
        elif step in ("join_y", "join_mix"):
            out = outs.pop(0)
            side = y if step == "join_y" else mix
            out[side] = mine[0]
            out[1 - side] = flight[0]
        elif step == "spread":
            out = outs.pop(0)
            for at in range(2):
                out[core * (2 * at + y) + (1 - core) * (2 * x + at)] = mine[at]
                out[core * (2 * at + 1 - y) + (1 - core) * (2 * (1 - x) + at)] = flight[at]


def finish_kernel(parts, small, refs):
    info, mine, flight, refs = refs[0], refs[1], refs[2], list(refs[3:])
    core = info[0]
    outs = [refs.pop(0) for _ in parts]
    small_outs = [refs.pop(0) for _ in range(11)] if small else []
    link = refs.pop(0)
    link[...] = jnp.zeros_like(link)
    held = [refs.pop(0) for _ in parts]
    smalls = [refs.pop(0) for _ in small_outs]
    sems = refs.pop(0)
    copies = []
    quarters = mine.shape[0]
    for at, (offset, rows, shape) in enumerate(parts):
        target, columns, deep = held[at], shape[-1] // 256, len(shape) == 3
        for half, (source, side) in enumerate(((mine, core), (flight, 1 - core))):
            for quarter in range(quarters):
                here = slice(quarter * rows, (quarter + 1) * rows)
                for part in range(columns * (shape[0] if deep else 1)):
                    row = offset + part * rows
                    block = source[quarter, row : row + rows].astype(F32)
                    if deep:
                        target[half, part, here] = block
                    else:
                        target[half, here, part * 256 : (part + 1) * 256] = block
            spot = pl.ds(pl.multiple_of(side * quarters * rows, 16), quarters * rows)
            spot = (slice(None), spot) if deep else (spot,)
            copies.append(
                pltpu.make_async_copy(target.at[half], outs[at].at[spot], sems.at[len(copies)])
            )
            copies[-1].start()
    if small:
        total = refs.pop(0)
        offset, rows = small
        for source, side in ((mine, core), (flight, 1 - core)):
            for quarter in range(mine.shape[0]):
                spot = (side * mine.shape[0] + quarter) * rows
                total[pl.ds(pl.multiple_of(spot, 16), rows)] = source[
                    quarter, offset : offset + rows
                ].astype(F32)
        norm, gated, left, conv, inner, depth, point, project, output, expand, shrink = smalls
        local, width = left.shape[-1], output.shape[-1]
        for part in range(local // 256):
            lanes = slice(part * 256, (part + 1) * 256)
            spot = (info[1] // local * (local // 256) + part) * 16
            block = total[pl.ds(pl.multiple_of(spot, 16), 16)]
            left[:, lanes] = block[0:1]
            expand[:, lanes] = block[1:2]
            inner[:, lanes] = block[2:4]
            depth[:, lanes] = block[4:13]
        for part in range(width // 256):
            lanes = slice(part * 256, (part + 1) * 256)
            base = local * 2 // 16 + part * 16
            block = total[base : base + 16]
            for at in range(4):
                norm[at, :, lanes] = block[2 * at : 2 * at + 2]
            gated[:, lanes] = block[8:9]
            gated[:, width + part * 256 : width + (part + 1) * 256] = block[9:10]
            project[:, lanes] = block[10:12]
            output[:, lanes] = block[12:13]
            shrink[:, lanes] = block[13:14]
            (conv if part == 0 else point)[...] = block[14:15]
        for source, target in zip(smalls, small_outs):
            copies.append(pltpu.make_async_copy(source, target, sems.at[len(copies)]))
            copies[-1].start()
    for copy in copies:
        copy.wait()


def finish(chain, stream, small):
    parts = stream.parts
    shapes = [shaped(shape, F32) for _, _, shape in parts]
    scratch = [
        pltpu.VMEM((2,) + shape[:-2] + (shape[-2] // 2, shape[-1]), F32) for _, _, shape in parts
    ]
    names = []
    if small:
        names = [shaped(shape, F32) for shape in small[1]]
    scratch += [pltpu.VMEM(item.shape, F32) for item in names]
    scratch.append(pltpu.SemaphoreType.DMA((2 * len(parts) + len(names),)))
    if small:
        scratch.append(pltpu.VMEM((256, 256), F32))
    stream.mine = chain.run(
        lambda *refs: finish_kernel(parts, small[0] if small else None, refs),
        shapes + names + [shaped((8, 128), F32)],
        [stream.mine, stream.flight],
        scratch,
        ADV,
        len(parts) + len(names),
    )


def advance(chain, streams):
    jobs, ins, outs = [], [], []
    for stream in streams:
        step = stream.steps[0][0]
        jobs.append((stream.inner, step, stream.parts))
        ins += [stream.mine, stream.flight]
        lead, rows, columns = stream.mine.shape
        if step in ("quarter", "half_mix"):
            outs += [shaped((lead // 2, rows, columns), LOW)] * 2
        elif step == "half_near":
            outs += [shaped((lead, rows // 2, columns), LOW)] * 2
        elif step == "sum":
            outs.append(shaped((lead, rows, columns), LOW))
        elif step == "join_near":
            outs.append(shaped((lead, rows * 2, columns), LOW))
        else:
            outs.append(shaped((lead * 2, rows, columns), LOW))
    results = list(chain.run(lambda *refs: advance_kernel(jobs, refs), outs, ins, [], ADV))
    for stream in streams:
        step, partner = stream.steps.pop(0)
        stream.mine = results.pop(0)
        if step in ("quarter", "half_mix", "half_near"):
            stream.flight = flat_swap(results.pop(0), PARTNERS[partner])
        else:
            stream.flight = flat_swap(stream.mine, PARTNERS[partner])


def opened(packed, first, count, offset, rows, columns):
    parts = [
        packed[first : first + count, offset + at * rows : offset + (at + 1) * rows]
        for at in range(columns // 256)
    ]
    return jnp.concatenate(parts, 2).reshape(count * rows, columns)


class Weights:
    def __init__(self, packed, per):
        pieces = [packed]
        for bit in bits_of("mp"):
            pieces = pieces + [swap(item, "mp", bit) for item in pieces]
        self.blocks = [[item] for item in pieces[1:]]
        self.per = per

    def hop(self, after):
        if self.per == 4:
            for blocks in self.blocks:
                blocks[0], _ = lax.optimization_barrier((blocks[0], after))
                blocks.append(flat_swap(blocks[0], PARTNERS["hop"]))

    def share(self, after):
        found = []
        for blocks in self.blocks:
            held = [lax.optimization_barrier((item, after))[0] for item in blocks]
            found += held + [swap(item, "dp", 1) for item in held]
        return found


def finish_shared(mine, other, order):
    own = bit_of("dp", 1)
    values = add_low(mine, swap(other, "dp", 1))
    held = [("dp", 1, own)]
    for axis, bit in order[:-1]:
        own = bit_of(axis, bit)
        mine, other = split(values, own)
        values = add_low(mine, swap(other, axis, bit))
        held.append((axis, bit, own))
    axis, bit = order[-1]
    values = add_low(values, swap(values, axis, bit))
    for axis, bit, own in reversed(held):
        values = join(values, swap(values, axis, bit), own)
    return values.astype(F32)


def finish_inner(mine, other, order):
    values = add_low(mine, swap(other, "dp", 1))
    pieces = [values[at] for at in range(values.shape[0])]
    held = [("dp", 1, bit_of("dp", 1))]
    for axis, bit in order[:-1]:
        if axis == "mp":
            keep_count = len(pieces) // 2
            moved = [swap(item, axis, bit) for item in pieces[keep_count:]]
            pieces = [add_low(one, two) for one, two in zip(pieces[:keep_count], moved)]
            continue
        own = bit_of(axis, bit)
        parts = [split(item, own) for item in pieces]
        pieces = [add_low(mine, swap(other, axis, bit)) for mine, other in parts]
        held.append((axis, bit, own))
    axis, bit = order[-1]
    values = add_low(pieces[0], swap(pieces[0], axis, bit))
    for axis, bit, own in reversed(held):
        values = join(values, swap(values, axis, bit), own)
    return values.astype(F32)


def body(
    cell_input,
    lengths,
    out_grad,
    norm_params,
    gated_weight,
    gated_bias,
    left_weight,
    left_bias,
    conv_weight,
    conv_bias,
    inner_norm,
    depth_weight,
    point_weight,
    point_bias,
    project_weight,
    project_bias,
    output_weight,
    output_bias,
    expand_weight,
    expand_bias,
    shrink_weight,
    shrink_bias,
):
    width = cell_input.shape[1]
    channels = conv_weight.shape[2]
    local = left_weight.shape[1]
    pieces = lax.axis_size("mp")
    inner = local * pieces
    tokens = cell_input.shape[0]
    assert tokens == SEQ
    tuned = lax.axis_size("dp") == 16 and pieces == 2
    mp_bits = bits_of("mp")[::-1]
    dp_bits = bits_of("dp")[1:]
    mp_first = [("mp", bit) for bit in mp_bits] + [("dp", bit) for bit in dp_bits]
    core = bit_of("dp", 1)
    chain = Chain(local)

    def inner_rows(size):
        return (2 * pieces, size // 1024, 256)


    per = 4 if tuned else 2
    vectors = [left_bias, expand_bias, inner_norm, depth_weight]
    packed, own = cut([left_weight, point_weight], vectors, per, None)
    early = Weights(packed, per)
    (packed,) = cut([expand_weight, shrink_weight], [], per, own)
    late = Weights(packed, per)
    chain.link = packed
    a1, values, gates, x1, a2, right_pre, vec, kept, valid, *parts, right = chain.run(
        pre_kernel,
        [
            shaped((tokens, width), LOW),
            shaped((tokens, width), F32),
            shaped((tokens, width), F32),
            shaped((tokens, width), F32),
            shaped((tokens, width), LOW),
            shaped((tokens, channels), F32),
            shaped((16, width), F32),
            shaped((tokens, 128), F32),
            shaped((8, tokens), F32),
            shaped((tokens, local), F32),
            shaped((tokens, local), LOW),
            shaped((tokens, 128), F32),
            shaped((tokens, 128), F32),
            shaped((tokens, channels), LOW),
        ],
        [
            lengths,
            left_weight,
            own,
            cell_input,
            gated_weight,
            conv_weight,
            norm_params,
            gated_bias,
            conv_bias,
            point_bias,
            project_bias,
            output_bias,
            shrink_bias,
        ],
        [],
        int(2.2e9 * EARLY),
    )
    early.hop(right)
    early_blocks = early.share(right)
    normed, slope, depth, rstd, left_rest = chain.run(
        lambda *refs: inner_forward_kernel(pieces, per, refs),
        [
            shaped((tokens, inner), LOW),
            shaped((tokens, inner), LOW),
            shaped((tokens, inner), LOW),
            shaped((tokens, 128), F32),
            shaped((pieces - 1, width, local), LOW),
        ],
        [a2, right, *parts, own, kept] + early_blocks,
        [
            pltpu.VMEM((pieces - 1, tokens, local), F32),
            pltpu.VMEM((tokens, 128), F32),
            pltpu.VMEM((tokens, 128), F32),
            pltpu.VMEM((tokens, 128), F32),
            pltpu.VMEM((tokens + 16, 128), F32),
            pltpu.VMEM((tokens + 16, 128), F32),
        ],
        int(6.5e9 * EARLY),
    )
    late.hop(rstd)
    x2, a4, qkv, lse, attended, x3, a5, point_rest = chain.run(
        lambda *refs: attention_forward_kernel(pieces, per, refs),
        [
            shaped((tokens, width), F32),
            shaped((tokens, width), LOW),
            shaped((tokens, 3 * width), LOW),
            shaped((tokens, 128), F32),
            shaped((tokens, width), LOW),
            shaped((tokens, width), F32),
            shaped((tokens, width), LOW),
            shaped((pieces - 1, local, channels), LOW),
        ],
        [x1, depth, point_weight, vec, project_weight, output_weight, valid]
        + early_blocks,
        [],
        int(4.4e9 * EARLY),
    )
    keep_own, send_own, shrunk_own, d_a5_own, bias_own = chain.run(
        feed_own_kernel,
        [
            shaped((2, 2 * local * width // 1024, 256), LOW),
            shaped((2, 2 * local * width // 1024, 256), LOW),
            shaped((tokens, width), F32),
            shaped((tokens, width), F32),
            shaped((8, local), F32),
        ],
        [a5, out_grad, expand_weight, shrink_weight, own],
        [
            pltpu.VMEM((tokens, local), LOW),
            pltpu.VMEM((tokens, local), F32),
            pltpu.VMEM((tokens, local), LOW),
        ],
        int(3e9 * EARLY),
    )
    late_blocks = late.share(bias_own)
    cell_output, feed_keep, feed_send, dx3, fixed, expand_sum = chain.run(
        lambda *refs: feed_kernel(pieces, per, refs),
        [
            shaped((tokens, width), LOW),
            shaped(inner_rows(2 * local * width), LOW),
            shaped(inner_rows(2 * local * width), LOW),
            shaped((tokens, width), F32),
            shaped((16, width), F32),
            shaped((8, inner), F32),
        ],
        [a5, x3, out_grad, vec, keep_own, send_own, shrunk_own, d_a5_own, bias_own]
        + early_blocks
        + late_blocks,
        [
            pltpu.VMEM((tokens, local), LOW),
            pltpu.VMEM((tokens, local), F32),
            pltpu.VMEM((tokens, local), LOW),
            pltpu.VMEM((tokens, width), F32),
            pltpu.VMEM((tokens, width), F32),
            pltpu.VMEM((width, local), LOW),
            pltpu.VMEM((local, width), LOW),
        ],
        int(8e9 * SCALE),
    )
    if tuned:
        fee = Stream(
            True,
            feed_keep,
            feed_send,
            [
                (0, local // 4, (local, width)),
                (width * local // 1024, width // 4, (width, local)),
            ],
        )
    d_out, d_proj = chain.run(
        attention_backward_kernel,
        [shaped((tokens, width), LOW), shaped((tokens, 3 * width), LOW)],
        [dx3, attended, output_weight, qkv, lse, valid],
        [pltpu.VMEM((tokens, width), LOW)],
        int(5e9 * SCALE),
    )
    if tuned:
        advance(chain, [fee])
    proj_send, proj_keep, dx2, d_sep, fixed = chain.run(
        project_backward_kernel,
        [
            shaped((4, width * width // 512, 256), LOW),
            shaped((4, width * width // 512, 256), LOW),
            shaped((tokens, width), F32),
            shaped((tokens, channels), LOW),
            shaped((16, width), F32),
        ],
        [dx3, attended, a4, d_out, d_proj, project_weight, x2, vec, fixed],
        [],
        int(3e9 * SCALE),
    )
    if tuned:
        pro = Stream(
            False,
            proj_keep,
            proj_send,
            [
                (0, width // 8, (width, 3 * width)),
                (3 * width * width // 2048, width // 8, (width, width)),
            ],
            LENGTH_FIRST_STEPS,
        )
        advance(chain, [pro])
    left_keep, left_send, d_a2, d_right, wide_sums = chain.run(
        lambda *refs: inner_backward_kernel(pieces, per, refs),
        [
            shaped(inner_rows(local * (width + channels)), LOW),
            shaped(inner_rows(local * (width + channels)), LOW),
            shaped((tokens, width), F32),
            shaped((tokens, channels), F32),
            shaped((16, inner), F32),
        ],
        [
            d_sep,
            depth,
            normed,
            slope,
            rstd,
            a2,
            expand_sum,
            point_weight,
            point_rest,
            left_weight,
            left_rest,
            own,
            kept,
        ]
        + early_blocks,
        [
            pltpu.VMEM((inner // 128, tokens, 128), F32),
            pltpu.VMEM((tokens + 16, 128), F32),
            pltpu.VMEM((tokens + 16, 128), F32),
            pltpu.VMEM((tokens, inner), LOW),
            pltpu.VMEM((tokens, 128), F32),
            pltpu.VMEM((tokens, 128), F32),
            pltpu.VMEM((11, 8, inner), F32),
        ],
        int(11.5e9 * SCALE),
    )
    if tuned:
        lef = Stream(
            True,
            left_keep,
            left_send,
            [
                (0, width // 4, (width, local)),
                (width * local // 1024, local // 4, (local, channels)),
            ],
        )
        advance(chain, [fee])
    small = 32 if tuned else 0
    last_rows = width * (2 * width + 3 * channels) // 2048 + small
    last_send, last_keep, input_grad, fixed = chain.run(
        last_kernel if tuned else lambda *refs: last_kernel(*refs, None),
        [
            shaped((4, last_rows, 256), LOW),
            shaped((4, last_rows, 256), LOW),
            shaped((tokens, width), F32),
            shaped((16, width), F32),
        ],
        [
            d_a2,
            d_right,
            right_pre,
            conv_weight,
            a2,
            x1,
            dx2,
            values,
            gates,
            a1,
            gated_weight,
            cell_input,
            vec,
            kept,
            fixed,
            wide_sums,
        ],
        [
            pltpu.VMEM((tokens, 3 * channels), LOW),
            pltpu.VMEM((tokens, width), F32),
            pltpu.VMEM((tokens, 2 * width), LOW),
        ]
        + ([pltpu.VMEM((8 * small, 256), F32)] if tuned else []),
        int(4.0e9 * SCALE),
    )
    if tuned:
        lat = Stream(
            False,
            last_keep,
            last_send,
            [
                (0, width // 8, (width, 2 * width)),
                (width * width // 1024, width // 8, (3, width, channels)),
            ],
        )
        groups = {"a": [fee], "p": [pro], "c": [lef], "d": [lat]}
        small_shapes = [
            (4, 2, width),
            (1, 2 * width),
            (1, local),
            (1, channels),
            (2, local),
            (9, local),
            (1, channels),
            (2, width),
            (1, width),
            (1, local),
            (1, width),
        ]
        small_part = ((last_rows - small, small), small_shapes)
        for names in PLAN:
            if names[0] == "!":
                stream = groups[names[1]][0]
                finish(chain, stream, small_part if names == "!d" else None)
            else:
                advance(chain, [groups[name][0] for name in names])
        (grad_shrink, grad_expand, _), (grad_left, grad_point, _) = fee.mine, lef.mine
        (grad_proj, grad_out, _), (grad_gated, grad_conv) = pro.mine, lat.mine[:2]
        smalls = [
            item.reshape(-1) if item.shape[0] == 1 else item for item in lat.mine[2:-1]
        ]
    else:

        def whole(keep, send, offset, rows, columns):
            both = [
                jnp.stack([opened(item, 2 * at, 2, offset, rows, columns) for at in range(pieces)])
                for item in (keep, send)
            ]
            return finish_inner(both[0], both[1], mp_first)

        def shared(keep, send, offset, rows, columns):
            both = [opened(item, 0, 4, offset, rows, columns) for item in (keep, send)]
            return finish_shared(both[0], both[1], mp_first)

        eighth = width // 8
        grad_shrink = whole(feed_keep, feed_send, 0, local // 4, width)
        grad_expand = whole(
            feed_keep, feed_send, width * local // 1024, width // 4, local
        )
        grad_left = whole(left_keep, left_send, 0, width // 4, local)
        grad_point = whole(left_keep, left_send, width * local // 1024, local // 4, channels)
        grad_proj = shared(proj_keep, proj_send, 0, eighth, 3 * width)
        grad_out = shared(proj_keep, proj_send, 6 * eighth, eighth, width)
        grad_gated = shared(last_keep, last_send, 0, eighth, 2 * width)
        grad_conv = jnp.stack(
            [shared(last_keep, last_send, (4 + at) * eighth, eighth, channels) for at in range(3)]
        )
        chunks = [wide_sums[:, at : at + local] for at in range(0, inner, local)]
        for bit in mp_bits:
            count = len(chunks) // 2
            moved = [swap(item, "mp", bit) for item in chunks[count:]]
            chunks = [one + two for one, two in zip(chunks[:count], moved)]
            fixed = fixed + swap(fixed, "mp", bit)
        wide_total = chunks[0]
        for bit in bits_of("dp"):
            fixed = fixed + swap(fixed, "dp", bit)
            wide_total = wide_total + swap(wide_total, "dp", bit)
        smalls = [
            fixed[0:8].reshape(4, 2, width),
            fixed[8:10].reshape(2 * width),
            wide_total[0],
            fixed[14, :channels],
            wide_total[2:4],
            wide_total[4:13],
            fixed[14, channels:],
            fixed[10:12],
            fixed[12],
            wide_total[1],
            fixed[13],
        ]
    return (
        cell_output,
        input_grad,
        smalls[0],
        grad_gated,
        smalls[1],
        grad_left,
        smalls[2],
        grad_conv,
        smalls[3],
        smalls[4],
        smalls[5],
        grad_point,
        smalls[6],
        grad_proj,
        smalls[7],
        grad_out,
        smalls[8],
        grad_expand,
        smalls[9],
        grad_shrink,
        smalls[10],
    )


def solution(mesh):
    return jax.shard_map(
        body,
        mesh=mesh,
        in_specs=(
            P(("dp", "mp"), None),
            P(("dp", "mp")),
            P(("dp", "mp"), None),
            P(),
            P(),
            P(),
            P(None, "mp"),
            P("mp"),
            P(),
            P(),
            P(None, "mp"),
            P(None, "mp"),
            P("mp", None),
            P(),
            P(),
            P(),
            P(),
            P(),
            P(None, "mp"),
            P("mp"),
            P("mp", None),
            P(),
        ),
        out_specs=(
            P(("dp", "mp"), None),
            P(("dp", "mp"), None),
            P(),
            P(),
            P(),
            P(None, "mp"),
            P("mp"),
            P(),
            P(),
            P(None, "mp"),
            P(None, "mp"),
            P("mp", None),
            P(),
            P(),
            P(),
            P(),
            P(),
            P(None, "mp"),
            P("mp"),
            P("mp", None),
            P(),
        ),
        check_vma=False,
    )
```
